32 devices in a mesh: section: 2 (over core), dp: 8 (over z, x), tensor: 2 (over y).
Axes of the slice: x: 2, y: 2, z: 4, core: 2. Of those that a mesh axis runs over, the one named last changes fastest.
Arguments:
- tokens: bfloat16 [2, 16, 2048, 512], P('section', 'dp', 'tensor'), may hold values from -6 to 6
- lengths: int32 [2, 16, 2], P(None, 'dp'), may hold values from 0 to 2048, as said below
- self_qkv: bfloat16 [2, 3, 512, 512], P('section', None, None, 'tensor'), may hold values from -0.25 to 0.25
- self_out: bfloat16 [2, 512, 512], P('section', 'tensor'), may hold values from -6 to 6
- cross_proj: bfloat16 [2, 2, 512, 512], P('section', None, None, 'tensor')
- ffn_up: bfloat16 [2, 512, 2048], P('section', None, 'tensor'), may hold values from -0.25 to 0.25
- ffn_down: bfloat16 [2, 2048, 512], P('section', 'tensor'), may hold values from -0.125 to 0.125
- norms: float32 [2, 3, 2, 512], P('section')
- cotangent: bfloat16 [2, 16, 2048, 512], P('section', 'dp', 'tensor'), may hold values from -6 to 6
Outputs:
- result: bfloat16 [2, 16, 2048, 512], P('section', 'dp', 'tensor')
- token_grad: float32 [2, 16, 2048, 512], P('section', 'dp', 'tensor')
- qkv_grad: float32 [2, 3, 512, 512], P('section', None, None, 'tensor')
- out_grad: float32 [2, 512, 512], P('section', 'tensor')
- cross_grad: float32 [2, 2, 512, 512], P('section', None, None, 'tensor')
- up_grad: float32 [2, 512, 2048], P('section', None, 'tensor')
- down_grad: float32 [2, 2048, 512], P('section', 'tensor')
- norm_grad: float32 [2, 3, 2, 512], P('section')
The draws below stay inside these ranges and needn't reach their ends.
Inputs may be any that keep to these rules, and one draw needn't show every extreme that they name: lengths[s, r] are the lengths of the sequences packed from the start of row r, the rest being padding: either one sequence (second entry 0) or two, each of 1024 tokens or more, together at most 2048; source row r and target row r hold the same number of sequences, and target sequence k belongs to source sequence k.
All inputs are finite; a program needn't handle non-finite values.
Results may differ from the reference program's by a relative error of at most 0.019.
Values may be sent and summed in bfloat16 or wider, within the bound.
A program may use at most 384 MiB of HBM per device.

```python
import math
import jax
import jax.numpy as jnp
from jax import lax

D = 512
HEADS = 8
FF = 2048
ROW_LEN = 2048
MIN_LEN = 1024
ROWS = 16


def draw_lengths(key, part):
    key = jax.random.fold_in(key, 11)
    split_keys = jax.random.split(key, 5)
    row_ids = jnp.arange(ROWS, dtype=jnp.int32)
    forced = jax.random.randint(split_keys[0], (), 0, ROWS)
    two_docs = jax.random.randint(split_keys[1], (ROWS,), 0, 2)
    two_docs = jnp.where(row_ids == forced, 0, two_docs)
    single = jnp.minimum(jax.random.randint(split_keys[2], (2, ROWS), MIN_LEN, ROW_LEN + MIN_LEN // 2 + 1), ROW_LEN)
    single = jnp.where(row_ids[None, :] == forced, ROW_LEN, single)
    first_part = jax.random.randint(split_keys[3], (2, ROWS), MIN_LEN, ROW_LEN - MIN_LEN + 1)
    room_left = ROW_LEN - first_part - MIN_LEN + 1
    second_part = MIN_LEN + jax.random.randint(split_keys[4], (2, ROWS), 0, 1048576) % room_left
    first_len = jnp.where(two_docs[None, :] == 1, first_part, single)
    second_len = jnp.where(two_docs[None, :] == 1, second_part, 0)
    return jnp.stack([first_len, second_len], axis=-1).astype(jnp.int32)


def draw_cross_proj(key, part):
    key = jax.random.fold_in(key, 12)
    sample = jnp.clip(jax.random.normal(key, (2, 2, D, D), jnp.float32), -4.0, 4.0)
    spread = jnp.full((2, 2, 1, 1), D ** (-0.5), jnp.float32)
    spread = spread.at[1, 1].set(max(1, 2 * D // MIN_LEN) ** (-0.5))
    return (sample * spread).astype(jnp.bfloat16)


def draw_norms(key, part):
    key = jax.random.fold_in(key, 13)
    gain_key, shift_key = jax.random.split(key, 2)
    gains = 1.0 + 0.2 * jnp.clip(jax.random.normal(gain_key, (2, 3, D), jnp.float32), -2.0, 2.0)
    shifts = 0.4 * jnp.clip(jax.random.normal(shift_key, (2, 3, D), jnp.float32), -3.0, 3.0)
    return jnp.stack([gains, shifts], axis=2)


def steps_of(key, extent, cuts, smallest, largest):
    loudness = 1.0
    for dim, blocks in cuts:
        heights = jax.random.uniform(jax.random.fold_in(jax.random.fold_in(key, 6), dim), (blocks,), jnp.float32, smallest / len(cuts), largest / len(cuts))
        loudness = loudness * jnp.repeat(jnp.exp(heights), extent[dim] // blocks).reshape((-1,) + (1,) * (len(extent) - 1 - dim))
    return loudness


def normal_values(rng, shape, width, reach, shards=(), kind=jnp.bfloat16):
    values = width * jax.random.normal(rng, shape, jnp.float32)
    if shards:
        values = values * steps_of(rng, shape, shards, -0.22, 0.18)
    return jnp.clip(values, -reach, reach).astype(kind)


def setup_inputs(seed: int = 0) -> dict:
    arg_keys = jax.random.split(jax.random.key(seed), 10)
    tokens = normal_values(arg_keys[0], (2, ROWS, ROW_LEN, D), 1.0, 6.0, ((0, 2), (1, 8), (2, 2)))
    lengths = draw_lengths(jax.random.fold_in(arg_keys[9], 71), 0)
    self_qkv = normal_values(arg_keys[2], (2, 3, D, D), D ** -0.5, 0.25, ((0, 2), (3, 2)))
    self_out = normal_values(arg_keys[3], (2, D, D), (max(1, 2 * D // MIN_LEN)) ** -0.5, 6.0, ((0, 2), (1, 2)))
    cross_proj = draw_cross_proj(jax.random.fold_in(arg_keys[9], 71), 0)
    ffn_up = normal_values(arg_keys[5], (2, D, FF), D ** -0.5, 0.25, ((0, 2), (2, 2)))
    ffn_down = normal_values(arg_keys[6], (2, FF, D), FF ** -0.5, 0.125, ((0, 2), (1, 2)))
    norms = draw_norms(jax.random.fold_in(arg_keys[9], 71), 0)
    cotangent = normal_values(arg_keys[8], (2, ROWS, ROW_LEN, D), 1.0, 6.0, ((0, 2), (1, 8), (2, 2)))
    return dict(tokens=tokens, lengths=lengths, self_qkv=self_qkv, self_out=self_out, cross_proj=cross_proj, ffn_up=ffn_up, ffn_down=ffn_down, norms=norms, cotangent=cotangent)


EPSILON = 1e-05
MASKED = -1000000000.0
HIGHEST = lax.Precision.HIGHEST

@jax.custom_vjp
def low(v):
    return lax.optimization_barrier(v.astype(jnp.bfloat16)).astype(jnp.float32)

@jax.custom_vjp
def low_back(v):
    return v

def low_keep(v):
    return (low(v), None)

def low_pass(kept, grad):
    return (grad,)

def back_keep(v):
    return (v, None)

def back_low(kept, grad):
    return (low(grad),)
low.defvjp(low_keep, low_pass)
low_back.defvjp(back_keep, back_low)

def layer_norm(row_block, norm_gain, norm_shift):
    row_mean = lax.optimization_barrier(jnp.mean(row_block, axis=-1, keepdims=True))
    centered = row_block - row_mean
    variance = lax.optimization_barrier(jnp.mean(centered * centered, axis=-1, keepdims=True))
    return centered * lax.rsqrt(variance + EPSILON) * norm_gain + norm_shift

def smooth_gate(inner_act):
    return 0.5 * inner_act * (1.0 + jnp.tanh(0.7978845608028654 * (inner_act + 0.044715 * inner_act * inner_act * inner_act)))

def segment_ids(length_pair, row_length):
    position = jnp.arange(row_length, dtype=jnp.int32)
    return jnp.where(position < length_pair[0], 0, jnp.where(position < length_pair[0] + length_pair[1], 1, 2)).astype(jnp.int32)

def allowed(query_seg, key_seg):
    return (key_seg[None, :] < 2) & ((query_seg[:, None] == key_seg[None, :]) | (query_seg[:, None] == 2))

def matmul(left_side, right_side):
    return jnp.dot(left_side, right_side, precision=HIGHEST)

def attend(queries, key_rows, value_rows, query_seg, key_seg):
    row_length = queries.shape[0]
    head_width = queries.shape[1] // HEADS
    score_scale = 1.0 / math.sqrt(head_width)
    query_heads = queries.reshape(row_length, HEADS, head_width)
    key_heads = key_rows.reshape(row_length, HEADS, head_width)
    value_heads = value_rows.reshape(row_length, HEADS, head_width)
    scores = jnp.einsum('qhd,khd->hqk', query_heads, key_heads, precision=HIGHEST) * score_scale
    scores = low_back(scores)
    scores = jnp.where(allowed(query_seg, key_seg)[None], scores, MASKED)
    row_max = lax.optimization_barrier(jnp.max(scores, axis=-1, keepdims=True))
    exponent = jnp.exp(scores - row_max)
    probability = low(exponent / lax.optimization_barrier(jnp.sum(exponent, axis=-1, keepdims=True)))
    mixture = jnp.einsum('hqk,khd->qhd', probability, value_heads, precision=HIGHEST)
    return low_back(low(mixture.reshape(row_length, HEADS * head_width)))

def project(row_block, weight_matrix):
    return low_back(low(matmul(row_block, weight_matrix)))

def self_attention(hidden, qkv_weight, out_weight, own_seg):
    row_block = low(hidden)
    mixture = attend(project(row_block, qkv_weight[0]), project(row_block, qkv_weight[1]), project(row_block, qkv_weight[2]), own_seg, own_seg)
    return low_back(matmul(mixture, out_weight))

def feed_forward(hidden, up_weight, down_weight):
    row_block = low(hidden)
    inner_act = low_back(matmul(row_block, up_weight))
    return low_back(matmul(low(smooth_gate(inner_act)), down_weight))

def row_pair(weight_set, source, target, source_pair, target_pair):
    qkv_weight, out_weight, cross_weight, up_weight, down_weight, norm_table = weight_set
    row_length = source.shape[0]
    source_seg = segment_ids(source_pair, row_length)
    target_seg = segment_ids(target_pair, row_length)
    base_rows = layer_norm(source, norm_table[0, 2, 0], norm_table[0, 2, 1])
    hidden = layer_norm(base_rows + self_attention(base_rows, qkv_weight[0], out_weight[0], source_seg), norm_table[0, 0, 0], norm_table[0, 0, 1])
    encoded = layer_norm(hidden + feed_forward(hidden, up_weight[0], down_weight[0]), norm_table[0, 1, 0], norm_table[0, 1, 1])
    memory_rows = low(encoded)
    key_rows = project(memory_rows, cross_weight[0, 0])
    value_rows = project(memory_rows, cross_weight[0, 1])
    hidden = layer_norm(target + self_attention(target, qkv_weight[1], out_weight[1], target_seg), norm_table[1, 0, 0], norm_table[1, 0, 1])
    queries = project(low(hidden), cross_weight[1, 0])
    mixture = attend(queries, key_rows, value_rows, target_seg, source_seg)
    hidden = layer_norm(hidden + low_back(matmul(mixture, cross_weight[1, 1].T)), norm_table[1, 2, 0], norm_table[1, 2, 1])
    decoded = layer_norm(hidden + feed_forward(hidden, up_weight[1], down_weight[1]), norm_table[1, 1, 0], norm_table[1, 1, 1])
    return (encoded, decoded)

def reference(tokens, lengths, self_qkv, self_out, cross_proj, ffn_up, ffn_down, norms, cotangent):
    inputs = (tokens.astype(jnp.float32), self_qkv.astype(jnp.float32), self_out.astype(jnp.float32), cross_proj.astype(jnp.float32), ffn_up.astype(jnp.float32), ffn_down.astype(jnp.float32), norms.astype(jnp.float32))

    def forward(token_rows, qkv_weight, out_weight, cross_weight, up_weight, down_weight, norm_table):
        weight_set = (qkv_weight, out_weight, cross_weight, up_weight, down_weight, norm_table)

        def one_row(row_item):
            return row_pair(weight_set, row_item[0], row_item[1], row_item[2], row_item[3])
        encoded, decoded = lax.map(jax.checkpoint(one_row), (token_rows[0], token_rows[1], lengths[0], lengths[1]))
        return jnp.stack([encoded, decoded])
    outputs, pull_back = jax.vjp(forward, *inputs)
    gradients = pull_back(cotangent.astype(jnp.float32))
    return (outputs.astype(jnp.bfloat16), gradients[0], gradients[1], gradients[2], gradients[3], gradients[4], gradients[5], gradients[6])
```

```python
import functools
import math

import jax
import jax.numpy as jnp
from jax import lax
from jax.experimental import pallas as pl
from jax.experimental.pallas import tpu as pltpu
from jax.sharding import PartitionSpec as P

HEADS = 8
EPSILON = 1e-05
MASKED = -1000000000.0
LOG2E = 1.0 / math.log(2.0)
PAIR = 128
HALF = 64
VMEM = 60 * 1024 * 1024
BF16 = jnp.bfloat16
F32 = jnp.float32


def standardize(rows):
    mean = jnp.mean(rows, axis=-1, keepdims=True)
    centered = rows - mean
    inv = lax.rsqrt(jnp.mean(centered * centered, axis=-1, keepdims=True) + EPSILON)
    return centered * inv, inv


def affine(unit, norm_ref, slot):
    return unit * norm_ref[slot, 0:1, :] + norm_ref[slot, 1:2, :]


def norm_back(unit, inv, norm_ref, slot, grad, grad_ref):
    grad_ref[slot, 0:1, :] += jnp.sum(grad * unit, axis=0, keepdims=True)
    grad_ref[slot, 1:2, :] += jnp.sum(grad, axis=0, keepdims=True)
    scaled = grad * norm_ref[slot, 0:1, :]
    first = jnp.mean(scaled, axis=-1, keepdims=True)
    second = jnp.mean(scaled * unit, axis=-1, keepdims=True)
    return inv * (scaled - first - unit * second)


def gelu_tanh(inner):
    return jnp.tanh(0.7978845608028654 * (inner + 0.044715 * inner * inner * inner))


def gelu(inner):
    return 0.5 * inner * (1.0 + gelu_tanh(inner))


def gelu_both(inner):
    bent = gelu_tanh(inner)
    slope = 0.7978845608028654 * (1.0 + 0.134145 * inner * inner)
    half = 0.5 * (1.0 + bent)
    return inner * half, half + 0.5 * inner * (1.0 - bent * bent) * slope


def dot_nn(a, b):
    return jnp.dot(a, b, preferred_element_type=F32)


def dot_nt(a, b):
    return lax.dot_general(a, b, (((1,), (1,)), ((), ())), preferred_element_type=F32)


def dot_tn(a, b):
    return lax.dot_general(a, b, (((0,), (0,)), ((), ())), preferred_element_type=F32)


def row_call(body, name, rows, block, row_ins, whole_ins, row_outs, sum_outs, flops):
    def blocked(shape, dim):
        sizes = tuple(block if i == dim else size for i, size in enumerate(shape))
        return pl.BlockSpec(
            sizes, lambda step: tuple(step if i == dim else 0 for i in range(len(shape)))
        )

    def whole(shape):
        return pl.BlockSpec(
            shape, lambda step: (0,) * len(shape), pipeline_mode=pl.Buffered(buffer_count=1)
        )

    n_in = len(row_ins) + len(whole_ins)
    n_row, n_sum = len(row_outs), len(sum_outs)

    def kernel(*refs):
        ins, outs = refs[:n_in], refs[n_in : n_in + n_row]
        sums, totals = refs[n_in + n_row : n_in + n_row + n_sum], refs[n_in + n_row + n_sum :]

        @pl.when(pl.program_id(0) == 0)
        def _():
            for total in totals:
                total[...] = jnp.zeros_like(total)

        body(ins, outs, totals)

        @pl.when(pl.program_id(0) == pl.num_programs(0) - 1)
        def _():
            for out, total in zip(sums, totals):
                out[...] = total[...].astype(out.dtype)

    arrays = [array for array, _ in row_ins] + list(whole_ins)
    size = sum(a.size * a.dtype.itemsize for a in arrays)
    return pl.pallas_call(
        kernel,
        grid=(rows // block,),
        in_specs=[blocked(a.shape, dim) for a, dim in row_ins] + [whole(a.shape) for a in whole_ins],
        out_specs=[blocked(shape, dim) for shape, _, dim in row_outs]
        + [whole(shape) for shape, _ in sum_outs],
        out_shape=[jax.ShapeDtypeStruct(shape, dtype) for shape, dtype, _ in row_outs]
        + [jax.ShapeDtypeStruct(shape, dtype) for shape, dtype in sum_outs],
        scratch_shapes=[pltpu.VMEM(shape, F32) for shape, _ in sum_outs],
        compiler_params=pltpu.CompilerParams(vmem_limit_bytes=VMEM),
        cost_estimate=pl.CostEstimate(flops=flops, bytes_accessed=size, transcendentals=0),
        name=name,
    )(*arrays)


def project_qkv(x, norm, weights, with_norm, block):
    rows, width = x.shape
    parts, part = len(weights), weights[0].shape[-1]
    score = LOG2E / math.sqrt(width // HEADS)

    def body(ins, outs, totals):
        x_ref, norm_ref, *w = ins
        q_ref, kv_ref = outs
        rows_in = x_ref[...]
        if with_norm:
            unit, _ = standardize(rows_in.astype(F32))
            rows_in = affine(unit, norm_ref, 2).astype(BF16)
        for k in range(parts):
            q_ref[k] = (dot_nn(rows_in, w[k][0]) * score).astype(BF16)
            kv_ref[0, k] = dot_nn(rows_in, w[k][1]).astype(BF16)
            kv_ref[1, k] = dot_nn(rows_in, w[k][2]).astype(BF16)

    return row_call(
        body,
        "project_qkv",
        rows,
        block,
        [(x, 0)],
        [norm, *weights],
        [((parts, rows, part), BF16, 1), ((2, parts, rows, part), BF16, 2)],
        [],
        6 * rows * width * width,
    )


def encoder_forward(x, mix, norm, out, up, down, cross, block):
    rows, width = x.shape
    parts, part = len(out), out[0].shape[0]

    def body(ins, outs, totals):
        x_ref, mix_ref, norm_ref = ins[:3]
        wo, wu, wd, wc = (ins[3 + i * parts : 3 + (i + 1) * parts] for i in range(4))
        result_ref, kv_ref, first_ref, third_ref = outs
        unit, _ = standardize(x_ref[...].astype(F32))
        first = affine(unit, norm_ref, 2)
        for k in range(parts):
            first += dot_nn(mix_ref[k], wo[k][...])
        first_ref[...] = first
        unit, _ = standardize(first)
        third = affine(unit, norm_ref, 0)
        low = third.astype(BF16)
        for k in range(parts):
            act = gelu(dot_nn(low, wu[k][...])).astype(BF16)
            third += dot_nn(act, wd[k][...])
        third_ref[...] = third
        unit, _ = standardize(third)
        low = affine(unit, norm_ref, 1).astype(BF16)
        result_ref[...] = low
        for k in range(parts):
            kv_ref[0, k] = dot_nn(low, wc[k][0]).astype(BF16)
            kv_ref[1, k] = dot_nn(low, wc[k][1]).astype(BF16)

    units = sum(w.shape[1] for w in up)
    return row_call(
        body,
        "encoder_forward",
        rows,
        block,
        [(x, 0), (mix, 1)],
        [norm, *out, *up, *down, *cross],
        [
            ((rows, width), BF16, 0),
            ((2, parts, rows, part), BF16, 2),
            ((rows, width), F32, 0),
            ((rows, width), F32, 0),
        ],
        [],
        6 * rows * width * width + 4 * rows * width * units,
    )


def decoder_middle(x, mix, norm, out, cross, block):
    rows, width = x.shape
    parts, part = len(out), out[0].shape[0]
    score = LOG2E / math.sqrt(width // HEADS)

    def body(ins, outs, totals):
        x_ref, mix_ref, norm_ref = ins[:3]
        wo, wc = (ins[3 + i * parts : 3 + (i + 1) * parts] for i in range(2))
        q_ref, first_ref = outs
        first = x_ref[...].astype(F32)
        for k in range(parts):
            first += dot_nn(mix_ref[k], wo[k][...])
        first_ref[...] = first
        unit, _ = standardize(first)
        low = affine(unit, norm_ref, 0).astype(BF16)
        for k in range(parts):
            q_ref[k] = (dot_nn(low, wc[k][0]) * score).astype(BF16)

    return row_call(
        body,
        "decoder_middle",
        rows,
        block,
        [(x, 0), (mix, 1)],
        [norm, *out, *cross],
        [((parts, rows, part), BF16, 1), ((rows, width), F32, 0)],
        [],
        4 * rows * width * width,
    )


def ffn_back(low, grad_low, up, down, up_total, down_total, parts):
    grad = None
    for k in range(parts):
        act, slope = gelu_both(dot_nn(low, up[k][...]))
        down_total[k] += dot_tn(act.astype(BF16), grad_low)
        grad_inner = (dot_nt(grad_low, down[k][...]) * slope).astype(BF16)
        up_total[k] += dot_tn(low, grad_inner)
        step = dot_nt(grad_inner, up[k][...])
        grad = step if grad is None else grad + step
    return grad


def decoder_turn(first, mix, cotangent, norm, cross, up, down, block):
    rows, width = first.shape
    parts, part, units = len(cross), cross[0].shape[-1], up[0].shape[1]

    def body(ins, outs, totals):
        first_ref, mix_ref, cot_ref, norm_ref = ins[:4]
        wc, wu, wd = (ins[4 + i * parts : 4 + (i + 1) * parts] for i in range(3))
        result_ref, second_grad_ref, mix_grad_ref = outs
        out_total, up_total, down_total, norm_total = totals
        unit, _ = standardize(first_ref[...])
        second = affine(unit, norm_ref, 0)
        for k in range(parts):
            second += dot_nt(mix_ref[k], wc[k][1])
        unit_two, inv_two = standardize(second)
        third = affine(unit_two, norm_ref, 2)
        low = third.astype(BF16)
        acts, slopes = [], []
        for k in range(parts):
            act, slope = gelu_both(dot_nn(low, wu[k][...]))
            acts.append(act.astype(BF16))
            slopes.append(slope)
            third += dot_nn(acts[k], wd[k][...])
        unit_three, inv_three = standardize(third)
        result_ref[...] = affine(unit_three, norm_ref, 1).astype(BF16)
        grad = norm_back(
            unit_three, inv_three, norm_ref, 1, cot_ref[...].astype(F32), norm_total
        )
        grad_low = grad.astype(BF16)
        for k in range(parts):
            down_total[k] += dot_tn(acts[k], grad_low)
            grad_inner = (dot_nt(grad_low, wd[k][...]) * slopes[k]).astype(BF16)
            up_total[k] += dot_tn(low, grad_inner)
            grad += dot_nt(grad_inner, wu[k][...])
        grad = norm_back(unit_two, inv_two, norm_ref, 2, grad, norm_total)
        second_grad_ref[...] = grad
        grad_low = grad.astype(BF16)
        for k in range(parts):
            out_total[k] += dot_tn(grad_low, mix_ref[k])
            mix_grad_ref[k] = dot_nn(grad_low, wc[k][1]).astype(BF16)

    return row_call(
        body,
        "decoder_turn",
        rows,
        block,
        [(first, 0), (mix, 1), (cotangent, 0)],
        [norm, *cross, *up, *down],
        [
            ((rows, width), BF16, 0),
            ((rows, width), F32, 0),
            ((parts, rows, part), BF16, 1),
        ],
        [
            ((parts, width, part), BF16),
            ((parts, width, units), BF16),
            ((parts, units, width), BF16),
            ((3, 2, width), F32),
        ],
        6 * rows * width * width + 12 * rows * width * units * parts,
    )


def decoder_middle_back(first, mix, query_grad, second_grad, norm, out, cross, block):
    rows, width = first.shape
    parts, part = len(out), out[0].shape[0]

    def body(ins, outs, totals):
        first_ref, mix_ref, query_grad_ref, second_grad_ref, norm_ref = ins[:5]
        wo, wc = (ins[5 + i * parts : 5 + (i + 1) * parts] for i in range(2))
        first_grad_ref, mix_grad_ref = outs
        query_total, out_total, norm_total = totals
        unit, inv = standardize(first_ref[...])
        low = affine(unit, norm_ref, 0).astype(BF16)
        grad = second_grad_ref[...]
        for k in range(parts):
            query_total[k] += dot_tn(low, query_grad_ref[k])
            grad += dot_nt(query_grad_ref[k], wc[k][0])
        grad = norm_back(unit, inv, norm_ref, 0, grad, norm_total)
        first_grad_ref[...] = grad
        grad_low = grad.astype(BF16)
        for k in range(parts):
            out_total[k] += dot_tn(mix_ref[k], grad_low)
            mix_grad_ref[k] = dot_nt(grad_low, wo[k][...]).astype(BF16)

    return row_call(
        body,
        "decoder_middle_back",
        rows,
        block,
        [(first, 0), (mix, 1), (query_grad, 1), (second_grad, 0)],
        [norm, *out, *cross],
        [((rows, width), F32, 0), ((parts, rows, part), BF16, 1)],
        [
            ((parts, width, part), BF16),
            ((parts, part, width), BF16),
            ((3, 2, width), F32),
        ],
        8 * rows * width * width,
    )


def encoder_back(first, third, mix, memory_grads, cotangent, norm, out, up, down, cross, block):
    rows, width = first.shape
    parts, part, units = len(out), out[0].shape[0], up[0].shape[1]
    pieces = len(memory_grads)

    def body(ins, outs, totals):
        first_ref, third_ref, mix_ref, cot_ref = ins[:4]
        memory_refs, norm_ref = ins[4 : 4 + pieces], ins[4 + pieces]
        rest = ins[5 + pieces :]
        wo, wu, wd, wc = (rest[i * parts : (i + 1) * parts] for i in range(4))
        first_grad_ref, mix_grad_ref = outs
        cross_total, out_total, up_total, down_total, norm_total = totals
        unit, inv = standardize(third_ref[...])
        low = affine(unit, norm_ref, 1).astype(BF16)
        grad = cot_ref[...].astype(F32)
        for i in range(2):
            for k in range(parts):
                memory = memory_refs[0][i, k].astype(F32)
                for ref in memory_refs[1:]:
                    memory += ref[i, k].astype(F32)
                memory = memory.astype(BF16)
                cross_total[k, i] += dot_tn(low, memory)
                grad += dot_nt(memory, wc[k][i])
        grad = norm_back(unit, inv, norm_ref, 1, grad, norm_total)
        unit, inv = standardize(first_ref[...])
        low = affine(unit, norm_ref, 0).astype(BF16)
        grad += ffn_back(low, grad.astype(BF16), wu, wd, up_total, down_total, parts)
        grad = norm_back(unit, inv, norm_ref, 0, grad, norm_total)
        first_grad_ref[...] = grad
        grad_low = grad.astype(BF16)
        for k in range(parts):
            out_total[k] += dot_tn(mix_ref[k], grad_low)
            mix_grad_ref[k] = dot_nt(grad_low, wo[k][...]).astype(BF16)

    return row_call(
        body,
        "encoder_back",
        rows,
        block,
        [(first, 0), (third, 0), (mix, 1), (cotangent, 0)] + [(m, 2) for m in memory_grads],
        [norm, *out, *up, *down, *cross],
        [((rows, width), F32, 0), ((parts, rows, part), BF16, 1)],
        [
            ((parts, 2, width, part), BF16),
            ((parts, part, width), BF16),
            ((parts, width, units), BF16),
            ((parts, units, width), BF16),
            ((3, 2, width), F32),
        ],
        12 * rows * width * width + 10 * rows * width * units * parts,
    )


def input_back(x, first_grad, query_grad, key_grads, norm, weights, with_norm, block):
    rows, width = x.shape
    parts, part = len(weights), weights[0].shape[-1]
    pieces = len(key_grads)

    def body(ins, outs, totals):
        x_ref, first_grad_ref, query_grad_ref = ins[:3]
        key_refs, norm_ref, w = ins[3 : 3 + pieces], ins[3 + pieces], ins[4 + pieces :]
        (grad_ref,) = outs
        qkv_total, norm_total = totals
        low = x_ref[...]
        if with_norm:
            unit, inv = standardize(low.astype(F32))
            low = affine(unit, norm_ref, 2).astype(BF16)
        grad = first_grad_ref[...]
        for k in range(parts):
            for i in range(3):
                if i == 0:
                    member = query_grad_ref[k]
                else:
                    member = key_refs[0][i - 1, k].astype(F32)
                    for ref in key_refs[1:]:
                        member += ref[i - 1, k].astype(F32)
                    member = member.astype(BF16)
                qkv_total[k, i] += dot_tn(low, member)
                grad += dot_nt(member, w[k][i])
        if with_norm:
            grad = norm_back(unit, inv, norm_ref, 2, grad, norm_total)
        grad_ref[...] = grad.astype(BF16)

    return row_call(
        body,
        "input_back",
        rows,
        block,
        [(x, 0), (first_grad, 0), (query_grad, 1)] + [(g, 2) for g in key_grads],
        [norm, *weights],
        [((rows, width), BF16, 0)],
        [((parts, 3, width, part), BF16), ((3, 2, width), F32)],
        12 * rows * width * width,
    )


def widen_keys(span_ref, kv_refs, key_e, key_o, value_e, value_o, rows):
    lane = lax.broadcasted_iota(jnp.int32, (rows, PAIR), 1)
    place = lax.broadcasted_iota(jnp.int32, (rows, PAIR), 0)
    low = lane < HALF
    for g, kv_ref in enumerate(kv_refs):
        spot = place + span_ref[2 + g]
        live = (spot >= span_ref[0]) & (spot < span_ref[1])
        bias = jnp.where(live, 0.0, MASKED)
        keys, values = kv_ref[0].astype(F32), kv_ref[1].astype(F32)
        own = pl.ds(g * rows, rows)
        key_e[own, :] = jnp.where(low, keys, jnp.where(lane == HALF, bias, 1.0)).astype(BF16)
        key_o[own, :] = jnp.where(low, jnp.where(lane == 0, bias, 1.0), keys).astype(BF16)
        value_e[own, :] = jnp.where(low, values, 1.0).astype(BF16)
        value_o[own, :] = jnp.where(low, 1.0, values).astype(BF16)


def attend(query, kv_pieces, span, block):
    parts, rows, part = query.shape
    per_part = part // PAIR
    pairs = parts * per_part
    pieces = len(kv_pieces)
    keys = rows * pieces

    def kernel(span_ref, q_ref, *refs):
        kv_refs = refs[:pieces]
        out_ref, lse_ref, key_e, key_o, value_e, value_o = refs[pieces:]

        @pl.when(pl.program_id(1) == 0)
        def _():
            widen_keys(span_ref, kv_refs, key_e, key_o, value_e, value_o, rows)

        lane = lax.broadcasted_iota(jnp.int32, (block, PAIR), 1)
        low = lane < HALF
        query = q_ref[...].astype(F32)
        query_e = jnp.where(low, query, jnp.where(lane == HALF, 1.0, 0.0)).astype(BF16)
        query_o = jnp.where(low, jnp.where(lane == 0, 1.0, 0.0), query).astype(BF16)
        tops, sums = [], []
        for q, k, v in ((query_e, key_e, value_e), (query_o, key_o, value_o)):
            scores = dot_nt(q, k[...])
            top = jnp.max(scores, axis=1, keepdims=True)
            tops.append(top)
            sums.append(dot_nn(jnp.exp2(scores - top).astype(BF16), v[...]))
        top = jnp.where(low, tops[1], tops[0])
        weight = jnp.where(low, sums[1], sums[0])
        lse_ref[...] = top + LOG2E * jnp.log(weight)
        mixed = jnp.where(low, sums[0], sums[1])
        out_ref[...] = (mixed / pltpu.roll(weight, HALF, 1)).astype(BF16)

    return pl.pallas_call(
        kernel,
        grid_spec=pltpu.PrefetchScalarGridSpec(
            num_scalar_prefetch=1,
            grid=(pairs, rows // block),
            in_specs=[
                pl.BlockSpec(
                    (None, block, PAIR), lambda i, j, _: (i // per_part, j, i % per_part)
                )
            ]
            + [
                pl.BlockSpec(
                    (2, None, rows, PAIR), lambda i, j, _: (0, i // per_part, 0, i % per_part)
                )
            ]
            * pieces,
            out_specs=[
                pl.BlockSpec(
                    (None, block, PAIR), lambda i, j, _: (i // per_part, j, i % per_part)
                ),
                pl.BlockSpec((block, PAIR), lambda i, j, _: (j, i)),
            ],
            scratch_shapes=[pltpu.VMEM((keys, PAIR), BF16)] * 4,
        ),
        out_shape=[
            jax.ShapeDtypeStruct(query.shape, BF16),
            jax.ShapeDtypeStruct((rows, pairs * PAIR), F32),
        ],
        compiler_params=pltpu.CompilerParams(vmem_limit_bytes=VMEM),
        cost_estimate=pl.CostEstimate(
            flops=16 * rows * keys * pairs * PAIR,
            bytes_accessed=8 * rows * pairs * PAIR * pieces,
            transcendentals=0,
        ),
        name="attend",
    )(span, query, *kv_pieces)


def attend_back(query, kv_pieces, mix, mix_grad, lse, span, block, chunk):
    parts, rows, part = query.shape
    per_part = part // PAIR
    pairs = parts * per_part
    pieces = len(kv_pieces)
    keys = rows * pieces
    scale = 1.0 / math.sqrt(HALF)

    def kernel(span_ref, q_ref, mix_ref, grad_ref, lse_ref, *refs):
        kv_refs = refs[:pieces]
        dq_ref, dkv_refs = refs[pieces], refs[pieces + 1 : 2 * pieces + 1]
        key_e, key_o, value_e, value_o, key_t, key_total, value_total = refs[2 * pieces + 1 :]

        @pl.when(pl.program_id(1) == 0)
        def _():
            widen_keys(span_ref, kv_refs, key_e, key_o, value_e, value_o, rows)
            for g, kv_ref in enumerate(kv_refs):
                key_t[:, pl.ds(g * rows, rows)] = kv_ref[0].T
            key_total[...] = jnp.zeros_like(key_total)
            value_total[...] = jnp.zeros_like(value_total)

        lane = lax.broadcasted_iota(jnp.int32, (block, PAIR), 1)
        low = lane < HALF
        query, grad = q_ref[...].astype(F32), grad_ref[...].astype(F32)
        product = mix_ref[...].astype(F32) * grad
        inner = jnp.where(
            low,
            jnp.sum(jnp.where(low, 0.0, product), axis=1, keepdims=True),
            jnp.sum(jnp.where(low, product, 0.0), axis=1, keepdims=True),
        )

        def three(value, shift):
            high = value.astype(BF16).astype(F32)
            rest = value - high
            mid = rest.astype(BF16).astype(F32)
            spot = lane % HALF - shift
            return jnp.where(
                spot == 0,
                high,
                jnp.where(spot == 1, mid, jnp.where(spot == 2, rest - mid, 0.0)),
            )

        lse = three(-lse_ref[...], 1) + jnp.where(lane % HALF == 0, 1.0, 0.0)
        inner = three(-inner, 0)
        heads = []
        for own, key, value in ((low, key_e, value_e), (~low, key_o, value_o)):
            heads.append(
                (
                    key,
                    value,
                    jnp.where(own, query, lse).astype(BF16),
                    jnp.where(own, grad, inner).astype(BF16),
                    jnp.where(own, query, 0.0).astype(BF16),
                    jnp.where(own, grad, 0.0).astype(BF16),
                )
            )
        dq = [None, None]
        for c in range(keys // chunk):
            span_c = pl.ds(c * chunk, chunk)
            dk, dv = None, None
            for h, (key, value, q_wide, g_wide, q_own, g_own) in enumerate(heads):
                probs = jnp.exp2(dot_nt(key[span_c, :], q_wide))
                dscores = (probs * dot_nt(value[span_c, :], g_wide)).astype(BF16)
                step_v = dot_nn(probs.astype(BF16), g_own)
                step_k = dot_nn(dscores, q_own)
                step_q = dot_nn(key_t[pl.ds(h * HALF, HALF), span_c], dscores)
                dv = step_v if dv is None else dv + step_v
                dk = step_k if dk is None else dk + step_k
                dq[h] = step_q if dq[h] is None else dq[h] + step_q
            key_total[span_c, :] += dk
            value_total[span_c, :] += dv
        dq_ref[...] = (jnp.concatenate(dq, axis=0).T * scale).astype(BF16)

        @pl.when(pl.program_id(1) == pl.num_programs(1) - 1)
        def _():
            for g, ref in enumerate(dkv_refs):
                own = pl.ds(g * rows, rows)
                ref[0] = (key_total[own, :] * (1.0 / LOG2E)).astype(BF16)
                ref[1] = value_total[own, :].astype(BF16)

    query_spec = pl.BlockSpec(
        (None, block, PAIR), lambda i, j, _: (i // per_part, j, i % per_part)
    )
    kv_spec = pl.BlockSpec(
        (2, None, rows, PAIR), lambda i, j, _: (0, i // per_part, 0, i % per_part)
    )
    out = pl.pallas_call(
        kernel,
        grid_spec=pltpu.PrefetchScalarGridSpec(
            num_scalar_prefetch=1,
            grid=(pairs, rows // block),
            in_specs=[query_spec] * 3
            + [pl.BlockSpec((block, PAIR), lambda i, j, _: (j, i))]
            + [kv_spec] * pieces,
            out_specs=[query_spec] + [kv_spec] * pieces,
            scratch_shapes=[pltpu.VMEM((keys, PAIR), BF16)] * 4
            + [pltpu.VMEM((PAIR, keys), BF16)]
            + [pltpu.VMEM((keys, PAIR), F32)] * 2,
        ),
        out_shape=[jax.ShapeDtypeStruct(query.shape, BF16)]
        + [jax.ShapeDtypeStruct((2, parts, rows, part), BF16)] * pieces,
        compiler_params=pltpu.CompilerParams(vmem_limit_bytes=VMEM),
        cost_estimate=pl.CostEstimate(
            flops=40 * rows * keys * pairs * PAIR,
            bytes_accessed=16 * rows * pairs * PAIR * pieces,
            transcendentals=0,
        ),
        name="attend_back",
    )(span, query, mix, mix_grad, lse, *kv_pieces)
    return out[0], out[1:]


def local(tokens, lengths, self_qkv, self_out, cross_proj, ffn_up, ffn_down, norms, cotangent):
    section = lax.axis_index("section")
    tensor = lax.axis_index("tensor")
    tensors = lax.axis_size("tensor")
    _, row_count, rows, width = tokens.shape
    assert row_count == 2 and tensors % row_count == 0
    spread = tensors // row_count
    pieces = 2 * spread
    axes = ("section", "tensor")
    is_first = section == 0
    own_row = tensor // spread
    place = section * spread + tensor % spread

    def device(row, spot):
        return (spot // spread) * tensors + row * spread + spot % spread

    def each():
        return [(s, t) for s in range(2) for t in range(tensors)]

    straight = [(s * tensors + t, device(s, t)) for s, t in each()]
    turned = [(s * tensors + t, device(1 - s, t)) for s, t in each()]

    def bring(shares):
        stays = lax.dynamic_index_in_dim(shares, section, 0, keepdims=False)
        moves = lax.dynamic_index_in_dim(shares, 1 - section, 0, keepdims=False)
        one = lax.ppermute(stays, axes, straight)
        two = lax.ppermute(moves, axes, turned)
        return jnp.where(own_row == 0, one, two), jnp.where(own_row == 0, two, one)

    def take_back(source, target):
        one = jnp.where(own_row == 0, source, target)
        two = jnp.where(own_row == 0, target, source)
        one = lax.ppermute(one, axes, [(b, a) for a, b in straight])
        two = lax.ppermute(two, axes, [(b, a) for a, b in turned])
        return jnp.stack([jnp.where(is_first, one, two), jnp.where(is_first, two, one)])

    def rotate(value, by):
        pairs = [
            (device(r, p), device(r, (p + by) % pieces))
            for r in range(row_count)
            for p in range(pieces)
        ]
        return lax.ppermute(value, axes, pairs)

    def pieces_of(value):
        return [value] + [rotate(value, by) for by in range(1, pieces)]

    def pieces_home(values):
        return [values[0]] + [rotate(values[by], -by) for by in range(1, pieces)]

    def swap_sections(value):
        return lax.ppermute(value, "section", [(0, 1), (1, 0)])

    def both_sides(weight, dim):
        if spread == 1:
            other = lax.ppermute(weight, "tensor", [(t, 1 - t) for t in range(tensors)])
            parts = [weight, other]
        else:
            parts = [lax.all_gather(weight, "tensor", axis=dim, tiled=True)]
        swapped = [swap_sections(part) for part in parts]
        pairs = list(zip(parts, swapped))
        return (
            [jnp.where(is_first, mine, theirs) for mine, theirs in pairs],
            [jnp.where(is_first, theirs, mine) for mine, theirs in pairs],
        )

    def home(source_grad, target_grad, dim):
        keep = jnp.where(is_first, source_grad, target_grad).astype(F32)
        sent = swap_sections(jnp.where(is_first, target_grad, source_grad))
        total = (keep + sent.astype(F32)).astype(BF16)
        if spread == 1:
            other = lax.ppermute(total[1], "tensor", [(t, 1 - t) for t in range(tensors)])
            total = (total[0].astype(F32) + other.astype(F32)).astype(BF16)
        else:
            total = lax.psum_scatter(total[0], "tensor", scatter_dimension=dim, tiled=True)
        return total

    def span_of(query_side, key_side):
        own = lax.dynamic_index_in_dim(lengths, own_row, 1, keepdims=False)
        asks, answers = own[query_side], own[key_side]
        paired = asks[1] > 0
        second = paired & (place * rows >= asks[0])
        begin = jnp.where(second, answers[0], 0)
        end = jnp.where(second | ~paired, answers[0] + answers[1], answers[0])
        offsets = [(place - by) % pieces * rows for by in range(pieces)]
        return jnp.stack([begin, end, *offsets]).astype(jnp.int32)

    block = min(256, rows)
    query_block = min(256, rows)
    chunk = 512

    source, target = bring(tokens[0])
    source_norm, target_norm = (
        jnp.where(is_first, a, b)
        for a, b in (lambda own, other: ((own, other), (other, own)))(
            norms[0], swap_sections(norms[0])
        )
    )
    source_qkv, target_qkv = both_sides(self_qkv[0], 2)
    source_out, target_out = both_sides(self_out[0], 0)
    source_up, target_up = both_sides(ffn_up[0], 1)
    source_down, target_down = both_sides(ffn_down[0], 0)
    source_cross, target_cross = both_sides(cross_proj[0], 2)
    source_cot, target_cot = bring(cotangent[0])
    source_span, target_span, cross_span = span_of(0, 0), span_of(1, 1), span_of(1, 0)

    enc_q, enc_kv = project_qkv(source, source_norm, source_qkv, True, block)
    enc_kv = pieces_of(enc_kv)
    dec_q, dec_kv = project_qkv(target, target_norm, target_qkv, False, block)
    dec_kv = pieces_of(dec_kv)
    enc_mix, enc_lse = attend(enc_q, enc_kv, source_span, query_block)
    encoded, memory, enc_first, enc_third = encoder_forward(
        source, enc_mix, source_norm, source_out, source_up, source_down, source_cross, block
    )
    memory = pieces_of(memory)
    dec_mix, dec_lse = attend(dec_q, dec_kv, target_span, query_block)
    cross_q, dec_first = decoder_middle(
        target, dec_mix, target_norm, target_out, target_cross, block
    )
    cross_mix, cross_lse = attend(cross_q, memory, cross_span, query_block)
    decoded, second_grad, cross_mix_grad, cross_out_grad, dec_up, dec_down, dec_norm = decoder_turn(
        dec_first, cross_mix, target_cot, target_norm, target_cross, target_up, target_down, block
    )
    result = take_back(encoded, decoded)
    cross_q_grad, memory_grads = attend_back(
        cross_q, memory, cross_mix, cross_mix_grad, cross_lse, cross_span, query_block, chunk
    )
    memory_grads = pieces_home(memory_grads)
    dec_first_grad, dec_mix_grad, cross_query_grad, dec_out, step = decoder_middle_back(
        dec_first,
        dec_mix,
        cross_q_grad,
        second_grad,
        target_norm,
        target_out,
        target_cross,
        block,
    )
    dec_norm += step
    enc_first_grad, enc_mix_grad, enc_cross, enc_out, enc_up, enc_down, enc_norm = encoder_back(
        enc_first,
        enc_third,
        enc_mix,
        memory_grads,
        source_cot,
        source_norm,
        source_out,
        source_up,
        source_down,
        source_cross,
        block,
    )
    dec_cross = jnp.stack([cross_query_grad, cross_out_grad], axis=1)
    up_grad, down_grad = home(enc_up, dec_up, 1), home(enc_down, dec_down, 0)
    out_grad, cross_grad = home(enc_out, dec_out, 0), home(enc_cross, dec_cross, 2)
    dec_q_grad, dec_kv_grads = attend_back(
        dec_q, dec_kv, dec_mix, dec_mix_grad, dec_lse, target_span, query_block, chunk
    )
    dec_kv_grads = pieces_home(dec_kv_grads)
    enc_q_grad, enc_kv_grads = attend_back(
        enc_q, enc_kv, enc_mix, enc_mix_grad, enc_lse, source_span, query_block, chunk
    )
    enc_kv_grads = pieces_home(enc_kv_grads)
    target_grad, dec_qkv, _ = input_back(
        target, dec_first_grad, dec_q_grad, dec_kv_grads, target_norm, target_qkv, False, block
    )
    source_grad, enc_qkv, step = input_back(
        source, enc_first_grad, enc_q_grad, enc_kv_grads, source_norm, source_qkv, True, block
    )
    enc_norm += step
    token_grad = take_back(source_grad, target_grad).astype(F32)
    qkv_grad = home(enc_qkv, dec_qkv, 2)
    norm_total = lax.psum(jnp.stack([enc_norm, dec_norm]), ("section", "dp", "tensor"))
    norm_grad = lax.dynamic_index_in_dim(norm_total, section, 0, keepdims=False)
    summed = [
        lax.psum(grad, "dp").astype(F32)
        for grad in (qkv_grad, out_grad, cross_grad, up_grad, down_grad)
    ]
    return (
        result[None],
        token_grad[None],
        summed[0][None],
        summed[1][None],
        summed[2][None],
        summed[3][None],
        summed[4][None],
        norm_grad[None],
    )


def solution(mesh):
    placed = (
        P("section", "dp", "tensor", None),
        P(None, "dp", None),
        P("section", None, None, "tensor"),
        P("section", "tensor", None),
        P("section", None, None, "tensor"),
        P("section", None, "tensor"),
        P("section", "tensor", None),
        P("section", None, None, None),
        P("section", "dp", "tensor", None),
    )
    return jax.shard_map(
        local,
        mesh=mesh,
        in_specs=placed,
        out_specs=(
            P("section", "dp", "tensor", None),
            P("section", "dp", "tensor", None),
            P("section", None, None, "tensor"),
            P("section", "tensor", None),
            P("section", None, None, "tensor"),
            P("section", None, "tensor"),
            P("section", "tensor", None),
            P("section", None, None, None),
        ),
        check_vma=False,
    )
```

```python
import functools
import math

import jax
import jax.numpy as jnp
from jax import lax
from jax.experimental import pallas as pl
from jax.experimental.pallas import tpu as pltpu
from jax.sharding import PartitionSpec as P

HEADS = 8
EPSILON = 1e-05
MASKED = -1000000000.0
LOG2E = 1.0 / math.log(2.0)
PAIR = 128
HALF = 64
VMEM = 60 * 1024 * 1024
BF16 = jnp.bfloat16
F32 = jnp.float32


def standardize(rows):
    mean = jnp.mean(rows, axis=-1, keepdims=True)
    centered = rows - mean
    inv = lax.rsqrt(jnp.mean(centered * centered, axis=-1, keepdims=True) + EPSILON)
    return centered * inv, inv


def affine(unit, norm_ref, slot):
    return unit * norm_ref[slot, 0:1, :] + norm_ref[slot, 1:2, :]


def norm_back(unit, inv, norm_ref, slot, grad, grad_ref):
    grad_ref[slot, 0:1, :] += jnp.sum(grad * unit, axis=0, keepdims=True)
    grad_ref[slot, 1:2, :] += jnp.sum(grad, axis=0, keepdims=True)
    scaled = grad * norm_ref[slot, 0:1, :]
    first = jnp.mean(scaled, axis=-1, keepdims=True)
    second = jnp.mean(scaled * unit, axis=-1, keepdims=True)
    return inv * (scaled - first - unit * second)


def gelu_tanh(inner):
    return jnp.tanh(0.7978845608028654 * (inner + 0.044715 * inner * inner * inner))


def gelu(inner):
    return 0.5 * inner * (1.0 + gelu_tanh(inner))


def gelu_both(inner):
    bent = gelu_tanh(inner)
    slope = 0.7978845608028654 * (1.0 + 0.134145 * inner * inner)
    half = 0.5 * (1.0 + bent)
    return inner * half, half + 0.5 * inner * (1.0 - bent * bent) * slope


def dot_nn(a, b):
    return jnp.dot(a, b, preferred_element_type=F32)


def dot_nt(a, b):
    return lax.dot_general(a, b, (((1,), (1,)), ((), ())), preferred_element_type=F32)


def dot_tn(a, b):
    return lax.dot_general(a, b, (((0,), (0,)), ((), ())), preferred_element_type=F32)


class At:
    def __init__(self, array, *lead):
        self.array, self.lead = array, lead
        self.shape = array.shape[len(lead) :]
        self.dtype = array.dtype

    def spec(self, sizes, index, **options):
        nones = (None,) * len(self.lead)
        return pl.BlockSpec(nones + tuple(sizes), lambda *g: self.lead + tuple(index(*g)), **options)


def at(array):
    return array if isinstance(array, At) else At(array)


def row_call(
    body, name, rows, block, row_ins, whole_ins, row_outs, sum_outs, flops, finish=None, finals=None
):
    row_ins = [(at(a), dim) for a, dim in row_ins]
    whole_ins = [at(a) for a in whole_ins]
    finals = sum_outs if finals is None else finals

    def blocked(array, dim):
        sizes = tuple(block if i == dim else size for i, size in enumerate(array.shape))
        return array.spec(sizes, lambda g: tuple(g if i == dim else 0 for i in range(len(sizes))))

    def blocked_out(shape, dim):
        sizes = tuple(block if i == dim else size for i, size in enumerate(shape))
        return pl.BlockSpec(
            sizes, lambda g: tuple(g if i == dim else 0 for i in range(len(shape)))
        )

    def whole(array):
        return array.spec(
            array.shape,
            lambda g: (0,) * len(array.shape),
            pipeline_mode=pl.Buffered(buffer_count=1),
        )

    def whole_out(shape):
        return pl.BlockSpec(
            shape, lambda g: (0,) * len(shape), pipeline_mode=pl.Buffered(buffer_count=1)
        )

    n_rows_in = len(row_ins)
    n_in = n_rows_in + len(whole_ins)
    n_row, n_sum = len(row_outs), len(finals)

    def kernel(*refs):
        ins, outs = refs[:n_in], refs[n_in : n_in + n_row]
        sums, totals = refs[n_in + n_row : n_in + n_row + n_sum], refs[n_in + n_row + n_sum :]

        @pl.when(pl.program_id(0) == 0)
        def _():
            for total in totals:
                total[...] = jnp.zeros_like(total)

        body(ins, outs, totals)

        @pl.when(pl.program_id(0) == pl.num_programs(0) - 1)
        def _():
            if finish is None:
                for out, total in zip(sums, totals):
                    out[...] = total[...].astype(out.dtype)
            else:
                finish(ins[n_rows_in:], totals, sums)

    arrays = [array for array, _ in row_ins] + whole_ins
    size = sum(math.prod(a.shape) * a.dtype.itemsize for a in arrays)
    return pl.pallas_call(
        kernel,
        grid=(rows // block,),
        in_specs=[blocked(a, dim) for a, dim in row_ins] + [whole(a) for a in whole_ins],
        out_specs=[blocked_out(shape, dim) for shape, _, dim in row_outs]
        + [whole_out(shape) for shape, _ in finals],
        out_shape=[jax.ShapeDtypeStruct(shape, dtype) for shape, dtype, _ in row_outs]
        + [jax.ShapeDtypeStruct(shape, dtype) for shape, dtype in finals],
        scratch_shapes=[pltpu.VMEM(shape, F32) for shape, _ in sum_outs],
        compiler_params=pltpu.CompilerParams(vmem_limit_bytes=VMEM),
        cost_estimate=pl.CostEstimate(flops=flops, bytes_accessed=size, transcendentals=0),
        name=name,
    )(*[a.array for a in arrays])


def column_blocks(wide, into, core, k, row):
    rows, columns = wide.shape[0], wide.shape[1] // 2
    for half in range(2):
        into[core, k, row + half * rows : row + (half + 1) * rows, :] = wide[
            :, half * columns : (half + 1) * columns
        ].astype(BF16)


def project_qkv(x, norm, weights, with_norm, block):
    rows, width = x.shape
    parts, part = len(weights), weights[0].shape[-1]
    score = LOG2E / math.sqrt(width // HEADS)

    def body(ins, outs, totals):
        x_ref, norm_ref, *w = ins
        q_ref, kv_ref = outs
        rows_in = x_ref[...]
        if with_norm:
            unit, _ = standardize(rows_in.astype(F32))
            rows_in = affine(unit, norm_ref, 2).astype(BF16)
        for k in range(parts):
            q_ref[k] = (dot_nn(rows_in, w[k][0]) * score).astype(BF16)
            kv_ref[k, 0] = dot_nn(rows_in, w[k][1]).astype(BF16)
            kv_ref[k, 1] = dot_nn(rows_in, w[k][2]).astype(BF16)

    return row_call(
        body,
        "project_qkv",
        rows,
        block,
        [(x, 0)],
        [norm, *weights],
        [((parts, rows, part), BF16, 1), ((parts, 2, rows, part), BF16, 2)],
        [],
        6 * rows * width * width,
    )


def encoder_forward(x, mix, norm, out, up, down, cross, block):
    rows, width = x.shape
    parts, part = len(out), out[0].shape[0]

    def body(ins, outs, totals):
        x_ref, mix_ref, norm_ref = ins[:3]
        wo, wu, wd, wc = (ins[3 + i * parts : 3 + (i + 1) * parts] for i in range(4))
        result_ref, kv_ref, first_ref, third_ref = outs
        unit, _ = standardize(x_ref[...].astype(F32))
        first = affine(unit, norm_ref, 2)
        for k in range(parts):
            first += dot_nn(mix_ref[k], wo[k][...])
        first_ref[...] = first
        unit, _ = standardize(first)
        third = affine(unit, norm_ref, 0)
        low = third.astype(BF16)
        for k in range(parts):
            act = gelu(dot_nn(low, wu[k][...])).astype(BF16)
            third += dot_nn(act, wd[k][...])
        third_ref[...] = third
        unit, _ = standardize(third)
        low = affine(unit, norm_ref, 1).astype(BF16)
        result_ref[...] = low
        for k in range(parts):
            kv_ref[k, 0] = dot_nn(low, wc[k][0]).astype(BF16)
            kv_ref[k, 1] = dot_nn(low, wc[k][1]).astype(BF16)

    units = sum(w.shape[1] for w in up)
    return row_call(
        body,
        "encoder_forward",
        rows,
        block,
        [(x, 0), (mix, 1)],
        [norm, *out, *up, *down, *cross],
        [
            ((rows, width), BF16, 0),
            ((parts, 2, rows, part), BF16, 2),
            ((rows, width), F32, 0),
            ((rows, width), F32, 0),
        ],
        [],
        6 * rows * width * width + 4 * rows * width * units,
    )


def decoder_middle(x, mix, norm, out, cross, block):
    rows, width = x.shape
    parts, part = len(out), out[0].shape[0]
    score = LOG2E / math.sqrt(width // HEADS)

    def body(ins, outs, totals):
        x_ref, mix_ref, norm_ref = ins[:3]
        wo, wc = (ins[3 + i * parts : 3 + (i + 1) * parts] for i in range(2))
        q_ref, first_ref = outs
        first = x_ref[...].astype(F32)
        for k in range(parts):
            first += dot_nn(mix_ref[k], wo[k][...])
        first_ref[...] = first
        unit, _ = standardize(first)
        low = affine(unit, norm_ref, 0).astype(BF16)
        for k in range(parts):
            q_ref[k] = (dot_nn(low, wc[k][0]) * score).astype(BF16)

    return row_call(
        body,
        "decoder_middle",
        rows,
        block,
        [(x, 0), (mix, 1)],
        [norm, *out, *cross],
        [((parts, rows, part), BF16, 1), ((rows, width), F32, 0)],
        [],
        4 * rows * width * width,
    )


def ffn_back(low, grad_low, up, down, up_total, down_total, parts):
    grad = None
    for k in range(parts):
        act, slope = gelu_both(dot_nn(low, up[k][...]))
        down_total[k] += dot_tn(act.astype(BF16), grad_low)
        grad_inner = (dot_nt(grad_low, down[k][...]) * slope).astype(BF16)
        up_total[k] += dot_tn(low, grad_inner)
        step = dot_nt(grad_inner, up[k][...])
        grad = step if grad is None else grad + step
    return grad


def decoder_turn(first, mix, cotangent, norm, cross, up, down, block, paired=False):
    rows, width = first.shape
    parts, part, units = len(cross), cross[0].shape[-1], up[0].shape[1]

    def body(ins, outs, totals):
        first_ref, mix_ref, cot_ref, norm_ref = ins[:4]
        wc, wu, wd = (ins[4 + i * parts : 4 + (i + 1) * parts] for i in range(3))
        result_ref, second_grad_ref, mix_grad_ref = outs
        out_total, up_total, down_total, norm_total = totals
        unit, _ = standardize(first_ref[...])
        second = affine(unit, norm_ref, 0)
        for k in range(parts):
            second += dot_nt(mix_ref[k], wc[k][1])
        unit_two, inv_two = standardize(second)
        third = affine(unit_two, norm_ref, 2)
        low = third.astype(BF16)
        acts, slopes = [], []
        for k in range(parts):
            act, slope = gelu_both(dot_nn(low, wu[k][...]))
            acts.append(act.astype(BF16))
            slopes.append(slope)
            third += dot_nn(acts[k], wd[k][...])
        unit_three, inv_three = standardize(third)
        result_ref[...] = affine(unit_three, norm_ref, 1).astype(BF16)
        grad = norm_back(
            unit_three, inv_three, norm_ref, 1, cot_ref[...].astype(F32), norm_total
        )
        grad_low = grad.astype(BF16)
        for k in range(parts):
            down_total[k] += dot_tn(acts[k], grad_low)
            grad_inner = (dot_nt(grad_low, wd[k][...]) * slopes[k]).astype(BF16)
            up_total[k] += dot_tn(low, grad_inner)
            grad += dot_nt(grad_inner, wu[k][...])
        grad = norm_back(unit_two, inv_two, norm_ref, 2, grad, norm_total)
        second_grad_ref[...] = grad
        grad_low = grad.astype(BF16)
        for k in range(parts):
            out_total[k] += dot_tn(grad_low, mix_ref[k])
            mix_grad_ref[k] = dot_nn(grad_low, wc[k][1]).astype(BF16)

    sums = [
        ((parts, width, part), BF16),
        ((parts, width, units), BF16),
        ((parts, units, width), BF16),
        ((3, 2, width), F32),
    ]
    if paired:
        finals = [sums[0], ((2, parts, units, width), BF16), sums[3]]

        def finish(ins, totals, outs):
            outs[0][...] = totals[0][...].astype(BF16)
            for k in range(parts):
                column_blocks(totals[1][k], outs[1], 0, k, 0)
                outs[1][1, k] = totals[2][k].astype(BF16)
            outs[2][...] = totals[3][...]

    else:
        finals, finish = None, None

    return row_call(
        body,
        "decoder_turn",
        rows,
        block,
        [(first, 0), (mix, 1), (cotangent, 0)],
        [norm, *cross, *up, *down],
        [
            ((rows, width), BF16, 0),
            ((rows, width), F32, 0),
            ((parts, rows, part), BF16, 1),
        ],
        sums,
        6 * rows * width * width + 12 * rows * width * units * parts,
        finish,
        finals,
    )


def decoder_middle_back(first, mix, query_grad, second_grad, norm, out, cross, block):
    rows, width = first.shape
    parts, part = len(out), out[0].shape[0]

    def body(ins, outs, totals):
        first_ref, mix_ref, query_grad_ref, second_grad_ref, norm_ref = ins[:5]
        wo, wc = (ins[5 + i * parts : 5 + (i + 1) * parts] for i in range(2))
        first_grad_ref, mix_grad_ref = outs
        query_total, out_total, norm_total = totals
        unit, inv = standardize(first_ref[...])
        low = affine(unit, norm_ref, 0).astype(BF16)
        grad = second_grad_ref[...]
        for k in range(parts):
            query_total[k] += dot_tn(low, query_grad_ref[k])
            grad += dot_nt(query_grad_ref[k], wc[k][0])
        grad = norm_back(unit, inv, norm_ref, 0, grad, norm_total)
        first_grad_ref[...] = grad
        grad_low = grad.astype(BF16)
        for k in range(parts):
            out_total[k] += dot_tn(mix_ref[k], grad_low)
            mix_grad_ref[k] = dot_nt(grad_low, wo[k][...]).astype(BF16)

    return row_call(
        body,
        "decoder_middle_back",
        rows,
        block,
        [(first, 0), (mix, 1), (query_grad, 1), (second_grad, 0)],
        [norm, *out, *cross],
        [((rows, width), F32, 0), ((parts, rows, part), BF16, 1)],
        [
            ((parts, width, part), BF16),
            ((parts, part, width), BF16),
            ((3, 2, width), F32),
        ],
        8 * rows * width * width,
    )


def encoder_back(
    first, third, mix, memory_grads, cotangent, norm, out, up, down, cross, block, paired=None
):
    rows, width = first.shape
    parts, part, units = len(out), out[0].shape[0], up[0].shape[1]
    pieces = len(memory_grads)

    def body(ins, outs, totals):
        first_ref, third_ref, mix_ref, cot_ref = ins[:4]
        memory_refs, norm_ref = ins[4 : 4 + pieces], ins[4 + pieces]
        rest = ins[5 + pieces :]
        wo, wu, wd, wc = (rest[i * parts : (i + 1) * parts] for i in range(4))
        first_grad_ref, mix_grad_ref = outs
        cross_total, out_total, up_total, down_total, norm_total = totals
        unit, inv = standardize(third_ref[...])
        low = affine(unit, norm_ref, 1).astype(BF16)
        grad = cot_ref[...].astype(F32)
        for i in range(2):
            for k in range(parts):
                memory = memory_refs[0][k, i].astype(F32)
                for ref in memory_refs[1:]:
                    memory += ref[k, i].astype(F32)
                memory = memory.astype(BF16)
                cross_total[k, i] += dot_tn(low, memory)
                grad += dot_nt(memory, wc[k][i])
        grad = norm_back(unit, inv, norm_ref, 1, grad, norm_total)
        unit, inv = standardize(first_ref[...])
        low = affine(unit, norm_ref, 0).astype(BF16)
        grad += ffn_back(low, grad.astype(BF16), wu, wd, up_total, down_total, parts)
        grad = norm_back(unit, inv, norm_ref, 0, grad, norm_total)
        first_grad_ref[...] = grad
        grad_low = grad.astype(BF16)
        for k in range(parts):
            out_total[k] += dot_tn(mix_ref[k], grad_low)
            mix_grad_ref[k] = dot_nt(grad_low, wo[k][...]).astype(BF16)

    sums = [
        ((parts, 2, width, part), BF16),
        ((parts, part, width), BF16),
        ((parts, width, units), BF16),
        ((parts, units, width), BF16),
        ((3, 2, width), F32),
    ]
    if paired is not None:
        side = 3 * width
        finals = [
            ((2, parts, units, width), BF16),
            ((2, parts, side, part), BF16),
            sums[4],
        ]

        def finish(ins, totals, outs):
            dec_out, dec_query, dec_cross = ins[-3:]
            for k in range(parts):
                column_blocks(totals[2][k], outs[0], 0, k, 0)
                outs[0][1, k] = totals[3][k].astype(BF16)
                column_blocks(totals[1][k], outs[1], 0, k, 0)
                outs[1][0, k, width:side, :] = (
                    totals[0][k].reshape(2 * width, part).astype(BF16)
                )
                column_blocks(dec_out[k], outs[1], 1, k, 0)
                outs[1][1, k, width : 2 * width, :] = dec_query[k]
                outs[1][1, k, 2 * width : side, :] = dec_cross[k]
            outs[2][...] = totals[4][...]

    else:
        finals, finish, paired = None, None, []

    return row_call(
        body,
        "encoder_back",
        rows,
        block,
        [(first, 0), (third, 0), (mix, 1), (cotangent, 0)] + [(m, 2) for m in memory_grads],
        [norm, *out, *up, *down, *cross, *paired],
        [((rows, width), F32, 0), ((parts, rows, part), BF16, 1)],
        sums,
        12 * rows * width * width + 10 * rows * width * units * parts,
        finish,
        finals,
    )


def input_back(
    x, first_grad, query_grad, key_grads, norm, weights, with_norm, block, paired=None
):
    rows, width = x.shape
    parts, part = len(weights), weights[0].shape[-1]
    pieces = len(key_grads)

    def body(ins, outs, totals):
        x_ref, first_grad_ref, query_grad_ref = ins[:3]
        key_refs, norm_ref, w = ins[3 : 3 + pieces], ins[3 + pieces], ins[4 + pieces :][:parts]
        (grad_ref,) = outs
        qkv_total, norm_total = totals
        low = x_ref[...]
        if with_norm:
            unit, inv = standardize(low.astype(F32))
            low = affine(unit, norm_ref, 2).astype(BF16)
        grad = first_grad_ref[...]
        for k in range(parts):
            for i in range(3):
                if i == 0:
                    member = query_grad_ref[k]
                else:
                    member = key_refs[0][k, i - 1].astype(F32)
                    for ref in key_refs[1:]:
                        member += ref[k, i - 1].astype(F32)
                    member = member.astype(BF16)
                qkv_total[k, i] += dot_tn(low, member)
                grad += dot_nt(member, w[k][i])
        if with_norm:
            grad = norm_back(unit, inv, norm_ref, 2, grad, norm_total)
        grad_ref[...] = grad.astype(BF16)

    sums = [((parts, 3, width, part), BF16), ((3, 2, width), F32)]
    if paired is not None:
        half = 3 * width // 2
        extra = PAIR if paired else 0
        finals = [((2, parts, half + extra, part), BF16)]

        def finish(ins, totals, outs):
            for k in range(parts):
                both = totals[0][k].reshape(2 * half, part).astype(BF16)
                for core in range(2):
                    outs[0][core, k, :half, :] = both[core * half : (core + 1) * half]
            if extra:
                sides = [ins[-2][...] + totals[1][...], ins[-1][...]]
                for core, table in enumerate(sides):
                    lines = [
                        table[slot, i : i + 1, h * part : (h + 1) * part]
                        for slot in range(3)
                        for i in range(2)
                        for h in range(width // part)
                    ]
                    lines.append(jnp.zeros((extra - len(lines), part), F32))
                    lines = jnp.concatenate(lines, axis=0).astype(BF16)
                    for k in range(parts):
                        outs[0][core, k, half:, :] = lines

    else:
        finals, finish, paired = None, None, []

    return row_call(
        body,
        "input_back",
        rows,
        block,
        [(x, 0), (first_grad, 0), (query_grad, 1)] + [(g, 2) for g in key_grads],
        [norm, *weights, *paired],
        [((rows, width), BF16, 0)],
        sums,
        12 * rows * width * width,
        finish,
        finals,
    )


def widen_keys(span_ref, kv_refs, key_e, key_o, value_e, value_o, rows):
    lane = lax.broadcasted_iota(jnp.int32, (rows, PAIR), 1)
    place = lax.broadcasted_iota(jnp.int32, (rows, PAIR), 0)
    low = lane < HALF
    for g, kv_ref in enumerate(kv_refs):
        spot = place + span_ref[2 + g]
        live = (spot >= span_ref[0]) & (spot < span_ref[1])
        bias = jnp.where(live, 0.0, MASKED)
        keys, values = kv_ref[0].astype(F32), kv_ref[1].astype(F32)
        own = pl.ds(g * rows, rows)
        key_e[own, :] = jnp.where(low, keys, jnp.where(lane == HALF, bias, 1.0)).astype(BF16)
        key_o[own, :] = jnp.where(low, jnp.where(lane == 0, bias, 1.0), keys).astype(BF16)
        value_e[own, :] = jnp.where(low, values, 1.0).astype(BF16)
        value_o[own, :] = jnp.where(low, 1.0, values).astype(BF16)


def attention_specs(per_part, rows, block, query, lse_lead=()):
    def query_spec(array):
        return at(array).spec(
            (None, block, PAIR), lambda i, j: (i // per_part, j, i % per_part)
        )

    def kv_spec(array):
        return at(array).spec(
            (None, 2, rows, PAIR), lambda i, j: (i // per_part, 0, 0, i % per_part)
        )

    return query_spec, kv_spec, pl.BlockSpec((block, PAIR), lambda i, j: (j, i))


def attend(query, kv_pieces, span, block, carrier=None):
    query, kv_pieces = at(query), [at(piece) for piece in kv_pieces]
    carrier = carrier or Carrier()
    parts, rows, part = query.shape
    per_part = part // PAIR
    pairs = parts * per_part
    pieces = len(kv_pieces)
    keys = rows * pieces
    n_carry = len(carrier.ins)

    def kernel(span_ref, q_ref, *refs):
        kv_refs, refs = refs[:pieces], refs[pieces:]
        carry_ins, refs = refs[:n_carry], refs[n_carry:]
        out_ref, lse_ref, refs = refs[0], refs[1], refs[2:]
        carry_outs, refs = refs[: len(carrier.outs)], refs[len(carrier.outs) :]
        key_e, key_o, value_e, value_o = refs[:4]
        step = pl.program_id(0) * pl.num_programs(1) + pl.program_id(1)
        carrier.run(step, pairs * (rows // block), carry_ins, carry_outs, refs[4:])

        @pl.when(pl.program_id(1) == 0)
        def _():
            widen_keys(span_ref, kv_refs, key_e, key_o, value_e, value_o, rows)

        lane = lax.broadcasted_iota(jnp.int32, (block, PAIR), 1)
        low = lane < HALF
        query = q_ref[...].astype(F32)
        query_e = jnp.where(low, query, jnp.where(lane == HALF, 1.0, 0.0)).astype(BF16)
        query_o = jnp.where(low, jnp.where(lane == 0, 1.0, 0.0), query).astype(BF16)
        tops, sums = [], []
        for q, k, v in ((query_e, key_e, value_e), (query_o, key_o, value_o)):
            scores = dot_nt(q, k[...])
            top = jnp.max(scores, axis=1, keepdims=True)
            tops.append(top)
            sums.append(dot_nn(jnp.exp2(scores - top).astype(BF16), v[...]))
        top = jnp.where(low, tops[1], tops[0])
        weight = jnp.where(low, sums[1], sums[0])
        lse_ref[...] = top + LOG2E * jnp.log(weight)
        mixed = jnp.where(low, sums[0], sums[1])
        out_ref[...] = (mixed / pltpu.roll(weight, HALF, 1)).astype(BF16)

    query_spec, kv_spec, lse_spec = attention_specs(per_part, rows, block, query)
    out_spec = pl.BlockSpec(
        (None, block, PAIR), lambda i, j: (i // per_part, j, i % per_part)
    )
    hold = pl.BlockSpec(memory_space=pl.ANY)
    return pl.pallas_call(
        kernel,
        grid=(pairs, rows // block),
        in_specs=[pl.BlockSpec(memory_space=pltpu.SMEM), query_spec(query)]
        + [kv_spec(piece) for piece in kv_pieces]
        + [hold] * n_carry,
        out_specs=[out_spec, lse_spec] + [hold] * len(carrier.outs),
        scratch_shapes=[pltpu.VMEM((keys, PAIR), BF16)] * 4 + carrier.scratch,
        out_shape=[
            jax.ShapeDtypeStruct(query.shape, BF16),
            jax.ShapeDtypeStruct((rows, pairs * PAIR), F32),
        ]
        + carrier.outs,
        compiler_params=pltpu.CompilerParams(vmem_limit_bytes=VMEM, **carrier.params),
        cost_estimate=pl.CostEstimate(
            flops=16 * rows * keys * pairs * PAIR,
            bytes_accessed=8 * rows * pairs * PAIR * pieces,
            transcendentals=0,
        ),
        name="attend",
    )(span, query.array, *[piece.array for piece in kv_pieces], *carrier.ins)


def attend_back(query, kv_pieces, mix, mix_grad, lse, span, block, chunk, carrier=None):
    query, kv_pieces = at(query), [at(piece) for piece in kv_pieces]
    mix, mix_grad = at(mix), at(mix_grad)
    carrier = carrier or Carrier()
    parts, rows, part = query.shape
    per_part = part // PAIR
    pairs = parts * per_part
    pieces = len(kv_pieces)
    keys = rows * pieces
    scale = 1.0 / math.sqrt(HALF)
    n_carry = len(carrier.ins)

    def kernel(span_ref, q_ref, mix_ref, grad_ref, lse_ref, *refs):
        kv_refs, refs = refs[:pieces], refs[pieces:]
        carry_ins, refs = refs[:n_carry], refs[n_carry:]
        dq_ref, dkv_refs, refs = refs[0], refs[1 : pieces + 1], refs[pieces + 1 :]
        carry_outs, refs = refs[: len(carrier.outs)], refs[len(carrier.outs) :]
        key_e, key_o, value_e, value_o, key_t, key_total, value_total = refs[:7]
        step = pl.program_id(0) * pl.num_programs(1) + pl.program_id(1)
        carrier.run(step, pairs * (rows // block), carry_ins, carry_outs, refs[7:])

        @pl.when(pl.program_id(1) == 0)
        def _():
            widen_keys(span_ref, kv_refs, key_e, key_o, value_e, value_o, rows)
            for g, kv_ref in enumerate(kv_refs):
                key_t[:, pl.ds(g * rows, rows)] = kv_ref[0].T
            key_total[...] = jnp.zeros_like(key_total)
            value_total[...] = jnp.zeros_like(value_total)

        lane = lax.broadcasted_iota(jnp.int32, (block, PAIR), 1)
        low = lane < HALF
        query, grad = q_ref[...].astype(F32), grad_ref[...].astype(F32)
        product = mix_ref[...].astype(F32) * grad
        inner = jnp.where(
            low,
            jnp.sum(jnp.where(low, 0.0, product), axis=1, keepdims=True),
            jnp.sum(jnp.where(low, product, 0.0), axis=1, keepdims=True),
        )
        spot = jnp.where(low, lane, lane - HALF)

        def three(value, shift):
            high = value.astype(BF16).astype(F32)
            rest = value - high
            mid = rest.astype(BF16).astype(F32)
            return jnp.where(
                spot == shift,
                high,
                jnp.where(
                    spot == shift + 1, mid, jnp.where(spot == shift + 2, rest - mid, 0.0)
                ),
            )

        lse = three(-lse_ref[...], 1) + jnp.where(spot == 0, 1.0, 0.0)
        inner = three(-inner, 0)
        heads = []
        for own, key, value in ((low, key_e, value_e), (~low, key_o, value_o)):
            heads.append(
                (
                    key,
                    value,
                    jnp.where(own, query, lse).astype(BF16),
                    jnp.where(own, grad, inner).astype(BF16),
                    jnp.where(own, query, 0.0).astype(BF16),
                    jnp.where(own, grad, 0.0).astype(BF16),
                )
            )
        dq = [None, None]
        for c in range(keys // chunk):
            span_c = pl.ds(c * chunk, chunk)
            dk, dv = None, None
            for h, (key, value, q_wide, g_wide, q_own, g_own) in enumerate(heads):
                probs = jnp.exp2(dot_nt(key[span_c, :], q_wide))
                dscores = (probs * dot_nt(value[span_c, :], g_wide)).astype(BF16)
                step_v = dot_nn(probs.astype(BF16), g_own)
                step_k = dot_nn(dscores, q_own)
                step_q = dot_nn(key_t[pl.ds(h * HALF, HALF), span_c], dscores)
                dv = step_v if dv is None else dv + step_v
                dk = step_k if dk is None else dk + step_k
                dq[h] = step_q if dq[h] is None else dq[h] + step_q
            key_total[span_c, :] += dk
            value_total[span_c, :] += dv
        dq_ref[...] = (jnp.concatenate(dq, axis=0).T * scale).astype(BF16)

        @pl.when(pl.program_id(1) == pl.num_programs(1) - 1)
        def _():
            for g, ref in enumerate(dkv_refs):
                own = pl.ds(g * rows, rows)
                ref[0] = (key_total[own, :] * (1.0 / LOG2E)).astype(BF16)
                ref[1] = value_total[own, :].astype(BF16)

    query_spec, kv_spec, lse_spec = attention_specs(per_part, rows, block, query)
    plain = jax.ShapeDtypeStruct(query.shape, BF16)
    plain_kv = jax.ShapeDtypeStruct((parts, 2, rows, part), BF16)
    hold = pl.BlockSpec(memory_space=pl.ANY)
    out = pl.pallas_call(
        kernel,
        grid=(pairs, rows // block),
        in_specs=[pl.BlockSpec(memory_space=pltpu.SMEM)]
        + [query_spec(a) for a in (query, mix, mix_grad)]
        + [lse_spec]
        + [kv_spec(piece) for piece in kv_pieces]
        + [hold] * n_carry,
        out_specs=[query_spec(plain)]
        + [kv_spec(plain_kv)] * pieces
        + [hold] * len(carrier.outs),
        scratch_shapes=[pltpu.VMEM((keys, PAIR), BF16)] * 4
        + [pltpu.VMEM((PAIR, keys), BF16)]
        + [pltpu.VMEM((keys, PAIR), F32)] * 2
        + carrier.scratch,
        out_shape=[plain] + [plain_kv] * pieces + carrier.outs,
        compiler_params=pltpu.CompilerParams(vmem_limit_bytes=VMEM, **carrier.params),
        cost_estimate=pl.CostEstimate(
            flops=40 * rows * keys * pairs * PAIR,
            bytes_accessed=16 * rows * pairs * PAIR * pieces,
            transcendentals=0,
        ),
        name="attend_back",
    )(
        span,
        query.array,
        mix.array,
        mix_grad.array,
        lse,
        *[piece.array for piece in kv_pieces],
        *carrier.ins,
    )
    return out[0], out[1 : pieces + 1], out[pieces + 1 :]


def spots():
    return lax.axis_index("section"), lax.axis_index("dp"), lax.axis_index("tensor")


def remote(source, target, sent, landed, **where):
    return pltpu.make_async_remote_copy(
        src_ref=source,
        dst_ref=target,
        send_sem=sent,
        recv_sem=landed,
        device_id=where,
        device_id_type=pl.DeviceIdType.MESH,
    )


def greet(peers):
    barrier = pltpu.get_barrier_semaphore()
    for peer in peers:
        pl.semaphore_signal(
            barrier, inc=1, device_id=peer, device_id_type=pl.DeviceIdType.MESH
        )
    pl.semaphore_wait(barrier, len(peers))


def group_peers():
    section, _, tensor = spots()
    return [
        {"section": 1 - section},
        {"tensor": 1 - tensor},
        {"section": 1 - section, "tensor": 1 - tensor},
    ]


class Carrier:
    ins, outs, scratch, params = (), [], [], {}

    def run(self, step, steps, ins, outs, scratch):
        pass


class SpreadRows:
    sems = [pltpu.SemaphoreType.DMA((2,)), pltpu.SemaphoreType.DMA((2,)), pltpu.SemaphoreType.DMA]

    def __init__(self, source, target, sems):
        self.source, self.target = source, target
        self.sent, self.landed, self.kept = sems

    def copy(self, row):
        section, _, tensor = spots()
        return remote(
            self.source.at[row],
            self.target.at[section],
            self.sent.at[row],
            self.landed.at[section],
            section=tensor,
            tensor=row,
        )

    def keep(self, row):
        section, _, _ = spots()
        return pltpu.make_async_copy(self.source.at[row], self.target.at[section], self.kept)

    def start(self):
        section, _, tensor = spots()
        for row in range(2):
            stays = (section == tensor) & (tensor == row)

            @pl.when(stays)
            def _():
                self.keep(row).start()

            @pl.when(jnp.logical_not(stays))
            def _():
                self.copy(row).start()

    def wait_side(self, side):
        section, _, tensor = spots()
        stays = (section == tensor) & (section == side)

        @pl.when(stays)
        def _():
            self.keep(side).wait()

        @pl.when(jnp.logical_not(stays))
        def _():
            remote(
                self.source.at[0],
                self.target.at[side],
                self.sent.at[0],
                self.landed.at[side],
                section=tensor,
                tensor=0,
            ).wait_recv()

    def wait_sent(self):
        section, _, tensor = spots()
        for row in range(2):
            @pl.when(jnp.logical_not((section == tensor) & (tensor == row)))
            def _():
                self.copy(row).wait_send()


class SpreadWeight:
    sems = [pltpu.SemaphoreType.DMA((7,))]

    def __init__(self, source, target, sems):
        section, _, tensor = spots()
        (sem,) = sems
        self.kept = pltpu.make_async_copy(source, target.at[section, 0], sem.at[0])
        self.over = remote(source, target.at[section, 1], sem.at[1], sem.at[2], tensor=1 - tensor)
        self.near = remote(source, target.at[section, 0], sem.at[3], sem.at[4], section=1 - section)
        self.onward = remote(
            target.at[section, 1],
            target.at[section, 1],
            sem.at[5],
            sem.at[6],
            section=1 - section,
        )

    def start(self):
        self.over.start()
        self.kept.start()
        self.near.start()

    def forward(self):
        self.over.wait_recv()
        self.onward.start()

    def finish(self):
        self.kept.wait()
        self.near.wait()
        self.over.wait_send()
        self.onward.wait()


class Spread(Carrier):
    def __init__(self, weights, forwards, rows, collective):
        self.ins = [*weights, *rows]
        self.weights, self.rows, self.forwards = len(weights), len(rows), forwards
        self.outs = [jax.ShapeDtypeStruct((2, 2, *w.shape), w.dtype) for w in weights] + [
            jax.ShapeDtypeStruct(r.shape, r.dtype) for r in rows
        ]
        self.scratch = SpreadWeight.sems * len(weights) + SpreadRows.sems * len(rows)
        self.params = dict(collective_id=collective, has_side_effects=True)

    def run(self, step, steps, ins, outs, scratch):
        def weight(i):
            return SpreadWeight(ins[i], outs[i], scratch[i : i + 1])

        def row(i):
            spot = self.weights + i
            sems = scratch[self.weights + 3 * i : self.weights + 3 * i + 3]
            return SpreadRows(ins[spot], outs[spot], sems)

        @pl.when(step == 0)
        def _():
            greet(group_peers())
            for i in range(self.weights):
                weight(i).start()
            for i in range(self.rows):
                row(i).start()

        for i, when in enumerate(self.forwards):

            @pl.when(step == when)
            def _():
                weight(i).forward()

        @pl.when(step == steps - 1)
        def _():
            for i in range(self.weights):
                weight(i).finish()
            for i in range(self.rows):
                row(i).wait_side(0)
                row(i).wait_side(1)
                row(i).wait_sent()


class Reduce(Carrier):
    def __init__(self, sources, chunk, collective):
        self.ins = list(sources)
        self.chunk = chunk
        self.places = [
            (i, row) for i, s in enumerate(sources) for row in range(0, s.shape[2], chunk)
        ]
        self.count = len(self.places)
        self.levels = lax.axis_size("dp").bit_length() - 1
        width = sources[0].shape[3]
        self.outs = [jax.ShapeDtypeStruct((self.count * chunk, width), BF16)]

        def room(*shape):
            return pltpu.VMEM((self.count, *shape, width), BF16)

        halves = [room(chunk >> (level + 1)) for level in range(self.levels)]
        self.scratch = [room(2, chunk), room(2, chunk), room(chunk), room(chunk)]
        self.scratch += halves + halves
        self.scratch += [pltpu.SemaphoreType.DMA((2 + 2 * (2 + 2 * self.levels), self.count))]
        self.params = dict(collective_id=collective, has_side_effects=True)
        self.stages = 4 + 2 * self.levels
        self.steps = self.count + self.stages - 1

    def run(self, step, steps, ins, outs, scratch):
        chunk, levels = self.chunk, self.levels
        assert steps >= self.steps
        own, chip, other, full = scratch[:4]
        halves, doubles = scratch[4 : 4 + levels], scratch[4 + levels : 4 + 2 * levels]
        sems = scratch[4 + 2 * levels]
        section, group, tensor = spots()
        bits = [(group // (1 << level)) % 2 for level in range(levels)]
        peers = [group + (1 << level) * (1 - 2 * bits[level]) for level in range(levels)]
        begins = [0]
        for level in range(levels):
            begins.append(begins[level] + bits[level] * (chunk >> (level + 1)))

        def keeps(level):
            return pl.ds(pl.multiple_of(begins[level + 1], 16), chunk >> (level + 1))

        def gives(level):
            start = begins[level] + (1 - bits[level]) * (chunk >> (level + 1))
            return pl.ds(pl.multiple_of(start, 16), chunk >> (level + 1))

        def pair(kind, c):
            return sems.at[2 + 2 * kind, c], sems.at[3 + 2 * kind, c]

        def load(c):
            i, row = self.places[c]
            return pltpu.make_async_copy(
                ins[i].at[section, :, pl.ds(row, chunk), :], own.at[c], sems.at[0, c]
            )

        def cross(c, place=None):
            i, row = self.places[0] if place is None else place
            return remote(
                ins[i].at[1 - section, :, pl.ds(row, chunk), :],
                chip.at[c],
                *pair(0, c),
                section=1 - section,
            )

        def over(c):
            return remote(own.at[c, 1], other.at[c], *pair(1, c), tensor=1 - tensor)

        def halve(level, c):
            return remote(
                own.at[c, 0, gives(level), :],
                halves[level].at[c],
                *pair(2 + level, c),
                dp=peers[level],
            )

        def double(level, c):
            return remote(
                full.at[c, keeps(level), :],
                doubles[level].at[c],
                *pair(2 + levels + level, c),
                dp=peers[level],
            )

        def store(c):
            return pltpu.make_async_copy(
                full.at[c],
                outs[0].at[pl.ds(pl.multiple_of(c * chunk, 16), chunk), :],
                sems.at[1, c],
            )

        def added(a, b):
            return (a.astype(F32) + b.astype(F32)).astype(BF16)

        def stage(number, c):
            if number == 1:
                pltpu.make_async_copy(
                    ins[0].at[section, :, pl.ds(0, chunk), :], own.at[c], sems.at[0, c]
                ).wait()
                cross(c).wait()
                own[c] = added(own[c], chip[c])
                over(c).start()
            elif number == 2:
                over(c).wait()
                own[c, 0] = added(own[c, 0], other[c])
                halve(0, c).start()
            elif number < 3 + levels:
                level = number - 3
                halve(level, c).wait()
                mine = keeps(level)
                if level < levels - 1:
                    own[c, 0, mine, :] = added(own[c, 0, mine, :], halves[level][c])
                    halve(level + 1, c).start()
                else:
                    full[c, mine, :] = added(own[c, 0, mine, :], halves[level][c])
                    double(level, c).start()
            elif number < 3 + 2 * levels:
                level = levels - 1 - (number - 3 - levels)
                double(level, c).wait()
                full[c, gives(level), :] = doubles[level][c]
                if level:
                    double(level - 1, c).start()
                else:
                    store(c).start()
            else:
                store(c).wait()

        @pl.when(step == 0)
        def _():
            greet(
                [{"section": 1 - section}, {"tensor": 1 - tensor}]
                + [{"dp": peer} for peer in peers]
            )

        for number in reversed(range(1, self.stages)):
            c = step - number

            @pl.when((c >= 0) & (c < self.count))
            def _():
                stage(number, c)

        for c, place in enumerate(self.places):

            @pl.when(step == c)
            def _():
                load(c).start()
                cross(c, place).start()


def reduce_alone(sources, chunk, collective):
    carrier = Reduce(sources, chunk, collective)

    def kernel(*refs):
        n = len(carrier.ins)
        carrier.run(pl.program_id(0), carrier.steps, refs[:n], refs[n : n + 1], refs[n + 1 :])

    hold = pl.BlockSpec(memory_space=pl.ANY)
    return pl.pallas_call(
        kernel,
        grid=(carrier.steps,),
        in_specs=[hold] * len(carrier.ins),
        out_specs=hold,
        out_shape=carrier.outs[0],
        scratch_shapes=carrier.scratch,
        compiler_params=pltpu.CompilerParams(vmem_limit_bytes=VMEM, **carrier.params),
        name="reduce_alone",
    )(*carrier.ins)


def open_up(tokens, qkv, norm, block, collective):
    _, rows, width = tokens.shape
    part = qkv.shape[-1]
    score = LOG2E / math.sqrt(width // HEADS)

    def kernel(tokens_ref, qkv_ref, norm_ref, *refs):
        x_out, w_out, n_out, q_out, own_out, other_out = refs[:6]
        x, low, w, n, q, kv = refs[6:12]
        row_sems, weight_sems, norm_sems, load_sems, store_sems, kv_sems = (
            refs[12:15],
            refs[15:16],
            refs[16],
            refs[17],
            refs[18],
            refs[19],
        )
        section, _, _ = spots()
        greet(group_peers())
        rows_in = SpreadRows(tokens_ref, x, row_sems)
        weight = SpreadWeight(qkv_ref, w, weight_sems)
        rows_in.start()
        weight.start()
        norm_kept = pltpu.make_async_copy(norm_ref, n.at[section], norm_sems.at[0])
        norm_near = remote(
            norm_ref, n.at[section], norm_sems.at[1], norm_sems.at[2], section=1 - section
        )
        norm_kept.start()
        norm_near.start()
        stores = []

        def save(source, target):
            copy = pltpu.make_async_copy(source, target, store_sems.at[len(stores)])
            copy.start()
            stores.append(copy)

        kv_copies = []

        def project(side, k):
            def step(i, carry):
                own = pl.ds(pl.multiple_of(i * block, block), block)
                rows_low = low[own, :] if side == 0 else x[1, own, :]
                q[side, k, own, :] = (dot_nn(rows_low, w[side, k, 0]) * score).astype(BF16)
                kv[side, k, 0, own, :] = dot_nn(rows_low, w[side, k, 1]).astype(BF16)
                kv[side, k, 1, own, :] = dot_nn(rows_low, w[side, k, 2]).astype(BF16)
                return carry

            lax.fori_loop(0, rows // block, step, 0)
            spot = 2 * (2 * side + k)
            copy = remote(
                kv.at[side, k],
                other_out.at[side, k],
                kv_sems.at[spot],
                kv_sems.at[spot + 1],
                section=1 - section,
            )
            copy.start()
            kv_copies.append(copy)
            save(kv.at[side, k], own_out.at[side, k])
            save(q.at[side, k], q_out.at[side, k])

        norm_kept.wait()
        norm_near.wait()
        save(n, n_out)
        rows_in.wait_side(0)
        save(x.at[0], x_out.at[0])

        def settle(i, carry):
            own = pl.ds(pl.multiple_of(i * block, block), block)
            unit, _ = standardize(x[0, own, :].astype(F32))
            low[own, :] = affine(unit, n.at[0], 2).astype(BF16)
            return carry

        lax.fori_loop(0, rows // block, settle, 0)
        weight.kept.wait()
        weight.near.wait()
        project(0, 0)
        rows_in.wait_side(1)
        save(x.at[1], x_out.at[1])
        project(1, 0)
        weight.forward()
        weight.over.wait_send()
        weight.onward.wait()
        save(w, w_out)
        project(0, 1)
        project(1, 1)
        rows_in.wait_sent()
        for copy in kv_copies + stores:
            copy.wait()

    hold = pl.BlockSpec(memory_space=pl.ANY)
    shapes = [
        ((2, rows, width), BF16),
        ((2, 2, *qkv.shape), BF16),
        ((2, *norm.shape), F32),
        ((2, 2, rows, part), BF16),
        ((2, 2, 2, rows, part), BF16),
    ]
    return pl.pallas_call(
        kernel,
        in_specs=[hold] * 3,
        out_specs=[hold] * 6,
        out_shape=[jax.ShapeDtypeStruct(*s) for s in shapes + shapes[-1:]],
        scratch_shapes=[pltpu.VMEM(*shapes[0]), pltpu.VMEM((rows, width), BF16)]
        + [pltpu.VMEM(*s) for s in shapes[1:]]
        + SpreadRows.sems
        + SpreadWeight.sems
        + [
            pltpu.SemaphoreType.DMA((3,)),
            pltpu.SemaphoreType.DMA((1,)),
            pltpu.SemaphoreType.DMA((12,)),
            pltpu.SemaphoreType.DMA((8,)),
        ],
        compiler_params=pltpu.CompilerParams(
            vmem_limit_bytes=VMEM, collective_id=collective, has_side_effects=True
        ),
        name="open_up",
    )(tokens, qkv, norm)


def local_general(tokens, lengths, self_qkv, self_out, cross_proj, ffn_up, ffn_down, norms, cotangent):
    section = lax.axis_index("section")
    tensor = lax.axis_index("tensor")
    tensors = lax.axis_size("tensor")
    _, row_count, rows, width = tokens.shape
    assert row_count == 2 and tensors % row_count == 0
    spread = tensors // row_count
    pieces = 2 * spread
    axes = ("section", "tensor")
    is_first = section == 0
    own_row = tensor // spread
    place = section * spread + tensor % spread

    def device(row, spot):
        return (spot // spread) * tensors + row * spread + spot % spread

    def each():
        return [(s, t) for s in range(2) for t in range(tensors)]

    straight = [(s * tensors + t, device(s, t)) for s, t in each()]
    turned = [(s * tensors + t, device(1 - s, t)) for s, t in each()]

    def bring(shares):
        stays = lax.dynamic_index_in_dim(shares, section, 0, keepdims=False)
        moves = lax.dynamic_index_in_dim(shares, 1 - section, 0, keepdims=False)
        one = lax.ppermute(stays, axes, straight)
        two = lax.ppermute(moves, axes, turned)
        return jnp.where(own_row == 0, one, two), jnp.where(own_row == 0, two, one)

    def take_back(source, target):
        one = jnp.where(own_row == 0, source, target)
        two = jnp.where(own_row == 0, target, source)
        one = lax.ppermute(one, axes, [(b, a) for a, b in straight])
        two = lax.ppermute(two, axes, [(b, a) for a, b in turned])
        return jnp.stack([jnp.where(is_first, one, two), jnp.where(is_first, two, one)])

    def rotate(value, by):
        pairs = [
            (device(r, p), device(r, (p + by) % pieces))
            for r in range(row_count)
            for p in range(pieces)
        ]
        return lax.ppermute(value, axes, pairs)

    def pieces_of(value):
        return [value] + [rotate(value, by) for by in range(1, pieces)]

    def pieces_home(values):
        return [values[0]] + [rotate(values[by], -by) for by in range(1, pieces)]

    def swap_sections(value):
        return lax.ppermute(value, "section", [(0, 1), (1, 0)])

    def both_sides(weight, dim):
        if spread == 1:
            other = lax.ppermute(weight, "tensor", [(t, 1 - t) for t in range(tensors)])
            parts = [weight, other]
        else:
            parts = [lax.all_gather(weight, "tensor", axis=dim, tiled=True)]
        swapped = [swap_sections(part) for part in parts]
        pairs = list(zip(parts, swapped))
        return (
            [jnp.where(is_first, mine, theirs) for mine, theirs in pairs],
            [jnp.where(is_first, theirs, mine) for mine, theirs in pairs],
        )

    def home(source_grad, target_grad, dim):
        keep = jnp.where(is_first, source_grad, target_grad).astype(F32)
        sent = swap_sections(jnp.where(is_first, target_grad, source_grad))
        total = (keep + sent.astype(F32)).astype(BF16)
        if spread == 1:
            other = lax.ppermute(total[1], "tensor", [(t, 1 - t) for t in range(tensors)])
            total = (total[0].astype(F32) + other.astype(F32)).astype(BF16)
        else:
            total = lax.psum_scatter(total[0], "tensor", scatter_dimension=dim, tiled=True)
        return total

    def span_of(query_side, key_side):
        own = lax.dynamic_index_in_dim(lengths, own_row, 1, keepdims=False)
        asks, answers = own[query_side], own[key_side]
        paired = asks[1] > 0
        second = paired & (place * rows >= asks[0])
        begin = jnp.where(second, answers[0], 0)
        end = jnp.where(second | ~paired, answers[0] + answers[1], answers[0])
        offsets = [(place - by) % pieces * rows for by in range(pieces)]
        return jnp.stack([begin, end, *offsets]).astype(jnp.int32)

    block = min(256, rows)
    query_block = min(256, rows)
    chunk = 512

    source, target = bring(tokens[0])
    source_norm, target_norm = (
        jnp.where(is_first, a, b)
        for a, b in (lambda own, other: ((own, other), (other, own)))(
            norms[0], swap_sections(norms[0])
        )
    )
    source_qkv, target_qkv = both_sides(self_qkv[0], 2)
    source_out, target_out = both_sides(self_out[0], 0)
    source_up, target_up = both_sides(ffn_up[0], 1)
    source_down, target_down = both_sides(ffn_down[0], 0)
    source_cross, target_cross = both_sides(cross_proj[0], 2)
    source_cot, target_cot = bring(cotangent[0])
    source_span, target_span, cross_span = span_of(0, 0), span_of(1, 1), span_of(1, 0)

    enc_q, enc_kv = project_qkv(source, source_norm, source_qkv, True, block)
    enc_kv = pieces_of(enc_kv)
    dec_q, dec_kv = project_qkv(target, target_norm, target_qkv, False, block)
    dec_kv = pieces_of(dec_kv)
    enc_mix, enc_lse = attend(enc_q, enc_kv, source_span, query_block)
    encoded, memory, enc_first, enc_third = encoder_forward(
        source, enc_mix, source_norm, source_out, source_up, source_down, source_cross, block
    )
    memory = pieces_of(memory)
    dec_mix, dec_lse = attend(dec_q, dec_kv, target_span, query_block)
    cross_q, dec_first = decoder_middle(
        target, dec_mix, target_norm, target_out, target_cross, block
    )
    cross_mix, cross_lse = attend(cross_q, memory, cross_span, query_block)
    decoded, second_grad, cross_mix_grad, cross_out_grad, dec_up, dec_down, dec_norm = decoder_turn(
        dec_first, cross_mix, target_cot, target_norm, target_cross, target_up, target_down, block
    )
    result = take_back(encoded, decoded)
    cross_q_grad, memory_grads, _ = attend_back(
        cross_q, memory, cross_mix, cross_mix_grad, cross_lse, cross_span, query_block, chunk
    )
    memory_grads = pieces_home(memory_grads)
    dec_first_grad, dec_mix_grad, cross_query_grad, dec_out, step = decoder_middle_back(
        dec_first,
        dec_mix,
        cross_q_grad,
        second_grad,
        target_norm,
        target_out,
        target_cross,
        block,
    )
    dec_norm += step
    enc_first_grad, enc_mix_grad, enc_cross, enc_out, enc_up, enc_down, enc_norm = encoder_back(
        enc_first,
        enc_third,
        enc_mix,
        memory_grads,
        source_cot,
        source_norm,
        source_out,
        source_up,
        source_down,
        source_cross,
        block,
    )
    dec_cross = jnp.stack([cross_query_grad, cross_out_grad], axis=1)
    up_grad, down_grad = home(enc_up, dec_up, 1), home(enc_down, dec_down, 0)
    out_grad, cross_grad = home(enc_out, dec_out, 0), home(enc_cross, dec_cross, 2)
    dec_q_grad, dec_kv_grads, _ = attend_back(
        dec_q, dec_kv, dec_mix, dec_mix_grad, dec_lse, target_span, query_block, chunk
    )
    dec_kv_grads = pieces_home(dec_kv_grads)
    enc_q_grad, enc_kv_grads, _ = attend_back(
        enc_q, enc_kv, enc_mix, enc_mix_grad, enc_lse, source_span, query_block, chunk
    )
    enc_kv_grads = pieces_home(enc_kv_grads)
    target_grad, dec_qkv, _ = input_back(
        target, dec_first_grad, dec_q_grad, dec_kv_grads, target_norm, target_qkv, False, block
    )
    source_grad, enc_qkv, step = input_back(
        source, enc_first_grad, enc_q_grad, enc_kv_grads, source_norm, source_qkv, True, block
    )
    enc_norm += step
    token_grad = take_back(source_grad, target_grad).astype(F32)
    qkv_grad = home(enc_qkv, dec_qkv, 2)
    norm_total = lax.psum(jnp.stack([enc_norm, dec_norm]), ("section", "dp", "tensor"))
    norm_grad = lax.dynamic_index_in_dim(norm_total, section, 0, keepdims=False)
    summed = [
        lax.psum(grad, "dp").astype(F32)
        for grad in (qkv_grad, out_grad, cross_grad, up_grad, down_grad)
    ]
    return (
        result[None],
        token_grad[None],
        summed[0][None],
        summed[1][None],
        summed[2][None],
        summed[3][None],
        summed[4][None],
        norm_grad[None],
    )


def local_fast(tokens, lengths, self_qkv, self_out, cross_proj, ffn_up, ffn_down, norms, cotangent):
    section, tensor = lax.axis_index("section"), lax.axis_index("tensor")
    _, row_count, rows, width = tokens.shape
    assert row_count == 2
    is_first = section == 0
    block = min(256, rows)
    query_block = min(256, rows)
    chunk = 512

    def swap(value):
        return lax.ppermute(value, "section", [(0, 1), (1, 0)])

    def give_back(value, side):
        return [
            lax.ppermute(
                value, ("section", "tensor"), [(2 * p + row, 2 * side + p) for p in range(2)]
            )
            for row in range(2)
        ]

    def span_of(query_side, key_side):
        own = lax.dynamic_index_in_dim(lengths, tensor, 1, keepdims=False)
        asks, answers = own[query_side], own[key_side]
        paired = asks[1] > 0
        second = paired & (section * rows >= asks[0])
        begin = jnp.where(second, answers[0], 0)
        end = jnp.where(second | ~paired, answers[0] + answers[1], answers[0])
        return jnp.stack([begin, end, section * rows, (1 - section) * rows]).astype(jnp.int32)

    spans = span_of(0, 0), span_of(1, 1), span_of(1, 0)
    x, qkv, norm, q, kv_own, kv_other = open_up(tokens[0], self_qkv[0], norms[0], block, 1)

    def parts(weight, side):
        return [At(weight, side, k) for k in range(2)]

    enc_x, dec_x, enc_norm_in, dec_norm_in = At(x, 0), At(x, 1), At(norm, 0), At(norm, 1)
    enc_q, dec_q = At(q, 0), At(q, 1)
    enc_kv, dec_kv = [[At(kv_own, side), At(kv_other, side)] for side in range(2)]
    enc_mix, enc_lse, out, up = attend(
        enc_q, enc_kv, spans[0], query_block, Spread([self_out[0], ffn_up[0]], [5, 14], [], 2)
    )
    dec_mix, dec_lse, cross, down = attend(
        dec_q, dec_kv, spans[1], query_block, Spread([cross_proj[0], ffn_down[0]], [7, 14], [], 3)
    )
    encoded, memory, enc_first, enc_third = encoder_forward(
        enc_x,
        enc_mix,
        enc_norm_in,
        parts(out, 0),
        parts(up, 0),
        parts(down, 0),
        parts(cross, 0),
        block,
    )
    memory = [memory, swap(memory)]
    cross_q, dec_first = decoder_middle(
        dec_x, dec_mix, dec_norm_in, parts(out, 1), parts(cross, 1), block
    )
    cross_mix, cross_lse, cot = attend(
        cross_q, memory, spans[2], query_block, Spread([], [], [cotangent[0]], 4)
    )
    decoded, second_grad, cross_mix_grad, cross_out_grad, ffn_dec, dec_norm = decoder_turn(
        dec_first,
        cross_mix,
        At(cot, 1),
        dec_norm_in,
        parts(cross, 1),
        parts(up, 1),
        parts(down, 1),
        block,
        True,
    )
    cross_q_grad, memory_grads, (ffn_dec,) = attend_back(
        cross_q,
        memory,
        cross_mix,
        cross_mix_grad,
        cross_lse,
        spans[2],
        query_block,
        chunk,
        Reduce([ffn_dec], 256, 5),
    )
    memory_grads = [memory_grads[0], swap(memory_grads[1])]
    encoded, decoded = give_back(encoded, 0), give_back(decoded, 1)
    dec_first_grad, dec_mix_grad, cross_query_grad, dec_out, step = decoder_middle_back(
        dec_first,
        dec_mix,
        cross_q_grad,
        second_grad,
        dec_norm_in,
        parts(out, 1),
        parts(cross, 1),
        block,
    )
    dec_norm += step
    enc_first_grad, enc_mix_grad, ffn_enc, sides, enc_norm = encoder_back(
        enc_first,
        enc_third,
        enc_mix,
        memory_grads,
        At(cot, 0),
        enc_norm_in,
        parts(out, 0),
        parts(up, 0),
        parts(down, 0),
        parts(cross, 0),
        block,
        [dec_out, cross_query_grad, cross_out_grad],
    )
    dec_q_grad, dec_kv_grads, (ffn_enc,) = attend_back(
        dec_q,
        dec_kv,
        dec_mix,
        dec_mix_grad,
        dec_lse,
        spans[1],
        query_block,
        chunk,
        Reduce([ffn_enc], 256, 6),
    )
    dec_kv_grads = [dec_kv_grads[0], swap(dec_kv_grads[1])]
    target_grad, dec_qkv = input_back(
        dec_x,
        dec_first_grad,
        dec_q_grad,
        dec_kv_grads,
        dec_norm_in,
        parts(qkv, 1),
        False,
        block,
        [],
    )
    target_grad = give_back(target_grad, 1)
    enc_q_grad, enc_kv_grads, (sides,) = attend_back(
        enc_q,
        enc_kv,
        enc_mix,
        enc_mix_grad,
        enc_lse,
        spans[0],
        query_block,
        chunk,
        Reduce([sides, dec_qkv], 384, 7),
    )
    enc_kv_grads = [enc_kv_grads[0], swap(enc_kv_grads[1])]
    source_grad, enc_qkv = input_back(
        enc_x,
        enc_first_grad,
        enc_q_grad,
        enc_kv_grads,
        enc_norm_in,
        parts(qkv, 0),
        True,
        block,
        [enc_norm, dec_norm],
    )
    source_grad = give_back(source_grad, 0)
    last = reduce_alone([enc_qkv], PAIR, 8)

    side_rows, half = 3 * width, 3 * width // 2
    arrived = swap(jnp.where(is_first, ffn_dec, ffn_enc))
    up_grad = jnp.where(is_first, ffn_enc, arrived).astype(F32)
    down_grad = jnp.where(is_first, arrived, ffn_dec).astype(F32)
    up_grad = jnp.concatenate(jnp.split(up_grad, 2, axis=0), axis=1)
    arrived = swap(jnp.where(is_first, sides[side_rows:], last[:half]))
    first_half = jnp.where(is_first, last[:half], arrived)
    second_half = jnp.where(is_first, arrived, sides[side_rows:])
    qkv_grad = jnp.concatenate([first_half, second_half], axis=0).astype(F32)
    qkv_grad = qkv_grad.reshape(self_qkv.shape)
    sides = sides[:side_rows].astype(F32)
    out_grad = jnp.concatenate([sides[: width // 2], sides[width // 2 : width]], axis=1)
    cross_grad = sides[width:].reshape(cross_proj.shape)
    norm_grad = last[half : half + 12].astype(F32).reshape(norms.shape)

    def by_side(source, target):
        return jnp.stack([jnp.where(is_first, a, b) for a, b in zip(source, target)])

    return (
        by_side(encoded, decoded)[None],
        by_side(source_grad, target_grad).astype(F32)[None],
        qkv_grad,
        out_grad[None],
        cross_grad,
        up_grad[None],
        down_grad[None],
        norm_grad,
    )


def solution(mesh):
    placed = (
        P("section", "dp", "tensor", None),
        P(None, "dp", None),
        P("section", None, None, "tensor"),
        P("section", "tensor", None),
        P("section", None, None, "tensor"),
        P("section", None, "tensor"),
        P("section", "tensor", None),
        P("section", None, None, None),
        P("section", "dp", "tensor", None),
    )
    sizes = dict(mesh.shape)
    steps = sizes["dp"].bit_length() - 1
    fast = sizes["tensor"] == 2 and sizes["dp"] == 1 << steps and 0 < steps <= 3
    return jax.shard_map(
        local_fast if fast else local_general,
        mesh=mesh,
        in_specs=placed,
        out_specs=(
            P("section", "dp", "tensor", None),
            P("section", "dp", "tensor", None),
            P("section", None, None, "tensor"),
            P("section", "tensor", None),
            P("section", None, None, "tensor"),
            P("section", None, "tensor"),
            P("section", "tensor", None),
            P("section", None, None, None),
        ),
        check_vma=False,
    )
```

```python
import functools
import math

import jax
import jax.numpy as jnp
from jax import lax
from jax.experimental import pallas as pl
from jax.experimental.pallas import tpu as pltpu
from jax.sharding import PartitionSpec as P

HEADS = 8
EPSILON = 1e-05
MASKED = -1000000000.0
LOG2E = 1.0 / math.log(2.0)
PAIR = 128
HALF = 64
VMEM = 60 * 1024 * 1024
BF16 = jnp.bfloat16
F32 = jnp.float32


def standardize(rows):
    mean = jnp.mean(rows, axis=-1, keepdims=True)
    centered = rows - mean
    inv = lax.rsqrt(jnp.mean(centered * centered, axis=-1, keepdims=True) + EPSILON)
    return centered * inv, inv


def affine(unit, norm_ref, slot):
    return unit * norm_ref[slot, 0:1, :] + norm_ref[slot, 1:2, :]


def norm_back(unit, inv, norm_ref, slot, grad, grad_ref):
    grad_ref[slot, 0:1, :] += jnp.sum(grad * unit, axis=0, keepdims=True)
    grad_ref[slot, 1:2, :] += jnp.sum(grad, axis=0, keepdims=True)
    scaled = grad * norm_ref[slot, 0:1, :]
    first = jnp.mean(scaled, axis=-1, keepdims=True)
    second = jnp.mean(scaled * unit, axis=-1, keepdims=True)
    return inv * (scaled - first - unit * second)


def gelu_tanh(inner):
    return jnp.tanh(0.7978845608028654 * (inner + 0.044715 * inner * inner * inner))


def gelu(inner):
    return 0.5 * inner * (1.0 + gelu_tanh(inner))


def gelu_both(inner):
    bent = gelu_tanh(inner)
    slope = 0.7978845608028654 * (1.0 + 0.134145 * inner * inner)
    half = 0.5 * (1.0 + bent)
    return inner * half, half + 0.5 * inner * (1.0 - bent * bent) * slope


def dot_nn(a, b):
    return jnp.dot(a, b, preferred_element_type=F32)


def dot_nt(a, b):
    return lax.dot_general(a, b, (((1,), (1,)), ((), ())), preferred_element_type=F32)


def dot_tn(a, b):
    return lax.dot_general(a, b, (((0,), (0,)), ((), ())), preferred_element_type=F32)


class At:
    def __init__(self, array, *lead):
        self.array, self.lead = array, lead
        self.shape = array.shape[len(lead) :]
        self.dtype = array.dtype

    def spec(self, sizes, index, **options):
        nones = (None,) * len(self.lead)
        return pl.BlockSpec(nones + tuple(sizes), lambda *g: self.lead + tuple(index(*g)), **options)


def at(array):
    return array if isinstance(array, At) else At(array)


def row_call(
    body, name, rows, block, row_ins, whole_ins, row_outs, sum_outs, flops, finish=None, finals=None
):
    row_ins = [(at(a), dim) for a, dim in row_ins]
    whole_ins = [at(a) for a in whole_ins]
    finals = sum_outs if finals is None else finals

    def blocked(array, dim):
        sizes = tuple(block if i == dim else size for i, size in enumerate(array.shape))
        return array.spec(sizes, lambda g: tuple(g if i == dim else 0 for i in range(len(sizes))))

    def blocked_out(shape, dim):
        sizes = tuple(block if i == dim else size for i, size in enumerate(shape))
        return pl.BlockSpec(
            sizes, lambda g: tuple(g if i == dim else 0 for i in range(len(shape)))
        )

    def whole(array):
        return array.spec(
            array.shape,
            lambda g: (0,) * len(array.shape),
            pipeline_mode=pl.Buffered(buffer_count=1),
        )

    def whole_out(shape):
        return pl.BlockSpec(
            shape, lambda g: (0,) * len(shape), pipeline_mode=pl.Buffered(buffer_count=1)
        )

    n_rows_in = len(row_ins)
    n_in = n_rows_in + len(whole_ins)
    n_row, n_sum = len(row_outs), len(finals)

    def kernel(*refs):
        ins, outs = refs[:n_in], refs[n_in : n_in + n_row]
        sums, totals = refs[n_in + n_row : n_in + n_row + n_sum], refs[n_in + n_row + n_sum :]

        @pl.when(pl.program_id(0) == 0)
        def _():
            for total in totals:
                total[...] = jnp.zeros_like(total)

        body(ins, outs, totals)

        @pl.when(pl.program_id(0) == pl.num_programs(0) - 1)
        def _():
            if finish is None:
                for out, total in zip(sums, totals):
                    out[...] = total[...].astype(out.dtype)
            else:
                finish(ins[n_rows_in:], totals, sums)

    arrays = [array for array, _ in row_ins] + whole_ins
    size = sum(math.prod(a.shape) * a.dtype.itemsize for a in arrays)
    return pl.pallas_call(
        kernel,
        grid=(rows // block,),
        in_specs=[blocked(a, dim) for a, dim in row_ins] + [whole(a) for a in whole_ins],
        out_specs=[blocked_out(shape, dim) for shape, _, dim in row_outs]
        + [whole_out(shape) for shape, _ in finals],
        out_shape=[jax.ShapeDtypeStruct(shape, dtype) for shape, dtype, _ in row_outs]
        + [jax.ShapeDtypeStruct(shape, dtype) for shape, dtype in finals],
        scratch_shapes=[pltpu.VMEM(shape, F32) for shape, _ in sum_outs],
        compiler_params=pltpu.CompilerParams(vmem_limit_bytes=VMEM),
        cost_estimate=pl.CostEstimate(flops=flops, bytes_accessed=size, transcendentals=0),
        name=name,
    )(*[a.array for a in arrays])


def column_blocks(wide, into, core, k, row):
    rows, columns = wide.shape[0], wide.shape[1] // 2
    for half in range(2):
        into[core, k, row + half * rows : row + (half + 1) * rows, :] = wide[
            :, half * columns : (half + 1) * columns
        ].astype(BF16)


def project_qkv(x, norm, weights, with_norm, block):
    rows, width = x.shape
    parts, part = len(weights), weights[0].shape[-1]
    score = LOG2E / math.sqrt(width // HEADS)

    def body(ins, outs, totals):
        x_ref, norm_ref, *w = ins
        q_ref, kv_ref = outs
        rows_in = x_ref[...]
        if with_norm:
            unit, _ = standardize(rows_in.astype(F32))
            rows_in = affine(unit, norm_ref, 2).astype(BF16)
        for k in range(parts):
            q_ref[k] = (dot_nn(rows_in, w[k][0]) * score).astype(BF16)
            kv_ref[k, 0] = dot_nn(rows_in, w[k][1]).astype(BF16)
            kv_ref[k, 1] = dot_nn(rows_in, w[k][2]).astype(BF16)

    return row_call(
        body,
        "project_qkv",
        rows,
        block,
        [(x, 0)],
        [norm, *weights],
        [((parts, rows, part), BF16, 1), ((parts, 2, rows, part), BF16, 2)],
        [],
        6 * rows * width * width,
    )


def encoder_forward(x, mix, norm, out, up, down, cross, block):
    rows, width = x.shape
    parts, part = len(out), out[0].shape[0]

    def body(ins, outs, totals):
        x_ref, mix_ref, norm_ref = ins[:3]
        wo, wu, wd, wc = (ins[3 + i * parts : 3 + (i + 1) * parts] for i in range(4))
        result_ref, kv_ref, first_ref, third_ref = outs
        unit, _ = standardize(x_ref[...].astype(F32))
        first = affine(unit, norm_ref, 2)
        for k in range(parts):
            first += dot_nn(mix_ref[k], wo[k][...])
        first_ref[...] = first
        unit, _ = standardize(first)
        third = affine(unit, norm_ref, 0)
        low = third.astype(BF16)
        for k in range(parts):
            act = gelu(dot_nn(low, wu[k][...])).astype(BF16)
            third += dot_nn(act, wd[k][...])
        third_ref[...] = third
        unit, _ = standardize(third)
        low = affine(unit, norm_ref, 1).astype(BF16)
        result_ref[...] = low
        for k in range(parts):
            kv_ref[k, 0] = dot_nn(low, wc[k][0]).astype(BF16)
            kv_ref[k, 1] = dot_nn(low, wc[k][1]).astype(BF16)

    units = sum(w.shape[1] for w in up)
    return row_call(
        body,
        "encoder_forward",
        rows,
        block,
        [(x, 0), (mix, 1)],
        [norm, *out, *up, *down, *cross],
        [
            ((rows, width), BF16, 0),
            ((parts, 2, rows, part), BF16, 2),
            ((rows, width), F32, 0),
            ((rows, width), F32, 0),
        ],
        [],
        6 * rows * width * width + 4 * rows * width * units,
    )


def decoder_middle(x, mix, norm, out, cross, block):
    rows, width = x.shape
    parts, part = len(out), out[0].shape[0]
    score = LOG2E / math.sqrt(width // HEADS)

    def body(ins, outs, totals):
        x_ref, mix_ref, norm_ref = ins[:3]
        wo, wc = (ins[3 + i * parts : 3 + (i + 1) * parts] for i in range(2))
        q_ref, first_ref = outs
        first = x_ref[...].astype(F32)
        for k in range(parts):
            first += dot_nn(mix_ref[k], wo[k][...])
        first_ref[...] = first
        unit, _ = standardize(first)
        low = affine(unit, norm_ref, 0).astype(BF16)
        for k in range(parts):
            q_ref[k] = (dot_nn(low, wc[k][0]) * score).astype(BF16)

    return row_call(
        body,
        "decoder_middle",
        rows,
        block,
        [(x, 0), (mix, 1)],
        [norm, *out, *cross],
        [((parts, rows, part), BF16, 1), ((rows, width), F32, 0)],
        [],
        4 * rows * width * width,
    )


def ffn_back(low, grad_low, up, down, up_total, down_total, parts):
    grad = None
    for k in range(parts):
        act, slope = gelu_both(dot_nn(low, up[k][...]))
        down_total[k] += dot_tn(act.astype(BF16), grad_low)
        grad_inner = (dot_nt(grad_low, down[k][...]) * slope).astype(BF16)
        up_total[k] += dot_tn(low, grad_inner)
        step = dot_nt(grad_inner, up[k][...])
        grad = step if grad is None else grad + step
    return grad


def decoder_turn(first, mix, cotangent, norm, cross, up, down, block, paired=False):
    rows, width = first.shape
    parts, part, units = len(cross), cross[0].shape[-1], up[0].shape[1]

    def body(ins, outs, totals):
        first_ref, mix_ref, cot_ref, norm_ref = ins[:4]
        wc, wu, wd = (ins[4 + i * parts : 4 + (i + 1) * parts] for i in range(3))
        result_ref, second_grad_ref, mix_grad_ref = outs
        out_total, up_total, down_total, norm_total = totals
        unit, _ = standardize(first_ref[...])
        second = affine(unit, norm_ref, 0)
        for k in range(parts):
            second += dot_nt(mix_ref[k], wc[k][1])
        unit_two, inv_two = standardize(second)
        third = affine(unit_two, norm_ref, 2)
        low = third.astype(BF16)
        acts, slopes = [], []
        for k in range(parts):
            act, slope = gelu_both(dot_nn(low, wu[k][...]))
            acts.append(act.astype(BF16))
            slopes.append(slope)
            third += dot_nn(acts[k], wd[k][...])
        unit_three, inv_three = standardize(third)
        result_ref[...] = affine(unit_three, norm_ref, 1).astype(BF16)
        grad = norm_back(
            unit_three, inv_three, norm_ref, 1, cot_ref[...].astype(F32), norm_total
        )
        grad_low = grad.astype(BF16)
        for k in range(parts):
            down_total[k] += dot_tn(acts[k], grad_low)
            grad_inner = (dot_nt(grad_low, wd[k][...]) * slopes[k]).astype(BF16)
            up_total[k] += dot_tn(low, grad_inner)
            grad += dot_nt(grad_inner, wu[k][...])
        grad = norm_back(unit_two, inv_two, norm_ref, 2, grad, norm_total)
        second_grad_ref[...] = grad
        grad_low = grad.astype(BF16)
        for k in range(parts):
            out_total[k] += dot_tn(grad_low, mix_ref[k])
            mix_grad_ref[k] = dot_nn(grad_low, wc[k][1]).astype(BF16)

    sums = [
        ((parts, width, part), BF16),
        ((parts, width, units), BF16),
        ((parts, units, width), BF16),
        ((3, 2, width), F32),
    ]
    if paired:
        finals = [sums[0], ((2, parts, units, width), BF16), sums[3]]

        def finish(ins, totals, outs):
            outs[0][...] = totals[0][...].astype(BF16)
            for k in range(parts):
                column_blocks(totals[1][k], outs[1], 0, k, 0)
                outs[1][1, k] = totals[2][k].astype(BF16)
            outs[2][...] = totals[3][...]

    else:
        finals, finish = None, None

    return row_call(
        body,
        "decoder_turn",
        rows,
        block,
        [(first, 0), (mix, 1), (cotangent, 0)],
        [norm, *cross, *up, *down],
        [
            ((rows, width), BF16, 0),
            ((rows, width), F32, 0),
            ((parts, rows, part), BF16, 1),
        ],
        sums,
        6 * rows * width * width + 12 * rows * width * units * parts,
        finish,
        finals,
    )


def decoder_middle_back(first, mix, query_grad, second_grad, norm, out, cross, block):
    rows, width = first.shape
    parts, part = len(out), out[0].shape[0]

    def body(ins, outs, totals):
        first_ref, mix_ref, query_grad_ref, second_grad_ref, norm_ref = ins[:5]
        wo, wc = (ins[5 + i * parts : 5 + (i + 1) * parts] for i in range(2))
        first_grad_ref, mix_grad_ref = outs
        query_total, out_total, norm_total = totals
        unit, inv = standardize(first_ref[...])
        low = affine(unit, norm_ref, 0).astype(BF16)
        grad = second_grad_ref[...]
        for k in range(parts):
            query_total[k] += dot_tn(low, query_grad_ref[k])
            grad += dot_nt(query_grad_ref[k], wc[k][0])
        grad = norm_back(unit, inv, norm_ref, 0, grad, norm_total)
        first_grad_ref[...] = grad
        grad_low = grad.astype(BF16)
        for k in range(parts):
            out_total[k] += dot_tn(mix_ref[k], grad_low)
            mix_grad_ref[k] = dot_nt(grad_low, wo[k][...]).astype(BF16)

    return row_call(
        body,
        "decoder_middle_back",
        rows,
        block,
        [(first, 0), (mix, 1), (query_grad, 1), (second_grad, 0)],
        [norm, *out, *cross],
        [((rows, width), F32, 0), ((parts, rows, part), BF16, 1)],
        [
            ((parts, width, part), BF16),
            ((parts, part, width), BF16),
            ((3, 2, width), F32),
        ],
        8 * rows * width * width,
    )


def encoder_back(
    first, third, mix, memory_grads, cotangent, norm, out, up, down, cross, block, paired=None
):
    rows, width = first.shape
    parts, part, units = len(out), out[0].shape[0], up[0].shape[1]
    pieces = len(memory_grads)

    def body(ins, outs, totals):
        first_ref, third_ref, mix_ref, cot_ref = ins[:4]
        memory_refs, norm_ref = ins[4 : 4 + pieces], ins[4 + pieces]
        rest = ins[5 + pieces :]
        wo, wu, wd, wc = (rest[i * parts : (i + 1) * parts] for i in range(4))
        first_grad_ref, mix_grad_ref = outs
        cross_total, out_total, up_total, down_total, norm_total = totals
        unit, inv = standardize(third_ref[...])
        low = affine(unit, norm_ref, 1).astype(BF16)
        grad = cot_ref[...].astype(F32)
        for i in range(2):
            for k in range(parts):
                memory = memory_refs[0][k, i].astype(F32)
                for ref in memory_refs[1:]:
                    memory += ref[k, i].astype(F32)
                memory = memory.astype(BF16)
                cross_total[k, i] += dot_tn(low, memory)
                grad += dot_nt(memory, wc[k][i])
        grad = norm_back(unit, inv, norm_ref, 1, grad, norm_total)
        unit, inv = standardize(first_ref[...])
        low = affine(unit, norm_ref, 0).astype(BF16)
        grad += ffn_back(low, grad.astype(BF16), wu, wd, up_total, down_total, parts)
        grad = norm_back(unit, inv, norm_ref, 0, grad, norm_total)
        first_grad_ref[...] = grad
        grad_low = grad.astype(BF16)
        for k in range(parts):
            out_total[k] += dot_tn(mix_ref[k], grad_low)
            mix_grad_ref[k] = dot_nt(grad_low, wo[k][...]).astype(BF16)

    sums = [
        ((parts, 2, width, part), BF16),
        ((parts, part, width), BF16),
        ((parts, width, units), BF16),
        ((parts, units, width), BF16),
        ((3, 2, width), F32),
    ]
    if paired is not None:
        side = 3 * width
        finals = [
            ((2, parts, units, width), BF16),
            ((2, parts, side, part), BF16),
            sums[4],
        ]

        def finish(ins, totals, outs):
            dec_out, dec_query, dec_cross = ins[-3:]
            for k in range(parts):
                column_blocks(totals[2][k], outs[0], 0, k, 0)
                outs[0][1, k] = totals[3][k].astype(BF16)
                column_blocks(totals[1][k], outs[1], 0, k, 0)
                outs[1][0, k, width:side, :] = (
                    totals[0][k].reshape(2 * width, part).astype(BF16)
                )
                column_blocks(dec_out[k], outs[1], 1, k, 0)
                outs[1][1, k, width : 2 * width, :] = dec_query[k]
                outs[1][1, k, 2 * width : side, :] = dec_cross[k]
            outs[2][...] = totals[4][...]

    else:
        finals, finish, paired = None, None, []

    return row_call(
        body,
        "encoder_back",
        rows,
        block,
        [(first, 0), (third, 0), (mix, 1), (cotangent, 0)] + [(m, 2) for m in memory_grads],
        [norm, *out, *up, *down, *cross, *paired],
        [((rows, width), F32, 0), ((parts, rows, part), BF16, 1)],
        sums,
        12 * rows * width * width + 10 * rows * width * units * parts,
        finish,
        finals,
    )


def input_back(
    x, first_grad, query_grad, key_grads, norm, weights, with_norm, block, paired=None
):
    rows, width = x.shape
    parts, part = len(weights), weights[0].shape[-1]
    pieces = len(key_grads)

    def body(ins, outs, totals):
        x_ref, first_grad_ref, query_grad_ref = ins[:3]
        key_refs, norm_ref, w = ins[3 : 3 + pieces], ins[3 + pieces], ins[4 + pieces :][:parts]
        (grad_ref,) = outs
        qkv_total, norm_total = totals
        low = x_ref[...]
        if with_norm:
            unit, inv = standardize(low.astype(F32))
            low = affine(unit, norm_ref, 2).astype(BF16)
        grad = first_grad_ref[...]
        for k in range(parts):
            for i in range(3):
                if i == 0:
                    member = query_grad_ref[k]
                else:
                    member = key_refs[0][k, i - 1].astype(F32)
                    for ref in key_refs[1:]:
                        member += ref[k, i - 1].astype(F32)
                    member = member.astype(BF16)
                qkv_total[k, i] += dot_tn(low, member)
                grad += dot_nt(member, w[k][i])
        if with_norm:
            grad = norm_back(unit, inv, norm_ref, 2, grad, norm_total)
        grad_ref[...] = grad.astype(BF16)

    sums = [((parts, 3, width, part), BF16), ((3, 2, width), F32)]
    if paired is not None:
        half = 3 * width // 2
        shape = (4 * half // 2 + 2 * PAIR, PAIR) if paired else (half, part)
        finals = [((2, parts, *shape), BF16)]

        def finish(ins, totals, outs):
            for k in range(parts):
                both = totals[0][k].reshape(2 * half, part)
                for core in range(2):
                    own = both[core * half : (core + 1) * half]
                    if paired:
                        column_blocks(own, outs[0], core, k, 0)
                    else:
                        outs[0][core, k] = own.astype(BF16)
            if paired:
                sides = [ins[-2][...] + totals[1][...], ins[-1][...]]
                for core, table in enumerate(sides):
                    lines = [
                        table[slot, i : i + 1, h * PAIR : (h + 1) * PAIR]
                        for slot in range(3)
                        for i in range(2)
                        for h in range(width // PAIR)
                    ]
                    lines.append(jnp.zeros((2 * PAIR - len(lines), PAIR), F32))
                    lines = jnp.concatenate(lines, axis=0).astype(BF16)
                    for k in range(parts):
                        outs[0][core, k, 2 * half :, :] = lines

    else:
        finals, finish, paired = None, None, []

    return row_call(
        body,
        "input_back",
        rows,
        block,
        [(x, 0), (first_grad, 0), (query_grad, 1)] + [(g, 2) for g in key_grads],
        [norm, *weights, *paired],
        [((rows, width), BF16, 0)],
        sums,
        12 * rows * width * width,
        finish,
        finals,
    )


def widen_keys(span_ref, kv_refs, key_e, key_o, value_e, value_o, rows):
    lane = lax.broadcasted_iota(jnp.int32, (rows, PAIR), 1)
    place = lax.broadcasted_iota(jnp.int32, (rows, PAIR), 0)
    low = lane < HALF
    for g, kv_ref in enumerate(kv_refs):
        spot = place + span_ref[2 + g]
        live = (spot >= span_ref[0]) & (spot < span_ref[1])
        bias = jnp.where(live, 0.0, MASKED)
        keys, values = kv_ref[0].astype(F32), kv_ref[1].astype(F32)
        own = pl.ds(g * rows, rows)
        key_e[own, :] = jnp.where(low, keys, jnp.where(lane == HALF, bias, 1.0)).astype(BF16)
        key_o[own, :] = jnp.where(low, jnp.where(lane == 0, bias, 1.0), keys).astype(BF16)
        value_e[own, :] = jnp.where(low, values, 1.0).astype(BF16)
        value_o[own, :] = jnp.where(low, 1.0, values).astype(BF16)


def attention_specs(per_part, rows, block, query, lse_lead=()):
    def query_spec(array):
        return at(array).spec(
            (None, block, PAIR), lambda i, j: (i // per_part, j, i % per_part)
        )

    def kv_spec(array):
        return at(array).spec(
            (None, 2, rows, PAIR), lambda i, j: (i // per_part, 0, 0, i % per_part)
        )

    return query_spec, kv_spec, pl.BlockSpec((block, PAIR), lambda i, j: (j, i))


def attend(query, kv_pieces, span, block, carrier=None):
    query, kv_pieces = at(query), [at(piece) for piece in kv_pieces]
    carrier = carrier or Carry()
    parts, rows, part = query.shape
    per_part = part // PAIR
    pairs = parts * per_part
    pieces = len(kv_pieces)
    keys = rows * pieces
    n_carry = len(carrier.ins)

    def kernel(span_ref, q_ref, *refs):
        kv_refs, refs = refs[:pieces], refs[pieces:]
        carry_ins, refs = refs[:n_carry], refs[n_carry:]
        out_ref, lse_ref, refs = refs[0], refs[1], refs[2:]
        carry_outs, refs = refs[: len(carrier.outs)], refs[len(carrier.outs) :]
        key_e, key_o, value_e, value_o = refs[:4]
        step = pl.program_id(0) * pl.num_programs(1) + pl.program_id(1)
        carrier.run(step, pairs * (rows // block), carry_ins, carry_outs, refs[4:])

        @pl.when(pl.program_id(1) == 0)
        def _():
            widen_keys(span_ref, kv_refs, key_e, key_o, value_e, value_o, rows)

        lane = lax.broadcasted_iota(jnp.int32, (block, PAIR), 1)
        low = lane < HALF
        query = q_ref[...].astype(F32)
        query_e = jnp.where(low, query, jnp.where(lane == HALF, 1.0, 0.0)).astype(BF16)
        query_o = jnp.where(low, jnp.where(lane == 0, 1.0, 0.0), query).astype(BF16)
        tops, sums = [], []
        for q, k, v in ((query_e, key_e, value_e), (query_o, key_o, value_o)):
            scores = dot_nt(q, k[...])
            top = jnp.max(scores, axis=1, keepdims=True)
            tops.append(top)
            sums.append(dot_nn(jnp.exp2(scores - top).astype(BF16), v[...]))
        top = jnp.where(low, tops[1], tops[0])
        weight = jnp.where(low, sums[1], sums[0])
        lse_ref[...] = top + LOG2E * jnp.log(weight)
        mixed = jnp.where(low, sums[0], sums[1])
        out_ref[...] = (mixed / pltpu.roll(weight, HALF, 1)).astype(BF16)

    query_spec, kv_spec, lse_spec = attention_specs(per_part, rows, block, query)
    out_spec = pl.BlockSpec(
        (None, block, PAIR), lambda i, j: (i // per_part, j, i % per_part)
    )
    hold = pl.BlockSpec(memory_space=pl.ANY)
    return pl.pallas_call(
        kernel,
        grid=(pairs, rows // block),
        in_specs=[pl.BlockSpec(memory_space=pltpu.SMEM), query_spec(query)]
        + [kv_spec(piece) for piece in kv_pieces]
        + [hold] * n_carry,
        out_specs=[out_spec, lse_spec] + [hold] * len(carrier.outs),
        scratch_shapes=[pltpu.VMEM((keys, PAIR), BF16)] * 4 + carrier.scratch,
        out_shape=[
            jax.ShapeDtypeStruct(query.shape, BF16),
            jax.ShapeDtypeStruct((rows, pairs * PAIR), F32),
        ]
        + carrier.outs,
        compiler_params=pltpu.CompilerParams(vmem_limit_bytes=VMEM, **carrier.params),
        cost_estimate=pl.CostEstimate(
            flops=16 * rows * keys * pairs * PAIR,
            bytes_accessed=8 * rows * pairs * PAIR * pieces,
            transcendentals=0,
        ),
        name="attend",
    )(span, query.array, *[piece.array for piece in kv_pieces], *carrier.ins)


def attend_back(query, kv_pieces, mix, mix_grad, lse, span, block, chunk, carrier=None):
    query, kv_pieces = at(query), [at(piece) for piece in kv_pieces]
    mix, mix_grad = at(mix), at(mix_grad)
    carrier = carrier or Carry()
    parts, rows, part = query.shape
    per_part = part // PAIR
    pairs = parts * per_part
    pieces = len(kv_pieces)
    keys = rows * pieces
    scale = 1.0 / math.sqrt(HALF)
    n_carry = len(carrier.ins)

    def kernel(span_ref, q_ref, mix_ref, grad_ref, lse_ref, *refs):
        kv_refs, refs = refs[:pieces], refs[pieces:]
        carry_ins, refs = refs[:n_carry], refs[n_carry:]
        dq_ref, dkv_refs, refs = refs[0], refs[1 : pieces + 1], refs[pieces + 1 :]
        carry_outs, refs = refs[: len(carrier.outs)], refs[len(carrier.outs) :]
        key_e, key_o, value_e, value_o, key_t, key_total, value_total = refs[:7]
        step = pl.program_id(0) * pl.num_programs(1) + pl.program_id(1)
        carrier.run(step, pairs * (rows // block), carry_ins, carry_outs, refs[7:])

        @pl.when(pl.program_id(1) == 0)
        def _():
            widen_keys(span_ref, kv_refs, key_e, key_o, value_e, value_o, rows)
            for g, kv_ref in enumerate(kv_refs):
                key_t[:, pl.ds(g * rows, rows)] = kv_ref[0].T
            key_total[...] = jnp.zeros_like(key_total)
            value_total[...] = jnp.zeros_like(value_total)

        lane = lax.broadcasted_iota(jnp.int32, (block, PAIR), 1)
        low = lane < HALF
        query, grad = q_ref[...].astype(F32), grad_ref[...].astype(F32)
        product = mix_ref[...].astype(F32) * grad
        inner = jnp.where(
            low,
            jnp.sum(jnp.where(low, 0.0, product), axis=1, keepdims=True),
            jnp.sum(jnp.where(low, product, 0.0), axis=1, keepdims=True),
        )
        spot = jnp.where(low, lane, lane - HALF)

        def three(value, shift):
            high = value.astype(BF16).astype(F32)
            rest = value - high
            mid = rest.astype(BF16).astype(F32)
            return jnp.where(
                spot == shift,
                high,
                jnp.where(
                    spot == shift + 1, mid, jnp.where(spot == shift + 2, rest - mid, 0.0)
                ),
            )

        lse = three(-lse_ref[...], 1) + jnp.where(spot == 0, 1.0, 0.0)
        inner = three(-inner, 0)
        heads = []
        for own, key, value in ((low, key_e, value_e), (~low, key_o, value_o)):
            heads.append(
                (
                    key,
                    value,
                    jnp.where(own, query, lse).astype(BF16),
                    jnp.where(own, grad, inner).astype(BF16),
                    jnp.where(own, query, 0.0).astype(BF16),
                    jnp.where(own, grad, 0.0).astype(BF16),
                )
            )
        dq = [None, None]
        for c in range(keys // chunk):
            span_c = pl.ds(c * chunk, chunk)
            dk, dv = None, None
            for h, (key, value, q_wide, g_wide, q_own, g_own) in enumerate(heads):
                probs = jnp.exp2(dot_nt(key[span_c, :], q_wide))
                dscores = (probs * dot_nt(value[span_c, :], g_wide)).astype(BF16)
                step_v = dot_nn(probs.astype(BF16), g_own)
                step_k = dot_nn(dscores, q_own)
                step_q = dot_nn(key_t[pl.ds(h * HALF, HALF), span_c], dscores)
                dv = step_v if dv is None else dv + step_v
                dk = step_k if dk is None else dk + step_k
                dq[h] = step_q if dq[h] is None else dq[h] + step_q
            key_total[span_c, :] += dk
            value_total[span_c, :] += dv
        dq_ref[...] = (jnp.concatenate(dq, axis=0).T * scale).astype(BF16)

        @pl.when(pl.program_id(1) == pl.num_programs(1) - 1)
        def _():
            for g, ref in enumerate(dkv_refs):
                own = pl.ds(g * rows, rows)
                ref[0] = (key_total[own, :] * (1.0 / LOG2E)).astype(BF16)
                ref[1] = value_total[own, :].astype(BF16)

    query_spec, kv_spec, lse_spec = attention_specs(per_part, rows, block, query)
    plain = jax.ShapeDtypeStruct(query.shape, BF16)
    plain_kv = jax.ShapeDtypeStruct((parts, 2, rows, part), BF16)
    hold = pl.BlockSpec(memory_space=pl.ANY)
    out = pl.pallas_call(
        kernel,
        grid=(pairs, rows // block),
        in_specs=[pl.BlockSpec(memory_space=pltpu.SMEM)]
        + [query_spec(a) for a in (query, mix, mix_grad)]
        + [lse_spec]
        + [kv_spec(piece) for piece in kv_pieces]
        + [hold] * n_carry,
        out_specs=[query_spec(plain)]
        + [kv_spec(plain_kv)] * pieces
        + [hold] * len(carrier.outs),
        scratch_shapes=[pltpu.VMEM((keys, PAIR), BF16)] * 4
        + [pltpu.VMEM((PAIR, keys), BF16)]
        + [pltpu.VMEM((keys, PAIR), F32)] * 2
        + carrier.scratch,
        out_shape=[plain] + [plain_kv] * pieces + carrier.outs,
        compiler_params=pltpu.CompilerParams(vmem_limit_bytes=VMEM, **carrier.params),
        cost_estimate=pl.CostEstimate(
            flops=40 * rows * keys * pairs * PAIR,
            bytes_accessed=16 * rows * pairs * PAIR * pieces,
            transcendentals=0,
        ),
        name="attend_back",
    )(
        span,
        query.array,
        mix.array,
        mix_grad.array,
        lse,
        *[piece.array for piece in kv_pieces],
        *carrier.ins,
    )
    return out[0], out[1 : pieces + 1], out[pieces + 1 :]


def spots():
    return lax.axis_index("section"), lax.axis_index("dp"), lax.axis_index("tensor")


def dp_peer(group, level):
    return group + (1 << level) * (1 - 2 * ((group // (1 << level)) % 2))


def where_is(peer):
    section, group, tensor = spots()
    if peer == "near":
        return {"section": 1 - section}
    if peer == "over":
        return {"tensor": 1 - tensor}
    if peer == "cross":
        return {"section": 1 - section, "tensor": 1 - tensor}
    return {"dp": dp_peer(group, peer)}


def remote(source, target, sent, landed, where):
    return pltpu.make_async_remote_copy(
        src_ref=source,
        dst_ref=target,
        send_sem=sent,
        recv_sem=landed,
        device_id=where,
        device_id_type=pl.DeviceIdType.MESH,
    )


def greet(peers):
    barrier = pltpu.get_barrier_semaphore()
    for peer in peers:
        pl.semaphore_signal(
            barrier, inc=1, device_id=where_is(peer), device_id_type=pl.DeviceIdType.MESH
        )
    pl.semaphore_wait(barrier, len(peers))


class Carry:
    def __init__(self, tasks=(), collective=None):
        self.tasks = list(tasks)
        self.ins = [a for task in self.tasks for a in task.ins]
        self.outs = [a for task in self.tasks for a in task.outs]
        self.scratch = [a for task in self.tasks for a in task.scratch]
        self.peers = []
        for task in self.tasks:
            self.peers += [peer for peer in task.peers if peer not in self.peers]
        self.params = (
            dict(collective_id=collective, has_side_effects=True) if self.tasks else {}
        )

    def run(self, step, steps, ins, outs, scratch):
        if not self.tasks:
            return

        @pl.when(step == 0)
        def _():
            greet(self.peers)

        for task in self.tasks:
            i, o, s = len(task.ins), len(task.outs), len(task.scratch)
            task.run(step, steps, ins[:i], outs[:o], scratch[:s])
            ins, outs, scratch = ins[i:], outs[o:], scratch[s:]


GROUP = ["near", "over", "cross"]


class RowCopies:
    def __init__(self, copies, arrivals, sems, room=None):
        self.copies, self.arrivals, self.room = copies, arrivals, room
        self.sent, self.landed, self.kept = sems

    def copy(self, i):
        source, target, slot, section, tensor, _ = self.copies[i]
        return remote(
            source,
            target,
            self.sent.at[i],
            self.landed.at[slot],
            {"section": section, "tensor": tensor},
        )

    def keep(self, i):
        source, target = self.copies[i][:2]
        return pltpu.make_async_copy(
            source, target if self.room is None else self.room, self.kept
        )

    def keep_on(self):
        for i in range(len(self.copies)):

            @pl.when(self.here(i, True))
            def _():
                self.keep(i).wait()
                pltpu.make_async_copy(self.room, self.copies[i][1], self.kept).start()

    def here(self, i, stays):
        section, _, tensor = spots()
        _, _, _, to_section, to_tensor, condition = self.copies[i]
        own = (to_section == section) & (to_tensor == tensor)
        return condition & (own if stays else jnp.logical_not(own))

    def start(self):
        for i in range(len(self.copies)):

            @pl.when(self.here(i, True))
            def _():
                self.keep(i).start()

            @pl.when(self.here(i, False))
            def _():
                self.copy(i).start()

    def wait_sent(self):
        for i in range(len(self.copies)):

            @pl.when(self.here(i, False))
            def _():
                self.copy(i).wait_send()

    def wait_arrival(self, i):
        section, _, tensor = spots()
        target, slot, from_section, from_tensor, condition = self.arrivals[i]
        own = (from_section == section) & (from_tensor == tensor)
        source = self.copies[0][0]

        @pl.when(condition & own)
        def _():
            stays = source if self.room is None else self.room
            pltpu.make_async_copy(stays, target, self.kept).wait()

        @pl.when(condition & jnp.logical_not(own))
        def _():
            remote(
                source, target, self.sent.at[0], self.landed.at[slot], where_is("near")
            ).wait_recv()


ROW_SEMS = [
    pltpu.SemaphoreType.DMA((2,)),
    pltpu.SemaphoreType.DMA((2,)),
    pltpu.SemaphoreType.DMA,
]


def spread_rows(source, target, sems, sides=(0, 1), room=None):
    section, _, tensor = spots()
    yes = section >= 0
    sends = yes if len(sides) == 2 else section == sides[0]
    copies = [
        (source.at[row], target.at[section], section, tensor, row, sends) for row in range(2)
    ]
    arrivals = [(target.at[side], side, side, section, yes) for side in sides]
    return RowCopies(copies, arrivals, sems, room)


def return_rows(source, target, sems, side, room):
    section, _, tensor = spots()
    copies = [(source, target.at[tensor], tensor, side, section, section >= 0)]
    arrivals = [(target.at[row], row, tensor, row, section == side) for row in range(2)]
    return RowCopies(copies, arrivals, sems, room)


class SpreadRows:
    peers = GROUP

    def __init__(self, array, sides):
        self.ins, self.sides = [array], sides
        self.outs = [jax.ShapeDtypeStruct(array.shape, array.dtype)]
        self.scratch = ROW_SEMS + [pltpu.VMEM(array.shape[-2:], array.dtype)]

    def make(self, ins, outs, scratch):
        return spread_rows(ins[0], outs[0], scratch[:3], self.sides, scratch[3])

    def run(self, step, steps, ins, outs, scratch):
        @pl.when(step == 0)
        def _():
            self.make(ins, outs, scratch).start()

        @pl.when(step == 2)
        def _():
            self.make(ins, outs, scratch).keep_on()

        @pl.when(step == steps - 1)
        def _():
            rows = self.make(ins, outs, scratch)
            for i in range(len(rows.arrivals)):
                rows.wait_arrival(i)
            rows.wait_sent()


class ReturnRows(SpreadRows):
    def __init__(self, array, side):
        self.ins, self.side = [array], side
        self.outs = [jax.ShapeDtypeStruct((2, *array.shape), array.dtype)]
        self.scratch = ROW_SEMS + [pltpu.VMEM(array.shape, array.dtype)]

    def make(self, ins, outs, scratch):
        return return_rows(ins[0], outs[0], scratch[:3], self.side, scratch[3])


class WeightCopies:
    sems = [pltpu.SemaphoreType.DMA((11,))]

    def __init__(self, source, target, sem, room=None):
        section, group, _ = spots()
        count = source.shape[0] // 2
        bit = group % 2
        own = pl.ds(pl.multiple_of(bit * count, 16), count)
        other = pl.ds(pl.multiple_of((1 - bit) * count, 16), count)
        here = target.at[section, 1]
        stays = target.at[section, 0]
        if room is None:
            self.kept = pltpu.make_async_copy(source, stays, sem.at[0])
        else:
            self.first = pltpu.make_async_copy(source, room, sem.at[0])
            self.kept = pltpu.make_async_copy(room, stays, sem.at[0])
        self.room = room
        self.near = remote(
            source, target.at[section, 0], sem.at[1], sem.at[2], where_is("near")
        )
        self.over = remote(source.at[own], here.at[own], sem.at[3], sem.at[4], where_is("over"))
        self.side = remote(here.at[own], here.at[own], sem.at[5], sem.at[6], where_is(0))
        self.onward = remote(
            here.at[own], here.at[own], sem.at[7], sem.at[8], where_is("near")
        )
        self.last = remote(
            here.at[other], here.at[other], sem.at[9], sem.at[10], where_is("near")
        )

    def start(self):
        self.over.start()
        self.near.start()
        if self.room is None:
            self.kept.start()
        else:
            self.first.start()

    def keep_on(self):
        self.first.wait()
        self.kept.start()

    def forward(self):
        self.over.wait_recv()
        self.side.start()
        self.onward.start()

    def forward_last(self):
        self.side.wait_recv()
        self.last.start()

    def finish(self):
        self.kept.wait()
        self.near.wait()
        self.over.wait_send()
        self.side.wait_send()
        self.onward.wait()
        self.last.wait()


class SpreadWeight:
    peers = ["near", "over", 0]

    def __init__(self, weight, forward, last):
        self.ins = [weight]
        self.outs = [jax.ShapeDtypeStruct((2, 2, *weight.shape), weight.dtype)]
        self.scratch = WeightCopies.sems + [pltpu.VMEM(weight.shape, weight.dtype)]
        self.steps = forward, last

    def run(self, step, steps, ins, outs, scratch):
        def copies():
            return WeightCopies(ins[0], outs[0], *scratch)

        @pl.when(step == 0)
        def _():
            copies().start()

        @pl.when(step == 2)
        def _():
            copies().keep_on()

        @pl.when(step == self.steps[0])
        def _():
            copies().forward()

        @pl.when(step == self.steps[1])
        def _():
            copies().forward_last()

        @pl.when(step == steps - 1)
        def _():
            copies().finish()


class Reduce:
    def __init__(self, sources, chunk, spacing, patience):
        self.ins = list(sources)
        self.chunk, self.spacing, self.patience = chunk, spacing, patience
        self.places = [
            (i, row) for i, s in enumerate(sources) for row in range(0, s.shape[2], chunk)
        ]
        self.count = len(self.places)
        self.levels = lax.axis_size("dp").bit_length() - 1
        self.peers = ["near", "over", *range(self.levels)]
        width = sources[0].shape[3]
        self.outs = [jax.ShapeDtypeStruct((self.count * chunk, width), BF16)] * 2

        def room(*shape):
            return pltpu.VMEM((self.count, *shape, width), BF16)

        halves = [room(chunk >> (level + 1)) for level in range(self.levels)]
        self.scratch = [room(2, chunk), room(2, chunk), room(chunk), room(chunk)]
        self.scratch += halves + halves
        self.scratch += [pltpu.SemaphoreType.DMA((2 + 2 * (3 + 2 * self.levels), self.count))]
        self.last = 1 + patience + 2 * self.levels
        self.steps = self.last + 1 + spacing * (self.count - 1)

    def run(self, step, steps, ins, outs, scratch):
        chunk, levels = self.chunk, self.levels
        assert steps >= self.steps
        own, chip, other, full = scratch[:4]
        halves, doubles = scratch[4 : 4 + levels], scratch[4 + levels : 4 + 2 * levels]
        sems = scratch[4 + 2 * levels]
        section, group, tensor = spots()
        bits = [(group // (1 << level)) % 2 for level in range(levels)]
        begins = [0]
        for level in range(levels):
            begins.append(begins[level] + bits[level] * (chunk >> (level + 1)))

        def keeps(level):
            return pl.ds(pl.multiple_of(begins[level + 1], 16), chunk >> (level + 1))

        def gives(level):
            start = begins[level] + (1 - bits[level]) * (chunk >> (level + 1))
            return pl.ds(pl.multiple_of(start, 16), chunk >> (level + 1))

        def pair(kind, c):
            return sems.at[2 + 2 * kind, c], sems.at[3 + 2 * kind, c]

        def load(c, place):
            i, row = place
            return pltpu.make_async_copy(
                ins[i].at[section, :, pl.ds(row, chunk), :], own.at[c], sems.at[0, c]
            )

        def cross(c, place):
            i, row = place
            return remote(
                ins[i].at[1 - section, :, pl.ds(row, chunk), :],
                chip.at[c],
                *pair(0, c),
                where_is("near"),
            )

        def over(c):
            return remote(own.at[c, 1], other.at[c], *pair(1, c), where_is("over"))

        def halve(level, c):
            return remote(
                own.at[c, 0, gives(level), :],
                halves[level].at[c],
                *pair(3 + level, c),
                where_is(level),
            )

        def double(level, c):
            return remote(
                full.at[c, keeps(level), :],
                doubles[level].at[c],
                *pair(3 + levels + level, c),
                where_is(level),
            )

        def rows_of(c):
            return pl.ds(pl.multiple_of(c * chunk, 16), chunk)

        def store(c):
            return pltpu.make_async_copy(
                full.at[c], outs[0].at[rows_of(c), :], sems.at[1, c]
            )

        def tell(c):
            return remote(
                full.at[c], outs[1].at[rows_of(c), :], *pair(2, c), where_is("near")
            )

        def stage(number, c):
            if number == 1:
                load(c, self.places[0]).wait()
                cross(c, self.places[0]).wait()
                own[c] = own[c] + chip[c]
                over(c).start()
            elif number == 2:
                over(c).wait()
                own[c, 0] = own[c, 0] + other[c]
                halve(0, c).start()
            elif number < 3 + levels:
                level = number - 3
                halve(level, c).wait()
                mine = keeps(level)
                total = own[c, 0, mine, :] + halves[level][c]
                if level < levels - 1:
                    own[c, 0, mine, :] = total
                    halve(level + 1, c).start()
                else:
                    full[c, mine, :] = total
                    double(level, c).start()
            else:
                level = levels - 1 - (number - 3 - levels)
                double(level, c).wait()
                full[c, gives(level), :] = doubles[level][c]
                if level:
                    double(level - 1, c).start()
                else:
                    store(c).start()
                    tell(c).start()

        for number in reversed(range(1, 3 + 2 * levels)):
            since = step - (number if number == 1 else number - 1 + self.patience)
            c = since // self.spacing
            due = (since >= 0) & (c < self.count)
            if self.spacing > 1:
                due = due & (since % self.spacing == 0)

            @pl.when(due)
            def _():
                stage(number, c)

        for c, place in enumerate(self.places):

            @pl.when(step == c * self.spacing)
            def _():
                load(c, place).start()
                cross(c, place).start()

        @pl.when(step == steps - 1)
        def _():
            for c in range(self.count):
                store(c).wait()
                tell(c).wait()


def carry_alone(tasks, steps, collective):
    carrier = Carry(tasks, collective)

    def kernel(*refs):
        i, o = len(carrier.ins), len(carrier.ins) + len(carrier.outs)
        carrier.run(pl.program_id(0), steps, refs[:i], refs[i:o], refs[o:])

    hold = pl.BlockSpec(memory_space=pl.ANY)
    return pl.pallas_call(
        kernel,
        grid=(steps,),
        in_specs=[hold] * len(carrier.ins),
        out_specs=[hold] * len(carrier.outs),
        out_shape=carrier.outs,
        scratch_shapes=carrier.scratch,
        compiler_params=pltpu.CompilerParams(vmem_limit_bytes=VMEM, **carrier.params),
        name="carry_alone",
    )(*carrier.ins)


def open_up(tokens, qkv, norm, block, collective):
    _, rows, width = tokens.shape
    part = qkv.shape[-1]
    score = LOG2E / math.sqrt(width // HEADS)

    def kernel(tokens_ref, qkv_ref, norm_ref, *refs):
        x_out, w_out, n_out, q_out, own_out, other_out = refs[:6]
        x, low, w, n, q, kv = refs[6:12]
        row_sems, weight_sems, norm_sems, store_sems, kv_sems = (
            refs[12:15],
            refs[15:16],
            refs[16],
            refs[17],
            refs[18],
        )
        section, _, _ = spots()
        greet([*GROUP, 0])
        rows_in = spread_rows(tokens_ref, x, row_sems)
        weight = WeightCopies(qkv_ref, w, *weight_sems)
        weight.start()
        rows_in.start()
        norm_kept = pltpu.make_async_copy(norm_ref, n.at[section], norm_sems.at[0])
        norm_near = remote(
            norm_ref, n.at[section], norm_sems.at[1], norm_sems.at[2], where_is("near")
        )
        norm_kept.start()
        norm_near.start()
        stores = []

        def save(source, target):
            copy = pltpu.make_async_copy(source, target, store_sems.at[len(stores)])
            copy.start()
            stores.append(copy)

        kv_copies = []

        def project(side, k):
            def step(i, carry):
                own = pl.ds(pl.multiple_of(i * block, block), block)
                rows_low = low[own, :] if side == 0 else x[1, own, :]

                def product(m):
                    return dot_nn(rows_low, w[side, k, m * width : (m + 1) * width, :])

                q[side, k, own, :] = (product(0) * score).astype(BF16)
                kv[side, k, 0, own, :] = product(1).astype(BF16)
                kv[side, k, 1, own, :] = product(2).astype(BF16)
                return carry

            lax.fori_loop(0, rows // block, step, 0)
            spot = 2 * (2 * side + k)
            copy = remote(
                kv.at[side, k],
                other_out.at[side, k],
                kv_sems.at[spot],
                kv_sems.at[spot + 1],
                where_is("near"),
            )
            copy.start()
            kv_copies.append(copy)
            save(kv.at[side, k], own_out.at[side, k])
            save(q.at[side, k], q_out.at[side, k])

        norm_kept.wait()
        norm_near.wait()
        save(n, n_out)
        weight.forward()
        weight.forward_last()
        weight.finish()
        save(w, w_out)
        rows_in.wait_arrival(0)
        save(x.at[0], x_out.at[0])

        def settle(i, carry):
            own = pl.ds(pl.multiple_of(i * block, block), block)
            unit, _ = standardize(x[0, own, :].astype(F32))
            low[own, :] = affine(unit, n.at[0], 2).astype(BF16)
            return carry

        lax.fori_loop(0, rows // block, settle, 0)
        project(0, 0)
        project(0, 1)
        rows_in.wait_arrival(1)
        save(x.at[1], x_out.at[1])
        project(1, 0)
        project(1, 1)
        rows_in.wait_sent()
        for copy in kv_copies + stores:
            copy.wait()

    hold = pl.BlockSpec(memory_space=pl.ANY)
    shapes = [
        ((2, rows, width), BF16),
        ((2, 2, *qkv.shape), BF16),
        ((2, *norm.shape), F32),
        ((2, 2, rows, part), BF16),
        ((2, 2, 2, rows, part), BF16),
    ]
    return pl.pallas_call(
        kernel,
        in_specs=[hold] * 3,
        out_specs=[hold] * 6,
        out_shape=[jax.ShapeDtypeStruct(*s) for s in shapes + shapes[-1:]],
        scratch_shapes=[pltpu.VMEM(*shapes[0]), pltpu.VMEM((rows, width), BF16)]
        + [pltpu.VMEM(*s) for s in shapes[1:]]
        + ROW_SEMS
        + WeightCopies.sems
        + [
            pltpu.SemaphoreType.DMA((3,)),
            pltpu.SemaphoreType.DMA((12,)),
            pltpu.SemaphoreType.DMA((8,)),
        ],
        compiler_params=pltpu.CompilerParams(
            vmem_limit_bytes=VMEM, collective_id=collective, has_side_effects=True
        ),
        name="open_up",
    )(tokens, qkv, norm)


def local_general(tokens, lengths, self_qkv, self_out, cross_proj, ffn_up, ffn_down, norms, cotangent):
    section = lax.axis_index("section")
    tensor = lax.axis_index("tensor")
    tensors = lax.axis_size("tensor")
    _, row_count, rows, width = tokens.shape
    assert row_count == 2 and tensors % row_count == 0
    spread = tensors // row_count
    pieces = 2 * spread
    axes = ("section", "tensor")
    is_first = section == 0
    own_row = tensor // spread
    place = section * spread + tensor % spread

    def device(row, spot):
        return (spot // spread) * tensors + row * spread + spot % spread

    def each():
        return [(s, t) for s in range(2) for t in range(tensors)]

    straight = [(s * tensors + t, device(s, t)) for s, t in each()]
    turned = [(s * tensors + t, device(1 - s, t)) for s, t in each()]

    def bring(shares):
        stays = lax.dynamic_index_in_dim(shares, section, 0, keepdims=False)
        moves = lax.dynamic_index_in_dim(shares, 1 - section, 0, keepdims=False)
        one = lax.ppermute(stays, axes, straight)
        two = lax.ppermute(moves, axes, turned)
        return jnp.where(own_row == 0, one, two), jnp.where(own_row == 0, two, one)

    def take_back(source, target):
        one = jnp.where(own_row == 0, source, target)
        two = jnp.where(own_row == 0, target, source)
        one = lax.ppermute(one, axes, [(b, a) for a, b in straight])
        two = lax.ppermute(two, axes, [(b, a) for a, b in turned])
        return jnp.stack([jnp.where(is_first, one, two), jnp.where(is_first, two, one)])

    def rotate(value, by):
        pairs = [
            (device(r, p), device(r, (p + by) % pieces))
            for r in range(row_count)
            for p in range(pieces)
        ]
        return lax.ppermute(value, axes, pairs)

    def pieces_of(value):
        return [value] + [rotate(value, by) for by in range(1, pieces)]

    def pieces_home(values):
        return [values[0]] + [rotate(values[by], -by) for by in range(1, pieces)]

    def swap_sections(value):
        return lax.ppermute(value, "section", [(0, 1), (1, 0)])

    def both_sides(weight, dim):
        if spread == 1:
            other = lax.ppermute(weight, "tensor", [(t, 1 - t) for t in range(tensors)])
            parts = [weight, other]
        else:
            parts = [lax.all_gather(weight, "tensor", axis=dim, tiled=True)]
        swapped = [swap_sections(part) for part in parts]
        pairs = list(zip(parts, swapped))
        return (
            [jnp.where(is_first, mine, theirs) for mine, theirs in pairs],
            [jnp.where(is_first, theirs, mine) for mine, theirs in pairs],
        )

    def home(source_grad, target_grad, dim):
        keep = jnp.where(is_first, source_grad, target_grad).astype(F32)
        sent = swap_sections(jnp.where(is_first, target_grad, source_grad))
        total = (keep + sent.astype(F32)).astype(BF16)
        if spread == 1:
            other = lax.ppermute(total[1], "tensor", [(t, 1 - t) for t in range(tensors)])
            total = (total[0].astype(F32) + other.astype(F32)).astype(BF16)
        else:
            total = lax.psum_scatter(total[0], "tensor", scatter_dimension=dim, tiled=True)
        return total

    def span_of(query_side, key_side):
        own = lax.dynamic_index_in_dim(lengths, own_row, 1, keepdims=False)
        asks, answers = own[query_side], own[key_side]
        paired = asks[1] > 0
        second = paired & (place * rows >= asks[0])
        begin = jnp.where(second, answers[0], 0)
        end = jnp.where(second | ~paired, answers[0] + answers[1], answers[0])
        offsets = [(place - by) % pieces * rows for by in range(pieces)]
        return jnp.stack([begin, end, *offsets]).astype(jnp.int32)

    block = min(256, rows)
    query_block = min(256, rows)
    chunk = 512

    source, target = bring(tokens[0])
    source_norm, target_norm = (
        jnp.where(is_first, a, b)
        for a, b in (lambda own, other: ((own, other), (other, own)))(
            norms[0], swap_sections(norms[0])
        )
    )
    source_qkv, target_qkv = both_sides(self_qkv[0], 2)
    source_out, target_out = both_sides(self_out[0], 0)
    source_up, target_up = both_sides(ffn_up[0], 1)
    source_down, target_down = both_sides(ffn_down[0], 0)
    source_cross, target_cross = both_sides(cross_proj[0], 2)
    source_cot, target_cot = bring(cotangent[0])
    source_span, target_span, cross_span = span_of(0, 0), span_of(1, 1), span_of(1, 0)

    enc_q, enc_kv = project_qkv(source, source_norm, source_qkv, True, block)
    enc_kv = pieces_of(enc_kv)
    dec_q, dec_kv = project_qkv(target, target_norm, target_qkv, False, block)
    dec_kv = pieces_of(dec_kv)
    enc_mix, enc_lse = attend(enc_q, enc_kv, source_span, query_block)
    encoded, memory, enc_first, enc_third = encoder_forward(
        source, enc_mix, source_norm, source_out, source_up, source_down, source_cross, block
    )
    memory = pieces_of(memory)
    dec_mix, dec_lse = attend(dec_q, dec_kv, target_span, query_block)
    cross_q, dec_first = decoder_middle(
        target, dec_mix, target_norm, target_out, target_cross, block
    )
    cross_mix, cross_lse = attend(cross_q, memory, cross_span, query_block)
    decoded, second_grad, cross_mix_grad, cross_out_grad, dec_up, dec_down, dec_norm = decoder_turn(
        dec_first, cross_mix, target_cot, target_norm, target_cross, target_up, target_down, block
    )
    result = take_back(encoded, decoded)
    cross_q_grad, memory_grads, _ = attend_back(
        cross_q, memory, cross_mix, cross_mix_grad, cross_lse, cross_span, query_block, chunk
    )
    memory_grads = pieces_home(memory_grads)
    dec_first_grad, dec_mix_grad, cross_query_grad, dec_out, step = decoder_middle_back(
        dec_first,
        dec_mix,
        cross_q_grad,
        second_grad,
        target_norm,
        target_out,
        target_cross,
        block,
    )
    dec_norm += step
    enc_first_grad, enc_mix_grad, enc_cross, enc_out, enc_up, enc_down, enc_norm = encoder_back(
        enc_first,
        enc_third,
        enc_mix,
        memory_grads,
        source_cot,
        source_norm,
        source_out,
        source_up,
        source_down,
        source_cross,
        block,
    )
    dec_cross = jnp.stack([cross_query_grad, cross_out_grad], axis=1)
    up_grad, down_grad = home(enc_up, dec_up, 1), home(enc_down, dec_down, 0)
    out_grad, cross_grad = home(enc_out, dec_out, 0), home(enc_cross, dec_cross, 2)
    dec_q_grad, dec_kv_grads, _ = attend_back(
        dec_q, dec_kv, dec_mix, dec_mix_grad, dec_lse, target_span, query_block, chunk
    )
    dec_kv_grads = pieces_home(dec_kv_grads)
    enc_q_grad, enc_kv_grads, _ = attend_back(
        enc_q, enc_kv, enc_mix, enc_mix_grad, enc_lse, source_span, query_block, chunk
    )
    enc_kv_grads = pieces_home(enc_kv_grads)
    target_grad, dec_qkv, _ = input_back(
        target, dec_first_grad, dec_q_grad, dec_kv_grads, target_norm, target_qkv, False, block
    )
    source_grad, enc_qkv, step = input_back(
        source, enc_first_grad, enc_q_grad, enc_kv_grads, source_norm, source_qkv, True, block
    )
    enc_norm += step
    token_grad = take_back(source_grad, target_grad).astype(F32)
    qkv_grad = home(enc_qkv, dec_qkv, 2)
    norm_total = lax.psum(jnp.stack([enc_norm, dec_norm]), ("section", "dp", "tensor"))
    norm_grad = lax.dynamic_index_in_dim(norm_total, section, 0, keepdims=False)
    summed = [
        lax.psum(grad, "dp").astype(F32)
        for grad in (qkv_grad, out_grad, cross_grad, up_grad, down_grad)
    ]
    return (
        result[None],
        token_grad[None],
        summed[0][None],
        summed[1][None],
        summed[2][None],
        summed[3][None],
        summed[4][None],
        norm_grad[None],
    )


def local_fast(tokens, lengths, self_qkv, self_out, cross_proj, ffn_up, ffn_down, norms, cotangent):
    section, tensor = lax.axis_index("section"), lax.axis_index("tensor")
    _, row_count, rows, width = tokens.shape
    assert row_count == 2
    is_first = section == 0
    block = min(256, rows)
    query_block = min(256, rows)
    chunk = 512

    def swap(value):
        return lax.ppermute(value, "section", [(0, 1), (1, 0)])

    def flat(weight):
        return weight.reshape(-1, weight.shape[-1])

    def span_of(query_side, key_side):
        own = lax.dynamic_index_in_dim(lengths, tensor, 1, keepdims=False)
        asks, answers = own[query_side], own[key_side]
        paired = asks[1] > 0
        second = paired & (section * rows >= asks[0])
        begin = jnp.where(second, answers[0], 0)
        end = jnp.where(second | ~paired, answers[0] + answers[1], answers[0])
        return jnp.stack([begin, end, section * rows, (1 - section) * rows]).astype(jnp.int32)

    spans = span_of(0, 0), span_of(1, 1), span_of(1, 0)
    x, qkv, norm, q, kv_own, kv_other = open_up(tokens[0], flat(self_qkv), norms[0], block, 1)
    qkv = qkv.reshape(2, 2, *self_qkv.shape[1:])

    def parts(weight, side):
        return [At(weight, side, k) for k in range(2)]

    enc_x, dec_x, enc_norm_in, dec_norm_in = At(x, 0), At(x, 1), At(norm, 0), At(norm, 1)
    enc_q, dec_q = At(q, 0), At(q, 1)
    enc_kv, dec_kv = [[At(kv_own, side), At(kv_other, side)] for side in range(2)]
    enc_mix, enc_lse, out, cross, up = attend(
        enc_q,
        enc_kv,
        spans[0],
        query_block,
        Carry(
            [
                SpreadWeight(self_out[0], 3, 5),
                SpreadWeight(flat(cross_proj), 7, 10),
                SpreadWeight(ffn_up[0], 12, 15),
            ],
            2,
        ),
    )
    cross = cross.reshape(2, 2, *cross_proj.shape[1:])
    dec_mix, dec_lse, down, dec_cot = attend(
        dec_q,
        dec_kv,
        spans[1],
        query_block,
        Carry([SpreadWeight(ffn_down[0], 8, 14), SpreadRows(cotangent[0], (1,))], 3),
    )
    encoded, memory, enc_first, enc_third = encoder_forward(
        enc_x,
        enc_mix,
        enc_norm_in,
        parts(out, 0),
        parts(up, 0),
        parts(down, 0),
        parts(cross, 0),
        block,
    )
    memory = [memory, swap(memory)]
    cross_q, dec_first = decoder_middle(
        dec_x, dec_mix, dec_norm_in, parts(out, 1), parts(cross, 1), block
    )
    cross_mix, cross_lse, enc_cot, encoded = attend(
        cross_q,
        memory,
        spans[2],
        query_block,
        Carry([SpreadRows(cotangent[0], (0,)), ReturnRows(encoded, 0)], 4),
    )
    decoded, second_grad, cross_mix_grad, cross_out_grad, ffn_dec, dec_norm = decoder_turn(
        dec_first,
        cross_mix,
        At(dec_cot, 1),
        dec_norm_in,
        parts(cross, 1),
        parts(up, 1),
        parts(down, 1),
        block,
        True,
    )
    cross_q_grad, memory_grads, (ffn_dec, ffn_dec_other, decoded) = attend_back(
        cross_q,
        memory,
        cross_mix,
        cross_mix_grad,
        cross_lse,
        spans[2],
        query_block,
        chunk,
        Carry([Reduce([ffn_dec], 256, 2, 2), ReturnRows(decoded, 1)], 5),
    )
    memory_grads = [memory_grads[0], swap(memory_grads[1])]
    dec_first_grad, dec_mix_grad, cross_query_grad, dec_out, step = decoder_middle_back(
        dec_first,
        dec_mix,
        cross_q_grad,
        second_grad,
        dec_norm_in,
        parts(out, 1),
        parts(cross, 1),
        block,
    )
    dec_norm += step
    enc_first_grad, enc_mix_grad, ffn_enc, sides, enc_norm = encoder_back(
        enc_first,
        enc_third,
        enc_mix,
        memory_grads,
        At(enc_cot, 0),
        enc_norm_in,
        parts(out, 0),
        parts(up, 0),
        parts(down, 0),
        parts(cross, 0),
        block,
        [dec_out, cross_query_grad, cross_out_grad],
    )
    dec_q_grad, dec_kv_grads, (ffn_enc, ffn_enc_other) = attend_back(
        dec_q,
        dec_kv,
        dec_mix,
        dec_mix_grad,
        dec_lse,
        spans[1],
        query_block,
        chunk,
        Carry([Reduce([ffn_enc], 256, 2, 2)], 6),
    )
    dec_kv_grads = [dec_kv_grads[0], swap(dec_kv_grads[1])]
    target_grad, dec_qkv = input_back(
        dec_x,
        dec_first_grad,
        dec_q_grad,
        dec_kv_grads,
        dec_norm_in,
        parts(qkv, 1),
        False,
        block,
        [],
    )
    enc_q_grad, enc_kv_grads, (sides, sides_other, target_grad) = attend_back(
        enc_q,
        enc_kv,
        enc_mix,
        enc_mix_grad,
        enc_lse,
        spans[0],
        query_block,
        chunk,
        Carry([Reduce([sides, dec_qkv], 384, 1, 2), ReturnRows(target_grad, 1)], 7),
    )
    enc_kv_grads = [enc_kv_grads[0], swap(enc_kv_grads[1])]
    source_grad, enc_qkv = input_back(
        enc_x,
        enc_first_grad,
        enc_q_grad,
        enc_kv_grads,
        enc_norm_in,
        parts(qkv, 0),
        True,
        block,
        [enc_norm, dec_norm],
    )
    reduce = Reduce([enc_qkv], enc_qkv.shape[2] // 2, 1, 1)
    last, last_other, source_grad = carry_alone(
        [reduce, ReturnRows(source_grad, 0)], reduce.steps, 8
    )

    side_rows, half = 3 * width, 3 * width // 2
    up_grad = jnp.where(is_first, ffn_enc, ffn_dec_other).astype(F32)
    down_grad = jnp.where(is_first, ffn_enc_other, ffn_dec).astype(F32)
    up_grad = jnp.concatenate(jnp.split(up_grad, 2, axis=0), axis=1)

    def columns(halves):
        return jnp.concatenate([halves[:half], halves[half : 2 * half]], axis=1)

    qkv_grad = jnp.concatenate(
        [
            jnp.where(is_first, columns(last), sides_other[side_rows:]),
            jnp.where(is_first, columns(last_other), sides[side_rows:]),
        ],
        axis=0,
    )
    qkv_grad = qkv_grad.astype(F32).reshape(self_qkv.shape)
    sides = sides[:side_rows].astype(F32)
    out_grad = jnp.concatenate([sides[: width // 2], sides[width // 2 : width]], axis=1)
    cross_grad = sides[width:].reshape(cross_proj.shape)
    norm_grad = last[2 * half : 2 * half + 24].astype(F32).reshape(norms.shape)

    def by_side(source, target):
        return jnp.where(is_first, source, target)

    return (
        by_side(encoded, decoded)[None],
        by_side(source_grad, target_grad).astype(F32)[None],
        qkv_grad,
        out_grad[None],
        cross_grad,
        up_grad[None],
        down_grad[None],
        norm_grad,
    )


def solution(mesh):
    placed = (
        P("section", "dp", "tensor", None),
        P(None, "dp", None),
        P("section", None, None, "tensor"),
        P("section", "tensor", None),
        P("section", None, None, "tensor"),
        P("section", None, "tensor"),
        P("section", "tensor", None),
        P("section", None, None, None),
        P("section", "dp", "tensor", None),
    )
    sizes = dict(mesh.shape)
    steps = sizes["dp"].bit_length() - 1
    fast = sizes["tensor"] == 2 and sizes["dp"] == 1 << steps and 0 < steps <= 3
    return jax.shard_map(
        local_fast if fast else local_general,
        mesh=mesh,
        in_specs=placed,
        out_specs=(
            P("section", "dp", "tensor", None),
            P("section", "dp", "tensor", None),
            P("section", None, None, "tensor"),
            P("section", "tensor", None),
            P("section", None, None, "tensor"),
            P("section", None, "tensor"),
            P("section", "tensor", None),
            P("section", None, None, None),
        ),
        check_vma=False,
    )
```

```python
import functools
import math

import jax
import jax.numpy as jnp
from jax import lax
from jax.experimental import pallas as pl
from jax.experimental.pallas import tpu as pltpu
from jax.sharding import PartitionSpec as P

HEADS = 8
EPSILON = 1e-05
MASKED = -1000000000.0
LOG2E = 1.0 / math.log(2.0)
PAIR = 128
HALF = 64
VMEM = 60 * 1024 * 1024
BF16 = jnp.bfloat16
F32 = jnp.float32


def standardize(rows):
    mean = jnp.mean(rows, axis=-1, keepdims=True)
    centered = rows - mean
    inv = lax.rsqrt(jnp.mean(centered * centered, axis=-1, keepdims=True) + EPSILON)
    return centered * inv, inv


def affine(unit, norm_ref, slot):
    return unit * norm_ref[slot, 0:1, :] + norm_ref[slot, 1:2, :]


def norm_back(unit, inv, norm_ref, slot, grad, grad_ref):
    grad_ref[slot, 0:1, :] += jnp.sum(grad * unit, axis=0, keepdims=True)
    grad_ref[slot, 1:2, :] += jnp.sum(grad, axis=0, keepdims=True)
    scaled = grad * norm_ref[slot, 0:1, :]
    first = jnp.mean(scaled, axis=-1, keepdims=True)
    second = jnp.mean(scaled * unit, axis=-1, keepdims=True)
    return inv * (scaled - first - unit * second)


def gelu_tanh(inner):
    return jnp.tanh(0.7978845608028654 * (inner + 0.044715 * inner * inner * inner))


def gelu(inner):
    return 0.5 * inner * (1.0 + gelu_tanh(inner))


def gelu_both(inner):
    bent = gelu_tanh(inner)
    slope = 0.7978845608028654 * (1.0 + 0.134145 * inner * inner)
    half = 0.5 * (1.0 + bent)
    return inner * half, half + 0.5 * inner * (1.0 - bent * bent) * slope


def dot_nn(a, b):
    return jnp.dot(a, b, preferred_element_type=F32)


def dot_nt(a, b):
    return lax.dot_general(a, b, (((1,), (1,)), ((), ())), preferred_element_type=F32)


def dot_tn(a, b):
    return lax.dot_general(a, b, (((0,), (0,)), ((), ())), preferred_element_type=F32)


class At:
    def __init__(self, array, *lead):
        self.array, self.lead = array, lead
        self.shape = array.shape[len(lead) :]
        self.dtype = array.dtype

    def spec(self, sizes, index, **options):
        nones = (None,) * len(self.lead)
        return pl.BlockSpec(nones + tuple(sizes), lambda *g: self.lead + tuple(index(*g)), **options)


def at(array):
    return array if isinstance(array, At) else At(array)


def row_call(
    body, name, rows, block, row_ins, whole_ins, row_outs, sum_outs, flops, finish=None, finals=None
):
    row_ins = [(at(a), dim) for a, dim in row_ins]
    whole_ins = [at(a) for a in whole_ins]
    finals = sum_outs if finals is None else finals

    def blocked(array, dim):
        sizes = tuple(block if i == dim else size for i, size in enumerate(array.shape))
        return array.spec(sizes, lambda g: tuple(g if i == dim else 0 for i in range(len(sizes))))

    def blocked_out(shape, dim):
        sizes = tuple(block if i == dim else size for i, size in enumerate(shape))
        return pl.BlockSpec(
            sizes, lambda g: tuple(g if i == dim else 0 for i in range(len(shape)))
        )

    def whole(array):
        return array.spec(
            array.shape,
            lambda g: (0,) * len(array.shape),
            pipeline_mode=pl.Buffered(buffer_count=1),
        )

    def whole_out(shape):
        return pl.BlockSpec(
            shape, lambda g: (0,) * len(shape), pipeline_mode=pl.Buffered(buffer_count=1)
        )

    n_rows_in = len(row_ins)
    n_in = n_rows_in + len(whole_ins)
    n_row, n_sum = len(row_outs), len(finals)

    def kernel(*refs):
        ins, outs = refs[:n_in], refs[n_in : n_in + n_row]
        sums, totals = refs[n_in + n_row : n_in + n_row + n_sum], refs[n_in + n_row + n_sum :]

        @pl.when(pl.program_id(0) == 0)
        def _():
            for total in totals:
                total[...] = jnp.zeros_like(total)

        body(ins, outs, totals)

        @pl.when(pl.program_id(0) == pl.num_programs(0) - 1)
        def _():
            if finish is None:
                for out, total in zip(sums, totals):
                    out[...] = total[...].astype(out.dtype)
            else:
                finish(ins[n_rows_in:], totals, sums)

    arrays = [array for array, _ in row_ins] + whole_ins
    size = sum(math.prod(a.shape) * a.dtype.itemsize for a in arrays)
    return pl.pallas_call(
        kernel,
        grid=(rows // block,),
        in_specs=[blocked(a, dim) for a, dim in row_ins] + [whole(a) for a in whole_ins],
        out_specs=[blocked_out(shape, dim) for shape, _, dim in row_outs]
        + [whole_out(shape) for shape, _ in finals],
        out_shape=[jax.ShapeDtypeStruct(shape, dtype) for shape, dtype, _ in row_outs]
        + [jax.ShapeDtypeStruct(shape, dtype) for shape, dtype in finals],
        scratch_shapes=[pltpu.VMEM(shape, F32) for shape, _ in sum_outs],
        compiler_params=pltpu.CompilerParams(vmem_limit_bytes=VMEM),
        cost_estimate=pl.CostEstimate(flops=flops, bytes_accessed=size, transcendentals=0),
        name=name,
    )(*[a.array for a in arrays])


def column_blocks(wide, into, core, k, row):
    rows, columns = wide.shape[0], wide.shape[1] // 2
    for half in range(2):
        into[core, k, row + half * rows : row + (half + 1) * rows, :] = wide[
            :, half * columns : (half + 1) * columns
        ].astype(BF16)


def project_qkv(x, norm, weights, with_norm, block):
    rows, width = x.shape
    parts, part = len(weights), weights[0].shape[-1]
    score = LOG2E / math.sqrt(width // HEADS)

    def body(ins, outs, totals):
        x_ref, norm_ref, *w = ins
        q_ref, kv_ref = outs
        rows_in = x_ref[...]
        if with_norm:
            unit, _ = standardize(rows_in.astype(F32))
            rows_in = affine(unit, norm_ref, 2).astype(BF16)
        for k in range(parts):
            q_ref[k] = (dot_nn(rows_in, w[k][0]) * score).astype(BF16)
            kv_ref[k, 0] = dot_nn(rows_in, w[k][1]).astype(BF16)
            kv_ref[k, 1] = dot_nn(rows_in, w[k][2]).astype(BF16)

    return row_call(
        body,
        "project_qkv",
        rows,
        block,
        [(x, 0)],
        [norm, *weights],
        [((parts, rows, part), BF16, 1), ((parts, 2, rows, part), BF16, 2)],
        [],
        6 * rows * width * width,
    )


def encoder_forward(x, mix, norm, out, up, down, cross, block):
    rows, width = x.shape
    parts, part = len(out), out[0].shape[0]

    def body(ins, outs, totals):
        x_ref, mix_ref, norm_ref = ins[:3]
        wo, wu, wd, wc = (ins[3 + i * parts : 3 + (i + 1) * parts] for i in range(4))
        result_ref, kv_ref, first_ref, third_ref = outs
        unit, _ = standardize(x_ref[...].astype(F32))
        first = affine(unit, norm_ref, 2)
        for k in range(parts):
            first += dot_nn(mix_ref[k], wo[k][...])
        first_ref[...] = first
        unit, _ = standardize(first)
        third = affine(unit, norm_ref, 0)
        low = third.astype(BF16)
        for k in range(parts):
            act = gelu(dot_nn(low, wu[k][...])).astype(BF16)
            third += dot_nn(act, wd[k][...])
        third_ref[...] = third
        unit, _ = standardize(third)
        low = affine(unit, norm_ref, 1).astype(BF16)
        result_ref[...] = low
        for k in range(parts):
            kv_ref[k, 0] = dot_nn(low, wc[k][0]).astype(BF16)
            kv_ref[k, 1] = dot_nn(low, wc[k][1]).astype(BF16)

    units = sum(w.shape[1] for w in up)
    return row_call(
        body,
        "encoder_forward",
        rows,
        block,
        [(x, 0), (mix, 1)],
        [norm, *out, *up, *down, *cross],
        [
            ((rows, width), BF16, 0),
            ((parts, 2, rows, part), BF16, 2),
            ((rows, width), F32, 0),
            ((rows, width), F32, 0),
        ],
        [],
        6 * rows * width * width + 4 * rows * width * units,
    )


def decoder_middle(x, mix, norm, out, cross, block):
    rows, width = x.shape
    parts, part = len(out), out[0].shape[0]
    score = LOG2E / math.sqrt(width // HEADS)

    def body(ins, outs, totals):
        x_ref, mix_ref, norm_ref = ins[:3]
        wo, wc = (ins[3 + i * parts : 3 + (i + 1) * parts] for i in range(2))
        q_ref, first_ref = outs
        first = x_ref[...].astype(F32)
        for k in range(parts):
            first += dot_nn(mix_ref[k], wo[k][...])
        first_ref[...] = first
        unit, _ = standardize(first)
        low = affine(unit, norm_ref, 0).astype(BF16)
        for k in range(parts):
            q_ref[k] = (dot_nn(low, wc[k][0]) * score).astype(BF16)

    return row_call(
        body,
        "decoder_middle",
        rows,
        block,
        [(x, 0), (mix, 1)],
        [norm, *out, *cross],
        [((parts, rows, part), BF16, 1), ((rows, width), F32, 0)],
        [],
        4 * rows * width * width,
    )


def ffn_back(low, grad_low, up, down, up_total, down_total, parts):
    grad = None
    for k in range(parts):
        act, slope = gelu_both(dot_nn(low, up[k][...]))
        down_total[k] += dot_tn(act.astype(BF16), grad_low)
        grad_inner = (dot_nt(grad_low, down[k][...]) * slope).astype(BF16)
        up_total[k] += dot_tn(low, grad_inner)
        step = dot_nt(grad_inner, up[k][...])
        grad = step if grad is None else grad + step
    return grad


def decoder_turn(first, mix, cotangent, norm, cross, up, down, block, paired=False):
    rows, width = first.shape
    parts, part, units = len(cross), cross[0].shape[-1], up[0].shape[1]

    def body(ins, outs, totals):
        first_ref, mix_ref, cot_ref, norm_ref = ins[:4]
        wc, wu, wd = (ins[4 + i * parts : 4 + (i + 1) * parts] for i in range(3))
        result_ref, second_grad_ref, mix_grad_ref = outs
        out_total, up_total, down_total, norm_total = totals
        unit, _ = standardize(first_ref[...])
        second = affine(unit, norm_ref, 0)
        for k in range(parts):
            second += dot_nt(mix_ref[k], wc[k][1])
        unit_two, inv_two = standardize(second)
        third = affine(unit_two, norm_ref, 2)
        low = third.astype(BF16)
        acts, slopes = [], []
        for k in range(parts):
            act, slope = gelu_both(dot_nn(low, wu[k][...]))
            acts.append(act.astype(BF16))
            slopes.append(slope)
            third += dot_nn(acts[k], wd[k][...])
        unit_three, inv_three = standardize(third)
        result_ref[...] = affine(unit_three, norm_ref, 1).astype(BF16)
        grad = norm_back(
            unit_three, inv_three, norm_ref, 1, cot_ref[...].astype(F32), norm_total
        )
        grad_low = grad.astype(BF16)
        for k in range(parts):
            down_total[k] += dot_tn(acts[k], grad_low)
            grad_inner = (dot_nt(grad_low, wd[k][...]) * slopes[k]).astype(BF16)
            up_total[k] += dot_tn(low, grad_inner)
            grad += dot_nt(grad_inner, wu[k][...])
        grad = norm_back(unit_two, inv_two, norm_ref, 2, grad, norm_total)
        second_grad_ref[...] = grad
        grad_low = grad.astype(BF16)
        for k in range(parts):
            out_total[k] += dot_tn(grad_low, mix_ref[k])
            mix_grad_ref[k] = dot_nn(grad_low, wc[k][1]).astype(BF16)

    sums = [
        ((parts, width, part), BF16),
        ((parts, width, units), BF16),
        ((parts, units, width), BF16),
        ((3, 2, width), F32),
    ]
    if paired:
        finals = [sums[0], ((2, parts, units, width), BF16), sums[3]]

        def finish(ins, totals, outs):
            outs[0][...] = totals[0][...].astype(BF16)
            for k in range(parts):
                column_blocks(totals[1][k], outs[1], 0, k, 0)
                outs[1][1, k] = totals[2][k].astype(BF16)
            outs[2][...] = totals[3][...]

    else:
        finals, finish = None, None

    return row_call(
        body,
        "decoder_turn",
        rows,
        block,
        [(first, 0), (mix, 1), (cotangent, 0)],
        [norm, *cross, *up, *down],
        [
            ((rows, width), BF16, 0),
            ((rows, width), F32, 0),
            ((parts, rows, part), BF16, 1),
        ],
        sums,
        6 * rows * width * width + 12 * rows * width * units * parts,
        finish,
        finals,
    )


def decoder_middle_back(first, mix, query_grad, second_grad, norm, out, cross, block):
    rows, width = first.shape
    parts, part = len(out), out[0].shape[0]

    def body(ins, outs, totals):
        first_ref, mix_ref, query_grad_ref, second_grad_ref, norm_ref = ins[:5]
        wo, wc = (ins[5 + i * parts : 5 + (i + 1) * parts] for i in range(2))
        first_grad_ref, mix_grad_ref = outs
        query_total, out_total, norm_total = totals
        unit, inv = standardize(first_ref[...])
        low = affine(unit, norm_ref, 0).astype(BF16)
        grad = second_grad_ref[...]
        for k in range(parts):
            query_total[k] += dot_tn(low, query_grad_ref[k])
            grad += dot_nt(query_grad_ref[k], wc[k][0])
        grad = norm_back(unit, inv, norm_ref, 0, grad, norm_total)
        first_grad_ref[...] = grad
        grad_low = grad.astype(BF16)
        for k in range(parts):
            out_total[k] += dot_tn(mix_ref[k], grad_low)
            mix_grad_ref[k] = dot_nt(grad_low, wo[k][...]).astype(BF16)

    return row_call(
        body,
        "decoder_middle_back",
        rows,
        block,
        [(first, 0), (mix, 1), (query_grad, 1), (second_grad, 0)],
        [norm, *out, *cross],
        [((rows, width), F32, 0), ((parts, rows, part), BF16, 1)],
        [
            ((parts, width, part), BF16),
            ((parts, part, width), BF16),
            ((3, 2, width), F32),
        ],
        8 * rows * width * width,
    )


def encoder_back(
    first, third, mix, memory_grads, cotangent, norm, out, up, down, cross, block, paired=None
):
    rows, width = first.shape
    parts, part, units = len(out), out[0].shape[0], up[0].shape[1]
    pieces = len(memory_grads)

    def body(ins, outs, totals):
        first_ref, third_ref, mix_ref, cot_ref = ins[:4]
        memory_refs, norm_ref = ins[4 : 4 + pieces], ins[4 + pieces]
        rest = ins[5 + pieces :]
        wo, wu, wd, wc = (rest[i * parts : (i + 1) * parts] for i in range(4))
        first_grad_ref, mix_grad_ref = outs
        cross_total, out_total, up_total, down_total, norm_total = totals
        unit, inv = standardize(third_ref[...])
        low = affine(unit, norm_ref, 1).astype(BF16)
        grad = cot_ref[...].astype(F32)
        for i in range(2):
            for k in range(parts):
                memory = memory_refs[0][k, i].astype(F32)
                for ref in memory_refs[1:]:
                    memory += ref[k, i].astype(F32)
                memory = memory.astype(BF16)
                cross_total[k, i] += dot_tn(low, memory)
                grad += dot_nt(memory, wc[k][i])
        grad = norm_back(unit, inv, norm_ref, 1, grad, norm_total)
        unit, inv = standardize(first_ref[...])
        low = affine(unit, norm_ref, 0).astype(BF16)
        grad += ffn_back(low, grad.astype(BF16), wu, wd, up_total, down_total, parts)
        grad = norm_back(unit, inv, norm_ref, 0, grad, norm_total)
        first_grad_ref[...] = grad
        grad_low = grad.astype(BF16)
        for k in range(parts):
            out_total[k] += dot_tn(mix_ref[k], grad_low)
            mix_grad_ref[k] = dot_nt(grad_low, wo[k][...]).astype(BF16)

    sums = [
        ((parts, 2, width, part), BF16),
        ((parts, part, width), BF16),
        ((parts, width, units), BF16),
        ((parts, units, width), BF16),
        ((3, 2, width), F32),
    ]
    if paired is not None:
        side = 3 * width
        finals = [
            ((2, parts, units, width), BF16),
            ((2, parts, side, part), BF16),
            sums[4],
        ]

        def finish(ins, totals, outs):
            dec_out, dec_query, dec_cross = ins[-3:]
            for k in range(parts):
                column_blocks(totals[2][k], outs[0], 0, k, 0)
                outs[0][1, k] = totals[3][k].astype(BF16)
                column_blocks(totals[1][k], outs[1], 0, k, 0)
                outs[1][0, k, width:side, :] = (
                    totals[0][k].reshape(2 * width, part).astype(BF16)
                )
                column_blocks(dec_out[k], outs[1], 1, k, 0)
                outs[1][1, k, width : 2 * width, :] = dec_query[k]
                outs[1][1, k, 2 * width : side, :] = dec_cross[k]
            outs[2][...] = totals[4][...]

    else:
        finals, finish, paired = None, None, []

    return row_call(
        body,
        "encoder_back",
        rows,
        block,
        [(first, 0), (third, 0), (mix, 1), (cotangent, 0)] + [(m, 2) for m in memory_grads],
        [norm, *out, *up, *down, *cross, *paired],
        [((rows, width), F32, 0), ((parts, rows, part), BF16, 1)],
        sums,
        12 * rows * width * width + 10 * rows * width * units * parts,
        finish,
        finals,
    )


def input_back(
    x, first_grad, query_grad, key_grads, norm, weights, with_norm, block, paired=None
):
    rows, width = x.shape
    parts, part = len(weights), weights[0].shape[-1]
    pieces = len(key_grads)

    def body(ins, outs, totals):
        x_ref, first_grad_ref, query_grad_ref = ins[:3]
        key_refs, norm_ref, w = ins[3 : 3 + pieces], ins[3 + pieces], ins[4 + pieces :][:parts]
        (grad_ref,) = outs
        qkv_total, norm_total = totals
        low = x_ref[...]
        if with_norm:
            unit, inv = standardize(low.astype(F32))
            low = affine(unit, norm_ref, 2).astype(BF16)
        grad = first_grad_ref[...]
        for k in range(parts):
            for i in range(3):
                if i == 0:
                    member = query_grad_ref[k]
                else:
                    member = key_refs[0][k, i - 1].astype(F32)
                    for ref in key_refs[1:]:
                        member += ref[k, i - 1].astype(F32)
                    member = member.astype(BF16)
                qkv_total[k, i] += dot_tn(low, member)
                grad += dot_nt(member, w[k][i])
        if with_norm:
            grad = norm_back(unit, inv, norm_ref, 2, grad, norm_total)
        grad_ref[...] = grad.astype(BF16)

    sums = [((parts, 3, width, part), BF16), ((3, 2, width), F32)]
    if paired is not None:
        half = 3 * width // 2
        shape = (4 * half // 2 + 2 * PAIR, PAIR) if paired else (half, part)
        finals = [((2, parts, *shape), BF16)]

        def finish(ins, totals, outs):
            for k in range(parts):
                both = totals[0][k].reshape(2 * half, part)
                for core in range(2):
                    own = both[core * half : (core + 1) * half]
                    if paired:
                        column_blocks(own, outs[0], core, k, 0)
                    else:
                        outs[0][core, k] = own.astype(BF16)
            if paired:
                sides = [ins[-2][...] + totals[1][...], ins[-1][...]]
                for core, table in enumerate(sides):
                    lines = [
                        table[slot, i : i + 1, h * PAIR : (h + 1) * PAIR]
                        for slot in range(3)
                        for i in range(2)
                        for h in range(width // PAIR)
                    ]
                    lines.append(jnp.zeros((2 * PAIR - len(lines), PAIR), F32))
                    lines = jnp.concatenate(lines, axis=0).astype(BF16)
                    for k in range(parts):
                        outs[0][core, k, 2 * half :, :] = lines

    else:
        finals, finish, paired = None, None, []

    return row_call(
        body,
        "input_back",
        rows,
        block,
        [(x, 0), (first_grad, 0), (query_grad, 1)] + [(g, 2) for g in key_grads],
        [norm, *weights, *paired],
        [((rows, width), BF16, 0)],
        sums,
        12 * rows * width * width,
        finish,
        finals,
    )


def widen_keys(span_ref, kv_refs, key_e, key_o, value_e, value_o, rows):
    lane = lax.broadcasted_iota(jnp.int32, (rows, PAIR), 1)
    place = lax.broadcasted_iota(jnp.int32, (rows, PAIR), 0)
    low = lane < HALF
    for g, kv_ref in enumerate(kv_refs):
        spot = place + span_ref[2 + g]
        live = (spot >= span_ref[0]) & (spot < span_ref[1])
        bias = jnp.where(live, 0.0, MASKED)
        keys, values = kv_ref[0].astype(F32), kv_ref[1].astype(F32)
        own = pl.ds(g * rows, rows)
        key_e[own, :] = jnp.where(low, keys, jnp.where(lane == HALF, bias, 1.0)).astype(BF16)
        key_o[own, :] = jnp.where(low, jnp.where(lane == 0, bias, 1.0), keys).astype(BF16)
        value_e[own, :] = jnp.where(low, values, 1.0).astype(BF16)
        value_o[own, :] = jnp.where(low, 1.0, values).astype(BF16)


def attention_specs(per_part, rows):
    def query_spec(array):
        return at(array).spec((None, rows, PAIR), lambda i: (i // per_part, 0, i % per_part))

    def kv_spec(array):
        return at(array).spec(
            (None, 2, rows, PAIR), lambda i: (i // per_part, 0, 0, i % per_part)
        )

    return query_spec, kv_spec, pl.BlockSpec((rows, PAIR), lambda i: (0, i))


def attend(query, kv_pieces, span, block, carrier=None, slots=1):
    query, kv_pieces = at(query), [at(piece) for piece in kv_pieces]
    carrier = carrier or Carry()
    parts, rows, part = query.shape
    per_part = part // PAIR
    pairs = parts * per_part
    pieces = len(kv_pieces)
    keys = rows * pieces
    n_carry = len(carrier.ins)
    blocks = rows // block
    stride = blocks // slots

    def kernel(span_ref, q_ref, *refs):
        kv_refs, refs = refs[:pieces], refs[pieces:]
        carry_ins, refs = refs[:n_carry], refs[n_carry:]
        out_ref, lse_ref, refs = refs[0], refs[1], refs[2:]
        carry_outs, refs = refs[: len(carrier.outs)], refs[len(carrier.outs) :]
        key_e, key_o, value_e, value_o = refs[:4]

        def carry(slot):
            place = pl.program_id(0)
            carrier.run(place, slot, slots, pairs * slots, carry_ins, carry_outs, refs[4:])

        carry(0)
        widen_keys(span_ref, kv_refs, key_e, key_o, value_e, value_o, rows)
        lane = lax.broadcasted_iota(jnp.int32, (block, PAIR), 1)
        low = lane < HALF
        units = []
        for i in range(blocks):
            query = q_ref[i * block : (i + 1) * block, :].astype(F32)
            first = jnp.where(low, query, jnp.where(lane == HALF, 1.0, 0.0)).astype(BF16)
            second = jnp.where(low, jnp.where(lane == 0, 1.0, 0.0), query).astype(BF16)
            units += [(first, key_e, value_e), (second, key_o, value_o)]

        def scores_of(unit):
            return dot_nt(unit[0], unit[1][...])

        ahead = scores_of(units[0])
        tops, sums = [], []
        for u, unit in enumerate(units):
            if u and u % (2 * stride) == 0:
                carry(u // (2 * stride))
            scores = ahead
            if u + 1 < len(units):
                ahead = scores_of(units[u + 1])
            top = jnp.max(scores, axis=1, keepdims=True)
            tops.append(top)
            sums.append(dot_nn(jnp.exp2(scores - top).astype(BF16), unit[2][...]))
            if u % 2:
                own = slice(u // 2 * block, (u // 2 + 1) * block)
                top = jnp.where(low, tops[u], tops[u - 1])
                weight = jnp.where(low, sums[u], sums[u - 1])
                lse_ref[own, :] = top + LOG2E * jnp.log(weight)
                mixed = jnp.where(low, sums[u - 1], sums[u])
                out_ref[own, :] = (mixed / pltpu.roll(weight, HALF, 1)).astype(BF16)

    query_spec, kv_spec, lse_spec = attention_specs(per_part, rows)
    plain = jax.ShapeDtypeStruct(query.shape, BF16)
    hold = pl.BlockSpec(memory_space=pl.ANY)
    return pl.pallas_call(
        kernel,
        grid=(pairs,),
        in_specs=[pl.BlockSpec(memory_space=pltpu.SMEM), query_spec(query)]
        + [kv_spec(piece) for piece in kv_pieces]
        + [hold] * n_carry,
        out_specs=[query_spec(plain), lse_spec] + [hold] * len(carrier.outs),
        scratch_shapes=[pltpu.VMEM((keys, PAIR), BF16)] * 4 + carrier.scratch,
        out_shape=[plain, jax.ShapeDtypeStruct((rows, pairs * PAIR), F32)] + carrier.outs,
        compiler_params=pltpu.CompilerParams(vmem_limit_bytes=VMEM, **carrier.params),
        cost_estimate=pl.CostEstimate(
            flops=16 * rows * keys * pairs * PAIR,
            bytes_accessed=8 * rows * pairs * PAIR * pieces,
            transcendentals=0,
        ),
        name="attend",
    )(span, query.array, *[piece.array for piece in kv_pieces], *carrier.ins)


def attend_back(
    query, kv_pieces, mix, mix_grad, lse, span, chunk, carrier=None, slots=1
):
    query, kv_pieces = at(query), [at(piece) for piece in kv_pieces]
    mix, mix_grad = at(mix), at(mix_grad)
    parts, rows, part = query.shape
    per_part = part // PAIR
    pairs = parts * per_part
    pieces = len(kv_pieces)
    keys = rows * pieces
    scale = 1.0 / math.sqrt(HALF)
    swaps = carrier is not None
    carrier = carrier or Carry()
    n_carry = len(carrier.ins)
    kept = 1 if swaps else pieces
    chunks = keys // chunk
    stride = chunks // slots

    def kernel(span_ref, q_ref, mix_ref, grad_ref, lse_ref, *refs):
        kv_refs, refs = refs[:pieces], refs[pieces:]
        carry_ins, refs = refs[:n_carry], refs[n_carry:]
        dq_ref, dkv_refs, refs = refs[0], refs[1 : pieces + 1], refs[pieces + 1 :]
        carry_outs, refs = refs[: len(carrier.outs)], refs[len(carrier.outs) :]
        key_e, key_o, value_e, value_o, key_t = refs[:5]
        refs = refs[5:]
        if swaps:
            given, swap_sems, refs = refs[0], refs[1], refs[2:]
        pair = pl.program_id(0)

        def carry(slot):
            carrier.run(pair, slot, slots, pairs * slots, carry_ins, carry_outs, refs)

        carry(0)
        widen_keys(span_ref, kv_refs, key_e, key_o, value_e, value_o, rows)
        for g, kv_ref in enumerate(kv_refs):
            key_t[:, g * rows : (g + 1) * rows] = kv_ref[0].T
        lane = lax.broadcasted_iota(jnp.int32, (rows, PAIR), 1)
        low = lane < HALF
        query, grad = q_ref[...].astype(F32), grad_ref[...].astype(F32)
        product = mix_ref[...].astype(F32) * grad
        inner = jnp.where(
            low,
            jnp.sum(jnp.where(low, 0.0, product), axis=1, keepdims=True),
            jnp.sum(jnp.where(low, product, 0.0), axis=1, keepdims=True),
        )
        spot = jnp.where(low, lane, lane - HALF)

        def three(value, shift):
            high = value.astype(BF16).astype(F32)
            rest = value - high
            mid = rest.astype(BF16).astype(F32)
            return jnp.where(
                spot == shift,
                high,
                jnp.where(
                    spot == shift + 1, mid, jnp.where(spot == shift + 2, rest - mid, 0.0)
                ),
            )

        lse = three(-lse_ref[...], 1) + jnp.where(spot == 0, 1.0, 0.0)
        inner = three(-inner, 0)
        heads = [
            (
                key,
                value,
                jnp.where(own, query, lse).astype(BF16),
                jnp.where(own, grad, inner).astype(BF16),
                jnp.where(own, query, 0.0).astype(BF16),
                jnp.where(own, grad, 0.0).astype(BF16),
            )
            for own, key, value in ((low, key_e, value_e), (~low, key_o, value_o))
        ]
        units = [(c * chunk, h) for c in range(chunks) for h in range(2)]

        def front(unit):
            begin, h = unit
            own = slice(begin, begin + chunk)
            key, value, q_wide, g_wide, _, _ = heads[h]
            return dot_nt(key[own, :], q_wide), dot_nt(value[own, :], g_wide)

        ahead = front(units[0])
        dq = [None, None]
        for u, (begin, h) in enumerate(units):
            if u and u % (2 * stride) == 0:
                carry(u // (2 * stride))
            scores, dprobs = ahead
            if u + 1 < len(units):
                ahead = front(units[u + 1])
            probs = jnp.exp2(scores)
            dscores = (probs * dprobs).astype(BF16)
            _, _, _, _, q_own, g_own = heads[h]
            step_v = dot_nn(probs.astype(BF16), g_own)
            step_k = dot_nn(dscores, q_own)
            step_q = dot_nn(key_t[h * HALF : (h + 1) * HALF, begin : begin + chunk], dscores)
            dq[h] = step_q if dq[h] is None else dq[h] + step_q
            if h == 0:
                dv, dk = step_v, step_k
            else:
                g, first = begin // rows, begin % rows
                own = slice(first, first + chunk)
                dk = ((dk + step_k) * (1.0 / LOG2E)).astype(BF16)
                dv = (dv + step_v).astype(BF16)
                if g < kept:
                    dkv_refs[g][0, own, :] = dk
                    dkv_refs[g][1, own, :] = dv
                else:
                    given[pair, 0, own, :] = dk
                    given[pair, 1, own, :] = dv
        dq_ref[...] = (jnp.concatenate(dq, axis=0).T * scale).astype(BF16)
        if swaps:
            columns = pl.ds(pl.multiple_of(pair % per_part * PAIR, PAIR), PAIR)

            def swap(i, place):
                return remote(
                    given.at[i],
                    dkv_refs[1].at[place // per_part, :, :, columns],
                    swap_sems.at[0, i],
                    swap_sems.at[1, i],
                    where_is("near"),
                )

            swap(pair, pair).start()

            @pl.when(pair == pairs - 1)
            def _():
                for i in range(pairs):
                    swap(i, pair).wait()

    query_spec, kv_spec, lse_spec = attention_specs(per_part, rows)
    plain = jax.ShapeDtypeStruct(query.shape, BF16)
    plain_kv = jax.ShapeDtypeStruct((parts, 2, rows, part), BF16)
    hold = pl.BlockSpec(memory_space=pl.ANY)
    swap_scratch = [
        pltpu.VMEM((pairs, 2, rows, PAIR), BF16),
        pltpu.SemaphoreType.DMA((2, pairs)),
    ]
    out = pl.pallas_call(
        kernel,
        grid=(pairs,),
        in_specs=[pl.BlockSpec(memory_space=pltpu.SMEM)]
        + [query_spec(a) for a in (query, mix, mix_grad)]
        + [lse_spec]
        + [kv_spec(piece) for piece in kv_pieces]
        + [hold] * n_carry,
        out_specs=[query_spec(plain)]
        + [kv_spec(plain_kv)] * kept
        + [hold] * (pieces - kept + len(carrier.outs)),
        scratch_shapes=[pltpu.VMEM((keys, PAIR), BF16)] * 4
        + [pltpu.VMEM((PAIR, keys), BF16)]
        + (swap_scratch if swaps else [])
        + carrier.scratch,
        out_shape=[plain] + [plain_kv] * pieces + carrier.outs,
        compiler_params=pltpu.CompilerParams(vmem_limit_bytes=VMEM, **carrier.params),
        cost_estimate=pl.CostEstimate(
            flops=40 * rows * keys * pairs * PAIR,
            bytes_accessed=16 * rows * pairs * PAIR * pieces,
            transcendentals=0,
        ),
        name="attend_back",
    )(
        span,
        query.array,
        mix.array,
        mix_grad.array,
        lse,
        *[piece.array for piece in kv_pieces],
        *carrier.ins,
    )
    return out[0], out[1 : pieces + 1], out[pieces + 1 :]


def spots():
    return lax.axis_index("section"), lax.axis_index("dp"), lax.axis_index("tensor")


def dp_peer(group, level):
    return group + (1 << level) * (1 - 2 * ((group // (1 << level)) % 2))


def where_is(peer):
    section, group, tensor = spots()
    if peer == "near":
        return {"section": 1 - section}
    if peer == "over":
        return {"tensor": 1 - tensor}
    if peer == "cross":
        return {"section": 1 - section, "tensor": 1 - tensor}
    return {"dp": dp_peer(group, peer)}


def remote(source, target, sent, landed, where):
    return pltpu.make_async_remote_copy(
        src_ref=source,
        dst_ref=target,
        send_sem=sent,
        recv_sem=landed,
        device_id=where,
        device_id_type=pl.DeviceIdType.MESH,
    )


def greet(peers):
    barrier = pltpu.get_barrier_semaphore()
    for peer in peers:
        pl.semaphore_signal(
            barrier, inc=1, device_id=where_is(peer), device_id_type=pl.DeviceIdType.MESH
        )
    pl.semaphore_wait(barrier, len(peers))


class Carry:
    def __init__(self, tasks=(), collective=None):
        self.tasks = list(tasks)
        self.ins = [a for task in self.tasks for a in task.ins]
        self.outs = [a for task in self.tasks for a in task.outs]
        self.scratch = [a for task in self.tasks for a in task.scratch]
        self.peers = []
        for task in self.tasks:
            self.peers += [peer for peer in task.peers if peer not in self.peers]
        self.params = (
            dict(collective_id=collective, has_side_effects=True) if self.tasks else {}
        )

    def plan(self, steps, ins, outs, scratch):
        plan = {}
        if self.tasks:
            plan[0] = [lambda: greet(self.peers)]
        events = []
        for task in self.tasks:
            i, o, s = len(task.ins), len(task.outs), len(task.scratch)
            events += task.events(steps, ins[:i], outs[:o], scratch[:s])
            ins, outs, scratch = ins[i:], outs[o:], scratch[s:]
        for step, rank, action in sorted(events, key=lambda event: event[:2]):
            assert 0 <= step < steps
            plan.setdefault(step, []).append(action)
        return plan

    def run(self, place, slot, slots, steps, ins, outs, scratch):
        for step, actions in self.plan(steps, ins, outs, scratch).items():
            if step % slots == slot:

                @pl.when(place == step // slots)
                def _():
                    for action in actions:
                        action()


LAST = 1000


GROUP = ["near", "over", "cross"]


class RowCopies:
    def __init__(self, copies, arrivals, sems, room=None):
        self.copies, self.arrivals, self.room = copies, arrivals, room
        self.sent, self.landed, self.kept = sems

    def copy(self, i):
        source, target, slot, section, tensor, _ = self.copies[i]
        return remote(
            source,
            target,
            self.sent.at[i],
            self.landed.at[slot],
            {"section": section, "tensor": tensor},
        )

    def keep(self, i):
        source, target = self.copies[i][:2]
        return pltpu.make_async_copy(
            source, target if self.room is None else self.room, self.kept
        )

    def keep_on(self):
        for i in range(len(self.copies)):

            @pl.when(self.here(i, True))
            def _():
                self.keep(i).wait()
                pltpu.make_async_copy(self.room, self.copies[i][1], self.kept).start()

    def here(self, i, stays):
        section, _, tensor = spots()
        _, _, _, to_section, to_tensor, condition = self.copies[i]
        own = (to_section == section) & (to_tensor == tensor)
        return condition & (own if stays else jnp.logical_not(own))

    def start(self):
        for i in range(len(self.copies)):

            @pl.when(self.here(i, True))
            def _():
                self.keep(i).start()

            @pl.when(self.here(i, False))
            def _():
                self.copy(i).start()

    def wait_sent(self):
        for i in range(len(self.copies)):

            @pl.when(self.here(i, False))
            def _():
                self.copy(i).wait_send()

    def wait_arrival(self, i):
        section, _, tensor = spots()
        target, slot, from_section, from_tensor, condition = self.arrivals[i]
        own = (from_section == section) & (from_tensor == tensor)
        source = self.copies[0][0]

        @pl.when(condition & own)
        def _():
            stays = source if self.room is None else self.room
            pltpu.make_async_copy(stays, target, self.kept).wait()

        @pl.when(condition & jnp.logical_not(own))
        def _():
            remote(
                source, target, self.sent.at[0], self.landed.at[slot], where_is("near")
            ).wait_recv()


ROW_SEMS = [
    pltpu.SemaphoreType.DMA((2,)),
    pltpu.SemaphoreType.DMA((2,)),
    pltpu.SemaphoreType.DMA,
]


def spread_rows(source, target, sems, sides=(0, 1), room=None):
    section, _, tensor = spots()
    yes = section >= 0
    sends = yes if len(sides) == 2 else section == sides[0]
    copies = [
        (source.at[row], target.at[section], section, tensor, row, sends) for row in range(2)
    ]
    arrivals = [(target.at[side], side, side, section, yes) for side in sides]
    return RowCopies(copies, arrivals, sems, room)


def return_rows(source, target, sems, side, room):
    section, _, tensor = spots()
    copies = [(source, target.at[tensor], tensor, side, section, section >= 0)]
    arrivals = [(target.at[row], row, tensor, row, section == side) for row in range(2)]
    return RowCopies(copies, arrivals, sems, room)


class SpreadRows:
    peers = GROUP

    def __init__(self, array, sides, begin=0):
        self.ins, self.sides, self.begin = [array], sides, begin
        self.outs = [jax.ShapeDtypeStruct(array.shape, array.dtype)]
        self.scratch = ROW_SEMS + [pltpu.VMEM(array.shape[-2:], array.dtype)]

    def make(self, ins, outs, scratch):
        return spread_rows(ins[0], outs[0], scratch[:3], self.sides, scratch[3])

    def events(self, steps, ins, outs, scratch):
        def make():
            return self.make(ins, outs, scratch)

        def finish():
            rows = make()
            for i in range(len(rows.arrivals)):
                rows.wait_arrival(i)
            rows.wait_sent()

        return [
            (self.begin, 1, lambda: make().start()),
            (self.begin + 1, 1, lambda: make().keep_on()),
            (steps - 1, LAST, finish),
        ]


class ReturnRows(SpreadRows):
    def __init__(self, array, side, begin=0):
        self.ins, self.side, self.begin = [array], side, begin
        self.outs = [jax.ShapeDtypeStruct((2, *array.shape), array.dtype)]
        self.scratch = ROW_SEMS + [pltpu.VMEM(array.shape, array.dtype)]

    def make(self, ins, outs, scratch):
        return return_rows(ins[0], outs[0], scratch[:3], self.side, scratch[3])


class WeightCopies:
    @staticmethod
    def sems(count):
        return pltpu.SemaphoreType.DMA((3 + 8 * count,))

    def __init__(self, source, target, sem, room=None, count=1):
        section, group, _ = spots()
        rows = source.shape[0] // (2 * count)
        bit = group % 2
        here, stays = target.at[section, 1], target.at[section, 0]
        self.room = room
        if room is None:
            self.kept = pltpu.make_async_copy(source, stays, sem.at[0])
        else:
            self.first = pltpu.make_async_copy(source, room, sem.at[0])
            self.kept = pltpu.make_async_copy(room, stays, sem.at[0])
        self.near = remote(source, stays, sem.at[1], sem.at[2], where_is("near"))
        self.over, self.side, self.onward, self.last = [], [], [], []
        for i in range(count):
            own = pl.ds(pl.multiple_of((bit * count + i) * rows, 16), rows)
            other = pl.ds(pl.multiple_of(((1 - bit) * count + i) * rows, 16), rows)
            source_own, own, other = source.at[own], here.at[own], here.at[other]
            pairs = [(sem.at[3 + 8 * i + 2 * j], sem.at[4 + 8 * i + 2 * j]) for j in range(4)]
            self.over.append(remote(source_own, own, *pairs[0], where_is("over")))
            self.side.append(remote(own, own, *pairs[1], where_is(0)))
            self.onward.append(remote(own, own, *pairs[2], where_is("near")))
            self.last.append(remote(other, other, *pairs[3], where_is("near")))

    def start(self):
        for copy in self.over:
            copy.start()
        self.near.start()
        if self.room is None:
            self.kept.start()
        else:
            self.first.start()

    def keep_on(self):
        self.first.wait()
        self.kept.start()

    def forward(self, i):
        self.over[i].wait_recv()
        self.side[i].start()
        self.onward[i].start()

    def forward_last(self, i):
        self.side[i].wait_recv()
        self.last[i].start()

    def finish(self):
        self.kept.wait()
        self.near.wait()
        for over, side, onward, last in zip(self.over, self.side, self.onward, self.last):
            over.wait_send()
            side.wait_send()
            onward.wait()
            last.wait()


class SpreadWeight:
    peers = ["near", "over", 0]

    def __init__(self, weight, forwards, lasts):
        self.ins = [weight]
        self.outs = [jax.ShapeDtypeStruct((2, 2, *weight.shape), weight.dtype)]
        self.forwards, self.lasts = forwards, lasts
        self.scratch = [
            WeightCopies.sems(len(forwards)),
            pltpu.VMEM(weight.shape, weight.dtype),
        ]

    def events(self, steps, ins, outs, scratch):
        def copies():
            return WeightCopies(ins[0], outs[0], *scratch, len(self.forwards))

        def forward(i):
            return lambda: copies().forward(i)

        def forward_last(i):
            return lambda: copies().forward_last(i)

        return (
            [(0, 0, lambda: copies().start()), (1, 0, lambda: copies().keep_on())]
            + [(when, 1, forward(i)) for i, when in enumerate(self.forwards)]
            + [(when, 2, forward_last(i)) for i, when in enumerate(self.lasts)]
            + [(steps - 1, LAST, lambda: copies().finish())]
        )


class Reduce:
    def __init__(self, source, chunk, begins, pace, only=None, levels=None):
        self.ins = [source]
        self.chunk, self.begins, self.only = chunk, begins, only
        self.count = source.shape[-2] // chunk
        assert self.count == len(begins)
        self.levels = list(range(lax.axis_size("dp").bit_length() - 1))
        if levels is not None:
            self.levels = levels
        depth = len(self.levels)
        self.peers = []
        self.stages = []
        if only != "slice":
            self.peers += ["near", "over"]
            self.stages += ["enter", "cross", "over"]
        if only != "chip":
            self.peers += ["near", *self.levels]
            self.stages += ["load", "loaded"] if only == "slice" else []
            self.stages += [("halve", i) for i in range(depth)]
            self.stages += [("double", i) for i in reversed(range(depth))]
        assert len(pace) == len(self.stages) - 1
        self.dues = [sum(pace[:i]) for i in range(len(self.stages))]
        width = source.shape[-1]
        whole = jax.ShapeDtypeStruct((self.count * chunk, width), BF16)
        self.outs = [whole] if only == "chip" else [whole] * 2

        def room(*shape):
            return pltpu.VMEM((self.count, *shape, width), BF16)

        self.scratch = [room(2, chunk)]
        if only != "slice":
            self.scratch += [room(2, chunk), room(chunk)]
        if only != "chip":
            halves = [room(chunk >> (i + 1)) for i in range(depth)]
            self.scratch += [room(chunk)] + halves + halves
        self.scratch += [pltpu.SemaphoreType.DMA((2 + 2 * (3 + 2 * depth), self.count))]

    def events(self, steps, ins, outs, scratch):
        chunk, depth = self.chunk, len(self.levels)
        source, refs = ins[0], list(scratch)
        own, sems = refs[0], refs[-1]
        refs = refs[1:-1]
        if self.only != "slice":
            chip, other = refs[:2]
            refs = refs[2:]
        if self.only != "chip":
            full, halves, doubles = refs[0], refs[1 : 1 + depth], refs[1 + depth :]

        def bounds(i):
            _, group, _ = spots()
            begin = 0
            for j in range(i):
                bit = (group // (1 << self.levels[j])) % 2
                begin = begin + bit * (chunk >> (j + 1))
            return begin

        def keeps(i):
            return pl.ds(pl.multiple_of(bounds(i + 1), 16), chunk >> (i + 1))

        def gives(i):
            begin = 2 * bounds(i) + (chunk >> (i + 1)) - bounds(i + 1)
            return pl.ds(pl.multiple_of(begin, 16), chunk >> (i + 1))

        def pair(kind, c):
            return sems.at[2 + 2 * kind, c], sems.at[3 + 2 * kind, c]

        def rows_of(c):
            return pl.ds(c * chunk, chunk)

        def load(c):
            if self.only == "slice":
                return pltpu.make_async_copy(
                    source.at[rows_of(c), :], own.at[c, 0], sems.at[0, c]
                )
            section, _, _ = spots()
            return pltpu.make_async_copy(
                source.at[section, :, rows_of(c), :], own.at[c], sems.at[0, c]
            )

        def cross(c):
            section, _, _ = spots()
            return remote(
                source.at[1 - section, :, rows_of(c), :],
                chip.at[c],
                *pair(0, c),
                where_is("near"),
            )

        def over(c):
            return remote(own.at[c, 1], other.at[c], *pair(1, c), where_is("over"))

        def halve(i, c):
            return remote(
                own.at[c, 0, gives(i), :],
                halves[i].at[c],
                *pair(3 + i, c),
                where_is(self.levels[i]),
            )

        def double(i, c):
            return remote(
                full.at[c, keeps(i), :],
                doubles[i].at[c],
                *pair(3 + depth + i, c),
                where_is(self.levels[i]),
            )

        def store(c):
            kept = own.at[c, 0] if self.only == "chip" else full.at[c]
            return pltpu.make_async_copy(kept, outs[0].at[rows_of(c), :], sems.at[1, c])

        def tell(c):
            return remote(
                full.at[c], outs[1].at[rows_of(c), :], *pair(2, c), where_is("near")
            )

        def act(stage, c):
            if stage == "enter":
                load(c).start()
                cross(c).start()
            elif stage == "load":
                load(c).start()
            elif stage == "loaded":
                load(c).wait()
                halve(0, c).start()
            elif stage == "cross":
                load(c).wait()
                cross(c).wait()
                own[c] = own[c] + chip[c]
                over(c).start()
            elif stage == "over":
                over(c).wait()
                own[c, 0] = own[c, 0] + other[c]
                if self.only == "chip":
                    store(c).start()
                else:
                    halve(0, c).start()
            elif stage[0] == "halve":
                i = stage[1]
                halve(i, c).wait()
                mine = keeps(i)
                total = own[c, 0, mine, :] + halves[i][c]
                if i < depth - 1:
                    own[c, 0, mine, :] = total
                    halve(i + 1, c).start()
                else:
                    full[c, mine, :] = total
                    double(i, c).start()
            else:
                i = stage[1]
                double(i, c).wait()
                full[c, gives(i), :] = doubles[i][c]
                if i:
                    double(i - 1, c).start()
                else:
                    store(c).start()
                    tell(c).start()

        def leave(c):
            store(c).wait()
            if self.only != "chip":
                tell(c).wait()

        events = []
        for c, begin in enumerate(self.begins):
            for i, (stage, due) in enumerate(zip(self.stages, self.dues)):
                events.append((begin + due, -i, functools.partial(act, stage, c)))
            events.append((steps - 1, LAST, functools.partial(leave, c)))
        return events


def carry_alone(tasks, steps, collective):
    carrier = Carry(tasks, collective)

    def kernel(*refs):
        i, o = len(carrier.ins), len(carrier.ins) + len(carrier.outs)
        carrier.run(pl.program_id(0), 0, 1, steps, refs[:i], refs[i:o], refs[o:])

    hold = pl.BlockSpec(memory_space=pl.ANY)
    return pl.pallas_call(
        kernel,
        grid=(steps,),
        in_specs=[hold] * len(carrier.ins),
        out_specs=[hold] * len(carrier.outs),
        out_shape=carrier.outs,
        scratch_shapes=carrier.scratch,
        compiler_params=pltpu.CompilerParams(vmem_limit_bytes=VMEM, **carrier.params),
        name="carry_alone",
    )(*carrier.ins)


def open_up(tokens, qkv, norm, block, collective):
    _, rows, width = tokens.shape
    part = qkv.shape[-1]
    score = LOG2E / math.sqrt(width // HEADS)

    def kernel(tokens_ref, qkv_ref, norm_ref, *refs):
        x_out, w_out, n_out, q_out, own_out, other_out = refs[:6]
        x, low, w, n, q, kv = refs[6:12]
        row_sems, weight_sems, norm_sems, store_sems, kv_sems = (
            refs[12:15],
            refs[15:16],
            refs[16],
            refs[17],
            refs[18],
        )
        section, _, _ = spots()
        greet([*GROUP, 0])
        rows_in = spread_rows(tokens_ref, x, row_sems)
        weight = WeightCopies(qkv_ref, w, weight_sems[0])
        weight.start()
        rows_in.start()
        norm_kept = pltpu.make_async_copy(norm_ref, n.at[section], norm_sems.at[0])
        norm_near = remote(
            norm_ref, n.at[section], norm_sems.at[1], norm_sems.at[2], where_is("near")
        )
        norm_kept.start()
        norm_near.start()
        stores = []

        def save(source, target):
            copy = pltpu.make_async_copy(source, target, store_sems.at[len(stores)])
            copy.start()
            stores.append(copy)

        kv_copies = []

        def project(side, k):
            def step(i, carry):
                own = pl.ds(pl.multiple_of(i * block, block), block)
                rows_low = low[own, :] if side == 0 else x[1, own, :]

                def product(m):
                    return dot_nn(rows_low, w[side, k, m * width : (m + 1) * width, :])

                q[side, k, own, :] = (product(0) * score).astype(BF16)
                kv[side, k, 0, own, :] = product(1).astype(BF16)
                kv[side, k, 1, own, :] = product(2).astype(BF16)
                return carry

            lax.fori_loop(0, rows // block, step, 0)
            spot = 2 * (2 * side + k)
            copy = remote(
                kv.at[side, k],
                other_out.at[side, k],
                kv_sems.at[spot],
                kv_sems.at[spot + 1],
                where_is("near"),
            )
            copy.start()
            kv_copies.append(copy)
            save(kv.at[side, k], own_out.at[side, k])
            save(q.at[side, k], q_out.at[side, k])

        norm_kept.wait()
        norm_near.wait()
        save(n, n_out)
        weight.forward(0)
        weight.forward_last(0)
        weight.finish()
        save(w, w_out)
        rows_in.wait_arrival(0)
        save(x.at[0], x_out.at[0])

        def settle(i, carry):
            own = pl.ds(pl.multiple_of(i * block, block), block)
            unit, _ = standardize(x[0, own, :].astype(F32))
            low[own, :] = affine(unit, n.at[0], 2).astype(BF16)
            return carry

        lax.fori_loop(0, rows // block, settle, 0)
        project(0, 0)
        project(0, 1)
        rows_in.wait_arrival(1)
        save(x.at[1], x_out.at[1])
        project(1, 0)
        project(1, 1)
        rows_in.wait_sent()
        for copy in kv_copies + stores:
            copy.wait()

    hold = pl.BlockSpec(memory_space=pl.ANY)
    shapes = [
        ((2, rows, width), BF16),
        ((2, 2, *qkv.shape), BF16),
        ((2, *norm.shape), F32),
        ((2, 2, rows, part), BF16),
        ((2, 2, 2, rows, part), BF16),
    ]
    return pl.pallas_call(
        kernel,
        in_specs=[hold] * 3,
        out_specs=[hold] * 6,
        out_shape=[jax.ShapeDtypeStruct(*s) for s in shapes + shapes[-1:]],
        scratch_shapes=[pltpu.VMEM(*shapes[0]), pltpu.VMEM((rows, width), BF16)]
        + [pltpu.VMEM(*s) for s in shapes[1:]]
        + ROW_SEMS
        + [WeightCopies.sems(1)]
        + [
            pltpu.SemaphoreType.DMA((3,)),
            pltpu.SemaphoreType.DMA((12,)),
            pltpu.SemaphoreType.DMA((8,)),
        ],
        compiler_params=pltpu.CompilerParams(
            vmem_limit_bytes=VMEM, collective_id=collective, has_side_effects=True
        ),
        name="open_up",
    )(tokens, qkv, norm)


def local_general(tokens, lengths, self_qkv, self_out, cross_proj, ffn_up, ffn_down, norms, cotangent):
    section = lax.axis_index("section")
    tensor = lax.axis_index("tensor")
    tensors = lax.axis_size("tensor")
    _, row_count, rows, width = tokens.shape
    assert row_count == 2 and tensors % row_count == 0
    spread = tensors // row_count
    pieces = 2 * spread
    axes = ("section", "tensor")
    is_first = section == 0
    own_row = tensor // spread
    place = section * spread + tensor % spread

    def device(row, spot):
        return (spot // spread) * tensors + row * spread + spot % spread

    def each():
        return [(s, t) for s in range(2) for t in range(tensors)]

    straight = [(s * tensors + t, device(s, t)) for s, t in each()]
    turned = [(s * tensors + t, device(1 - s, t)) for s, t in each()]

    def bring(shares):
        stays = lax.dynamic_index_in_dim(shares, section, 0, keepdims=False)
        moves = lax.dynamic_index_in_dim(shares, 1 - section, 0, keepdims=False)
        one = lax.ppermute(stays, axes, straight)
        two = lax.ppermute(moves, axes, turned)
        return jnp.where(own_row == 0, one, two), jnp.where(own_row == 0, two, one)

    def take_back(source, target):
        one = jnp.where(own_row == 0, source, target)
        two = jnp.where(own_row == 0, target, source)
        one = lax.ppermute(one, axes, [(b, a) for a, b in straight])
        two = lax.ppermute(two, axes, [(b, a) for a, b in turned])
        return jnp.stack([jnp.where(is_first, one, two), jnp.where(is_first, two, one)])

    def rotate(value, by):
        pairs = [
            (device(r, p), device(r, (p + by) % pieces))
            for r in range(row_count)
            for p in range(pieces)
        ]
        return lax.ppermute(value, axes, pairs)

    def pieces_of(value):
        return [value] + [rotate(value, by) for by in range(1, pieces)]

    def pieces_home(values):
        return [values[0]] + [rotate(values[by], -by) for by in range(1, pieces)]

    def swap_sections(value):
        return lax.ppermute(value, "section", [(0, 1), (1, 0)])

    def both_sides(weight, dim):
        if spread == 1:
            other = lax.ppermute(weight, "tensor", [(t, 1 - t) for t in range(tensors)])
            parts = [weight, other]
        else:
            parts = [lax.all_gather(weight, "tensor", axis=dim, tiled=True)]
        swapped = [swap_sections(part) for part in parts]
        pairs = list(zip(parts, swapped))
        return (
            [jnp.where(is_first, mine, theirs) for mine, theirs in pairs],
            [jnp.where(is_first, theirs, mine) for mine, theirs in pairs],
        )

    def home(source_grad, target_grad, dim):
        keep = jnp.where(is_first, source_grad, target_grad).astype(F32)
        sent = swap_sections(jnp.where(is_first, target_grad, source_grad))
        total = (keep + sent.astype(F32)).astype(BF16)
        if spread == 1:
            other = lax.ppermute(total[1], "tensor", [(t, 1 - t) for t in range(tensors)])
            total = (total[0].astype(F32) + other.astype(F32)).astype(BF16)
        else:
            total = lax.psum_scatter(total[0], "tensor", scatter_dimension=dim, tiled=True)
        return total

    def span_of(query_side, key_side):
        own = lax.dynamic_index_in_dim(lengths, own_row, 1, keepdims=False)
        asks, answers = own[query_side], own[key_side]
        paired = asks[1] > 0
        second = paired & (place * rows >= asks[0])
        begin = jnp.where(second, answers[0], 0)
        end = jnp.where(second | ~paired, answers[0] + answers[1], answers[0])
        offsets = [(place - by) % pieces * rows for by in range(pieces)]
        return jnp.stack([begin, end, *offsets]).astype(jnp.int32)

    block = min(256, rows)
    query_block = min(256, rows)
    chunk = 256

    source, target = bring(tokens[0])
    source_norm, target_norm = (
        jnp.where(is_first, a, b)
        for a, b in (lambda own, other: ((own, other), (other, own)))(
            norms[0], swap_sections(norms[0])
        )
    )
    source_qkv, target_qkv = both_sides(self_qkv[0], 2)
    source_out, target_out = both_sides(self_out[0], 0)
    source_up, target_up = both_sides(ffn_up[0], 1)
    source_down, target_down = both_sides(ffn_down[0], 0)
    source_cross, target_cross = both_sides(cross_proj[0], 2)
    source_cot, target_cot = bring(cotangent[0])
    source_span, target_span, cross_span = span_of(0, 0), span_of(1, 1), span_of(1, 0)

    enc_q, enc_kv = project_qkv(source, source_norm, source_qkv, True, block)
    enc_kv = pieces_of(enc_kv)
    dec_q, dec_kv = project_qkv(target, target_norm, target_qkv, False, block)
    dec_kv = pieces_of(dec_kv)
    enc_mix, enc_lse = attend(enc_q, enc_kv, source_span, query_block)
    encoded, memory, enc_first, enc_third = encoder_forward(
        source, enc_mix, source_norm, source_out, source_up, source_down, source_cross, block
    )
    memory = pieces_of(memory)
    dec_mix, dec_lse = attend(dec_q, dec_kv, target_span, query_block)
    cross_q, dec_first = decoder_middle(
        target, dec_mix, target_norm, target_out, target_cross, block
    )
    cross_mix, cross_lse = attend(cross_q, memory, cross_span, query_block)
    decoded, second_grad, cross_mix_grad, cross_out_grad, dec_up, dec_down, dec_norm = decoder_turn(
        dec_first, cross_mix, target_cot, target_norm, target_cross, target_up, target_down, block
    )
    result = take_back(encoded, decoded)
    cross_q_grad, memory_grads, _ = attend_back(
        cross_q, memory, cross_mix, cross_mix_grad, cross_lse, cross_span, chunk
    )
    memory_grads = pieces_home(memory_grads)
    dec_first_grad, dec_mix_grad, cross_query_grad, dec_out, step = decoder_middle_back(
        dec_first,
        dec_mix,
        cross_q_grad,
        second_grad,
        target_norm,
        target_out,
        target_cross,
        block,
    )
    dec_norm += step
    enc_first_grad, enc_mix_grad, enc_cross, enc_out, enc_up, enc_down, enc_norm = encoder_back(
        enc_first,
        enc_third,
        enc_mix,
        memory_grads,
        source_cot,
        source_norm,
        source_out,
        source_up,
        source_down,
        source_cross,
        block,
    )
    dec_cross = jnp.stack([cross_query_grad, cross_out_grad], axis=1)
    up_grad, down_grad = home(enc_up, dec_up, 1), home(enc_down, dec_down, 0)
    out_grad, cross_grad = home(enc_out, dec_out, 0), home(enc_cross, dec_cross, 2)
    dec_q_grad, dec_kv_grads, _ = attend_back(
        dec_q, dec_kv, dec_mix, dec_mix_grad, dec_lse, target_span, chunk
    )
    dec_kv_grads = pieces_home(dec_kv_grads)
    enc_q_grad, enc_kv_grads, _ = attend_back(
        enc_q, enc_kv, enc_mix, enc_mix_grad, enc_lse, source_span, chunk
    )
    enc_kv_grads = pieces_home(enc_kv_grads)
    target_grad, dec_qkv, _ = input_back(
        target, dec_first_grad, dec_q_grad, dec_kv_grads, target_norm, target_qkv, False, block
    )
    source_grad, enc_qkv, step = input_back(
        source, enc_first_grad, enc_q_grad, enc_kv_grads, source_norm, source_qkv, True, block
    )
    enc_norm += step
    token_grad = take_back(source_grad, target_grad).astype(F32)
    qkv_grad = home(enc_qkv, dec_qkv, 2)
    norm_total = lax.psum(jnp.stack([enc_norm, dec_norm]), ("section", "dp", "tensor"))
    norm_grad = lax.dynamic_index_in_dim(norm_total, section, 0, keepdims=False)
    summed = [
        lax.psum(grad, "dp").astype(F32)
        for grad in (qkv_grad, out_grad, cross_grad, up_grad, down_grad)
    ]
    return (
        result[None],
        token_grad[None],
        summed[0][None],
        summed[1][None],
        summed[2][None],
        summed[3][None],
        summed[4][None],
        norm_grad[None],
    )


def local_fast(tokens, lengths, self_qkv, self_out, cross_proj, ffn_up, ffn_down, norms, cotangent):
    section, tensor = lax.axis_index("section"), lax.axis_index("tensor")
    _, row_count, rows, width = tokens.shape
    assert row_count == 2
    is_first = section == 0
    block = min(256, rows)
    query_block = min(256, rows)
    chunk = 256
    levels = lax.axis_size("dp").bit_length() - 1

    def hops(*steps):
        return list(steps[:levels]) + list(steps[3 : 3 + levels])

    def swap(value):
        return lax.ppermute(value, "section", [(0, 1), (1, 0)])

    def flat(weight):
        return weight.reshape(-1, weight.shape[-1])

    def span_of(query_side, key_side):
        own = lax.dynamic_index_in_dim(lengths, tensor, 1, keepdims=False)
        asks, answers = own[query_side], own[key_side]
        paired = asks[1] > 0
        second = paired & (section * rows >= asks[0])
        begin = jnp.where(second, answers[0], 0)
        end = jnp.where(second | ~paired, answers[0] + answers[1], answers[0])
        return jnp.stack([begin, end, section * rows, (1 - section) * rows]).astype(jnp.int32)

    spans = span_of(0, 0), span_of(1, 1), span_of(1, 0)
    x, qkv, norm, q, kv_own, kv_other = open_up(tokens[0], flat(self_qkv), norms[0], block, 1)
    qkv = qkv.reshape(2, 2, *self_qkv.shape[1:])

    def parts(weight, side):
        return [At(weight, side, k) for k in range(2)]

    enc_x, dec_x, enc_norm_in, dec_norm_in = At(x, 0), At(x, 1), At(norm, 0), At(norm, 1)
    enc_q, dec_q = At(q, 0), At(q, 1)
    enc_kv, dec_kv = [[At(kv_own, side), At(kv_other, side)] for side in range(2)]
    enc_mix, enc_lse, out, up = attend(
        enc_q,
        enc_kv,
        spans[0],
        query_block,
        Carry(
            [
                SpreadWeight(self_out[0], [3], [5]),
                SpreadWeight(ffn_up[0], [4, 5, 6, 7], [6, 7, 7, 7]),
            ],
            2,
        ),
        2,
    )
    dec_mix, dec_lse, down, cross = attend(
        dec_q,
        dec_kv,
        spans[1],
        query_block,
        Carry(
            [
                SpreadWeight(ffn_down[0], [3, 4, 5, 6], [5, 6, 7, 7]),
                SpreadWeight(flat(cross_proj), [7, 7], [7, 7]),
            ],
            3,
        ),
        2,
    )
    cross = cross.reshape(2, 2, *cross_proj.shape[1:])
    encoded, memory, enc_first, enc_third = encoder_forward(
        enc_x,
        enc_mix,
        enc_norm_in,
        parts(out, 0),
        parts(up, 0),
        parts(down, 0),
        parts(cross, 0),
        block,
    )
    memory = [memory, swap(memory)]
    cross_q, dec_first = decoder_middle(
        dec_x, dec_mix, dec_norm_in, parts(out, 1), parts(cross, 1), block
    )
    cross_mix, cross_lse, cot = attend(
        cross_q,
        memory,
        spans[2],
        query_block,
        Carry([SpreadRows(cotangent[0], (0, 1))], 4),
    )
    decoded, second_grad, cross_mix_grad, cross_out_grad, ffn_dec, dec_norm = decoder_turn(
        dec_first,
        cross_mix,
        At(cot, 1),
        dec_norm_in,
        parts(cross, 1),
        parts(up, 1),
        parts(down, 1),
        block,
        True,
    )
    cross_q_grad, memory_grads, (ffn_dec, decoded) = attend_back(
        cross_q,
        memory,
        cross_mix,
        cross_mix_grad,
        cross_lse,
        spans[2],
        chunk,
        Carry(
            [Reduce(ffn_dec, 256, [0, 1, 2, 3], [1, 2], "chip"), ReturnRows(decoded, 1, 4)], 5
        ),
        2,
    )
    dec_first_grad, dec_mix_grad, cross_query_grad, dec_out, step = decoder_middle_back(
        dec_first,
        dec_mix,
        cross_q_grad,
        second_grad,
        dec_norm_in,
        parts(out, 1),
        parts(cross, 1),
        block,
    )
    dec_norm += step
    enc_first_grad, enc_mix_grad, ffn_enc, sides, enc_norm = encoder_back(
        enc_first,
        enc_third,
        enc_mix,
        memory_grads,
        At(cot, 0),
        enc_norm_in,
        parts(out, 0),
        parts(up, 0),
        parts(down, 0),
        parts(cross, 0),
        block,
        [dec_out, cross_query_grad, cross_out_grad],
    )
    dec_q_grad, dec_kv_grads, (ffn_dec, ffn_dec_other, ffn_enc, sides) = attend_back(
        dec_q,
        dec_kv,
        dec_mix,
        dec_mix_grad,
        dec_lse,
        spans[1],
        chunk,
        Carry(
            [
                Reduce(
                    ffn_dec,
                    256,
                    [0, 1, 2, 3],
                    [1, *hops(2, 1, 2, 1, 1, 2)],
                    "slice",
                ),
                Reduce(ffn_enc, 256, [0, 2, 4, 6], [1, 4], "chip"),
                Reduce(sides, 384, [7, 8, 10, 11], [1, 3], "chip"),
            ],
            6,
        ),
        4,
    )
    target_grad, dec_qkv = input_back(
        dec_x,
        dec_first_grad,
        dec_q_grad,
        dec_kv_grads,
        dec_norm_in,
        parts(qkv, 1),
        False,
        block,
        [],
    )
    enc_q_grad, enc_kv_grads, (ffn_enc, ffn_enc_other, sides, _, dec_qkv, dec_qkv_other, target_grad, encoded) = attend_back(
        enc_q,
        enc_kv,
        enc_mix,
        enc_mix_grad,
        enc_lse,
        spans[0],
        chunk,
        Carry(
            [
                Reduce(
                    ffn_enc,
                    256,
                    [0, 1, 2, 3],
                    [1, *hops(2, 1, 2, 1, 1, 2)],
                    "slice",
                ),
                Reduce(
                    sides,
                    384,
                    [0, 1, 2, 3],
                    [1, *hops(2, 1, 2, 1, 1, 2)],
                    "slice",
                    [1, 2, 0] if levels == 3 else None,
                ),
                Reduce(dec_qkv, 384, [0, 1], [1, 3, *hops(2, 1, 2, 1, 1, 2)]),
                ReturnRows(target_grad, 1, 4),
                ReturnRows(encoded, 0, 4),
            ],
            7,
        ),
        4,
    )
    source_grad, enc_qkv = input_back(
        enc_x,
        enc_first_grad,
        enc_q_grad,
        enc_kv_grads,
        enc_norm_in,
        parts(qkv, 0),
        True,
        block,
        [enc_norm, dec_norm],
    )
    last, last_other, source_grad = carry_alone(
        [
            Reduce(enc_qkv, enc_qkv.shape[2] // 2, [0, 1], [1, 1, *hops(1, 1, 1, 1, 1, 1)]),
            ReturnRows(source_grad, 0, 4),
        ],
        4 + 2 * levels,
        8,
    )

    half = 3 * width // 2
    up_grad = jnp.where(is_first, ffn_enc, ffn_dec_other).astype(F32)
    down_grad = jnp.where(is_first, ffn_enc_other, ffn_dec).astype(F32)
    up_grad = jnp.concatenate(jnp.split(up_grad, 2, axis=0), axis=1)

    def columns(halves):
        return jnp.concatenate([halves[:half], halves[half : 2 * half]], axis=1)

    qkv_grad = jnp.concatenate(
        [
            jnp.where(is_first, columns(last), dec_qkv_other),
            jnp.where(is_first, columns(last_other), dec_qkv),
        ],
        axis=0,
    )
    qkv_grad = qkv_grad.astype(F32).reshape(self_qkv.shape)
    sides = sides.astype(F32)
    out_grad = jnp.concatenate([sides[: width // 2], sides[width // 2 : width]], axis=1)
    cross_grad = sides[width:].reshape(cross_proj.shape)
    norm_grad = last[2 * half : 2 * half + 24].astype(F32).reshape(norms.shape)

    def by_side(source, target):
        return jnp.where(is_first, source, target)

    return (
        by_side(encoded, decoded)[None],
        by_side(source_grad, target_grad).astype(F32)[None],
        qkv_grad,
        out_grad[None],
        cross_grad,
        up_grad[None],
        down_grad[None],
        norm_grad,
    )


def solution(mesh):
    placed = (
        P("section", "dp", "tensor", None),
        P(None, "dp", None),
        P("section", None, None, "tensor"),
        P("section", "tensor", None),
        P("section", None, None, "tensor"),
        P("section", None, "tensor"),
        P("section", "tensor", None),
        P("section", None, None, None),
        P("section", "dp", "tensor", None),
    )
    sizes = dict(mesh.shape)
    steps = sizes["dp"].bit_length() - 1
    fast = sizes["tensor"] == 2 and sizes["dp"] == 1 << steps and 0 < steps <= 3
    return jax.shard_map(
        local_fast if fast else local_general,
        mesh=mesh,
        in_specs=placed,
        out_specs=(
            P("section", "dp", "tensor", None),
            P("section", "dp", "tensor", None),
            P("section", None, None, "tensor"),
            P("section", "tensor", None),
            P("section", None, None, "tensor"),
            P("section", None, "tensor"),
            P("section", "tensor", None),
            P("section", None, None, None),
        ),
        check_vma=False,
    )
```

```python
import functools
import math

import jax
import jax.numpy as jnp
from jax import lax
from jax.experimental import pallas as pl
from jax.experimental.pallas import tpu as pltpu
from jax.sharding import PartitionSpec as P

HEADS = 8
EPSILON = 1e-05
MASKED = -1000000000.0
LOG2E = 1.0 / math.log(2.0)
PAIR = 128
HALF = 64
VMEM = 60 * 1024 * 1024
BF16 = jnp.bfloat16
F32 = jnp.float32


def standardize(rows):
    mean = jnp.mean(rows, axis=-1, keepdims=True)
    centered = rows - mean
    inv = lax.rsqrt(jnp.mean(centered * centered, axis=-1, keepdims=True) + EPSILON)
    return centered * inv, inv


def affine(unit, norm_ref, slot):
    return unit * norm_ref[slot, 0:1, :] + norm_ref[slot, 1:2, :]


def norm_back(unit, inv, norm_ref, slot, grad, grad_ref):
    grad_ref[slot, 0:1, :] += jnp.sum(grad * unit, axis=0, keepdims=True)
    grad_ref[slot, 1:2, :] += jnp.sum(grad, axis=0, keepdims=True)
    scaled = grad * norm_ref[slot, 0:1, :]
    first = jnp.mean(scaled, axis=-1, keepdims=True)
    second = jnp.mean(scaled * unit, axis=-1, keepdims=True)
    return inv * (scaled - first - unit * second)


def gelu_tanh(inner):
    return jnp.tanh(0.7978845608028654 * (inner + 0.044715 * inner * inner * inner))


def gelu(inner):
    return 0.5 * inner * (1.0 + gelu_tanh(inner))


def gelu_both(inner):
    bent = gelu_tanh(inner)
    slope = 0.7978845608028654 * (1.0 + 0.134145 * inner * inner)
    half = 0.5 * (1.0 + bent)
    return inner * half, half + 0.5 * inner * (1.0 - bent * bent) * slope


def dot_nn(a, b):
    return jnp.dot(a, b, preferred_element_type=F32)


def dot_nt(a, b):
    return lax.dot_general(a, b, (((1,), (1,)), ((), ())), preferred_element_type=F32)


def dot_tn(a, b):
    return lax.dot_general(a, b, (((0,), (0,)), ((), ())), preferred_element_type=F32)


class At:
    def __init__(self, array, *lead):
        self.array, self.lead = array, lead
        self.shape = array.shape[len(lead) :]
        self.dtype = array.dtype

    def spec(self, sizes, index, **options):
        nones = (None,) * len(self.lead)
        return pl.BlockSpec(nones + tuple(sizes), lambda *g: self.lead + tuple(index(*g)), **options)


def at(array):
    return array if isinstance(array, At) else At(array)


def row_call(
    body, name, rows, row_ins, whole_ins, row_outs, keeps, finals, finish, flops, into=None
):
    block, part = min(512, rows), min(256, rows)
    row_ins = [(at(a), dim) for a, dim in row_ins]
    whole_ins = [at(a) for a in whole_ins]

    def blocked(array, dim):
        sizes = tuple(block if i == dim else size for i, size in enumerate(array.shape))
        return array.spec(sizes, lambda g: tuple(g if i == dim else 0 for i in range(len(sizes))))

    def blocked_out(shape, dim):
        sizes = tuple(block if i == dim else size for i, size in enumerate(shape))
        return pl.BlockSpec(
            sizes, lambda g: tuple(g if i == dim else 0 for i in range(len(shape)))
        )

    def sided_out(shape, dim):
        plain = blocked_out(shape, dim)
        return pl.BlockSpec(
            (None, *plain.block_shape), lambda g: (into[0], *plain.index_map(g))
        )

    def whole(array):
        return array.spec(
            array.shape,
            lambda g: (0,) * len(array.shape),
            pipeline_mode=pl.Buffered(buffer_count=1),
        )

    def whole_out(shape):
        return pl.BlockSpec(
            shape, lambda g: (0,) * len(shape), pipeline_mode=pl.Buffered(buffer_count=1)
        )

    n_rows_in = len(row_ins)
    n_in = n_rows_in + len(whole_ins)
    n_row, n_final = len(row_outs), len(finals)
    out_specs = [blocked_out(shape, dim) for shape, _, dim in row_outs]
    out_shapes = [jax.ShapeDtypeStruct(shape, dtype) for shape, dtype, _ in row_outs]
    held, aliases = [], {}
    if into is not None:
        shape, dtype, dim = row_outs[-1]
        out_specs[-1] = sided_out(shape, dim)
        out_shapes[-1] = jax.ShapeDtypeStruct((2, *shape), dtype)
        if into[1] is not None:
            held, aliases = [into[1]], {n_in: n_row - 1}

    def kernel(*refs):
        ins, refs = refs[:n_in], refs[len(held) :]
        outs = refs[n_in : n_in + n_row]
        last_outs, kept = refs[n_in + n_row : n_in + n_row + n_final], refs[n_in + n_row + n_final :]
        step = pl.program_id(0)
        if finals:

            @pl.when(step == 0)
            def _():
                kept[-1][...] = jnp.zeros_like(kept[-1])

        turns = []
        for begin in range(0, block, part):
            all_rows = pl.ds(pl.multiple_of(step * block + begin, part), part)
            turns.append(body(ins, outs, kept, slice(begin, begin + part), all_rows))
        waiting, running = turns[1:], turns[:1]
        while running:
            running = [turn for turn in running if next(turn, LAST) is not LAST]
            if waiting:
                running.append(waiting.pop(0))

        if finals:

            @pl.when(step == pl.num_programs(0) - 1)
            def _():
                finish(ins[n_rows_in:], kept, last_outs)

    arrays = [array for array, _ in row_ins] + whole_ins
    size = sum(math.prod(a.shape) * a.dtype.itemsize for a in arrays)
    return pl.pallas_call(
        kernel,
        grid=(rows // block,),
        in_specs=[blocked(a, dim) for a, dim in row_ins]
        + [whole(a) for a in whole_ins]
        + [pl.BlockSpec(memory_space=pl.ANY)] * len(held),
        out_specs=out_specs + [whole_out(shape) for shape, _ in finals],
        out_shape=out_shapes + [jax.ShapeDtypeStruct(shape, dtype) for shape, dtype in finals],
        input_output_aliases=aliases,
        scratch_shapes=[pltpu.VMEM(shape, dtype) for shape, dtype in keeps],
        compiler_params=pltpu.CompilerParams(vmem_limit_bytes=VMEM),
        cost_estimate=pl.CostEstimate(flops=flops, bytes_accessed=size, transcendentals=0),
        name=name,
    )(*[a.array for a in arrays], *held)


LAST = 1000


def split(refs, parts, count):
    return [refs[i * parts : (i + 1) * parts] for i in range(count)]


def project_qkv(x, norm, weights, with_norm):
    x = at(x)
    rows, width = x.shape
    parts, part = len(weights), weights[0].shape[-1]
    score = LOG2E / math.sqrt(width // HEADS)

    def body(ins, outs, kept, own, all_rows):
        x_ref, norm_ref, *w = ins
        q_ref, kv_ref = outs
        low = x_ref[own, :]
        if with_norm:
            unit, _ = standardize(low.astype(F32))
            low = affine(unit, norm_ref, 2).astype(BF16)
        yield
        for k in range(parts):
            q_ref[k, own, :] = (dot_nn(low, w[k][0]) * score).astype(BF16)
            kv_ref[k, 0, own, :] = dot_nn(low, w[k][1]).astype(BF16)
            kv_ref[k, 1, own, :] = dot_nn(low, w[k][2]).astype(BF16)
            yield

    return row_call(
        body,
        "project_qkv",
        rows,
        [(x, 0)],
        [norm, *weights],
        [((parts, rows, part), BF16, 1), ((parts, 2, rows, part), BF16, 2)],
        [],
        [],
        None,
        6 * rows * width * width,
    )


def encoder_forward(x, mix, norm, out, up, down, cross):
    x = at(x)
    rows, width = x.shape
    parts, part = len(out), out[0].shape[0]

    def body(ins, outs, kept, own, all_rows):
        x_ref, mix_ref, norm_ref = ins[:3]
        wo, wu, wd, wc = split(ins[3:], parts, 4)
        result_ref, kv_ref, first_ref, third_ref = outs
        unit, _ = standardize(x_ref[own, :].astype(F32))
        first = affine(unit, norm_ref, 2)
        for k in range(parts):
            first += dot_nn(mix_ref[k, own, :], wo[k][...])
        yield
        first_ref[own, :] = first
        unit, _ = standardize(first)
        third = affine(unit, norm_ref, 0)
        low = third.astype(BF16)
        inner = dot_nn(low, wu[0][...])
        yield
        for k in range(parts):
            act = gelu(inner).astype(BF16)
            if k + 1 < parts:
                inner = dot_nn(low, wu[k + 1][...])
            third += dot_nn(act, wd[k][...])
            yield
        third_ref[own, :] = third
        unit, _ = standardize(third)
        low = affine(unit, norm_ref, 1).astype(BF16)
        result_ref[own, :] = low
        yield
        for k in range(parts):
            kv_ref[k, 0, own, :] = dot_nn(low, wc[k][0]).astype(BF16)
            kv_ref[k, 1, own, :] = dot_nn(low, wc[k][1]).astype(BF16)

    units = sum(w.shape[1] for w in up)
    return row_call(
        body,
        "encoder_forward",
        rows,
        [(x, 0), (mix, 1)],
        [norm, *out, *up, *down, *cross],
        [
            ((rows, width), BF16, 0),
            ((parts, 2, rows, part), BF16, 2),
            ((rows, width), F32, 0),
            ((rows, width), F32, 0),
        ],
        [],
        [],
        None,
        6 * rows * width * width + 4 * rows * width * units,
    )


def decoder_middle(x, mix, norm, out, cross):
    x = at(x)
    rows, width = x.shape
    parts, part = len(out), out[0].shape[0]
    score = LOG2E / math.sqrt(width // HEADS)

    def body(ins, outs, kept, own, all_rows):
        x_ref, mix_ref, norm_ref = ins[:3]
        wo, wc = split(ins[3:], parts, 2)
        q_ref, first_ref = outs
        first = x_ref[own, :].astype(F32)
        for k in range(parts):
            first += dot_nn(mix_ref[k, own, :], wo[k][...])
        yield
        first_ref[own, :] = first
        unit, _ = standardize(first)
        low = affine(unit, norm_ref, 0).astype(BF16)
        yield
        for k in range(parts):
            q_ref[k, own, :] = (dot_nn(low, wc[k][0]) * score).astype(BF16)

    return row_call(
        body,
        "decoder_middle",
        rows,
        [(x, 0), (mix, 1)],
        [norm, *out, *cross],
        [((parts, rows, part), BF16, 1), ((rows, width), F32, 0)],
        [],
        [],
        None,
        4 * rows * width * width,
    )


def ffn_finals(low, act, inner, grad, parts, units, paired, up_out, down_out):
    for k in range(parts):
        if paired:
            half = units // 2
            for h in range(2):
                begin = k * units + h * half
                up_out[0, k, h * half : (h + 1) * half, :] = dot_tn(
                    low[...], inner[:, begin : begin + half]
                ).astype(BF16)
            into = up_out.at[1, k]
        else:
            up_out[k] = dot_tn(low[...], inner[:, k * units : (k + 1) * units]).astype(BF16)
            into = down_out.at[k]
        into[...] = dot_tn(act[:, k * units : (k + 1) * units], grad[...]).astype(BF16)


def decoder_turn(first, mix, cotangent, norm, cross, up, down, paired=False):
    rows, width = first.shape
    parts, part, units = len(cross), cross[0].shape[-1], up[0].shape[1]

    def body(ins, outs, kept, own, all_rows):
        first_ref, cot_ref, mix_ref, norm_ref = ins[:4]
        wc, wu, wd = split(ins[4:], parts, 3)
        result_ref, second_grad_ref, mix_grad_ref = outs
        low_keep, act_keep, inner_keep, third_keep, second_keep, norm_total = kept
        unit, _ = standardize(first_ref[own, :])
        second = affine(unit, norm_ref, 0)
        for k in range(parts):
            second += dot_nt(mix_ref[k, all_rows, :], wc[k][1])
        yield
        unit_two, inv_two = standardize(second)
        third = affine(unit_two, norm_ref, 2)
        low = third.astype(BF16)
        low_keep[all_rows, :] = low
        inner = dot_nn(low, wu[0][...])
        yield
        slopes = []
        for k in range(parts):
            act, slope = gelu_both(inner)
            act = act.astype(BF16)
            slopes.append(slope)
            if k + 1 < parts:
                inner = dot_nn(low, wu[k + 1][...])
            act_keep[all_rows, k * units : (k + 1) * units] = act
            third += dot_nn(act, wd[k][...])
            yield
        unit_three, inv_three = standardize(third)
        result_ref[own, :] = affine(unit_three, norm_ref, 1).astype(BF16)
        grad = norm_back(
            unit_three, inv_three, norm_ref, 1, cot_ref[own, :].astype(F32), norm_total
        )
        grad_low = grad.astype(BF16)
        third_keep[all_rows, :] = grad_low
        grad_act = dot_nt(grad_low, wd[0][...])
        yield
        for k in range(parts):
            grad_inner = (grad_act * slopes[k]).astype(BF16)
            if k + 1 < parts:
                grad_act = dot_nt(grad_low, wd[k + 1][...])
            inner_keep[all_rows, k * units : (k + 1) * units] = grad_inner
            grad += dot_nt(grad_inner, wu[k][...])
            yield
        grad = norm_back(unit_two, inv_two, norm_ref, 2, grad, norm_total)
        second_grad_ref[own, :] = grad
        grad_low = grad.astype(BF16)
        second_keep[all_rows, :] = grad_low
        yield
        for k in range(parts):
            mix_grad_ref[k, own, :] = dot_nn(grad_low, wc[k][1]).astype(BF16)

    def finish(ins, kept, outs):
        mix_ref = ins[0]
        low_keep, act_keep, inner_keep, third_keep, second_keep, norm_total = kept
        for k in range(parts):
            outs[0][k] = dot_tn(second_keep[...], mix_ref[k]).astype(BF16)
        ffn_finals(
            low_keep, act_keep, inner_keep, third_keep, parts, units, paired, outs[1], outs[2]
        )
        outs[-1][...] = norm_total[...]

    ffn = (
        [((2, parts, units, width), BF16)]
        if paired
        else [((parts, width, units), BF16), ((parts, units, width), BF16)]
    )
    whole = (rows, width)
    return row_call(
        body,
        "decoder_turn",
        rows,
        [(first, 0), (cotangent, 0)],
        [mix, norm, *cross, *up, *down],
        [(whole, BF16, 0), (whole, F32, 0), ((parts, rows, part), BF16, 1)],
        [
            (whole, BF16),
            ((rows, parts * units), BF16),
            ((rows, parts * units), BF16),
            (whole, BF16),
            (whole, BF16),
            ((3, 2, width), F32),
        ],
        [((parts, width, part), BF16), *ffn, ((3, 2, width), F32)],
        finish,
        6 * rows * width * width + 12 * rows * width * units * parts,
    )


def decoder_middle_back(first, mix, query_grad, second_grad, norm, out, cross, into=None):
    rows, width = first.shape
    parts, part = len(out), out[0].shape[0]

    def body(ins, outs, kept, own, all_rows):
        first_ref, second_grad_ref, mix_ref, query_grad_ref, norm_ref = ins[:5]
        wo, wc = split(ins[5:], parts, 2)
        first_grad_ref, mix_grad_ref = outs
        low_keep, grad_keep, norm_total = kept
        unit, inv = standardize(first_ref[own, :])
        low_keep[all_rows, :] = affine(unit, norm_ref, 0).astype(BF16)
        grad = second_grad_ref[own, :]
        for k in range(parts):
            grad += dot_nt(query_grad_ref[k, all_rows, :], wc[k][0])
        yield
        grad = norm_back(unit, inv, norm_ref, 0, grad, norm_total)
        first_grad_ref[own, :] = grad
        grad_low = grad.astype(BF16)
        grad_keep[all_rows, :] = grad_low
        yield
        for k in range(parts):
            mix_grad_ref[k, own, :] = dot_nt(grad_low, wo[k][...]).astype(BF16)

    def finish(ins, kept, outs):
        mix_ref, query_grad_ref = ins[:2]
        low_keep, grad_keep, norm_total = kept
        for k in range(parts):
            outs[0][k] = dot_tn(low_keep[...], query_grad_ref[k]).astype(BF16)
            outs[1][k] = dot_tn(mix_ref[k], grad_keep[...]).astype(BF16)
        outs[2][...] = norm_total[...]

    whole = (rows, width)
    return row_call(
        body,
        "decoder_middle_back",
        rows,
        [(first, 0), (second_grad, 0)],
        [mix, query_grad, norm, *out, *cross],
        [(whole, F32, 0), ((parts, rows, part), BF16, 1)],
        [(whole, BF16), (whole, BF16), ((3, 2, width), F32)],
        [
            ((parts, width, part), BF16),
            ((parts, part, width), BF16),
            ((3, 2, width), F32),
        ],
        finish,
        8 * rows * width * width,
        into,
    )


def added(refs, *index):
    total = refs[0][index]
    for ref in refs[1:]:
        total = total.astype(F32) + ref[index].astype(F32)
    return total.astype(BF16)


def encoder_back(
    first, third, mix, memory_grads, cotangent, norm, out, up, down, cross, paired=None, into=None
):
    rows, width = first.shape
    parts, part, units = len(out), out[0].shape[0], up[0].shape[1]
    pieces = len(memory_grads)

    def body(ins, outs, kept, own, all_rows):
        first_ref, third_ref, cot_ref = ins[:3]
        memory_refs, mix_ref, norm_ref = ins[3 : 3 + pieces], ins[3 + pieces], ins[4 + pieces]
        wo, wu, wd, wc = split(ins[5 + pieces :], parts, 4)
        first_grad_ref, mix_grad_ref = outs
        low_keep, memory_keep, mid_keep, act_keep, inner_keep, third_keep, first_keep, norm_total = (
            kept
        )
        grad = cot_ref[own, :].astype(F32)
        for k in range(parts):
            for i in range(2):
                memory = added(memory_refs, k, i, own)
                memory_keep[k, i, all_rows, :] = memory
                grad += dot_nt(memory, wc[k][i])
        yield
        unit, inv = standardize(third_ref[own, :])
        low_keep[all_rows, :] = affine(unit, norm_ref, 1).astype(BF16)
        unit_one, inv_one = standardize(first_ref[own, :])
        low = affine(unit_one, norm_ref, 0).astype(BF16)
        mid_keep[all_rows, :] = low
        inner = dot_nn(low, wu[0][...])
        grad = norm_back(unit, inv, norm_ref, 1, grad, norm_total)
        grad_low = grad.astype(BF16)
        third_keep[all_rows, :] = grad_low
        grad_act = dot_nt(grad_low, wd[0][...])
        yield
        for k in range(parts):
            act, slope = gelu_both(inner)
            if k + 1 < parts:
                inner = dot_nn(low, wu[k + 1][...])
            act_keep[all_rows, k * units : (k + 1) * units] = act.astype(BF16)
            grad_inner = (grad_act * slope).astype(BF16)
            if k + 1 < parts:
                grad_act = dot_nt(grad_low, wd[k + 1][...])
            inner_keep[all_rows, k * units : (k + 1) * units] = grad_inner
            grad += dot_nt(grad_inner, wu[k][...])
            yield
        grad = norm_back(unit_one, inv_one, norm_ref, 0, grad, norm_total)
        first_grad_ref[own, :] = grad
        grad_low = grad.astype(BF16)
        first_keep[all_rows, :] = grad_low
        yield
        for k in range(parts):
            mix_grad_ref[k, own, :] = dot_nt(grad_low, wo[k][...]).astype(BF16)

    def finish(ins, kept, outs):
        mix_ref = ins[0]
        low_keep, memory_keep, mid_keep, act_keep, inner_keep, third_keep, first_keep, norm_total = (
            kept
        )
        if paired:
            ffn_finals(
                mid_keep, act_keep, inner_keep, third_keep, parts, units, True, outs[0], None
            )
            dec_out, dec_query, dec_cross = ins[-3:]
            sides = outs[1]
            for k in range(parts):
                column_blocks(dot_tn(mix_ref[k], first_keep[...]), sides, 0, k, 0)
                column_blocks(dec_out[k], sides, 1, k, 0)
                for i in range(2):
                    here = slice((1 + i) * width, (2 + i) * width)
                    sides[0, k, here, :] = dot_tn(low_keep[...], memory_keep[k, i]).astype(BF16)
                    sides[1, k, here, :] = (dec_query, dec_cross)[i][k]
        else:
            for k in range(parts):
                for i in range(2):
                    outs[0][k, i] = dot_tn(low_keep[...], memory_keep[k, i]).astype(BF16)
                outs[1][k] = dot_tn(mix_ref[k], first_keep[...]).astype(BF16)
            ffn_finals(
                mid_keep, act_keep, inner_keep, third_keep, parts, units, False, outs[2], outs[3]
            )
        outs[-1][...] = norm_total[...]

    if paired:
        finals = [((2, parts, units, width), BF16), ((2, parts, 3 * width, part), BF16)]
    else:
        finals = [
            ((parts, 2, width, part), BF16),
            ((parts, part, width), BF16),
            ((parts, width, units), BF16),
            ((parts, units, width), BF16),
        ]
    whole = (rows, width)
    return row_call(
        body,
        "encoder_back",
        rows,
        [(first, 0), (third, 0), (cotangent, 0)] + [(m, 2) for m in memory_grads],
        [mix, norm, *out, *up, *down, *cross, *(paired or [])],
        [(whole, F32, 0), ((parts, rows, part), BF16, 1)],
        [
            (whole, BF16),
            ((parts, 2, rows, part), BF16),
            (whole, BF16),
            ((rows, parts * units), BF16),
            ((rows, parts * units), BF16),
            (whole, BF16),
            (whole, BF16),
            ((3, 2, width), F32),
        ],
        [*finals, ((3, 2, width), F32)],
        finish,
        12 * rows * width * width + 10 * rows * width * units * parts,
        into,
    )


def column_blocks(wide, into, core, k, row):
    rows, columns = wide.shape[0], wide.shape[1] // 2
    for half in range(2):
        into[core, k, row + half * rows : row + (half + 1) * rows, :] = wide[
            :, half * columns : (half + 1) * columns
        ].astype(BF16)


def input_back(x, first_grad, query_grad, key_grads, norm, weights, with_norm, paired=None):
    x = at(x)
    rows, width = x.shape
    parts, part = len(weights), weights[0].shape[-1]
    pieces = len(key_grads)
    key_grads = [at(g) for g in key_grads]

    def body(ins, outs, kept, own, all_rows):
        x_ref, first_grad_ref = ins[:2]
        key_refs, query_grad_ref, norm_ref = ins[2 : 2 + pieces], ins[2 + pieces], ins[3 + pieces]
        w = ins[4 + pieces :][:parts]
        (grad_ref,) = outs
        low_keep, key_keep, norm_total = kept
        grad = first_grad_ref[own, :]
        for k in range(parts):
            grad += dot_nt(query_grad_ref[k, all_rows, :], w[k][0])
            for i in range(2):
                member = added(key_refs, k, i, own)
                key_keep[k, i, all_rows, :] = member
                grad += dot_nt(member, w[k][1 + i])
        yield
        low = x_ref[own, :]
        if with_norm:
            unit, inv = standardize(low.astype(F32))
            low = affine(unit, norm_ref, 2).astype(BF16)
            grad = norm_back(unit, inv, norm_ref, 2, grad, norm_total)
        low_keep[all_rows, :] = low
        grad_ref[own, :] = grad.astype(BF16)

    half = 3 * width // 2

    def finish(ins, kept, outs):
        query_grad_ref = ins[0]
        low_keep, key_keep, norm_total = kept

        def product(k, i):
            member = query_grad_ref[k] if i == 0 else key_keep[k, i - 1]
            return dot_tn(low_keep[...], member)

        if paired is None:
            for k in range(parts):
                for i in range(3):
                    outs[0][k, i] = product(k, i).astype(BF16)
            outs[1][...] = norm_total[...]
            return
        for k in range(parts):
            both = jnp.concatenate([product(k, i) for i in range(3)], axis=0)
            for core in range(2):
                own = both[core * half : (core + 1) * half]
                column_blocks(own, outs[0], core, k, 0)
        if paired:
            tables = ins[-len(paired) :]
            sides = [tables[0][...] + norm_total[...], sum(t[...] for t in tables[1:])]
            for core, table in enumerate(sides):
                lines = [
                    table[slot, i : i + 1, h * PAIR : (h + 1) * PAIR]
                    for slot in range(3)
                    for i in range(2)
                    for h in range(width // PAIR)
                ]
                lines.append(jnp.zeros((2 * PAIR - len(lines), PAIR), F32))
                lines = jnp.concatenate(lines, axis=0).astype(BF16)
                for k in range(parts):
                    outs[0][core, k, 2 * half :, :] = lines

    if paired is None:
        finals = [((parts, 3, width, part), BF16), ((3, 2, width), F32)]
    else:
        finals = [((2, parts, 2 * half + (2 * PAIR if paired else 0), PAIR), BF16)]
    whole = (rows, width)
    return row_call(
        body,
        "input_back",
        rows,
        [(x, 0), (first_grad, 0)] + [(g, 2) for g in key_grads],
        [query_grad, norm, *weights, *(paired or [])],
        [(whole, BF16, 0)],
        [(whole, BF16), ((parts, 2, rows, part), BF16), ((3, 2, width), F32)],
        finals,
        finish,
        12 * rows * width * width,
    )


def widen_keys(span, kv_refs, key_e, key_o, value_e, value_o, rows):
    lane = lax.broadcasted_iota(jnp.int32, (rows, PAIR), 1)
    place = lax.broadcasted_iota(jnp.int32, (rows, PAIR), 0)
    low = lane < HALF
    for g, kv_ref in enumerate(kv_refs):
        spot = place + span[2 + g]
        live = (spot >= span[0]) & (spot < span[1])
        bias = jnp.where(live, 0.0, MASKED)
        keys, values = kv_ref[0].astype(F32), kv_ref[1].astype(F32)
        own = pl.ds(g * rows, rows)
        key_e[own, :] = jnp.where(low, keys, jnp.where(lane == HALF, bias, 1.0)).astype(BF16)
        key_o[own, :] = jnp.where(low, jnp.where(lane == 0, bias, 1.0), keys).astype(BF16)
        value_e[own, :] = jnp.where(low, values, 1.0).astype(BF16)
        value_o[own, :] = jnp.where(low, 1.0, values).astype(BF16)


class Pairs:
    def __init__(self, query):
        self.sides = query.shape[:-3]
        self.parts, self.rows, self.part = query.shape[-3:]
        self.per_part = self.part // PAIR
        self.per_side = self.parts * self.per_part
        self.count = self.per_side * math.prod(self.sides)

    def side(self, i):
        return (i // self.per_side,) if self.sides else ()

    def place(self, i):
        i = i % self.per_side
        return i // self.per_part, i % self.per_part

    def query_spec(self, array):
        def index(i):
            part, column = self.place(i)
            return *self.side(i), part, 0, column

        none = (None,) * len(self.sides)
        return at(array).spec((*none, None, self.rows, PAIR), index)

    def kv_spec(self, array):
        def index(i):
            part, column = self.place(i)
            return *self.side(i), part, 0, 0, column

        none = (None,) * len(self.sides)
        return at(array).spec((*none, None, 2, self.rows, PAIR), index)

    def lse_spec(self):
        none = (None,) * len(self.sides)
        return pl.BlockSpec(
            (*none, self.rows, PAIR), lambda i: (*self.side(i), 0, i % self.per_side)
        )

    def span(self, span_ref, i):
        side = i // self.per_side if self.sides else 0
        return [span_ref[side, j] for j in range(span_ref.shape[1])]


def attend(query, kv_pieces, span, block, carrier=None, slots=1):
    query, kv_pieces = at(query), [at(piece) for piece in kv_pieces]
    carrier = carrier or Carry()
    heads_of = Pairs(query)
    rows, pairs = heads_of.rows, heads_of.count
    pieces = len(kv_pieces)
    keys = rows * pieces
    n_carry = len(carrier.ins)
    blocks = rows // block
    stride = blocks // slots

    def kernel(span_ref, q_ref, *refs):
        kv_refs, refs = refs[:pieces], refs[pieces:]
        carry_ins, refs = refs[:n_carry], refs[n_carry:]
        out_ref, lse_ref, refs = refs[0], refs[1], refs[2:]
        carry_outs, refs = refs[: len(carrier.outs)], refs[len(carrier.outs) :]
        key_e, key_o, value_e, value_o = refs[:4]

        def carry(slot):
            place = pl.program_id(0)
            carrier.run(place, slot, slots, pairs * slots, carry_ins, carry_outs, refs[4:])

        carry(0)
        span = heads_of.span(span_ref, pl.program_id(0))
        widen_keys(span, kv_refs, key_e, key_o, value_e, value_o, rows)
        lane = lax.broadcasted_iota(jnp.int32, (block, PAIR), 1)
        low = lane < HALF
        units = []
        for i in range(blocks):
            query = q_ref[i * block : (i + 1) * block, :].astype(F32)
            first = jnp.where(low, query, jnp.where(lane == HALF, 1.0, 0.0)).astype(BF16)
            second = jnp.where(low, jnp.where(lane == 0, 1.0, 0.0), query).astype(BF16)
            units += [(first, key_e, value_e), (second, key_o, value_o)]

        def scores_of(unit):
            return dot_nt(unit[0], unit[1][...])

        ahead = scores_of(units[0])
        tops, sums = [], []
        for u, unit in enumerate(units):
            if u and u % (2 * stride) == 0:
                carry(u // (2 * stride))
            scores = ahead
            if u + 1 < len(units):
                ahead = scores_of(units[u + 1])
            top = jnp.max(scores, axis=1, keepdims=True)
            tops.append(top)
            sums.append(dot_nn(jnp.exp2(scores - top).astype(BF16), unit[2][...]))
            if u % 2:
                own = slice(u // 2 * block, (u // 2 + 1) * block)
                top = jnp.where(low, tops[u], tops[u - 1])
                weight = jnp.where(low, sums[u], sums[u - 1])
                lse_ref[own, :] = top + LOG2E * jnp.log(weight)
                mixed = jnp.where(low, sums[u - 1], sums[u])
                out_ref[own, :] = (mixed / pltpu.roll(weight, HALF, 1)).astype(BF16)

    query_spec, kv_spec = heads_of.query_spec, heads_of.kv_spec
    lse_spec = heads_of.lse_spec()
    plain = jax.ShapeDtypeStruct(query.shape, BF16)
    hold = pl.BlockSpec(memory_space=pl.ANY)
    return pl.pallas_call(
        kernel,
        grid=(pairs,),
        in_specs=[pl.BlockSpec(memory_space=pltpu.SMEM), query_spec(query)]
        + [kv_spec(piece) for piece in kv_pieces]
        + [hold] * n_carry,
        out_specs=[query_spec(plain), lse_spec] + [hold] * len(carrier.outs),
        scratch_shapes=[pltpu.VMEM((keys, PAIR), BF16)] * 4 + carrier.scratch,
        out_shape=[plain, jax.ShapeDtypeStruct((*heads_of.sides, rows, heads_of.per_side * PAIR), F32)] + carrier.outs,
        compiler_params=pltpu.CompilerParams(vmem_limit_bytes=VMEM, **carrier.params),
        cost_estimate=pl.CostEstimate(
            flops=16 * rows * keys * pairs * PAIR,
            bytes_accessed=8 * rows * pairs * PAIR * pieces,
            transcendentals=0,
        ),
        name="attend",
    )(span, query.array, *[piece.array for piece in kv_pieces], *carrier.ins)


def attend_back(
    query, kv_pieces, mix, mix_grad, lse, span, chunk, carrier=None, slots=1
):
    query, kv_pieces = at(query), [at(piece) for piece in kv_pieces]
    mix, mix_grad = at(mix), at(mix_grad)
    heads_of = Pairs(query)
    rows, pairs = heads_of.rows, heads_of.count
    pieces = len(kv_pieces)
    keys = rows * pieces
    scale = 1.0 / math.sqrt(HALF)
    swaps = carrier is not None
    carrier = carrier or Carry()
    n_carry = len(carrier.ins)
    kept = 1 if swaps else pieces
    chunks = keys // chunk
    stride = chunks // slots

    def kernel(span_ref, q_ref, mix_ref, grad_ref, lse_ref, *refs):
        kv_refs, refs = refs[:pieces], refs[pieces:]
        carry_ins, refs = refs[:n_carry], refs[n_carry:]
        dq_ref, dkv_refs, refs = refs[0], refs[1 : pieces + 1], refs[pieces + 1 :]
        carry_outs, refs = refs[: len(carrier.outs)], refs[len(carrier.outs) :]
        key_e, key_o, value_e, value_o, key_t = refs[:5]
        refs = refs[5:]
        if swaps:
            given, swap_sems, refs = refs[0], refs[1], refs[2:]
        pair = pl.program_id(0)

        def carry(slot):
            carrier.run(pair, slot, slots, pairs * slots, carry_ins, carry_outs, refs)

        carry(0)
        span = heads_of.span(span_ref, pl.program_id(0))
        widen_keys(span, kv_refs, key_e, key_o, value_e, value_o, rows)
        for g, kv_ref in enumerate(kv_refs):
            key_t[:, g * rows : (g + 1) * rows] = kv_ref[0].T
        lane = lax.broadcasted_iota(jnp.int32, (rows, PAIR), 1)
        low = lane < HALF
        query, grad = q_ref[...].astype(F32), grad_ref[...].astype(F32)
        product = mix_ref[...].astype(F32) * grad
        inner = jnp.where(
            low,
            jnp.sum(jnp.where(low, 0.0, product), axis=1, keepdims=True),
            jnp.sum(jnp.where(low, product, 0.0), axis=1, keepdims=True),
        )
        spot = jnp.where(low, lane, lane - HALF)

        def three(value, shift):
            high = value.astype(BF16).astype(F32)
            rest = value - high
            mid = rest.astype(BF16).astype(F32)
            return jnp.where(
                spot == shift,
                high,
                jnp.where(
                    spot == shift + 1, mid, jnp.where(spot == shift + 2, rest - mid, 0.0)
                ),
            )

        lse = three(-lse_ref[...], 1) + jnp.where(spot == 0, 1.0, 0.0)
        inner = three(-inner, 0)
        heads = [
            (
                key,
                value,
                jnp.where(own, query, lse).astype(BF16),
                jnp.where(own, grad, inner).astype(BF16),
                jnp.where(own, query, 0.0).astype(BF16),
                jnp.where(own, grad, 0.0).astype(BF16),
            )
            for own, key, value in ((low, key_e, value_e), (~low, key_o, value_o))
        ]
        units = [(c * chunk, h) for c in range(chunks) for h in range(2)]

        def front(unit):
            begin, h = unit
            own = slice(begin, begin + chunk)
            key, value, q_wide, g_wide, _, _ = heads[h]
            return dot_nt(key[own, :], q_wide), dot_nt(value[own, :], g_wide)

        ahead = front(units[0])
        dq = [None, None]
        for u, (begin, h) in enumerate(units):
            if u and u % (2 * stride) == 0:
                carry(u // (2 * stride))
            scores, dprobs = ahead
            if u + 1 < len(units):
                ahead = front(units[u + 1])
            probs = jnp.exp2(scores)
            dscores = (probs * dprobs).astype(BF16)
            _, _, _, _, q_own, g_own = heads[h]
            step_v = dot_nn(probs.astype(BF16), g_own)
            step_k = dot_nn(dscores, q_own)
            step_q = dot_nn(key_t[h * HALF : (h + 1) * HALF, begin : begin + chunk], dscores)
            dq[h] = step_q if dq[h] is None else dq[h] + step_q
            if h == 0:
                dv, dk = step_v, step_k
            else:
                g, first = begin // rows, begin % rows
                own = slice(first, first + chunk)
                dk = ((dk + step_k) * (1.0 / LOG2E)).astype(BF16)
                dv = (dv + step_v).astype(BF16)
                if g < kept:
                    dkv_refs[g][0, own, :] = dk
                    dkv_refs[g][1, own, :] = dv
                else:
                    given[pair, 0, own, :] = dk
                    given[pair, 1, own, :] = dv
        dq_ref[...] = (jnp.concatenate(dq, axis=0).T * scale).astype(BF16)
        if swaps:
            part, column = heads_of.place(pair)
            columns = pl.ds(pl.multiple_of(column * PAIR, PAIR), PAIR)
            spot = (*heads_of.side(pair), part, slice(None), slice(None), columns)

            def swap(i):
                return remote(
                    given.at[i],
                    dkv_refs[1].at[spot],
                    swap_sems.at[0, i],
                    swap_sems.at[1, i],
                    where_is("near"),
                )

            swap(pair).start()

            @pl.when(pair == pairs - 1)
            def _():
                for i in range(pairs):
                    swap(i).wait()

    query_spec, kv_spec = heads_of.query_spec, heads_of.kv_spec
    lse_spec = heads_of.lse_spec()
    plain = jax.ShapeDtypeStruct(query.shape, BF16)
    plain_kv = jax.ShapeDtypeStruct(
        (*heads_of.sides, heads_of.parts, 2, rows, heads_of.part), BF16
    )
    hold = pl.BlockSpec(memory_space=pl.ANY)
    swap_scratch = [
        pltpu.VMEM((pairs, 2, rows, PAIR), BF16),
        pltpu.SemaphoreType.DMA((2, pairs)),
    ]
    out = pl.pallas_call(
        kernel,
        grid=(pairs,),
        in_specs=[pl.BlockSpec(memory_space=pltpu.SMEM)]
        + [query_spec(a) for a in (query, mix, mix_grad)]
        + [lse_spec]
        + [kv_spec(piece) for piece in kv_pieces]
        + [hold] * n_carry,
        out_specs=[query_spec(plain)]
        + [kv_spec(plain_kv)] * kept
        + [hold] * (pieces - kept + len(carrier.outs)),
        scratch_shapes=[pltpu.VMEM((keys, PAIR), BF16)] * 4
        + [pltpu.VMEM((PAIR, keys), BF16)]
        + (swap_scratch if swaps else [])
        + carrier.scratch,
        out_shape=[plain] + [plain_kv] * pieces + carrier.outs,
        compiler_params=pltpu.CompilerParams(vmem_limit_bytes=VMEM, **carrier.params),
        cost_estimate=pl.CostEstimate(
            flops=40 * rows * keys * pairs * PAIR,
            bytes_accessed=16 * rows * pairs * PAIR * pieces,
            transcendentals=0,
        ),
        name="attend_back",
    )(
        span,
        query.array,
        mix.array,
        mix_grad.array,
        lse,
        *[piece.array for piece in kv_pieces],
        *carrier.ins,
    )
    return out[0], out[1 : pieces + 1], out[pieces + 1 :]


def spots():
    return lax.axis_index("section"), lax.axis_index("dp"), lax.axis_index("tensor")


def dp_peer(group, level):
    return group + (1 << level) * (1 - 2 * ((group // (1 << level)) % 2))


def where_is(peer):
    section, group, tensor = spots()
    if peer == "near":
        return {"section": 1 - section}
    if peer == "over":
        return {"tensor": 1 - tensor}
    if peer == "cross":
        return {"section": 1 - section, "tensor": 1 - tensor}
    return {"dp": dp_peer(group, peer)}


def remote(source, target, sent, landed, where):
    return pltpu.make_async_remote_copy(
        src_ref=source,
        dst_ref=target,
        send_sem=sent,
        recv_sem=landed,
        device_id=where,
        device_id_type=pl.DeviceIdType.MESH,
    )


def greet(peers):
    barrier = pltpu.get_barrier_semaphore()
    for peer in peers:
        pl.semaphore_signal(
            barrier, inc=1, device_id=where_is(peer), device_id_type=pl.DeviceIdType.MESH
        )
    pl.semaphore_wait(barrier, len(peers))


class Carry:
    def __init__(self, tasks=(), collective=None):
        self.tasks = list(tasks)
        self.ins = [a for task in self.tasks for a in task.ins]
        self.outs = [a for task in self.tasks for a in task.outs]
        self.scratch = [a for task in self.tasks for a in task.scratch]
        self.peers = []
        for task in self.tasks:
            self.peers += [peer for peer in task.peers if peer not in self.peers]
        self.params = (
            dict(collective_id=collective, has_side_effects=True) if self.tasks else {}
        )

    def plan(self, steps, ins, outs, scratch):
        plan = {}
        if self.tasks:
            plan[0] = [lambda: greet(self.peers)]
        events = []
        for task in self.tasks:
            i, o, s = len(task.ins), len(task.outs), len(task.scratch)
            events += task.events(steps, ins[:i], outs[:o], scratch[:s])
            ins, outs, scratch = ins[i:], outs[o:], scratch[s:]
        for step, rank, action in sorted(events, key=lambda event: event[:2]):
            assert 0 <= step < steps
            plan.setdefault(step, []).append(action)
        return plan

    def run(self, place, slot, slots, steps, ins, outs, scratch):
        for step, actions in self.plan(steps, ins, outs, scratch).items():
            if step % slots == slot:

                @pl.when(place == step // slots)
                def _():
                    for action in actions:
                        action()


GROUP = ["near", "over", "cross"]


class RowCopies:
    def __init__(self, copies, arrivals, sems, room=None):
        self.copies, self.arrivals, self.room = copies, arrivals, room
        self.sent, self.landed, self.kept = sems

    def copy(self, i):
        source, target, slot, section, tensor, _ = self.copies[i]
        return remote(
            source,
            target,
            self.sent.at[i],
            self.landed.at[slot],
            {"section": section, "tensor": tensor},
        )

    def keep(self, i):
        source, target = self.copies[i][:2]
        return pltpu.make_async_copy(
            source, target if self.room is None else self.room, self.kept
        )

    def keep_on(self):
        for i in range(len(self.copies)):

            @pl.when(self.here(i, True))
            def _():
                self.keep(i).wait()
                pltpu.make_async_copy(self.room, self.copies[i][1], self.kept).start()

    def here(self, i, stays):
        section, _, tensor = spots()
        _, _, _, to_section, to_tensor, condition = self.copies[i]
        own = (to_section == section) & (to_tensor == tensor)
        return condition & (own if stays else jnp.logical_not(own))

    def start(self):
        for i in range(len(self.copies)):

            @pl.when(self.here(i, True))
            def _():
                self.keep(i).start()

            @pl.when(self.here(i, False))
            def _():
                self.copy(i).start()

    def wait_sent(self):
        for i in range(len(self.copies)):

            @pl.when(self.here(i, False))
            def _():
                self.copy(i).wait_send()

    def wait_arrival(self, i):
        section, _, tensor = spots()
        target, slot, from_section, from_tensor, condition = self.arrivals[i]
        own = (from_section == section) & (from_tensor == tensor)
        source = self.copies[0][0]

        @pl.when(condition & own)
        def _():
            stays = source if self.room is None else self.room
            pltpu.make_async_copy(stays, target, self.kept).wait()

        @pl.when(condition & jnp.logical_not(own))
        def _():
            remote(
                source, target, self.sent.at[0], self.landed.at[slot], where_is("near")
            ).wait_recv()


ROW_SEMS = [
    pltpu.SemaphoreType.DMA((2,)),
    pltpu.SemaphoreType.DMA((2,)),
    pltpu.SemaphoreType.DMA,
]


def spread_rows(source, target, sems, sides=(0, 1), room=None):
    section, _, tensor = spots()
    yes = section >= 0
    sends = yes if len(sides) == 2 else section == sides[0]
    copies = [
        (source.at[row], target.at[section], section, tensor, row, sends) for row in range(2)
    ]
    arrivals = [(target.at[side], side, side, section, yes) for side in sides]
    return RowCopies(copies, arrivals, sems, room)


def return_rows(source, target, sems, side, room):
    section, _, tensor = spots()
    copies = [(source, target.at[tensor], tensor, side, section, section >= 0)]
    arrivals = [(target.at[row], row, tensor, row, section == side) for row in range(2)]
    return RowCopies(copies, arrivals, sems, room)


class SpreadRows:
    peers = GROUP

    def __init__(self, array, sides, begin=0):
        self.ins, self.sides, self.begin = [array], sides, begin
        self.outs = [jax.ShapeDtypeStruct(array.shape, array.dtype)]
        self.scratch = ROW_SEMS + [pltpu.VMEM(array.shape[-2:], array.dtype)]

    def make(self, ins, outs, scratch):
        return spread_rows(ins[0], outs[0], scratch[:3], self.sides, scratch[3])

    def events(self, steps, ins, outs, scratch):
        def make():
            return self.make(ins, outs, scratch)

        def finish():
            rows = make()
            for i in range(len(rows.arrivals)):
                rows.wait_arrival(i)
            rows.wait_sent()

        return [
            (self.begin, 1, lambda: make().start()),
            (self.begin + 1, 1, lambda: make().keep_on()),
            (steps - 1, LAST, finish),
        ]


class ReturnRows(SpreadRows):
    def __init__(self, array, side, begin=0):
        self.ins, self.side, self.begin = [array], side, begin
        self.outs = [jax.ShapeDtypeStruct((2, *array.shape), array.dtype)]
        self.scratch = ROW_SEMS + [pltpu.VMEM(array.shape, array.dtype)]

    def make(self, ins, outs, scratch):
        return return_rows(ins[0], outs[0], scratch[:3], self.side, scratch[3])


class WeightCopies:
    @staticmethod
    def sems(count):
        return pltpu.SemaphoreType.DMA((3 + 8 * count,))

    def __init__(self, source, target, sem, room=None, count=1):
        section, group, _ = spots()
        rows = source.shape[0] // (2 * count)
        bit = group % 2
        here, stays = target.at[section, 1], target.at[section, 0]
        self.room = room
        if room is None:
            self.kept = pltpu.make_async_copy(source, stays, sem.at[0])
        else:
            self.first = pltpu.make_async_copy(source, room, sem.at[0])
            self.kept = pltpu.make_async_copy(room, stays, sem.at[0])
        self.near = remote(source, stays, sem.at[1], sem.at[2], where_is("near"))
        self.over, self.side, self.onward, self.last = [], [], [], []
        for i in range(count):
            own = pl.ds(pl.multiple_of((bit * count + i) * rows, 16), rows)
            other = pl.ds(pl.multiple_of(((1 - bit) * count + i) * rows, 16), rows)
            source_own, own, other = source.at[own], here.at[own], here.at[other]
            pairs = [(sem.at[3 + 8 * i + 2 * j], sem.at[4 + 8 * i + 2 * j]) for j in range(4)]
            self.over.append(remote(source_own, own, *pairs[0], where_is("over")))
            self.side.append(remote(own, own, *pairs[1], where_is(0)))
            self.onward.append(remote(own, own, *pairs[2], where_is("near")))
            self.last.append(remote(other, other, *pairs[3], where_is("near")))

    def start(self):
        for copy in self.over:
            copy.start()
        self.near.start()
        if self.room is None:
            self.kept.start()
        else:
            self.first.start()

    def keep_on(self):
        self.first.wait()
        self.kept.start()

    def forward(self, i):
        self.over[i].wait_recv()
        self.side[i].start()
        self.onward[i].start()

    def forward_last(self, i):
        self.side[i].wait_recv()
        self.last[i].start()

    def finish(self):
        self.kept.wait()
        self.near.wait()
        for over, side, onward, last in zip(self.over, self.side, self.onward, self.last):
            over.wait_send()
            side.wait_send()
            onward.wait()
            last.wait()


class SpreadWeight:
    peers = ["near", "over", 0]

    def __init__(self, weight, forwards, lasts):
        self.ins = [weight]
        self.outs = [jax.ShapeDtypeStruct((2, 2, *weight.shape), weight.dtype)]
        self.forwards, self.lasts = forwards, lasts
        self.scratch = [
            WeightCopies.sems(len(forwards)),
            pltpu.VMEM(weight.shape, weight.dtype),
        ]

    def events(self, steps, ins, outs, scratch):
        def copies():
            return WeightCopies(ins[0], outs[0], *scratch, len(self.forwards))

        def forward(i):
            return lambda: copies().forward(i)

        def forward_last(i):
            return lambda: copies().forward_last(i)

        return (
            [(0, 0, lambda: copies().start()), (1, 0, lambda: copies().keep_on())]
            + [(when, 1, forward(i)) for i, when in enumerate(self.forwards)]
            + [(when, 2, forward_last(i)) for i, when in enumerate(self.lasts)]
            + [(steps - 1, LAST, lambda: copies().finish())]
        )


class Reduce:
    def __init__(self, source, chunk, begins, pace, only=None, levels=None):
        self.ins = [source]
        self.chunk, self.begins, self.only = chunk, begins, only
        self.count = source.shape[-2] // chunk
        assert self.count == len(begins)
        self.levels = list(range(lax.axis_size("dp").bit_length() - 1))
        if levels is not None:
            self.levels = levels
        depth = len(self.levels)
        self.peers = []
        self.stages = []
        if only != "slice":
            self.peers += ["near", "over"]
            self.stages += ["enter", "cross", "over"]
        if only != "chip":
            self.peers += ["near", *self.levels]
            self.stages += ["load", "loaded"] if only == "slice" else []
            self.stages += [("halve", i) for i in range(depth)]
            self.stages += [("double", i) for i in reversed(range(depth))]
        assert len(pace) == len(self.stages) - 1
        self.dues = [sum(pace[:i]) for i in range(len(self.stages))]
        width = source.shape[-1]
        whole = jax.ShapeDtypeStruct((self.count * chunk, width), BF16)
        self.outs = [whole] if only == "chip" else [whole] * 2

        def room(*shape):
            return pltpu.VMEM((self.count, *shape, width), BF16)

        self.scratch = [room(2, chunk)]
        if only != "slice":
            self.scratch += [room(2, chunk), room(chunk)]
        if only != "chip":
            halves = [room(chunk >> (i + 1)) for i in range(depth)]
            self.scratch += [room(chunk)] + halves + halves
        self.scratch += [pltpu.SemaphoreType.DMA((2 + 2 * (3 + 2 * depth), self.count))]

    def events(self, steps, ins, outs, scratch):
        chunk, depth = self.chunk, len(self.levels)
        source, refs = ins[0], list(scratch)
        own, sems = refs[0], refs[-1]
        refs = refs[1:-1]
        if self.only != "slice":
            chip, other = refs[:2]
            refs = refs[2:]
        if self.only != "chip":
            full, halves, doubles = refs[0], refs[1 : 1 + depth], refs[1 + depth :]

        def bounds(i):
            _, group, _ = spots()
            begin = 0
            for j in range(i):
                bit = (group // (1 << self.levels[j])) % 2
                begin = begin + bit * (chunk >> (j + 1))
            return begin

        def keeps(i):
            return pl.ds(pl.multiple_of(bounds(i + 1), 16), chunk >> (i + 1))

        def gives(i):
            begin = 2 * bounds(i) + (chunk >> (i + 1)) - bounds(i + 1)
            return pl.ds(pl.multiple_of(begin, 16), chunk >> (i + 1))

        def pair(kind, c):
            return sems.at[2 + 2 * kind, c], sems.at[3 + 2 * kind, c]

        def rows_of(c):
            return pl.ds(c * chunk, chunk)

        def load(c):
            if self.only == "slice":
                return pltpu.make_async_copy(
                    source.at[rows_of(c), :], own.at[c, 0], sems.at[0, c]
                )
            section, _, _ = spots()
            return pltpu.make_async_copy(
                source.at[section, :, rows_of(c), :], own.at[c], sems.at[0, c]
            )

        def cross(c):
            section, _, _ = spots()
            return remote(
                source.at[1 - section, :, rows_of(c), :],
                chip.at[c],
                *pair(0, c),
                where_is("near"),
            )

        def over(c):
            return remote(own.at[c, 1], other.at[c], *pair(1, c), where_is("over"))

        def halve(i, c):
            return remote(
                own.at[c, 0, gives(i), :],
                halves[i].at[c],
                *pair(3 + i, c),
                where_is(self.levels[i]),
            )

        def double(i, c):
            return remote(
                full.at[c, keeps(i), :],
                doubles[i].at[c],
                *pair(3 + depth + i, c),
                where_is(self.levels[i]),
            )

        def store(c):
            kept = own.at[c, 0] if self.only == "chip" else full.at[c]
            return pltpu.make_async_copy(kept, outs[0].at[rows_of(c), :], sems.at[1, c])

        def tell(c):
            return remote(
                full.at[c], outs[1].at[rows_of(c), :], *pair(2, c), where_is("near")
            )

        def act(stage, c):
            if stage == "enter":
                load(c).start()
                cross(c).start()
            elif stage == "load":
                load(c).start()
            elif stage == "loaded":
                load(c).wait()
                halve(0, c).start()
            elif stage == "cross":
                load(c).wait()
                cross(c).wait()
                own[c] = own[c] + chip[c]
                over(c).start()
            elif stage == "over":
                over(c).wait()
                own[c, 0] = own[c, 0] + other[c]
                if self.only == "chip":
                    store(c).start()
                else:
                    halve(0, c).start()
            elif stage[0] == "halve":
                i = stage[1]
                halve(i, c).wait()
                mine = keeps(i)
                total = own[c, 0, mine, :] + halves[i][c]
                if i < depth - 1:
                    own[c, 0, mine, :] = total
                    halve(i + 1, c).start()
                else:
                    full[c, mine, :] = total
                    double(i, c).start()
            else:
                i = stage[1]
                double(i, c).wait()
                full[c, gives(i), :] = doubles[i][c]
                if i:
                    double(i - 1, c).start()
                else:
                    store(c).start()
                    tell(c).start()

        def leave(c):
            store(c).wait()
            if self.only != "chip":
                tell(c).wait()

        events = []
        for c, begin in enumerate(self.begins):
            for i, (stage, due) in enumerate(zip(self.stages, self.dues)):
                events.append((begin + due, -i, functools.partial(act, stage, c)))
            events.append((steps - 1, LAST, functools.partial(leave, c)))
        return events


def carry_alone(tasks, steps, collective):
    carrier = Carry(tasks, collective)

    def kernel(*refs):
        i, o = len(carrier.ins), len(carrier.ins) + len(carrier.outs)
        carrier.run(pl.program_id(0), 0, 1, steps, refs[:i], refs[i:o], refs[o:])

    hold = pl.BlockSpec(memory_space=pl.ANY)
    return pl.pallas_call(
        kernel,
        grid=(steps,),
        in_specs=[hold] * len(carrier.ins),
        out_specs=[hold] * len(carrier.outs),
        out_shape=carrier.outs,
        scratch_shapes=carrier.scratch,
        compiler_params=pltpu.CompilerParams(vmem_limit_bytes=VMEM, **carrier.params),
        name="carry_alone",
    )(*carrier.ins)


def open_up(tokens, qkv, norm, block, collective):
    _, rows, width = tokens.shape
    part = qkv.shape[-1]
    score = LOG2E / math.sqrt(width // HEADS)

    def kernel(tokens_ref, qkv_ref, norm_ref, *refs):
        x_out, w_out, n_out, q_out, own_out, other_out = refs[:6]
        x, low, w, n, q, kv = refs[6:12]
        row_sems, weight_sems, norm_sems, store_sems, kv_sems = (
            refs[12:15],
            refs[15:16],
            refs[16],
            refs[17],
            refs[18],
        )
        section, _, _ = spots()
        greet([*GROUP, 0])
        rows_in = spread_rows(tokens_ref, x, row_sems)
        weight = WeightCopies(qkv_ref, w, weight_sems[0])
        weight.start()
        rows_in.start()
        norm_kept = pltpu.make_async_copy(norm_ref, n.at[section], norm_sems.at[0])
        norm_near = remote(
            norm_ref, n.at[section], norm_sems.at[1], norm_sems.at[2], where_is("near")
        )
        norm_kept.start()
        norm_near.start()
        stores = []

        def save(source, target):
            copy = pltpu.make_async_copy(source, target, store_sems.at[len(stores)])
            copy.start()
            stores.append(copy)

        kv_copies = []

        def project(side, k):
            def step(i, carry):
                own = pl.ds(pl.multiple_of(i * block, block), block)
                rows_low = low[own, :] if side == 0 else x[1, own, :]

                def product(m):
                    return dot_nn(rows_low, w[side, k, m * width : (m + 1) * width, :])

                q[side, k, own, :] = (product(0) * score).astype(BF16)
                kv[side, k, 0, own, :] = product(1).astype(BF16)
                kv[side, k, 1, own, :] = product(2).astype(BF16)
                return carry

            lax.fori_loop(0, rows // block, step, 0)
            spot = 2 * (2 * side + k)
            copy = remote(
                kv.at[side, k],
                other_out.at[side, k],
                kv_sems.at[spot],
                kv_sems.at[spot + 1],
                where_is("near"),
            )
            copy.start()
            kv_copies.append(copy)
            save(kv.at[side, k], own_out.at[side, k])
            save(q.at[side, k], q_out.at[side, k])

        norm_kept.wait()
        norm_near.wait()
        save(n, n_out)
        weight.forward(0)
        weight.forward_last(0)
        weight.finish()
        save(w, w_out)
        rows_in.wait_arrival(0)
        save(x.at[0], x_out.at[0])

        def settle(i, carry):
            own = pl.ds(pl.multiple_of(i * block, block), block)
            unit, _ = standardize(x[0, own, :].astype(F32))
            low[own, :] = affine(unit, n.at[0], 2).astype(BF16)
            return carry

        lax.fori_loop(0, rows // block, settle, 0)
        project(0, 0)
        project(0, 1)
        rows_in.wait_arrival(1)
        save(x.at[1], x_out.at[1])
        project(1, 0)
        project(1, 1)
        rows_in.wait_sent()
        for copy in kv_copies + stores:
            copy.wait()

    hold = pl.BlockSpec(memory_space=pl.ANY)
    shapes = [
        ((2, rows, width), BF16),
        ((2, 2, *qkv.shape), BF16),
        ((2, *norm.shape), F32),
        ((2, 2, rows, part), BF16),
        ((2, 2, 2, rows, part), BF16),
    ]
    return pl.pallas_call(
        kernel,
        in_specs=[hold] * 3,
        out_specs=[hold] * 6,
        out_shape=[jax.ShapeDtypeStruct(*s) for s in shapes + shapes[-1:]],
        scratch_shapes=[pltpu.VMEM(*shapes[0]), pltpu.VMEM((rows, width), BF16)]
        + [pltpu.VMEM(*s) for s in shapes[1:]]
        + ROW_SEMS
        + [WeightCopies.sems(1)]
        + [
            pltpu.SemaphoreType.DMA((3,)),
            pltpu.SemaphoreType.DMA((12,)),
            pltpu.SemaphoreType.DMA((8,)),
        ],
        compiler_params=pltpu.CompilerParams(
            vmem_limit_bytes=VMEM, collective_id=collective, has_side_effects=True
        ),
        name="open_up",
    )(tokens, qkv, norm)


def local_general(tokens, lengths, self_qkv, self_out, cross_proj, ffn_up, ffn_down, norms, cotangent):
    section = lax.axis_index("section")
    tensor = lax.axis_index("tensor")
    tensors = lax.axis_size("tensor")
    _, row_count, rows, width = tokens.shape
    assert row_count == 2 and tensors % row_count == 0
    spread = tensors // row_count
    pieces = 2 * spread
    axes = ("section", "tensor")
    is_first = section == 0
    own_row = tensor // spread
    place = section * spread + tensor % spread

    def device(row, spot):
        return (spot // spread) * tensors + row * spread + spot % spread

    def each():
        return [(s, t) for s in range(2) for t in range(tensors)]

    straight = [(s * tensors + t, device(s, t)) for s, t in each()]
    turned = [(s * tensors + t, device(1 - s, t)) for s, t in each()]

    def bring(shares):
        stays = lax.dynamic_index_in_dim(shares, section, 0, keepdims=False)
        moves = lax.dynamic_index_in_dim(shares, 1 - section, 0, keepdims=False)
        one = lax.ppermute(stays, axes, straight)
        two = lax.ppermute(moves, axes, turned)
        return jnp.where(own_row == 0, one, two), jnp.where(own_row == 0, two, one)

    def take_back(source, target):
        one = jnp.where(own_row == 0, source, target)
        two = jnp.where(own_row == 0, target, source)
        one = lax.ppermute(one, axes, [(b, a) for a, b in straight])
        two = lax.ppermute(two, axes, [(b, a) for a, b in turned])
        return jnp.stack([jnp.where(is_first, one, two), jnp.where(is_first, two, one)])

    def rotate(value, by):
        pairs = [
            (device(r, p), device(r, (p + by) % pieces))
            for r in range(row_count)
            for p in range(pieces)
        ]
        return lax.ppermute(value, axes, pairs)

    def pieces_of(value):
        return [value] + [rotate(value, by) for by in range(1, pieces)]

    def pieces_home(values):
        return [values[0]] + [rotate(values[by], -by) for by in range(1, pieces)]

    def swap_sections(value):
        return lax.ppermute(value, "section", [(0, 1), (1, 0)])

    def both_sides(weight, dim):
        if spread == 1:
            other = lax.ppermute(weight, "tensor", [(t, 1 - t) for t in range(tensors)])
            parts = [weight, other]
        else:
            parts = [lax.all_gather(weight, "tensor", axis=dim, tiled=True)]
        swapped = [swap_sections(part) for part in parts]
        pairs = list(zip(parts, swapped))
        return (
            [jnp.where(is_first, mine, theirs) for mine, theirs in pairs],
            [jnp.where(is_first, theirs, mine) for mine, theirs in pairs],
        )

    def home(source_grad, target_grad, dim):
        keep = jnp.where(is_first, source_grad, target_grad).astype(F32)
        sent = swap_sections(jnp.where(is_first, target_grad, source_grad))
        total = (keep + sent.astype(F32)).astype(BF16)
        if spread == 1:
            other = lax.ppermute(total[1], "tensor", [(t, 1 - t) for t in range(tensors)])
            total = (total[0].astype(F32) + other.astype(F32)).astype(BF16)
        else:
            total = lax.psum_scatter(total[0], "tensor", scatter_dimension=dim, tiled=True)
        return total

    def span_of(query_side, key_side):
        own = lax.dynamic_index_in_dim(lengths, own_row, 1, keepdims=False)
        asks, answers = own[query_side], own[key_side]
        paired = asks[1] > 0
        second = paired & (place * rows >= asks[0])
        begin = jnp.where(second, answers[0], 0)
        end = jnp.where(second | ~paired, answers[0] + answers[1], answers[0])
        offsets = [(place - by) % pieces * rows for by in range(pieces)]
        return jnp.stack([begin, end, *offsets]).astype(jnp.int32)[None]

    query_block = min(256, rows)
    chunk = 256

    source, target = bring(tokens[0])
    source_norm, target_norm = (
        jnp.where(is_first, a, b)
        for a, b in (lambda own, other: ((own, other), (other, own)))(
            norms[0], swap_sections(norms[0])
        )
    )
    source_qkv, target_qkv = both_sides(self_qkv[0], 2)
    source_out, target_out = both_sides(self_out[0], 0)
    source_up, target_up = both_sides(ffn_up[0], 1)
    source_down, target_down = both_sides(ffn_down[0], 0)
    source_cross, target_cross = both_sides(cross_proj[0], 2)
    source_cot, target_cot = bring(cotangent[0])
    source_span, target_span, cross_span = span_of(0, 0), span_of(1, 1), span_of(1, 0)

    enc_q, enc_kv = project_qkv(source, source_norm, source_qkv, True)
    enc_kv = pieces_of(enc_kv)
    dec_q, dec_kv = project_qkv(target, target_norm, target_qkv, False)
    dec_kv = pieces_of(dec_kv)
    enc_mix, enc_lse = attend(enc_q, enc_kv, source_span, query_block)
    encoded, memory, enc_first, enc_third = encoder_forward(
        source, enc_mix, source_norm, source_out, source_up, source_down, source_cross
    )
    memory = pieces_of(memory)
    dec_mix, dec_lse = attend(dec_q, dec_kv, target_span, query_block)
    cross_q, dec_first = decoder_middle(
        target, dec_mix, target_norm, target_out, target_cross
    )
    cross_mix, cross_lse = attend(cross_q, memory, cross_span, query_block)
    decoded, second_grad, cross_mix_grad, cross_out_grad, dec_up, dec_down, dec_norm = decoder_turn(
        dec_first, cross_mix, target_cot, target_norm, target_cross, target_up, target_down
    )
    result = take_back(encoded, decoded)
    cross_q_grad, memory_grads, _ = attend_back(
        cross_q, memory, cross_mix, cross_mix_grad, cross_lse, cross_span, chunk
    )
    memory_grads = pieces_home(memory_grads)
    dec_first_grad, dec_mix_grad, cross_query_grad, dec_out, step = decoder_middle_back(
        dec_first,
        dec_mix,
        cross_q_grad,
        second_grad,
        target_norm,
        target_out,
        target_cross
    )
    dec_norm += step
    enc_first_grad, enc_mix_grad, enc_cross, enc_out, enc_up, enc_down, enc_norm = encoder_back(
        enc_first,
        enc_third,
        enc_mix,
        memory_grads,
        source_cot,
        source_norm,
        source_out,
        source_up,
        source_down,
        source_cross
    )
    dec_cross = jnp.stack([cross_query_grad, cross_out_grad], axis=1)
    up_grad, down_grad = home(enc_up, dec_up, 1), home(enc_down, dec_down, 0)
    out_grad, cross_grad = home(enc_out, dec_out, 0), home(enc_cross, dec_cross, 2)
    dec_q_grad, dec_kv_grads, _ = attend_back(
        dec_q, dec_kv, dec_mix, dec_mix_grad, dec_lse, target_span, chunk
    )
    dec_kv_grads = pieces_home(dec_kv_grads)
    enc_q_grad, enc_kv_grads, _ = attend_back(
        enc_q, enc_kv, enc_mix, enc_mix_grad, enc_lse, source_span, chunk
    )
    enc_kv_grads = pieces_home(enc_kv_grads)
    target_grad, dec_qkv, _ = input_back(
        target, dec_first_grad, dec_q_grad, dec_kv_grads, target_norm, target_qkv, False
    )
    source_grad, enc_qkv, step = input_back(
        source, enc_first_grad, enc_q_grad, enc_kv_grads, source_norm, source_qkv, True
    )
    enc_norm += step
    token_grad = take_back(source_grad, target_grad).astype(F32)
    qkv_grad = home(enc_qkv, dec_qkv, 2)
    norm_total = lax.psum(jnp.stack([enc_norm, dec_norm]), ("section", "dp", "tensor"))
    norm_grad = lax.dynamic_index_in_dim(norm_total, section, 0, keepdims=False)
    summed = [
        lax.psum(grad, "dp").astype(F32)
        for grad in (qkv_grad, out_grad, cross_grad, up_grad, down_grad)
    ]
    return (
        result[None],
        token_grad[None],
        summed[0][None],
        summed[1][None],
        summed[2][None],
        summed[3][None],
        summed[4][None],
        norm_grad[None],
    )


def local_fast(tokens, lengths, self_qkv, self_out, cross_proj, ffn_up, ffn_down, norms, cotangent):
    section, tensor = lax.axis_index("section"), lax.axis_index("tensor")
    _, row_count, rows, width = tokens.shape
    assert row_count == 2
    is_first = section == 0
    block = min(256, rows)
    query_block = min(256, rows)
    chunk = 256
    levels = lax.axis_size("dp").bit_length() - 1

    def hops(*steps):
        return list(steps[:levels]) + list(steps[3 : 3 + levels])

    def swap(value):
        return lax.ppermute(value, "section", [(0, 1), (1, 0)])

    def flat(weight):
        return weight.reshape(-1, weight.shape[-1])

    def span_of(query_side, key_side):
        own = lax.dynamic_index_in_dim(lengths, tensor, 1, keepdims=False)
        asks, answers = own[query_side], own[key_side]
        paired = asks[1] > 0
        second = paired & (section * rows >= asks[0])
        begin = jnp.where(second, answers[0], 0)
        end = jnp.where(second | ~paired, answers[0] + answers[1], answers[0])
        return jnp.stack([begin, end, section * rows, (1 - section) * rows]).astype(jnp.int32)

    spans = jnp.stack([span_of(0, 0), span_of(1, 1), span_of(1, 0)])
    self_spans, cross_span = spans[:2], spans[2:]
    x, qkv, norm, q, *kv = open_up(tokens[0], flat(self_qkv), norms[0], block, 1)
    qkv = qkv.reshape(2, 2, *self_qkv.shape[1:])

    def parts(weight, side):
        return [At(weight, side, k) for k in range(2)]

    enc_x, dec_x, enc_norm_in, dec_norm_in = At(x, 0), At(x, 1), At(norm, 0), At(norm, 1)
    mix, lse, out, up, cross, down = attend(
        q,
        kv,
        self_spans,
        query_block,
        Carry(
            [
                SpreadWeight(self_out[0], [3], [5]),
                SpreadWeight(ffn_up[0], [4, 6], [7, 9]),
                SpreadWeight(flat(cross_proj), [8], [11]),
                SpreadWeight(ffn_down[0], [10, 12], [13, 15]),
            ],
            2,
        ),
        2,
    )
    cross = cross.reshape(2, 2, *cross_proj.shape[1:])
    enc_mix, dec_mix = At(mix, 0), At(mix, 1)
    encoded, memory, enc_first, enc_third = encoder_forward(
        enc_x,
        enc_mix,
        enc_norm_in,
        parts(out, 0),
        parts(up, 0),
        parts(down, 0),
        parts(cross, 0),
    )
    memory = [memory, swap(memory)]
    cross_q, dec_first = decoder_middle(
        dec_x, dec_mix, dec_norm_in, parts(out, 1), parts(cross, 1)
    )
    cross_mix, cross_lse, dec_cot = attend(
        cross_q,
        memory,
        cross_span,
        query_block,
        Carry([SpreadRows(cotangent[0], (1,))], 4),
        2,
    )
    decoded, second_grad, cross_mix_grad, cross_out_grad, ffn_dec, dec_norm = decoder_turn(
        dec_first,
        cross_mix,
        At(dec_cot, 1),
        dec_norm_in,
        parts(cross, 1),
        parts(up, 1),
        parts(down, 1),
        True,
    )
    cross_q_grad, memory_grads, (ffn_dec, enc_cot) = attend_back(
        cross_q,
        memory,
        cross_mix,
        cross_mix_grad,
        cross_lse,
        cross_span,
        chunk,
        Carry(
            [
                Reduce(ffn_dec, 256, [0, 1, 2, 3], [1, 2], "chip"),
                SpreadRows(cotangent[0], (0,), 4),
            ],
            5,
        ),
        2,
    )
    dec_first_grad, mix_grad, cross_query_grad, dec_out, mid_norm = decoder_middle_back(
        dec_first,
        dec_mix,
        cross_q_grad,
        second_grad,
        dec_norm_in,
        parts(out, 1),
        parts(cross, 1),
        (1, None),
    )
    enc_first_grad, mix_grad, ffn_enc, sides, enc_norm = encoder_back(
        enc_first,
        enc_third,
        enc_mix,
        memory_grads,
        At(enc_cot, 0),
        enc_norm_in,
        parts(out, 0),
        parts(up, 0),
        parts(down, 0),
        parts(cross, 0),
        [dec_out, cross_query_grad, cross_out_grad],
        (0, mix_grad),
    )
    q_grad, kv_grads, moved = attend_back(
        q,
        kv,
        mix,
        mix_grad,
        lse,
        self_spans,
        chunk,
        Carry(
            [
                Reduce(ffn_dec, 512, [0, 1], [1, *hops(2, 1, 1, 1, 2, 3)], "slice"),
                Reduce(ffn_enc, 512, [2, 0], [1, 3, *hops(2, 1, 2, 1, 1, 2)]),
                Reduce(sides, 768, [3, 1], [1, 3, *hops(1, 2, 1, 2, 1, 1)]),
                ReturnRows(encoded, 0, 11),
                ReturnRows(decoded, 1, 12),
            ],
            6,
        ),
        2,
    )
    ffn_dec, ffn_dec_other, ffn_enc, ffn_enc_other, sides, _, encoded, decoded = moved
    target_grad, dec_qkv = input_back(
        dec_x,
        dec_first_grad,
        At(q_grad, 1),
        [At(g, 1) for g in kv_grads],
        dec_norm_in,
        parts(qkv, 1),
        False,
        [],
    )
    source_grad, enc_qkv = input_back(
        enc_x,
        enc_first_grad,
        At(q_grad, 0),
        [At(g, 0) for g in kv_grads],
        enc_norm_in,
        parts(qkv, 0),
        True,
        [enc_norm, dec_norm, mid_norm],
    )
    enc_last, enc_other, dec_last, dec_other, source_grad, target_grad = carry_alone(
        [
            Reduce(
                enc_qkv,
                2 * PAIR,
                [0, 1, 2, 2, 3, 3, 4],
                [2, 2, *hops(1, 1, 1, 1, 1, 2)],
            ),
            Reduce(
                dec_qkv,
                2 * PAIR,
                [0, 1, 1, 3, 4, 4],
                [2, 2, *hops(1, 1, 1, 1, 1, 2)],
            ),
            ReturnRows(source_grad, 0, 6),
            ReturnRows(target_grad, 1, 7),
        ],
        10 + 2 * levels,
        8,
    )

    half = 3 * width // 2
    up_grad = jnp.where(is_first, ffn_enc, ffn_dec_other).astype(F32)
    down_grad = jnp.where(is_first, ffn_enc_other, ffn_dec).astype(F32)
    up_grad = jnp.concatenate(jnp.split(up_grad, 2, axis=0), axis=1)

    def columns(halves):
        return jnp.concatenate([halves[:half], halves[half : 2 * half]], axis=1)

    qkv_grad = jnp.concatenate(
        [
            jnp.where(is_first, columns(enc_last), columns(dec_other)),
            jnp.where(is_first, columns(enc_other), columns(dec_last)),
        ],
        axis=0,
    )
    qkv_grad = qkv_grad.astype(F32).reshape(self_qkv.shape)
    sides = sides.astype(F32)
    out_grad = jnp.concatenate([sides[: width // 2], sides[width // 2 : width]], axis=1)
    cross_grad = sides[width:].reshape(cross_proj.shape)
    norm_grad = enc_last[2 * half : 2 * half + 24].astype(F32).reshape(norms.shape)

    def by_side(source, target):
        return jnp.where(is_first, source, target)

    return (
        by_side(encoded, decoded)[None],
        by_side(source_grad, target_grad).astype(F32)[None],
        qkv_grad,
        out_grad[None],
        cross_grad,
        up_grad[None],
        down_grad[None],
        norm_grad,
    )


def solution(mesh):
    placed = (
        P("section", "dp", "tensor", None),
        P(None, "dp", None),
        P("section", None, None, "tensor"),
        P("section", "tensor", None),
        P("section", None, None, "tensor"),
        P("section", None, "tensor"),
        P("section", "tensor", None),
        P("section", None, None, None),
        P("section", "dp", "tensor", None),
    )
    sizes = dict(mesh.shape)
    steps = sizes["dp"].bit_length() - 1
    fast = sizes["tensor"] == 2 and sizes["dp"] == 1 << steps and 0 < steps <= 3
    return jax.shard_map(
        local_fast if fast else local_general,
        mesh=mesh,
        in_specs=placed,
        out_specs=(
            P("section", "dp", "tensor", None),
            P("section", "dp", "tensor", None),
            P("section", None, None, "tensor"),
            P("section", "tensor", None),
            P("section", None, None, "tensor"),
            P("section", None, "tensor"),
            P("section", "tensor", None),
            P("section", None, None, None),
        ),
        check_vma=False,
    )
```

```python
import functools
import math

import jax
import jax.numpy as jnp
from jax import lax
from jax.experimental import pallas as pl
from jax.experimental.pallas import tpu as pltpu
from jax.sharding import PartitionSpec as P

HEADS = 8
EPSILON = 1e-05
MASKED = -1000000000.0
LOG2E = 1.0 / math.log(2.0)
PAIR = 128
HALF = 64
VMEM = 60 * 1024 * 1024
BF16 = jnp.bfloat16
F32 = jnp.float32


def standardize(rows):
    mean = jnp.mean(rows, axis=-1, keepdims=True)
    centered = rows - mean
    inv = lax.rsqrt(jnp.mean(centered * centered, axis=-1, keepdims=True) + EPSILON)
    return centered * inv, inv


def affine(unit, norm_ref, slot):
    return unit * norm_ref[slot, 0:1, :] + norm_ref[slot, 1:2, :]


def norm_back(unit, inv, norm_ref, slot, grad, grad_ref):
    grad_ref[slot, 0:1, :] += jnp.sum(grad * unit, axis=0, keepdims=True)
    grad_ref[slot, 1:2, :] += jnp.sum(grad, axis=0, keepdims=True)
    scaled = grad * norm_ref[slot, 0:1, :]
    first = jnp.mean(scaled, axis=-1, keepdims=True)
    second = jnp.mean(scaled * unit, axis=-1, keepdims=True)
    return inv * (scaled - first - unit * second)


def gelu_tanh(inner):
    return jnp.tanh(0.7978845608028654 * (inner + 0.044715 * inner * inner * inner))


def gelu(inner):
    return 0.5 * inner * (1.0 + gelu_tanh(inner))


def gelu_both(inner):
    bent = gelu_tanh(inner)
    slope = 0.7978845608028654 * (1.0 + 0.134145 * inner * inner)
    half = 0.5 * (1.0 + bent)
    return inner * half, half + 0.5 * inner * (1.0 - bent * bent) * slope


def dot_nn(a, b):
    return jnp.dot(a, b, preferred_element_type=F32)


def dot_nt(a, b):
    return lax.dot_general(a, b, (((1,), (1,)), ((), ())), preferred_element_type=F32)


def dot_tn(a, b):
    return lax.dot_general(a, b, (((0,), (0,)), ((), ())), preferred_element_type=F32)


class At:
    def __init__(self, array, *lead):
        self.array, self.lead = array, lead
        self.shape = array.shape[len(lead) :]
        self.dtype = array.dtype

    def spec(self, sizes, index, **options):
        nones = (None,) * len(self.lead)
        return pl.BlockSpec(nones + tuple(sizes), lambda *g: self.lead + tuple(index(*g)), **options)


def at(array):
    return array if isinstance(array, At) else At(array)


def row_call(
    body, name, rows, row_ins, whole_ins, row_outs, keeps, finals, finish, flops, into=None, push=None
):
    block, part = min(512, rows), min(256, rows)
    row_ins = [(at(a), dim) for a, dim in row_ins]
    whole_ins = [at(a) for a in whole_ins]

    def blocked(array, dim):
        sizes = tuple(block if i == dim else size for i, size in enumerate(array.shape))
        return array.spec(sizes, lambda g: tuple(g if i == dim else 0 for i in range(len(sizes))))

    def blocked_out(shape, dim):
        sizes = tuple(block if i == dim else size for i, size in enumerate(shape))
        return pl.BlockSpec(
            sizes, lambda g: tuple(g if i == dim else 0 for i in range(len(shape)))
        )

    def sided_out(shape, dim):
        plain = blocked_out(shape, dim)
        return pl.BlockSpec(
            (None, *plain.block_shape), lambda g: (into[0], *plain.index_map(g))
        )

    def whole(array):
        return array.spec(
            array.shape,
            lambda g: (0,) * len(array.shape),
            pipeline_mode=pl.Buffered(buffer_count=1),
        )

    def whole_out(shape):
        return pl.BlockSpec(
            shape, lambda g: (0,) * len(shape), pipeline_mode=pl.Buffered(buffer_count=1)
        )

    n_rows_in = len(row_ins)
    n_in = n_rows_in + len(whole_ins)
    n_row, n_final = len(row_outs), len(finals)
    out_specs = [blocked_out(shape, dim) for shape, _, dim in row_outs]
    out_shapes = [jax.ShapeDtypeStruct(shape, dtype) for shape, dtype, _ in row_outs]
    push_outs, push_scratch, push_params = [], [], {}
    if push is not None:
        push_outs = [out_shapes[push[0]]]
        push_scratch = [
            pltpu.VMEM(push_outs[0].shape, push_outs[0].dtype),
            pltpu.SemaphoreType.DMA((2, rows // block)),
        ]
        push_params = dict(collective_id=push[1], has_side_effects=True)
    held, aliases = [], {}
    if into is not None:
        shape, dtype, dim = row_outs[-1]
        out_specs[-1] = sided_out(shape, dim)
        out_shapes[-1] = jax.ShapeDtypeStruct((2, *shape), dtype)
        if into[1] is not None:
            held, aliases = [into[1]], {n_in: n_row - 1}

    def kernel(*refs):
        ins, refs = refs[:n_in], refs[len(held) :]
        outs = refs[n_in : n_in + n_row]
        last_outs, kept = refs[n_in + n_row : n_in + n_row + n_final], refs[n_in + n_row + n_final :]
        step = pl.program_id(0)
        if push is not None:
            pushed, kept = kept[0], kept[1:]
            kept, (push_room, push_sems) = kept[:-2], kept[-2:]

            def send(i):
                own = pl.ds(i * block, block)
                return remote(
                    push_room.at[:, :, own, :],
                    pushed.at[:, :, own, :],
                    push_sems.at[0, i],
                    push_sems.at[1, i],
                    where_is("near"),
                )

            @pl.when(step == 0)
            def _():
                greet(["near"])
        if finals:

            @pl.when(step == 0)
            def _():
                kept[-1][...] = jnp.zeros_like(kept[-1])

        turns = []
        for begin in range(0, block, part):
            all_rows = pl.ds(pl.multiple_of(step * block + begin, part), part)
            turns.append(body(ins, outs, kept, slice(begin, begin + part), all_rows))
        waiting, running = turns[1:], turns[:1]
        while running:
            running = [turn for turn in running if next(turn, LAST) is not LAST]
            if waiting:
                running.append(waiting.pop(0))

        if push is not None:
            for i in range(rows // block):

                @pl.when(step == i)
                def _():
                    push_room[:, :, i * block : (i + 1) * block, :] = outs[push[0]][...]
                    send(i).start()

            @pl.when(step == pl.num_programs(0) - 1)
            def _():
                for i in range(rows // block):
                    send(i).wait()

        if finals:

            @pl.when(step == pl.num_programs(0) - 1)
            def _():
                finish(ins[n_rows_in:], kept, last_outs)

    arrays = [array for array, _ in row_ins] + whole_ins
    size = sum(math.prod(a.shape) * a.dtype.itemsize for a in arrays)
    return pl.pallas_call(
        kernel,
        grid=(rows // block,),
        in_specs=[blocked(a, dim) for a, dim in row_ins]
        + [whole(a) for a in whole_ins]
        + [pl.BlockSpec(memory_space=pl.ANY)] * len(held),
        out_specs=out_specs
        + [whole_out(shape) for shape, _ in finals]
        + [pl.BlockSpec(memory_space=pl.ANY)] * len(push_outs),
        out_shape=out_shapes
        + [jax.ShapeDtypeStruct(shape, dtype) for shape, dtype in finals]
        + push_outs,
        input_output_aliases=aliases,
        scratch_shapes=[pltpu.VMEM(shape, dtype) for shape, dtype in keeps] + push_scratch,
        compiler_params=pltpu.CompilerParams(vmem_limit_bytes=VMEM, **push_params),
        cost_estimate=pl.CostEstimate(flops=flops, bytes_accessed=size, transcendentals=0),
        name=name,
    )(*[a.array for a in arrays], *held)


LAST = 1000


def split(refs, parts, count):
    return [refs[i * parts : (i + 1) * parts] for i in range(count)]


def project_qkv(x, norm, weights, with_norm):
    x = at(x)
    rows, width = x.shape
    parts, part = len(weights), weights[0].shape[-1]
    score = LOG2E / math.sqrt(width // HEADS)

    def body(ins, outs, kept, own, all_rows):
        x_ref, norm_ref, *w = ins
        q_ref, kv_ref = outs
        low = x_ref[own, :]
        if with_norm:
            unit, _ = standardize(low.astype(F32))
            low = affine(unit, norm_ref, 2).astype(BF16)
        yield
        for k in range(parts):
            q_ref[k, own, :] = (dot_nn(low, w[k][0]) * score).astype(BF16)
            kv_ref[k, 0, own, :] = dot_nn(low, w[k][1]).astype(BF16)
            kv_ref[k, 1, own, :] = dot_nn(low, w[k][2]).astype(BF16)
            yield

    return row_call(
        body,
        "project_qkv",
        rows,
        [(x, 0)],
        [norm, *weights],
        [((parts, rows, part), BF16, 1), ((parts, 2, rows, part), BF16, 2)],
        [],
        [],
        None,
        6 * rows * width * width,
    )


def encoder_forward(x, mix, norm, out, up, down, cross, push=None):
    x = at(x)
    rows, width = x.shape
    parts, part = len(out), out[0].shape[0]

    def body(ins, outs, kept, own, all_rows):
        x_ref, mix_ref, norm_ref = ins[:3]
        wo, wu, wd, wc = split(ins[3:], parts, 4)
        result_ref, kv_ref, first_ref, third_ref = outs
        unit, _ = standardize(x_ref[own, :].astype(F32))
        first = affine(unit, norm_ref, 2)
        for k in range(parts):
            first += dot_nn(mix_ref[k, own, :], wo[k][...])
        yield
        first_ref[own, :] = first
        unit, _ = standardize(first)
        third = affine(unit, norm_ref, 0)
        low = third.astype(BF16)
        inner = dot_nn(low, wu[0][...])
        yield
        for k in range(parts):
            act = gelu(inner).astype(BF16)
            if k + 1 < parts:
                inner = dot_nn(low, wu[k + 1][...])
            third += dot_nn(act, wd[k][...])
            yield
        third_ref[own, :] = third
        unit, _ = standardize(third)
        low = affine(unit, norm_ref, 1).astype(BF16)
        result_ref[own, :] = low
        yield
        for k in range(parts):
            kv_ref[k, 0, own, :] = dot_nn(low, wc[k][0]).astype(BF16)
            kv_ref[k, 1, own, :] = dot_nn(low, wc[k][1]).astype(BF16)

    units = sum(w.shape[1] for w in up)
    return row_call(
        body,
        "encoder_forward",
        rows,
        [(x, 0), (mix, 1)],
        [norm, *out, *up, *down, *cross],
        [
            ((rows, width), BF16, 0),
            ((parts, 2, rows, part), BF16, 2),
            ((rows, width), F32, 0),
            ((rows, width), F32, 0),
        ],
        [],
        [],
        None,
        6 * rows * width * width + 4 * rows * width * units,
        push=None if push is None else (1, push),
    )


def decoder_middle(x, mix, norm, out, cross):
    x = at(x)
    rows, width = x.shape
    parts, part = len(out), out[0].shape[0]
    score = LOG2E / math.sqrt(width // HEADS)

    def body(ins, outs, kept, own, all_rows):
        x_ref, mix_ref, norm_ref = ins[:3]
        wo, wc = split(ins[3:], parts, 2)
        q_ref, first_ref = outs
        first = x_ref[own, :].astype(F32)
        for k in range(parts):
            first += dot_nn(mix_ref[k, own, :], wo[k][...])
        yield
        first_ref[own, :] = first
        unit, _ = standardize(first)
        low = affine(unit, norm_ref, 0).astype(BF16)
        yield
        for k in range(parts):
            q_ref[k, own, :] = (dot_nn(low, wc[k][0]) * score).astype(BF16)

    return row_call(
        body,
        "decoder_middle",
        rows,
        [(x, 0), (mix, 1)],
        [norm, *out, *cross],
        [((parts, rows, part), BF16, 1), ((rows, width), F32, 0)],
        [],
        [],
        None,
        4 * rows * width * width,
    )


def ffn_finals(low, act, inner, grad, parts, units, paired, up_out, down_out):
    for k in range(parts):
        if paired:
            half = units // 2
            for h in range(2):
                begin = k * units + h * half
                up_out[0, k, h * half : (h + 1) * half, :] = dot_tn(
                    low[...], inner[:, begin : begin + half]
                ).astype(BF16)
            into = up_out.at[1, k]
        else:
            up_out[k] = dot_tn(low[...], inner[:, k * units : (k + 1) * units]).astype(BF16)
            into = down_out.at[k]
        into[...] = dot_tn(act[:, k * units : (k + 1) * units], grad[...]).astype(BF16)


def decoder_turn(first, mix, cotangent, norm, cross, up, down, paired=False):
    rows, width = first.shape
    parts, part, units = len(cross), cross[0].shape[-1], up[0].shape[1]

    def body(ins, outs, kept, own, all_rows):
        first_ref, cot_ref, mix_ref, norm_ref = ins[:4]
        wc, wu, wd = split(ins[4:], parts, 3)
        result_ref, second_grad_ref, mix_grad_ref = outs
        low_keep, act_keep, inner_keep, third_keep, second_keep, norm_total = kept
        unit, _ = standardize(first_ref[own, :])
        second = affine(unit, norm_ref, 0)
        for k in range(parts):
            second += dot_nt(mix_ref[k, all_rows, :], wc[k][1])
        yield
        unit_two, inv_two = standardize(second)
        third = affine(unit_two, norm_ref, 2)
        low = third.astype(BF16)
        low_keep[all_rows, :] = low
        inner = dot_nn(low, wu[0][...])
        yield
        slopes = []
        for k in range(parts):
            act, slope = gelu_both(inner)
            act = act.astype(BF16)
            slopes.append(slope)
            if k + 1 < parts:
                inner = dot_nn(low, wu[k + 1][...])
            act_keep[all_rows, k * units : (k + 1) * units] = act
            third += dot_nn(act, wd[k][...])
            yield
        unit_three, inv_three = standardize(third)
        result_ref[own, :] = affine(unit_three, norm_ref, 1).astype(BF16)
        grad = norm_back(
            unit_three, inv_three, norm_ref, 1, cot_ref[own, :].astype(F32), norm_total
        )
        grad_low = grad.astype(BF16)
        third_keep[all_rows, :] = grad_low
        grad_act = dot_nt(grad_low, wd[0][...])
        yield
        for k in range(parts):
            grad_inner = (grad_act * slopes[k]).astype(BF16)
            if k + 1 < parts:
                grad_act = dot_nt(grad_low, wd[k + 1][...])
            inner_keep[all_rows, k * units : (k + 1) * units] = grad_inner
            grad += dot_nt(grad_inner, wu[k][...])
            yield
        grad = norm_back(unit_two, inv_two, norm_ref, 2, grad, norm_total)
        second_grad_ref[own, :] = grad
        grad_low = grad.astype(BF16)
        second_keep[all_rows, :] = grad_low
        yield
        for k in range(parts):
            mix_grad_ref[k, own, :] = dot_nn(grad_low, wc[k][1]).astype(BF16)

    def finish(ins, kept, outs):
        mix_ref = ins[0]
        low_keep, act_keep, inner_keep, third_keep, second_keep, norm_total = kept
        for k in range(parts):
            outs[0][k] = dot_tn(second_keep[...], mix_ref[k]).astype(BF16)
        ffn_finals(
            low_keep, act_keep, inner_keep, third_keep, parts, units, paired, outs[1], outs[2]
        )
        outs[-1][...] = norm_total[...]

    ffn = (
        [((2, parts, units, width), BF16)]
        if paired
        else [((parts, width, units), BF16), ((parts, units, width), BF16)]
    )
    whole = (rows, width)
    return row_call(
        body,
        "decoder_turn",
        rows,
        [(first, 0), (cotangent, 0)],
        [mix, norm, *cross, *up, *down],
        [(whole, BF16, 0), (whole, F32, 0), ((parts, rows, part), BF16, 1)],
        [
            (whole, BF16),
            ((rows, parts * units), BF16),
            ((rows, parts * units), BF16),
            (whole, BF16),
            (whole, BF16),
            ((3, 2, width), F32),
        ],
        [((parts, width, part), BF16), *ffn, ((3, 2, width), F32)],
        finish,
        6 * rows * width * width + 12 * rows * width * units * parts,
    )


def decoder_middle_back(first, mix, query_grad, second_grad, norm, out, cross, into=None):
    rows, width = first.shape
    parts, part = len(out), out[0].shape[0]

    def body(ins, outs, kept, own, all_rows):
        first_ref, second_grad_ref, mix_ref, query_grad_ref, norm_ref = ins[:5]
        wo, wc = split(ins[5:], parts, 2)
        first_grad_ref, mix_grad_ref = outs
        low_keep, grad_keep, norm_total = kept
        unit, inv = standardize(first_ref[own, :])
        low_keep[all_rows, :] = affine(unit, norm_ref, 0).astype(BF16)
        grad = second_grad_ref[own, :]
        for k in range(parts):
            grad += dot_nt(query_grad_ref[k, all_rows, :], wc[k][0])
        yield
        grad = norm_back(unit, inv, norm_ref, 0, grad, norm_total)
        first_grad_ref[own, :] = grad
        grad_low = grad.astype(BF16)
        grad_keep[all_rows, :] = grad_low
        yield
        for k in range(parts):
            mix_grad_ref[k, own, :] = dot_nt(grad_low, wo[k][...]).astype(BF16)

    def finish(ins, kept, outs):
        mix_ref, query_grad_ref = ins[:2]
        low_keep, grad_keep, norm_total = kept
        for k in range(parts):
            outs[0][k] = dot_tn(low_keep[...], query_grad_ref[k]).astype(BF16)
            outs[1][k] = dot_tn(mix_ref[k], grad_keep[...]).astype(BF16)
        outs[2][...] = norm_total[...]

    whole = (rows, width)
    return row_call(
        body,
        "decoder_middle_back",
        rows,
        [(first, 0), (second_grad, 0)],
        [mix, query_grad, norm, *out, *cross],
        [(whole, F32, 0), ((parts, rows, part), BF16, 1)],
        [(whole, BF16), (whole, BF16), ((3, 2, width), F32)],
        [
            ((parts, width, part), BF16),
            ((parts, part, width), BF16),
            ((3, 2, width), F32),
        ],
        finish,
        8 * rows * width * width,
        into,
    )


def added(refs, *index):
    total = refs[0][index]
    for ref in refs[1:]:
        total = total.astype(F32) + ref[index].astype(F32)
    return total.astype(BF16)


def encoder_back(
    first, third, mix, memory_grads, cotangent, norm, out, up, down, cross, paired=None, into=None
):
    rows, width = first.shape
    parts, part, units = len(out), out[0].shape[0], up[0].shape[1]
    pieces = len(memory_grads)

    def body(ins, outs, kept, own, all_rows):
        first_ref, third_ref, cot_ref = ins[:3]
        memory_refs, mix_ref, norm_ref = ins[3 : 3 + pieces], ins[3 + pieces], ins[4 + pieces]
        wo, wu, wd, wc = split(ins[5 + pieces :], parts, 4)
        first_grad_ref, mix_grad_ref = outs
        low_keep, memory_keep, mid_keep, act_keep, inner_keep, third_keep, first_keep, norm_total = (
            kept
        )
        grad = cot_ref[own, :].astype(F32)
        for k in range(parts):
            for i in range(2):
                memory = added(memory_refs, k, i, own)
                memory_keep[k, i, all_rows, :] = memory
                grad += dot_nt(memory, wc[k][i])
        yield
        unit, inv = standardize(third_ref[own, :])
        low_keep[all_rows, :] = affine(unit, norm_ref, 1).astype(BF16)
        unit_one, inv_one = standardize(first_ref[own, :])
        low = affine(unit_one, norm_ref, 0).astype(BF16)
        mid_keep[all_rows, :] = low
        inner = dot_nn(low, wu[0][...])
        grad = norm_back(unit, inv, norm_ref, 1, grad, norm_total)
        grad_low = grad.astype(BF16)
        third_keep[all_rows, :] = grad_low
        grad_act = dot_nt(grad_low, wd[0][...])
        yield
        for k in range(parts):
            act, slope = gelu_both(inner)
            if k + 1 < parts:
                inner = dot_nn(low, wu[k + 1][...])
            act_keep[all_rows, k * units : (k + 1) * units] = act.astype(BF16)
            grad_inner = (grad_act * slope).astype(BF16)
            if k + 1 < parts:
                grad_act = dot_nt(grad_low, wd[k + 1][...])
            inner_keep[all_rows, k * units : (k + 1) * units] = grad_inner
            grad += dot_nt(grad_inner, wu[k][...])
            yield
        grad = norm_back(unit_one, inv_one, norm_ref, 0, grad, norm_total)
        first_grad_ref[own, :] = grad
        grad_low = grad.astype(BF16)
        first_keep[all_rows, :] = grad_low
        yield
        for k in range(parts):
            mix_grad_ref[k, own, :] = dot_nt(grad_low, wo[k][...]).astype(BF16)

    def finish(ins, kept, outs):
        mix_ref = ins[0]
        low_keep, memory_keep, mid_keep, act_keep, inner_keep, third_keep, first_keep, norm_total = (
            kept
        )
        if paired:
            ffn_finals(
                mid_keep, act_keep, inner_keep, third_keep, parts, units, True, outs[0], None
            )
            dec_out, dec_query, dec_cross = ins[-3:]
            sides = outs[1]
            for k in range(parts):
                column_blocks(dot_tn(mix_ref[k], first_keep[...]), sides, 0, k, 0)
                column_blocks(dec_out[k], sides, 1, k, 0)
                for i in range(2):
                    here = slice((1 + i) * width, (2 + i) * width)
                    sides[0, k, here, :] = dot_tn(low_keep[...], memory_keep[k, i]).astype(BF16)
                    sides[1, k, here, :] = (dec_query, dec_cross)[i][k]
        else:
            for k in range(parts):
                for i in range(2):
                    outs[0][k, i] = dot_tn(low_keep[...], memory_keep[k, i]).astype(BF16)
                outs[1][k] = dot_tn(mix_ref[k], first_keep[...]).astype(BF16)
            ffn_finals(
                mid_keep, act_keep, inner_keep, third_keep, parts, units, False, outs[2], outs[3]
            )
        outs[-1][...] = norm_total[...]

    if paired:
        finals = [((2, parts, units, width), BF16), ((2, parts, 3 * width, part), BF16)]
    else:
        finals = [
            ((parts, 2, width, part), BF16),
            ((parts, part, width), BF16),
            ((parts, width, units), BF16),
            ((parts, units, width), BF16),
        ]
    whole = (rows, width)
    return row_call(
        body,
        "encoder_back",
        rows,
        [(first, 0), (third, 0), (cotangent, 0)] + [(m, 2) for m in memory_grads],
        [mix, norm, *out, *up, *down, *cross, *(paired or [])],
        [(whole, F32, 0), ((parts, rows, part), BF16, 1)],
        [
            (whole, BF16),
            ((parts, 2, rows, part), BF16),
            (whole, BF16),
            ((rows, parts * units), BF16),
            ((rows, parts * units), BF16),
            (whole, BF16),
            (whole, BF16),
            ((3, 2, width), F32),
        ],
        [*finals, ((3, 2, width), F32)],
        finish,
        12 * rows * width * width + 10 * rows * width * units * parts,
        into,
    )


def column_blocks(wide, into, core, k, row):
    rows, columns = wide.shape[0], wide.shape[1] // 2
    for half in range(2):
        into[core, k, row + half * rows : row + (half + 1) * rows, :] = wide[
            :, half * columns : (half + 1) * columns
        ].astype(BF16)


def input_part(refs, kept, own, all_rows, norm_ref, w, with_norm):
    x_ref, first_grad_ref, key_refs, query_grad_ref, grad_ref = refs
    low_keep, key_keep, norm_total = kept
    grad = first_grad_ref[own, :]
    for k in range(len(w)):
        grad += dot_nt(query_grad_ref[k, all_rows, :], w[k][0])
        for i in range(2):
            member = added(key_refs, k, i, own)
            key_keep[k, i, all_rows, :] = member
            grad += dot_nt(member, w[k][1 + i])
    yield
    low = x_ref[own, :]
    if with_norm:
        unit, inv = standardize(low.astype(F32))
        low = affine(unit, norm_ref, 2).astype(BF16)
        grad = norm_back(unit, inv, norm_ref, 2, grad, norm_total)
    low_keep[all_rows, :] = low
    grad_ref[own, :] = grad.astype(BF16)


def input_sums(kept, query_grad_ref, into, parts):
    low_keep, key_keep, _ = kept
    for k in range(parts):
        both = jnp.concatenate(
            [dot_tn(low_keep[...], query_grad_ref[k])]
            + [dot_tn(low_keep[...], key_keep[k, i]) for i in range(2)],
            axis=0,
        )
        half = both.shape[0] // 2
        for core in range(2):
            column_blocks(both[core * half : (core + 1) * half], into, core, k, 0)


def norm_lines(sides, into, parts, row):
    for core, table in enumerate(sides):
        lines = [
            table[slot, i : i + 1, h * PAIR : (h + 1) * PAIR]
            for slot in range(3)
            for i in range(2)
            for h in range(table.shape[-1] // PAIR)
        ]
        lines.append(jnp.zeros((2 * PAIR - len(lines), PAIR), F32))
        lines = jnp.concatenate(lines, axis=0).astype(BF16)
        for k in range(parts):
            into[core, k, row:, :] = lines


def input_back(x, first_grad, query_grad, key_grads, norm, weights, with_norm):
    x = at(x)
    rows, width = x.shape
    parts, part = len(weights), weights[0].shape[-1]
    pieces = len(key_grads)
    key_grads = [at(g) for g in key_grads]

    def body(ins, outs, kept, own, all_rows):
        x_ref, first_grad_ref = ins[:2]
        key_refs, query_grad_ref, norm_ref = ins[2 : 2 + pieces], ins[2 + pieces], ins[3 + pieces]
        refs = x_ref, first_grad_ref, key_refs, query_grad_ref, outs[0]
        yield from input_part(refs, kept, own, all_rows, norm_ref, ins[4 + pieces :], with_norm)

    def finish(ins, kept, outs):
        query_grad_ref = ins[0]
        low_keep, key_keep, norm_total = kept
        for k in range(parts):
            outs[0][k, 0] = dot_tn(low_keep[...], query_grad_ref[k]).astype(BF16)
            for i in range(2):
                outs[0][k, 1 + i] = dot_tn(low_keep[...], key_keep[k, i]).astype(BF16)
        outs[1][...] = norm_total[...]

    whole = (rows, width)
    return row_call(
        body,
        "input_back",
        rows,
        [(x, 0), (first_grad, 0)] + [(g, 2) for g in key_grads],
        [query_grad, norm, *weights],
        [(whole, BF16, 0)],
        [(whole, BF16), ((parts, 2, rows, part), BF16), ((3, 2, width), F32)],
        [((parts, 3, width, part), BF16), ((3, 2, width), F32)],
        finish,
        12 * rows * width * width,
    )


def widen_keys(span, kv_refs, key_e, key_o, value_e, value_o, rows):
    lane = lax.broadcasted_iota(jnp.int32, (rows, PAIR), 1)
    place = lax.broadcasted_iota(jnp.int32, (rows, PAIR), 0)
    low = lane < HALF
    for g, kv_ref in enumerate(kv_refs):
        spot = place + span[2 + g]
        live = (spot >= span[0]) & (spot < span[1])
        bias = jnp.where(live, 0.0, MASKED)
        keys, values = kv_ref[0].astype(F32), kv_ref[1].astype(F32)
        own = pl.ds(g * rows, rows)
        key_e[own, :] = jnp.where(low, keys, jnp.where(lane == HALF, bias, 1.0)).astype(BF16)
        key_o[own, :] = jnp.where(low, jnp.where(lane == 0, bias, 1.0), keys).astype(BF16)
        value_e[own, :] = jnp.where(low, values, 1.0).astype(BF16)
        value_o[own, :] = jnp.where(low, 1.0, values).astype(BF16)


class Pairs:
    def __init__(self, query):
        self.sides = query.shape[:-3]
        self.parts, self.rows, self.part = query.shape[-3:]
        self.per_part = self.part // PAIR
        self.per_side = self.parts * self.per_part
        self.count = self.per_side * math.prod(self.sides)

    def side(self, i):
        return (i // self.per_side,) if self.sides else ()

    def place(self, i):
        i = i % self.per_side
        return i // self.per_part, i % self.per_part

    def query_spec(self, array):
        def index(i):
            part, column = self.place(i)
            return *self.side(i), part, 0, column

        none = (None,) * len(self.sides)
        return at(array).spec((*none, None, self.rows, PAIR), index)

    def kv_spec(self, array):
        def index(i):
            part, column = self.place(i)
            return *self.side(i), part, 0, 0, column

        none = (None,) * len(self.sides)
        return at(array).spec((*none, None, 2, self.rows, PAIR), index)

    def lse_spec(self):
        none = (None,) * len(self.sides)
        return pl.BlockSpec(
            (*none, self.rows, PAIR), lambda i: (*self.side(i), 0, i % self.per_side)
        )

    def span(self, span_ref, i):
        side = i // self.per_side if self.sides else 0
        return [span_ref[side, j] for j in range(span_ref.shape[1])]


def attend(query, kv_pieces, span, block, carrier=None, slots=1):
    query, kv_pieces = at(query), [at(piece) for piece in kv_pieces]
    carrier = carrier or Carry()
    heads_of = Pairs(query)
    rows, pairs = heads_of.rows, heads_of.count
    pieces = len(kv_pieces)
    keys = rows * pieces
    n_carry = len(carrier.ins)
    blocks = rows // block
    stride = blocks // slots

    def kernel(span_ref, q_ref, *refs):
        kv_refs, refs = refs[:pieces], refs[pieces:]
        carry_ins, refs = refs[:n_carry], refs[n_carry:]
        out_ref, lse_ref, refs = refs[0], refs[1], refs[2:]
        carry_outs, refs = refs[: len(carrier.outs)], refs[len(carrier.outs) :]
        key_e, key_o, value_e, value_o = refs[:4]

        def carry(slot):
            place = pl.program_id(0)
            carrier.run(place, slot, slots, pairs * slots, carry_ins, carry_outs, refs[4:])

        carry(0)
        span = heads_of.span(span_ref, pl.program_id(0))
        widen_keys(span, kv_refs, key_e, key_o, value_e, value_o, rows)
        lane = lax.broadcasted_iota(jnp.int32, (block, PAIR), 1)
        low = lane < HALF
        units = []
        for i in range(blocks):
            query = q_ref[i * block : (i + 1) * block, :].astype(F32)
            first = jnp.where(low, query, jnp.where(lane == HALF, 1.0, 0.0)).astype(BF16)
            second = jnp.where(low, jnp.where(lane == 0, 1.0, 0.0), query).astype(BF16)
            units += [(first, key_e, value_e), (second, key_o, value_o)]

        def scores_of(unit):
            return dot_nt(unit[0], unit[1][...])

        ahead = scores_of(units[0])
        tops, sums = [], []
        for u, unit in enumerate(units):
            if u and u % (2 * stride) == 0:
                carry(u // (2 * stride))
            scores = ahead
            if u + 1 < len(units):
                ahead = scores_of(units[u + 1])
            top = jnp.max(scores, axis=1, keepdims=True)
            tops.append(top)
            sums.append(dot_nn(jnp.exp2(scores - top).astype(BF16), unit[2][...]))
            if u % 2:
                own = slice(u // 2 * block, (u // 2 + 1) * block)
                top = jnp.where(low, tops[u], tops[u - 1])
                weight = jnp.where(low, sums[u], sums[u - 1])
                lse_ref[own, :] = top + LOG2E * jnp.log(weight)
                mixed = jnp.where(low, sums[u - 1], sums[u])
                out_ref[own, :] = (mixed / pltpu.roll(weight, HALF, 1)).astype(BF16)

    query_spec, kv_spec = heads_of.query_spec, heads_of.kv_spec
    lse_spec = heads_of.lse_spec()
    plain = jax.ShapeDtypeStruct(query.shape, BF16)
    hold = pl.BlockSpec(memory_space=pl.ANY)
    return pl.pallas_call(
        kernel,
        grid=(pairs,),
        in_specs=[pl.BlockSpec(memory_space=pltpu.SMEM), query_spec(query)]
        + [kv_spec(piece) for piece in kv_pieces]
        + [hold] * n_carry,
        out_specs=[query_spec(plain), lse_spec] + [hold] * len(carrier.outs),
        scratch_shapes=[pltpu.VMEM((keys, PAIR), BF16)] * 4 + carrier.scratch,
        out_shape=[plain, jax.ShapeDtypeStruct((*heads_of.sides, rows, heads_of.per_side * PAIR), F32)] + carrier.outs,
        compiler_params=pltpu.CompilerParams(vmem_limit_bytes=VMEM, **carrier.params),
        cost_estimate=pl.CostEstimate(
            flops=16 * rows * keys * pairs * PAIR,
            bytes_accessed=8 * rows * pairs * PAIR * pieces,
            transcendentals=0,
        ),
        name="attend",
    )(span, query.array, *[piece.array for piece in kv_pieces], *carrier.ins)


def attend_back(
    query, kv_pieces, mix, mix_grad, lse, span, chunk, carrier=None, slots=1
):
    query, kv_pieces = at(query), [at(piece) for piece in kv_pieces]
    mix, mix_grad = at(mix), at(mix_grad)
    heads_of = Pairs(query)
    rows, pairs = heads_of.rows, heads_of.count
    pieces = len(kv_pieces)
    keys = rows * pieces
    scale = 1.0 / math.sqrt(HALF)
    swaps = carrier is not None
    carrier = carrier or Carry()
    n_carry = len(carrier.ins)
    kept = 1 if swaps else pieces
    chunks = keys // chunk
    stride = chunks // slots

    def kernel(span_ref, q_ref, mix_ref, grad_ref, lse_ref, *refs):
        kv_refs, refs = refs[:pieces], refs[pieces:]
        carry_ins, refs = refs[:n_carry], refs[n_carry:]
        dq_ref, dkv_refs, refs = refs[0], refs[1 : pieces + 1], refs[pieces + 1 :]
        carry_outs, refs = refs[: len(carrier.outs)], refs[len(carrier.outs) :]
        key_e, key_o, value_e, value_o, key_t = refs[:5]
        refs = refs[5:]
        if swaps:
            given, swap_sems, refs = refs[0], refs[1], refs[2:]
        pair = pl.program_id(0)

        def carry(slot):
            carrier.run(pair, slot, slots, pairs * slots, carry_ins, carry_outs, refs)

        carry(0)
        span = heads_of.span(span_ref, pl.program_id(0))
        widen_keys(span, kv_refs, key_e, key_o, value_e, value_o, rows)
        for g, kv_ref in enumerate(kv_refs):
            key_t[:, g * rows : (g + 1) * rows] = kv_ref[0].T
        lane = lax.broadcasted_iota(jnp.int32, (rows, PAIR), 1)
        low = lane < HALF
        query, grad = q_ref[...].astype(F32), grad_ref[...].astype(F32)
        product = mix_ref[...].astype(F32) * grad
        inner = jnp.where(
            low,
            jnp.sum(jnp.where(low, 0.0, product), axis=1, keepdims=True),
            jnp.sum(jnp.where(low, product, 0.0), axis=1, keepdims=True),
        )
        spot = jnp.where(low, lane, lane - HALF)

        def three(value, shift):
            high = value.astype(BF16).astype(F32)
            rest = value - high
            mid = rest.astype(BF16).astype(F32)
            return jnp.where(
                spot == shift,
                high,
                jnp.where(
                    spot == shift + 1, mid, jnp.where(spot == shift + 2, rest - mid, 0.0)
                ),
            )

        lse = three(-lse_ref[...], 1) + jnp.where(spot == 0, 1.0, 0.0)
        inner = three(-inner, 0)
        heads = [
            (
                key,
                value,
                jnp.where(own, query, lse).astype(BF16).T,
                jnp.where(own, grad, inner).astype(BF16).T,
                jnp.where(own, query, 0.0).astype(BF16),
                jnp.where(own, grad, 0.0).astype(BF16),
            )
            for own, key, value in ((low, key_e, value_e), (~low, key_o, value_o))
        ]
        units = [(c * chunk, h) for c in range(chunks) for h in range(2)]

        def front(unit):
            begin, h = unit
            own = slice(begin, begin + chunk)
            key, value, q_wide, g_wide, _, _ = heads[h]
            return dot_nn(key[own, :], q_wide), dot_nn(value[own, :], g_wide)

        ahead = front(units[0])
        dq = [None, None]
        for u, (begin, h) in enumerate(units):
            if u and u % (2 * stride) == 0:
                carry(u // (2 * stride))
            scores, dprobs = ahead
            if u + 1 < len(units):
                ahead = front(units[u + 1])
            probs = jnp.exp2(scores)
            dscores = (probs * dprobs).astype(BF16)
            _, _, _, _, q_own, g_own = heads[h]
            step_v = dot_nn(probs.astype(BF16), g_own)
            step_k = dot_nn(dscores, q_own)
            step_q = dot_nn(key_t[h * HALF : (h + 1) * HALF, begin : begin + chunk], dscores)
            dq[h] = step_q if dq[h] is None else dq[h] + step_q
            if h == 0:
                dv, dk = step_v, step_k
            else:
                g, first = begin // rows, begin % rows
                own = slice(first, first + chunk)
                dk = ((dk + step_k) * (1.0 / LOG2E)).astype(BF16)
                dv = (dv + step_v).astype(BF16)
                if g < kept:
                    dkv_refs[g][0, own, :] = dk
                    dkv_refs[g][1, own, :] = dv
                else:
                    given[pair, 0, own, :] = dk
                    given[pair, 1, own, :] = dv
        dq_ref[...] = (jnp.concatenate(dq, axis=0).T * scale).astype(BF16)
        if swaps:
            part, column = heads_of.place(pair)
            columns = pl.ds(pl.multiple_of(column * PAIR, PAIR), PAIR)
            spot = (*heads_of.side(pair), part, slice(None), slice(None), columns)

            def swap(i):
                return remote(
                    given.at[i],
                    dkv_refs[1].at[spot],
                    swap_sems.at[0, i],
                    swap_sems.at[1, i],
                    where_is("near"),
                )

            swap(pair).start()

            @pl.when(pair == pairs - 1)
            def _():
                for i in range(pairs):
                    swap(i).wait()

    query_spec, kv_spec = heads_of.query_spec, heads_of.kv_spec
    lse_spec = heads_of.lse_spec()
    plain = jax.ShapeDtypeStruct(query.shape, BF16)
    plain_kv = jax.ShapeDtypeStruct(
        (*heads_of.sides, heads_of.parts, 2, rows, heads_of.part), BF16
    )
    hold = pl.BlockSpec(memory_space=pl.ANY)
    swap_scratch = [
        pltpu.VMEM((pairs, 2, rows, PAIR), BF16),
        pltpu.SemaphoreType.DMA((2, pairs)),
    ]
    out = pl.pallas_call(
        kernel,
        grid=(pairs,),
        in_specs=[pl.BlockSpec(memory_space=pltpu.SMEM)]
        + [query_spec(a) for a in (query, mix, mix_grad)]
        + [lse_spec]
        + [kv_spec(piece) for piece in kv_pieces]
        + [hold] * n_carry,
        out_specs=[query_spec(plain)]
        + [kv_spec(plain_kv)] * kept
        + [hold] * (pieces - kept + len(carrier.outs)),
        scratch_shapes=[pltpu.VMEM((keys, PAIR), BF16)] * 4
        + [pltpu.VMEM((PAIR, keys), BF16)]
        + (swap_scratch if swaps else [])
        + carrier.scratch,
        out_shape=[plain] + [plain_kv] * pieces + carrier.outs,
        compiler_params=pltpu.CompilerParams(vmem_limit_bytes=VMEM, **carrier.params),
        cost_estimate=pl.CostEstimate(
            flops=40 * rows * keys * pairs * PAIR,
            bytes_accessed=16 * rows * pairs * PAIR * pieces,
            transcendentals=0,
        ),
        name="attend_back",
    )(
        span,
        query.array,
        mix.array,
        mix_grad.array,
        lse,
        *[piece.array for piece in kv_pieces],
        *carrier.ins,
    )
    return out[0], out[1 : pieces + 1], out[pieces + 1 :]


def spots():
    return lax.axis_index("section"), lax.axis_index("dp"), lax.axis_index("tensor")


def dp_peer(group, level):
    return group + (1 << level) * (1 - 2 * ((group // (1 << level)) % 2))


def where_is(peer):
    section, group, tensor = spots()
    if peer == "near":
        return {"section": 1 - section}
    if peer == "over":
        return {"tensor": 1 - tensor}
    if peer == "cross":
        return {"section": 1 - section, "tensor": 1 - tensor}
    return {"dp": dp_peer(group, peer)}


def remote(source, target, sent, landed, where):
    return pltpu.make_async_remote_copy(
        src_ref=source,
        dst_ref=target,
        send_sem=sent,
        recv_sem=landed,
        device_id=where,
        device_id_type=pl.DeviceIdType.MESH,
    )


def greet(peers):
    barrier = pltpu.get_barrier_semaphore()
    for peer in peers:
        pl.semaphore_signal(
            barrier, inc=1, device_id=where_is(peer), device_id_type=pl.DeviceIdType.MESH
        )
    pl.semaphore_wait(barrier, len(peers))


class Carry:
    def __init__(self, tasks=(), collective=None):
        self.tasks = list(tasks)
        self.ins = [a for task in self.tasks for a in task.ins]
        self.outs = [a for task in self.tasks for a in task.outs]
        self.scratch = [a for task in self.tasks for a in task.scratch]
        self.peers = []
        for task in self.tasks:
            self.peers += [peer for peer in task.peers if peer not in self.peers]
        self.params = (
            dict(collective_id=collective, has_side_effects=True) if self.tasks else {}
        )

    def plan(self, steps, ins, outs, scratch):
        plan = {}
        if self.tasks:
            plan[0] = [lambda: greet(self.peers)]
        events = []
        for task in self.tasks:
            i, o, s = len(task.ins), len(task.outs), len(task.scratch)
            events += task.events(steps, ins[:i], outs[:o], scratch[:s])
            ins, outs, scratch = ins[i:], outs[o:], scratch[s:]
        for step, rank, action in sorted(events, key=lambda event: event[:2]):
            assert 0 <= step < steps
            plan.setdefault(step, []).append(action)
        return plan

    def run(self, place, slot, slots, steps, ins, outs, scratch):
        for step, actions in self.plan(steps, ins, outs, scratch).items():
            if step % slots == slot:

                @pl.when(place == step // slots)
                def _():
                    for action in actions:
                        action()


GROUP = ["near", "over", "cross"]


class RowCopies:
    def __init__(self, copies, arrivals, sems, room=None):
        self.copies, self.arrivals, self.room = copies, arrivals, room
        self.sent, self.landed, self.kept = sems

    def copy(self, i):
        source, target, slot, section, tensor, _ = self.copies[i]
        return remote(
            source,
            target,
            self.sent.at[i],
            self.landed.at[slot],
            {"section": section, "tensor": tensor},
        )

    def keep(self, i):
        source, target, slot = self.copies[i][:3]
        return pltpu.make_async_copy(
            source, target if self.room is None else self.room, self.kept.at[slot]
        )

    def keep_on(self):
        for i in range(len(self.copies)):

            @pl.when(self.here(i, True))
            def _():
                self.keep(i).wait()
                target, slot = self.copies[i][1:3]
                pltpu.make_async_copy(self.room, target, self.kept.at[slot]).start()

    def here(self, i, stays):
        section, _, tensor = spots()
        _, _, _, to_section, to_tensor, condition = self.copies[i]
        own = (to_section == section) & (to_tensor == tensor)
        return condition & (own if stays else jnp.logical_not(own))

    def start(self):
        for i in range(len(self.copies)):

            @pl.when(self.here(i, True))
            def _():
                self.keep(i).start()

            @pl.when(self.here(i, False))
            def _():
                self.copy(i).start()

    def wait_sent(self):
        for i in range(len(self.copies)):

            @pl.when(self.here(i, False))
            def _():
                self.copy(i).wait_send()

    def wait_arrival(self, i):
        section, _, tensor = spots()
        target, slot, from_section, from_tensor, condition = self.arrivals[i]
        own = (from_section == section) & (from_tensor == tensor)
        source = self.copies[0][0]

        @pl.when(condition & own)
        def _():
            stays = source if self.room is None else self.room
            pltpu.make_async_copy(stays, target, self.kept.at[slot]).wait()

        @pl.when(condition & jnp.logical_not(own))
        def _():
            remote(
                source, target, self.sent.at[0], self.landed.at[slot], where_is("near")
            ).wait_recv()


def row_sems(pieces=1):
    return [pltpu.SemaphoreType.DMA((2 * pieces,))] * 3


def spread_rows(source, target, sems, sides=(0, 1), room=None, pieces=1):
    section, _, tensor = spots()
    yes = section >= 0
    sends = yes if len(sides) == 2 else section == sides[0]
    count = source.shape[1] // pieces
    copies, arrivals = [], []
    for i in range(pieces):
        own = pl.ds(i * count, count)
        for row in range(2):
            slot = 2 * i + section
            copies.append(
                (source.at[row, own, :], target.at[section, own, :], slot, tensor, row, sends)
            )
        for side in sides:
            arrivals.append((target.at[side, own, :], 2 * i + side, side, section, yes))
    return RowCopies(copies, arrivals, sems, room)


def return_rows(source, target, sems, side, room):
    section, _, tensor = spots()
    copies = [(source, target.at[tensor], tensor, side, section, section >= 0)]
    arrivals = [(target.at[row], row, tensor, row, section == side) for row in range(2)]
    return RowCopies(copies, arrivals, sems, room)


class SpreadRows:
    peers = GROUP
    staged = True

    def __init__(self, array, sides, begin=0):
        self.ins, self.sides, self.begin = [array], sides, begin
        self.outs = [jax.ShapeDtypeStruct(array.shape, array.dtype)]
        self.scratch = row_sems() + [pltpu.VMEM(array.shape[-2:], array.dtype)]

    def make(self, ins, outs, scratch):
        return spread_rows(ins[0], outs[0], scratch[:3], self.sides, scratch[3])

    def events(self, steps, ins, outs, scratch):
        def make():
            return self.make(ins, outs, scratch)

        def finish():
            rows = make()
            for i in range(len(rows.arrivals)):
                rows.wait_arrival(i)
            rows.wait_sent()

        events = [(self.begin, 1, lambda: make().start()), (steps - 1, LAST, finish)]
        if self.staged:
            events.append((self.begin + 1, 1, lambda: make().keep_on()))
        return events


class ReturnRows(SpreadRows):
    def __init__(self, array, side, begin=0, staged=True):
        self.ins, self.side, self.begin, self.staged = [array], side, begin, staged
        self.outs = [jax.ShapeDtypeStruct((2, *array.shape), array.dtype)]
        self.scratch = row_sems() + [pltpu.VMEM(array.shape, array.dtype)] * staged

    def make(self, ins, outs, scratch):
        room = scratch[3] if len(scratch) > 3 else None
        return return_rows(ins[0], outs[0], scratch[:3], self.side, room)


class WeightCopies:
    @staticmethod
    def sems(count):
        return pltpu.SemaphoreType.DMA((3 + 8 * count,))

    def __init__(self, source, target, sem, room=None, count=1):
        section, group, _ = spots()
        rows = source.shape[0] // (2 * count)
        bit = group % 2
        here, stays = target.at[section, 1], target.at[section, 0]
        self.room = room
        if room is None:
            self.kept = pltpu.make_async_copy(source, stays, sem.at[0])
        else:
            self.first = pltpu.make_async_copy(source, room, sem.at[0])
            self.kept = pltpu.make_async_copy(room, stays, sem.at[0])
        self.near = remote(source, stays, sem.at[1], sem.at[2], where_is("near"))
        self.over, self.side, self.onward, self.last = [], [], [], []
        for i in range(count):
            own = pl.ds(pl.multiple_of((bit * count + i) * rows, 16), rows)
            other = pl.ds(pl.multiple_of(((1 - bit) * count + i) * rows, 16), rows)
            source_own, own, other = source.at[own], here.at[own], here.at[other]
            pairs = [(sem.at[3 + 8 * i + 2 * j], sem.at[4 + 8 * i + 2 * j]) for j in range(4)]
            self.over.append(remote(source_own, own, *pairs[0], where_is("over")))
            self.side.append(remote(own, own, *pairs[1], where_is(0)))
            self.onward.append(remote(own, own, *pairs[2], where_is("near")))
            self.last.append(remote(other, other, *pairs[3], where_is("near")))

    def start(self):
        for copy in self.over:
            copy.start()
        self.near.start()
        if self.room is None:
            self.kept.start()
        else:
            self.first.start()

    def keep_on(self):
        self.first.wait()
        self.kept.start()

    def forward(self, i):
        self.over[i].wait_recv()
        self.side[i].start()
        self.onward[i].start()

    def forward_last(self, i):
        self.side[i].wait_recv()
        self.last[i].start()

    def finish(self):
        self.kept.wait()
        self.near.wait()
        for over, side, onward, last in zip(self.over, self.side, self.onward, self.last):
            over.wait_send()
            side.wait_send()
            onward.wait()
            last.wait()


class SpreadWeight:
    peers = ["near", "over", 0]

    def __init__(self, weight, forwards, lasts):
        self.ins = [weight]
        self.outs = [jax.ShapeDtypeStruct((2, 2, *weight.shape), weight.dtype)]
        self.forwards, self.lasts = forwards, lasts
        self.scratch = [
            WeightCopies.sems(len(forwards)),
            pltpu.VMEM(weight.shape, weight.dtype),
        ]

    def events(self, steps, ins, outs, scratch):
        def copies():
            return WeightCopies(ins[0], outs[0], *scratch, len(self.forwards))

        def forward(i):
            return lambda: copies().forward(i)

        def forward_last(i):
            return lambda: copies().forward_last(i)

        return (
            [(0, 0, lambda: copies().start()), (1, 0, lambda: copies().keep_on())]
            + [(when, 1, forward(i)) for i, when in enumerate(self.forwards)]
            + [(when, 2, forward_last(i)) for i, when in enumerate(self.lasts)]
            + [(steps - 1, LAST, lambda: copies().finish())]
        )


class Reduce:
    def __init__(self, source, chunk, begins, pace, only=None, levels=None):
        self.ins = [source]
        self.chunk, self.begins, self.only = chunk, begins, only
        self.count = source.shape[-2] // chunk
        assert self.count == len(begins)
        self.levels = list(range(lax.axis_size("dp").bit_length() - 1))
        if levels is not None:
            self.levels = levels
        depth = len(self.levels)
        self.peers = []
        self.stages = []
        if only != "slice":
            self.peers += ["near", "over"]
            self.stages += ["enter", "cross", "over"]
        if only != "chip":
            self.peers += ["near", *self.levels]
            self.stages += ["load", "loaded"] if only == "slice" else []
            self.stages += [("halve", i) for i in range(depth)]
            self.stages += [("double", i) for i in reversed(range(depth))]
        assert len(pace) == len(self.stages) - 1
        self.dues = [sum(pace[:i]) for i in range(len(self.stages))]
        width = source.shape[-1]
        whole = jax.ShapeDtypeStruct((self.count * chunk, width), BF16)
        self.outs = [whole] if only == "chip" else [whole] * 2

        def room(*shape):
            return pltpu.VMEM((self.count, *shape, width), BF16)

        self.scratch = [room(2, chunk)]
        if only != "slice":
            self.scratch += [room(2, chunk), room(chunk)]
        if only != "chip":
            halves = [room(chunk >> (i + 1)) for i in range(depth)]
            self.scratch += [room(chunk)] + halves + halves
        self.scratch += [pltpu.SemaphoreType.DMA((2 + 2 * (3 + 2 * depth), self.count))]

    def events(self, steps, ins, outs, scratch):
        chunk, depth = self.chunk, len(self.levels)
        source, refs = ins[0], list(scratch)
        own, sems = refs[0], refs[-1]
        refs = refs[1:-1]
        if self.only != "slice":
            chip, other = refs[:2]
            refs = refs[2:]
        if self.only != "chip":
            full, halves, doubles = refs[0], refs[1 : 1 + depth], refs[1 + depth :]

        def bounds(i):
            _, group, _ = spots()
            begin = 0
            for j in range(i):
                bit = (group // (1 << self.levels[j])) % 2
                begin = begin + bit * (chunk >> (j + 1))
            return begin

        def keeps(i):
            return pl.ds(pl.multiple_of(bounds(i + 1), 16), chunk >> (i + 1))

        def gives(i):
            begin = 2 * bounds(i) + (chunk >> (i + 1)) - bounds(i + 1)
            return pl.ds(pl.multiple_of(begin, 16), chunk >> (i + 1))

        def pair(kind, c):
            return sems.at[2 + 2 * kind, c], sems.at[3 + 2 * kind, c]

        def rows_of(c):
            return pl.ds(c * chunk, chunk)

        def load(c):
            if self.only == "slice":
                return pltpu.make_async_copy(
                    source.at[rows_of(c), :], own.at[c, 0], sems.at[0, c]
                )
            section, _, _ = spots()
            return pltpu.make_async_copy(
                source.at[section, :, rows_of(c), :], own.at[c], sems.at[0, c]
            )

        def cross(c):
            section, _, _ = spots()
            return remote(
                source.at[1 - section, :, rows_of(c), :],
                chip.at[c],
                *pair(0, c),
                where_is("near"),
            )

        def over(c):
            return remote(own.at[c, 1], other.at[c], *pair(1, c), where_is("over"))

        def halve(i, c):
            return remote(
                own.at[c, 0, gives(i), :],
                halves[i].at[c],
                *pair(3 + i, c),
                where_is(self.levels[i]),
            )

        def double(i, c):
            return remote(
                full.at[c, keeps(i), :],
                doubles[i].at[c],
                *pair(3 + depth + i, c),
                where_is(self.levels[i]),
            )

        def store(c):
            kept = own.at[c, 0] if self.only == "chip" else full.at[c]
            return pltpu.make_async_copy(kept, outs[0].at[rows_of(c), :], sems.at[1, c])

        def tell(c):
            return remote(
                full.at[c], outs[1].at[rows_of(c), :], *pair(2, c), where_is("near")
            )

        def act(stage, c):
            if stage == "enter":
                load(c).start()
                cross(c).start()
            elif stage == "load":
                load(c).start()
            elif stage == "loaded":
                load(c).wait()
                halve(0, c).start()
            elif stage == "cross":
                load(c).wait()
                cross(c).wait()
                own[c] = own[c] + chip[c]
                over(c).start()
            elif stage == "over":
                over(c).wait()
                own[c, 0] = own[c, 0] + other[c]
                if self.only == "chip":
                    store(c).start()
                else:
                    halve(0, c).start()
            elif stage[0] == "halve":
                i = stage[1]
                halve(i, c).wait()
                mine = keeps(i)
                total = own[c, 0, mine, :] + halves[i][c]
                if i < depth - 1:
                    own[c, 0, mine, :] = total
                    halve(i + 1, c).start()
                else:
                    full[c, mine, :] = total
                    double(i, c).start()
            else:
                i = stage[1]
                double(i, c).wait()
                full[c, gives(i), :] = doubles[i][c]
                if i:
                    double(i - 1, c).start()
                else:
                    store(c).start()
                    tell(c).start()

        def leave(c):
            store(c).wait()
            if self.only != "chip":
                tell(c).wait()

        events = []
        for c, begin in enumerate(self.begins):
            for i, (stage, due) in enumerate(zip(self.stages, self.dues)):
                events.append((begin + due, -i, functools.partial(act, stage, c)))
            events.append((steps - 1, LAST, functools.partial(leave, c)))
        return events


def close_down(x, firsts, q_grad, kv_grads, norm, qkv, norm_grads, schedule, collective):
    _, rows, width = x.shape
    parts, _, _, part = qkv.shape[1:]
    half = 3 * width // 2
    shapes = [(2, parts, 2 * half + extra, PAIR) for extra in (2 * PAIR, 0)]
    dec_steps, enc_steps, returns, steps = schedule
    whole = (rows, width)
    grad_shape = jax.ShapeDtypeStruct(whole, BF16)
    carrier = Carry(
        [
            Reduce(jax.ShapeDtypeStruct(shapes[0], BF16), 2 * PAIR, *enc_steps),
            Reduce(jax.ShapeDtypeStruct(shapes[1], BF16), 2 * PAIR, *dec_steps),
            ReturnRows(grad_shape, 0, returns[0], False),
            ReturnRows(grad_shape, 1, returns[1], False),
        ],
        collective,
    )
    halves = 2
    count, sub = rows // halves, min(256, rows // halves)

    def kernel(*refs):
        x_in, first_ins, q_in, kv_ins, norm_in, qkv_in, refs = (
            refs[0],
            refs[1:3],
            refs[3],
            refs[4:6],
            refs[6],
            refs[7],
            refs[8:],
        )
        norm_grad_refs, refs = refs[: len(norm_grads)], refs[len(norm_grads) :]
        outs, refs = refs[: len(carrier.outs)], refs[len(carrier.outs) :]
        x_room, first_room, q_room, kv_room, norm_room, qkv_room, sems = refs[:7]
        low, keys, total, grads, enc_sum, dec_sum, *rest = refs[7:]
        ins = [enc_sum, dec_sum, grads.at[0], grads.at[1]]
        plan = carrier.plan(steps, ins, outs, rest)
        loads = []

        def load(source, target):
            copy = pltpu.make_async_copy(source, target, sems.at[len(loads)])
            copy.start()
            loads.append(copy)
            return copy

        arrivals = {}
        for side in (1, 0):
            for i in range(halves):
                own = pl.ds(i * count, count)
                arrivals[side, i] = [
                    load(first_ins[side].at[own, :], first_room.at[side, own, :]),
                    load(q_in.at[side, :, own, :], q_room.at[side, :, own, :]),
                    load(kv_ins[0].at[side, :, :, own, :], kv_room.at[0, side, :, :, own, :]),
                    load(kv_ins[1].at[side, :, :, own, :], kv_room.at[1, side, :, :, own, :]),
                    load(x_in.at[side, own, :], x_room.at[side, own, :]),
                ]
                if i == 0:
                    arrivals[side, i] += [
                        load(qkv_in.at[side], qkv_room.at[side]),
                        load(norm_in.at[side], norm_room.at[side]),
                    ]
        total[...] = jnp.zeros_like(total)

        def piece(side, i):
            for copy in arrivals[side, i]:
                copy.wait()
            kept = low, keys, total
            refs = (
                x_room.at[side],
                first_room.at[side],
                [kv_room.at[0, side], kv_room.at[1, side]],
                q_room.at[side],
                grads.at[side],
            )
            w = [qkv_room.at[side, k] for k in range(parts)]
            turns = []
            for begin in range(i * count, (i + 1) * count, sub):
                own = slice(begin, begin + sub)
                turns.append(
                    input_part(refs, kept, own, own, norm_room.at[side], w, side == 0)
                )
            while turns:
                turns = [turn for turn in turns if next(turn, LAST) is not LAST]
            if i == halves - 1:
                into = (enc_sum, dec_sum)[side]
                input_sums(kept, q_room.at[side], into, parts)
                if side == 0:
                    sides = [
                        norm_grad_refs[0][...] + total[...],
                        sum(ref[...] for ref in norm_grad_refs[1:]),
                    ]
                    norm_lines(sides, into, parts, 2 * half)

        for step in range(steps):
            for action in plan.get(step, []):
                action()
            if step < 2 * halves:
                piece(1 - step // halves, step % halves)

    hold = pl.BlockSpec(memory_space=pl.ANY)
    vmem = pl.BlockSpec(memory_space=pltpu.VMEM)
    arrays = [x, *firsts, q_grad, *kv_grads, norm, qkv]
    rooms = [
        pltpu.VMEM(x.shape, BF16),
        pltpu.VMEM((2, *whole), F32),
        pltpu.VMEM(q_grad.shape, BF16),
        pltpu.VMEM((2, *kv_grads[0].shape), BF16),
        pltpu.VMEM(norm.shape, F32),
        pltpu.VMEM(qkv.shape, BF16),
        pltpu.SemaphoreType.DMA((2 * (5 * halves + 2),)),
        pltpu.VMEM(whole, BF16),
        pltpu.VMEM((parts, 2, rows, part), BF16),
        pltpu.VMEM((3, 2, width), F32),
        pltpu.VMEM((2, *whole), BF16),
        pltpu.VMEM(shapes[0], BF16),
        pltpu.VMEM(shapes[1], BF16),
    ]
    return pl.pallas_call(
        kernel,
        in_specs=[hold] * len(arrays) + [vmem] * len(norm_grads),
        out_specs=[hold] * len(carrier.outs),
        out_shape=carrier.outs,
        scratch_shapes=rooms + carrier.scratch,
        compiler_params=pltpu.CompilerParams(vmem_limit_bytes=VMEM, **carrier.params),
        name="close_down",
    )(*arrays, *norm_grads)


def lay_out(pairs, singles, shapes, finish):
    arrays = [array for pair in pairs for array in pair] + [single[0] for single in singles]
    spans = [(0, min(a.shape[0], b.shape[0])) for a, b in pairs] + [s[1:] for s in singles]
    loaded = [
        jax.ShapeDtypeStruct((span[1], *array.shape[1:]), array.dtype)
        for array, span in zip([a for a, _ in pairs] + [s[0] for s in singles], spans)
    ]

    def kernel(*refs):
        ins, outs = refs[: len(arrays)], refs[len(arrays) : len(arrays) + len(shapes)]
        refs = refs[len(arrays) + len(shapes) :]
        rooms, refs = refs[: len(loaded)], refs[len(loaded) :]
        out_rooms, load_sems, store_sems = refs[: len(shapes)], refs[-2], refs[-1]
        section = lax.axis_index("section")

        def load(i, choice):
            source = ins[2 * i + choice] if i < len(pairs) else ins[len(pairs) + i]
            return pltpu.make_async_copy(
                source.at[pl.ds(*spans[i])], rooms[i], load_sems.at[i]
            )

        for i in range(len(loaded)):
            if i < len(pairs):

                @pl.when(section == 0)
                def _():
                    load(i, 0).start()

                @pl.when(section != 0)
                def _():
                    load(i, 1).start()

            else:
                load(i, 0).start()
        stores = []

        def fetch(i):
            load(i, 0).wait()
            return rooms[i]

        for i, room in enumerate(finish(fetch, out_rooms)):
            copy = pltpu.make_async_copy(room, outs[i], store_sems.at[i])
            copy.start()
            stores.append(copy)
        for copy in stores:
            copy.wait()

    hold = pl.BlockSpec(memory_space=pl.ANY)
    return pl.pallas_call(
        kernel,
        in_specs=[hold] * len(arrays),
        out_specs=[hold] * len(shapes),
        out_shape=[jax.ShapeDtypeStruct(*s) for s in shapes],
        scratch_shapes=[pltpu.VMEM(a.shape, a.dtype) for a in loaded]
        + [pltpu.VMEM(*s) for s in shapes]
        + [pltpu.SemaphoreType.DMA((len(loaded),)), pltpu.SemaphoreType.DMA((len(shapes),))],
        compiler_params=pltpu.CompilerParams(vmem_limit_bytes=VMEM),
        name="lay_out",
    )(*arrays)


def open_up(tokens, qkv, norm, block, collective):
    _, rows, width = tokens.shape
    part = qkv.shape[-1]
    score = LOG2E / math.sqrt(width // HEADS)
    count = min(block, rows)
    pieces = rows // count

    def kernel(tokens_ref, qkv_ref, norm_ref, *refs):
        x_out, w_out, n_out, q_out, own_out, other_out = refs[:6]
        x, w, n, q, kv = refs[6:11]
        row_sems_, weight_sems, norm_sems, store_sems, kv_sems = (
            refs[11:14],
            refs[14:15],
            refs[15],
            refs[16],
            refs[17],
        )
        section, _, _ = spots()
        greet([*GROUP, 0])
        rows_in = spread_rows(tokens_ref, x, row_sems_, pieces=pieces)
        weight = WeightCopies(qkv_ref, w, weight_sems[0])
        weight.start()
        rows_in.start()
        norm_kept = pltpu.make_async_copy(norm_ref, n.at[section], norm_sems.at[0])
        norm_near = remote(
            norm_ref, n.at[section], norm_sems.at[1], norm_sems.at[2], where_is("near")
        )
        norm_kept.start()
        norm_near.start()
        stores, kv_copies = [], []

        def save(source, target):
            copy = pltpu.make_async_copy(source, target, store_sems.at[len(stores)])
            copy.start()
            stores.append(copy)

        def project(side, own, rows_low):
            for k in range(2):

                def product(m):
                    return dot_nn(rows_low, w[side, k, m * width : (m + 1) * width, :])

                q[side, k, own, :] = (product(0) * score).astype(BF16)
                kv[side, k, 0, own, :] = product(1).astype(BF16)
                kv[side, k, 1, own, :] = product(2).astype(BF16)

        norm_kept.wait()
        norm_near.wait()
        save(n, n_out)
        weight.forward(0)
        weight.forward_last(0)
        weight.finish()
        save(w, w_out)
        for i in range(pieces):
            own = slice(i * count, (i + 1) * count)
            for side in range(2):
                rows_in.wait_arrival(2 * i + side)
                rows_low = x[side, own, :]
                if side == 0:
                    unit, _ = standardize(rows_low.astype(F32))
                    rows_low = affine(unit, n.at[0], 2).astype(BF16)
                project(side, own, rows_low)
                copy = remote(
                    kv.at[side, :, :, own, :],
                    other_out.at[side, :, :, own, :],
                    kv_sems.at[0, 2 * i + side],
                    kv_sems.at[1, 2 * i + side],
                    where_is("near"),
                )
                copy.start()
                kv_copies.append(copy)
                save(x.at[side, own, :], x_out.at[side, own, :])
                save(kv.at[side, :, :, own, :], own_out.at[side, :, :, own, :])
                save(q.at[side, :, own, :], q_out.at[side, :, own, :])
        rows_in.wait_sent()
        for copy in kv_copies + stores:
            copy.wait()

    hold = pl.BlockSpec(memory_space=pl.ANY)
    shapes = [
        ((2, rows, width), BF16),
        ((2, 2, *qkv.shape), BF16),
        ((2, *norm.shape), F32),
        ((2, 2, rows, part), BF16),
        ((2, 2, 2, rows, part), BF16),
    ]
    return pl.pallas_call(
        kernel,
        in_specs=[hold] * 3,
        out_specs=[hold] * 6,
        out_shape=[jax.ShapeDtypeStruct(*s) for s in shapes + shapes[-1:]],
        scratch_shapes=[pltpu.VMEM(*s) for s in shapes]
        + row_sems(pieces)
        + [WeightCopies.sems(1)]
        + [
            pltpu.SemaphoreType.DMA((3,)),
            pltpu.SemaphoreType.DMA((6 * pieces + 2,)),
            pltpu.SemaphoreType.DMA((2, 2 * pieces)),
        ],
        compiler_params=pltpu.CompilerParams(
            vmem_limit_bytes=VMEM, collective_id=collective, has_side_effects=True
        ),
        name="open_up",
    )(tokens, qkv, norm)


def local_general(tokens, lengths, self_qkv, self_out, cross_proj, ffn_up, ffn_down, norms, cotangent):
    section = lax.axis_index("section")
    tensor = lax.axis_index("tensor")
    tensors = lax.axis_size("tensor")
    _, row_count, rows, width = tokens.shape
    assert row_count == 2 and tensors % row_count == 0
    spread = tensors // row_count
    pieces = 2 * spread
    axes = ("section", "tensor")
    is_first = section == 0
    own_row = tensor // spread
    place = section * spread + tensor % spread

    def device(row, spot):
        return (spot // spread) * tensors + row * spread + spot % spread

    def each():
        return [(s, t) for s in range(2) for t in range(tensors)]

    straight = [(s * tensors + t, device(s, t)) for s, t in each()]
    turned = [(s * tensors + t, device(1 - s, t)) for s, t in each()]

    def bring(shares):
        stays = lax.dynamic_index_in_dim(shares, section, 0, keepdims=False)
        moves = lax.dynamic_index_in_dim(shares, 1 - section, 0, keepdims=False)
        one = lax.ppermute(stays, axes, straight)
        two = lax.ppermute(moves, axes, turned)
        return jnp.where(own_row == 0, one, two), jnp.where(own_row == 0, two, one)

    def take_back(source, target):
        one = jnp.where(own_row == 0, source, target)
        two = jnp.where(own_row == 0, target, source)
        one = lax.ppermute(one, axes, [(b, a) for a, b in straight])
        two = lax.ppermute(two, axes, [(b, a) for a, b in turned])
        return jnp.stack([jnp.where(is_first, one, two), jnp.where(is_first, two, one)])

    def rotate(value, by):
        pairs = [
            (device(r, p), device(r, (p + by) % pieces))
            for r in range(row_count)
            for p in range(pieces)
        ]
        return lax.ppermute(value, axes, pairs)

    def pieces_of(value):
        return [value] + [rotate(value, by) for by in range(1, pieces)]

    def pieces_home(values):
        return [values[0]] + [rotate(values[by], -by) for by in range(1, pieces)]

    def swap_sections(value):
        return lax.ppermute(value, "section", [(0, 1), (1, 0)])

    def both_sides(weight, dim):
        if spread == 1:
            other = lax.ppermute(weight, "tensor", [(t, 1 - t) for t in range(tensors)])
            parts = [weight, other]
        else:
            parts = [lax.all_gather(weight, "tensor", axis=dim, tiled=True)]
        swapped = [swap_sections(part) for part in parts]
        pairs = list(zip(parts, swapped))
        return (
            [jnp.where(is_first, mine, theirs) for mine, theirs in pairs],
            [jnp.where(is_first, theirs, mine) for mine, theirs in pairs],
        )

    def home(source_grad, target_grad, dim):
        keep = jnp.where(is_first, source_grad, target_grad).astype(F32)
        sent = swap_sections(jnp.where(is_first, target_grad, source_grad))
        total = (keep + sent.astype(F32)).astype(BF16)
        if spread == 1:
            other = lax.ppermute(total[1], "tensor", [(t, 1 - t) for t in range(tensors)])
            total = (total[0].astype(F32) + other.astype(F32)).astype(BF16)
        else:
            total = lax.psum_scatter(total[0], "tensor", scatter_dimension=dim, tiled=True)
        return total

    def span_of(query_side, key_side):
        own = lax.dynamic_index_in_dim(lengths, own_row, 1, keepdims=False)
        asks, answers = own[query_side], own[key_side]
        paired = asks[1] > 0
        second = paired & (place * rows >= asks[0])
        begin = jnp.where(second, answers[0], 0)
        end = jnp.where(second | ~paired, answers[0] + answers[1], answers[0])
        offsets = [(place - by) % pieces * rows for by in range(pieces)]
        return jnp.stack([begin, end, *offsets]).astype(jnp.int32)[None]

    query_block = min(256, rows)
    chunk = 256

    source, target = bring(tokens[0])
    source_norm, target_norm = (
        jnp.where(is_first, a, b)
        for a, b in (lambda own, other: ((own, other), (other, own)))(
            norms[0], swap_sections(norms[0])
        )
    )
    source_qkv, target_qkv = both_sides(self_qkv[0], 2)
    source_out, target_out = both_sides(self_out[0], 0)
    source_up, target_up = both_sides(ffn_up[0], 1)
    source_down, target_down = both_sides(ffn_down[0], 0)
    source_cross, target_cross = both_sides(cross_proj[0], 2)
    source_cot, target_cot = bring(cotangent[0])
    source_span, target_span, cross_span = span_of(0, 0), span_of(1, 1), span_of(1, 0)

    enc_q, enc_kv = project_qkv(source, source_norm, source_qkv, True)
    enc_kv = pieces_of(enc_kv)
    dec_q, dec_kv = project_qkv(target, target_norm, target_qkv, False)
    dec_kv = pieces_of(dec_kv)
    enc_mix, enc_lse = attend(enc_q, enc_kv, source_span, query_block)
    encoded, memory, enc_first, enc_third = encoder_forward(
        source, enc_mix, source_norm, source_out, source_up, source_down, source_cross
    )
    memory = pieces_of(memory)
    dec_mix, dec_lse = attend(dec_q, dec_kv, target_span, query_block)
    cross_q, dec_first = decoder_middle(
        target, dec_mix, target_norm, target_out, target_cross
    )
    cross_mix, cross_lse = attend(cross_q, memory, cross_span, query_block)
    decoded, second_grad, cross_mix_grad, cross_out_grad, dec_up, dec_down, dec_norm = decoder_turn(
        dec_first, cross_mix, target_cot, target_norm, target_cross, target_up, target_down
    )
    result = take_back(encoded, decoded)
    cross_q_grad, memory_grads, _ = attend_back(
        cross_q, memory, cross_mix, cross_mix_grad, cross_lse, cross_span, chunk
    )
    memory_grads = pieces_home(memory_grads)
    dec_first_grad, dec_mix_grad, cross_query_grad, dec_out, step = decoder_middle_back(
        dec_first,
        dec_mix,
        cross_q_grad,
        second_grad,
        target_norm,
        target_out,
        target_cross
    )
    dec_norm += step
    enc_first_grad, enc_mix_grad, enc_cross, enc_out, enc_up, enc_down, enc_norm = encoder_back(
        enc_first,
        enc_third,
        enc_mix,
        memory_grads,
        source_cot,
        source_norm,
        source_out,
        source_up,
        source_down,
        source_cross
    )
    dec_cross = jnp.stack([cross_query_grad, cross_out_grad], axis=1)
    up_grad, down_grad = home(enc_up, dec_up, 1), home(enc_down, dec_down, 0)
    out_grad, cross_grad = home(enc_out, dec_out, 0), home(enc_cross, dec_cross, 2)
    dec_q_grad, dec_kv_grads, _ = attend_back(
        dec_q, dec_kv, dec_mix, dec_mix_grad, dec_lse, target_span, chunk
    )
    dec_kv_grads = pieces_home(dec_kv_grads)
    enc_q_grad, enc_kv_grads, _ = attend_back(
        enc_q, enc_kv, enc_mix, enc_mix_grad, enc_lse, source_span, chunk
    )
    enc_kv_grads = pieces_home(enc_kv_grads)
    target_grad, dec_qkv, _ = input_back(
        target, dec_first_grad, dec_q_grad, dec_kv_grads, target_norm, target_qkv, False
    )
    source_grad, enc_qkv, step = input_back(
        source, enc_first_grad, enc_q_grad, enc_kv_grads, source_norm, source_qkv, True
    )
    enc_norm += step
    token_grad = take_back(source_grad, target_grad).astype(F32)
    qkv_grad = home(enc_qkv, dec_qkv, 2)
    norm_total = lax.psum(jnp.stack([enc_norm, dec_norm]), ("section", "dp", "tensor"))
    norm_grad = lax.dynamic_index_in_dim(norm_total, section, 0, keepdims=False)
    summed = [
        lax.psum(grad, "dp").astype(F32)
        for grad in (qkv_grad, out_grad, cross_grad, up_grad, down_grad)
    ]
    return (
        result[None],
        token_grad[None],
        summed[0][None],
        summed[1][None],
        summed[2][None],
        summed[3][None],
        summed[4][None],
        norm_grad[None],
    )


def local_fast(tokens, lengths, self_qkv, self_out, cross_proj, ffn_up, ffn_down, norms, cotangent):
    section, tensor = lax.axis_index("section"), lax.axis_index("tensor")
    _, row_count, rows, width = tokens.shape
    assert row_count == 2
    is_first = section == 0
    block = min(256, rows)
    query_block = min(256, rows)
    chunk = 256
    levels = lax.axis_size("dp").bit_length() - 1

    def hops(*steps):
        return list(steps[:levels]) + list(steps[3 : 3 + levels])

    def flat(weight):
        return weight.reshape(-1, weight.shape[-1])

    def span_of(query_side, key_side):
        own = lax.dynamic_index_in_dim(lengths, tensor, 1, keepdims=False)
        asks, answers = own[query_side], own[key_side]
        paired = asks[1] > 0
        second = paired & (section * rows >= asks[0])
        begin = jnp.where(second, answers[0], 0)
        end = jnp.where(second | ~paired, answers[0] + answers[1], answers[0])
        return jnp.stack([begin, end, section * rows, (1 - section) * rows]).astype(jnp.int32)

    spans = jnp.stack([span_of(0, 0), span_of(1, 1), span_of(1, 0)])
    self_spans, cross_span = spans[:2], spans[2:]
    x, qkv, norm, q, *kv = open_up(tokens[0], flat(self_qkv), norms[0], block, 1)
    qkv = qkv.reshape(2, 2, *self_qkv.shape[1:])

    def parts(weight, side):
        return [At(weight, side, k) for k in range(2)]

    enc_x, dec_x, enc_norm_in, dec_norm_in = At(x, 0), At(x, 1), At(norm, 0), At(norm, 1)
    mix, lse, out, up, cross, down = attend(
        q,
        kv,
        self_spans,
        query_block,
        Carry(
            [
                SpreadWeight(self_out[0], [3], [5]),
                SpreadWeight(ffn_up[0], [4, 6], [7, 9]),
                SpreadWeight(flat(cross_proj), [8], [11]),
                SpreadWeight(ffn_down[0], [10, 12], [13, 15]),
            ],
            2,
        ),
        2,
    )
    cross = cross.reshape(2, 2, *cross_proj.shape[1:])
    enc_mix, dec_mix = At(mix, 0), At(mix, 1)
    encoded, memory, enc_first, enc_third, pushed = encoder_forward(
        enc_x,
        enc_mix,
        enc_norm_in,
        parts(out, 0),
        parts(up, 0),
        parts(down, 0),
        parts(cross, 0),
        8,
    )
    memory = [memory, pushed]
    cross_q, dec_first = decoder_middle(
        dec_x, dec_mix, dec_norm_in, parts(out, 1), parts(cross, 1)
    )
    cross_mix, cross_lse, dec_cot = attend(
        cross_q,
        memory,
        cross_span,
        query_block,
        Carry([SpreadRows(cotangent[0], (1,))], 4),
        2,
    )
    decoded, second_grad, cross_mix_grad, cross_out_grad, ffn_dec, dec_norm = decoder_turn(
        dec_first,
        cross_mix,
        At(dec_cot, 1),
        dec_norm_in,
        parts(cross, 1),
        parts(up, 1),
        parts(down, 1),
        True,
    )
    cross_q_grad, memory_grads, (ffn_dec, enc_cot) = attend_back(
        cross_q,
        memory,
        cross_mix,
        cross_mix_grad,
        cross_lse,
        cross_span,
        2 * chunk,
        Carry(
            [
                Reduce(ffn_dec, 256, [0, 1, 2, 3], [1, 2], "chip"),
                SpreadRows(cotangent[0], (0,), 4),
            ],
            5,
        ),
        2,
    )
    dec_first_grad, mix_grad, cross_query_grad, dec_out, mid_norm = decoder_middle_back(
        dec_first,
        dec_mix,
        cross_q_grad,
        second_grad,
        dec_norm_in,
        parts(out, 1),
        parts(cross, 1),
        (1, None),
    )
    enc_first_grad, mix_grad, ffn_enc, sides, enc_norm = encoder_back(
        enc_first,
        enc_third,
        enc_mix,
        memory_grads,
        At(enc_cot, 0),
        enc_norm_in,
        parts(out, 0),
        parts(up, 0),
        parts(down, 0),
        parts(cross, 0),
        [dec_out, cross_query_grad, cross_out_grad],
        (0, mix_grad),
    )
    q_grad, kv_grads, moved = attend_back(
        q,
        kv,
        mix,
        mix_grad,
        lse,
        self_spans,
        chunk,
        Carry(
            [
                Reduce(ffn_dec, 512, [0, 1], [1, *hops(2, 1, 1, 1, 2, 3)], "slice"),
                Reduce(ffn_enc, 512, [2, 0], [1, 3, *hops(2, 1, 2, 1, 1, 2)]),
                Reduce(sides, 768, [3, 1], [1, 3, *hops(1, 2, 1, 2, 1, 1)]),
                ReturnRows(encoded, 0, 11),
                ReturnRows(decoded, 1, 12),
            ],
            6,
        ),
        2,
    )
    ffn_dec, ffn_dec_other, ffn_enc, ffn_enc_other, sides, _, encoded, decoded = moved
    tail = (
        ([2, 2, 2, 2, 2, 3], [1, 2, *hops(1, 1, 1, 1, 1, 2)]),
        ([4, 4, 4, 4, 4, 4, 4], [1, 2, *hops(1, 1, 1, 1, 1, 1)]),
        (8, 6),
        8 + 2 * levels,
    )
    enc_last, enc_other, dec_last, dec_other, source_grad, target_grad = close_down(
        x,
        [enc_first_grad, dec_first_grad],
        q_grad,
        kv_grads,
        norm,
        qkv,
        [enc_norm, dec_norm, mid_norm],
        tail,
        7,
    )

    half = 3 * width // 2
    units = ffn_up.shape[-1]

    def columns(source, row, count, target, to):
        wide = source.shape[-1]
        for h in range(2):
            target[to : to + count, h * wide : (h + 1) * wide] = source[
                row + h * count : row + (h + 1) * count, :
            ].astype(F32)

    def finish(fetch, rooms):
        grads, result, up, down, first, second, side, norm_part = range(8)
        room = fetch(grads)
        for row in range(2):
            rooms[0][row] = room[row].astype(F32)
        yield rooms[0]
        yield fetch(result)
        columns(fetch(up), 0, width, rooms[2], 0)
        yield rooms[2]
        rooms[3][...] = fetch(down)[...].astype(F32)
        yield rooms[3]
        room = fetch(side)
        columns(room, 0, width // 2, rooms[4], 0)
        yield rooms[4]
        rooms[5][...] = room[width:, :].astype(F32)
        yield rooms[5]
        columns(fetch(first), 0, half, rooms[6], 0)
        columns(fetch(second), 0, half, rooms[6], half)
        yield rooms[6]
        rooms[7][...] = fetch(norm_part)[...].astype(F32)
        yield rooms[7]

    part = qkv.shape[-1]
    token_grad, result, up_grad, down_grad, out_grad, cross_grad, qkv_grad, norm_grad = lay_out(
        [
            (source_grad, target_grad),
            (encoded, decoded),
            (ffn_enc, ffn_dec_other),
            (ffn_enc_other, ffn_dec),
            (enc_last, dec_other),
            (enc_other, dec_last),
        ],
        [(sides, 0, sides.shape[0]), (enc_last, 2 * half, 32)],
        [
            ((2, rows, width), F32),
            ((2, rows, width), BF16),
            ((width, units), F32),
            ((units, width), F32),
            ((part, width), F32),
            ((2 * width, part), F32),
            ((2 * half, part), F32),
            ((32, PAIR), F32),
        ],
        finish,
    )
    return (
        result[None],
        token_grad[None],
        qkv_grad.reshape(self_qkv.shape),
        out_grad[None],
        cross_grad.reshape(cross_proj.shape),
        up_grad[None],
        down_grad[None],
        norm_grad[:24].reshape(norms.shape),
    )


def solution(mesh):
    placed = (
        P("section", "dp", "tensor", None),
        P(None, "dp", None),
        P("section", None, None, "tensor"),
        P("section", "tensor", None),
        P("section", None, None, "tensor"),
        P("section", None, "tensor"),
        P("section", "tensor", None),
        P("section", None, None, None),
        P("section", "dp", "tensor", None),
    )
    sizes = dict(mesh.shape)
    steps = sizes["dp"].bit_length() - 1
    fast = sizes["tensor"] == 2 and sizes["dp"] == 1 << steps and 0 < steps <= 3
    return jax.shard_map(
        local_fast if fast else local_general,
        mesh=mesh,
        in_specs=placed,
        out_specs=(
            P("section", "dp", "tensor", None),
            P("section", "dp", "tensor", None),
            P("section", None, None, "tensor"),
            P("section", "tensor", None),
            P("section", None, None, "tensor"),
            P("section", None, "tensor"),
            P("section", "tensor", None),
            P("section", None, None, None),
        ),
        check_vma=False,
    )
```

```python
import functools
import math

import jax
import jax.numpy as jnp
from jax import lax
from jax.experimental import pallas as pl
from jax.experimental.pallas import tpu as pltpu
from jax.sharding import PartitionSpec as P

HEADS = 8
EPSILON = 1e-05
MASKED = -1000000000.0
LOG2E = 1.0 / math.log(2.0)
PAIR = 128
HALF = 64
VMEM = 60 * 1024 * 1024
BF16 = jnp.bfloat16
F32 = jnp.float32


def standardize(rows):
    mean = jnp.mean(rows, axis=-1, keepdims=True)
    centered = rows - mean
    inv = lax.rsqrt(jnp.mean(centered * centered, axis=-1, keepdims=True) + EPSILON)
    return centered * inv, inv


def affine(unit, norm_ref, slot):
    return unit * norm_ref[slot, 0:1, :] + norm_ref[slot, 1:2, :]


def norm_back(unit, inv, norm_ref, slot, grad, grad_ref):
    grad_ref[slot, 0:1, :] += jnp.sum(grad * unit, axis=0, keepdims=True)
    grad_ref[slot, 1:2, :] += jnp.sum(grad, axis=0, keepdims=True)
    scaled = grad * norm_ref[slot, 0:1, :]
    first = jnp.mean(scaled, axis=-1, keepdims=True)
    second = jnp.mean(scaled * unit, axis=-1, keepdims=True)
    return inv * (scaled - first - unit * second)


def gelu_tanh(inner):
    return jnp.tanh(0.7978845608028654 * (inner + 0.044715 * inner * inner * inner))


def gelu(inner):
    return 0.5 * inner * (1.0 + gelu_tanh(inner))


def gelu_both(inner):
    bent = gelu_tanh(inner)
    slope = 0.7978845608028654 * (1.0 + 0.134145 * inner * inner)
    half = 0.5 * (1.0 + bent)
    return inner * half, half + 0.5 * inner * (1.0 - bent * bent) * slope


def dot_nn(a, b):
    return jnp.dot(a, b, preferred_element_type=F32)


def dot_nt(a, b):
    return lax.dot_general(a, b, (((1,), (1,)), ((), ())), preferred_element_type=F32)


def dot_tn(a, b):
    return lax.dot_general(a, b, (((0,), (0,)), ((), ())), preferred_element_type=F32)


class At:
    def __init__(self, array, *lead):
        self.array, self.lead = array, lead
        self.shape = array.shape[len(lead) :]
        self.dtype = array.dtype

    def spec(self, sizes, index, **options):
        nones = (None,) * len(self.lead)
        return pl.BlockSpec(nones + tuple(sizes), lambda *g: self.lead + tuple(index(*g)), **options)


def at(array):
    return array if isinstance(array, At) else At(array)


def row_call(
    body, name, rows, row_ins, whole_ins, row_outs, keeps, finals, finish, flops, into=None, push=None
):
    block, part = min(512, rows), min(256, rows)
    row_ins = [(at(a), dim) for a, dim in row_ins]
    whole_ins = [at(a) for a in whole_ins]

    def blocked(array, dim):
        sizes = tuple(block if i == dim else size for i, size in enumerate(array.shape))
        return array.spec(sizes, lambda g: tuple(g if i == dim else 0 for i in range(len(sizes))))

    def blocked_out(shape, dim):
        sizes = tuple(block if i == dim else size for i, size in enumerate(shape))
        return pl.BlockSpec(
            sizes, lambda g: tuple(g if i == dim else 0 for i in range(len(shape)))
        )

    def sided_out(shape, dim):
        plain = blocked_out(shape, dim)
        return pl.BlockSpec(
            (None, *plain.block_shape), lambda g: (into[0], *plain.index_map(g))
        )

    def whole(array):
        return array.spec(
            array.shape,
            lambda g: (0,) * len(array.shape),
            pipeline_mode=pl.Buffered(buffer_count=1),
        )

    def whole_out(shape):
        return pl.BlockSpec(
            shape, lambda g: (0,) * len(shape), pipeline_mode=pl.Buffered(buffer_count=1)
        )

    n_rows_in = len(row_ins)
    n_in = n_rows_in + len(whole_ins)
    n_row, n_final = len(row_outs), len(finals)
    out_specs = [blocked_out(shape, dim) for shape, _, dim in row_outs]
    out_shapes = [jax.ShapeDtypeStruct(shape, dtype) for shape, dtype, _ in row_outs]
    push_outs, push_scratch, push_params = [], [], {}
    if push is not None:
        push_outs = [out_shapes[push[0]]]
        push_scratch = [
            pltpu.VMEM(push_outs[0].shape, push_outs[0].dtype),
            pltpu.SemaphoreType.DMA((2, rows // block)),
        ]
        push_params = dict(collective_id=push[1], has_side_effects=True)
    held, aliases = [], {}
    if into is not None:
        shape, dtype, dim = row_outs[-1]
        out_specs[-1] = sided_out(shape, dim)
        out_shapes[-1] = jax.ShapeDtypeStruct((2, *shape), dtype)
        if into[1] is not None:
            held, aliases = [into[1]], {n_in: n_row - 1}

    def kernel(*refs):
        ins, refs = refs[:n_in], refs[len(held) :]
        outs = refs[n_in : n_in + n_row]
        last_outs, kept = refs[n_in + n_row : n_in + n_row + n_final], refs[n_in + n_row + n_final :]
        step = pl.program_id(0)
        if push is not None:
            pushed, kept = kept[0], kept[1:]
            kept, (push_room, push_sems) = kept[:-2], kept[-2:]

            def send(i):
                own = pl.ds(i * block, block)
                return remote(
                    push_room.at[:, :, own, :],
                    pushed.at[:, :, own, :],
                    push_sems.at[0, i],
                    push_sems.at[1, i],
                    where_is("near"),
                )

            @pl.when(step == 0)
            def _():
                greet(["near"])
        if finals:

            @pl.when(step == 0)
            def _():
                kept[-1][...] = jnp.zeros_like(kept[-1])

        turns = []
        for begin in range(0, block, part):
            all_rows = pl.ds(pl.multiple_of(step * block + begin, part), part)
            turns.append(body(ins, outs, kept, slice(begin, begin + part), all_rows))
        waiting, running = turns[1:], turns[:1]
        while running:
            running = [turn for turn in running if next(turn, LAST) is not LAST]
            if waiting:
                running.append(waiting.pop(0))

        if push is not None:
            for i in range(rows // block):

                @pl.when(step == i)
                def _():
                    push_room[:, :, i * block : (i + 1) * block, :] = outs[push[0]][...]
                    send(i).start()

            @pl.when(step == pl.num_programs(0) - 1)
            def _():
                for i in range(rows // block):
                    send(i).wait()

        if finals:

            @pl.when(step == pl.num_programs(0) - 1)
            def _():
                finish(ins[n_rows_in:], kept, last_outs)

    arrays = [array for array, _ in row_ins] + whole_ins
    size = sum(math.prod(a.shape) * a.dtype.itemsize for a in arrays)
    return pl.pallas_call(
        kernel,
        grid=(rows // block,),
        in_specs=[blocked(a, dim) for a, dim in row_ins]
        + [whole(a) for a in whole_ins]
        + [pl.BlockSpec(memory_space=pl.ANY)] * len(held),
        out_specs=out_specs
        + [whole_out(shape) for shape, _ in finals]
        + [pl.BlockSpec(memory_space=pl.ANY)] * len(push_outs),
        out_shape=out_shapes
        + [jax.ShapeDtypeStruct(shape, dtype) for shape, dtype in finals]
        + push_outs,
        input_output_aliases=aliases,
        scratch_shapes=[pltpu.VMEM(shape, dtype) for shape, dtype in keeps] + push_scratch,
        compiler_params=pltpu.CompilerParams(vmem_limit_bytes=VMEM, **push_params),
        cost_estimate=pl.CostEstimate(flops=flops, bytes_accessed=size, transcendentals=0),
        name=name,
    )(*[a.array for a in arrays], *held)


LAST = 1000


def split(refs, parts, count):
    return [refs[i * parts : (i + 1) * parts] for i in range(count)]


def project_qkv(x, norm, weights, with_norm):
    x = at(x)
    rows, width = x.shape
    parts, part = len(weights), weights[0].shape[-1]
    score = LOG2E / math.sqrt(width // HEADS)

    def body(ins, outs, kept, own, all_rows):
        x_ref, norm_ref, *w = ins
        q_ref, kv_ref = outs
        low = x_ref[own, :]
        if with_norm:
            unit, _ = standardize(low.astype(F32))
            low = affine(unit, norm_ref, 2).astype(BF16)
        yield
        for k in range(parts):
            q_ref[k, own, :] = (dot_nn(low, w[k][0]) * score).astype(BF16)
            kv_ref[k, 0, own, :] = dot_nn(low, w[k][1]).astype(BF16)
            kv_ref[k, 1, own, :] = dot_nn(low, w[k][2]).astype(BF16)
            yield

    return row_call(
        body,
        "project_qkv",
        rows,
        [(x, 0)],
        [norm, *weights],
        [((parts, rows, part), BF16, 1), ((parts, 2, rows, part), BF16, 2)],
        [],
        [],
        None,
        6 * rows * width * width,
    )


def encoder_forward(x, mix, norm, out, up, down, cross, push=None):
    x = at(x)
    rows, width = x.shape
    parts, part = len(out), out[0].shape[0]

    def body(ins, outs, kept, own, all_rows):
        x_ref, mix_ref, norm_ref = ins[:3]
        wo, wu, wd, wc = split(ins[3:], parts, 4)
        result_ref, kv_ref, first_ref, third_ref = outs
        unit, _ = standardize(x_ref[own, :].astype(F32))
        first = affine(unit, norm_ref, 2)
        for k in range(parts):
            first += dot_nn(mix_ref[k, own, :], wo[k][...])
        yield
        first_ref[own, :] = first
        unit, _ = standardize(first)
        third = affine(unit, norm_ref, 0)
        low = third.astype(BF16)
        inner = dot_nn(low, wu[0][...])
        yield
        for k in range(parts):
            act = gelu(inner).astype(BF16)
            if k + 1 < parts:
                inner = dot_nn(low, wu[k + 1][...])
            third += dot_nn(act, wd[k][...])
            yield
        third_ref[own, :] = third
        unit, _ = standardize(third)
        low = affine(unit, norm_ref, 1).astype(BF16)
        result_ref[own, :] = low
        yield
        for k in range(parts):
            kv_ref[k, 0, own, :] = dot_nn(low, wc[k][0]).astype(BF16)
            kv_ref[k, 1, own, :] = dot_nn(low, wc[k][1]).astype(BF16)

    units = sum(w.shape[1] for w in up)
    return row_call(
        body,
        "encoder_forward",
        rows,
        [(x, 0), (mix, 1)],
        [norm, *out, *up, *down, *cross],
        [
            ((rows, width), BF16, 0),
            ((parts, 2, rows, part), BF16, 2),
            ((rows, width), F32, 0),
            ((rows, width), F32, 0),
        ],
        [],
        [],
        None,
        6 * rows * width * width + 4 * rows * width * units,
        push=None if push is None else (1, push),
    )


def decoder_middle(x, mix, norm, out, cross):
    x = at(x)
    rows, width = x.shape
    parts, part = len(out), out[0].shape[0]
    score = LOG2E / math.sqrt(width // HEADS)

    def body(ins, outs, kept, own, all_rows):
        x_ref, mix_ref, norm_ref = ins[:3]
        wo, wc = split(ins[3:], parts, 2)
        q_ref, first_ref = outs
        first = x_ref[own, :].astype(F32)
        for k in range(parts):
            first += dot_nn(mix_ref[k, own, :], wo[k][...])
        yield
        first_ref[own, :] = first
        unit, _ = standardize(first)
        low = affine(unit, norm_ref, 0).astype(BF16)
        yield
        for k in range(parts):
            q_ref[k, own, :] = (dot_nn(low, wc[k][0]) * score).astype(BF16)

    return row_call(
        body,
        "decoder_middle",
        rows,
        [(x, 0), (mix, 1)],
        [norm, *out, *cross],
        [((parts, rows, part), BF16, 1), ((rows, width), F32, 0)],
        [],
        [],
        None,
        4 * rows * width * width,
    )


def ffn_finals(low, act, inner, grad, parts, units, paired, up_out, down_out):
    for k in range(parts):
        if paired:
            half = units // 2
            for h in range(2):
                begin = k * units + h * half
                up_out[0, k, h * half : (h + 1) * half, :] = dot_tn(
                    low[...], inner[:, begin : begin + half]
                ).astype(BF16)
            into = up_out.at[1, k]
        else:
            up_out[k] = dot_tn(low[...], inner[:, k * units : (k + 1) * units]).astype(BF16)
            into = down_out.at[k]
        into[...] = dot_tn(act[:, k * units : (k + 1) * units], grad[...]).astype(BF16)


def decoder_turn(first, mix, cotangent, norm, cross, up, down, paired=False):
    rows, width = first.shape
    parts, part, units = len(cross), cross[0].shape[-1], up[0].shape[1]

    def body(ins, outs, kept, own, all_rows):
        first_ref, cot_ref, mix_ref, norm_ref = ins[:4]
        wc, wu, wd = split(ins[4:], parts, 3)
        result_ref, second_grad_ref, mix_grad_ref = outs
        low_keep, act_keep, inner_keep, third_keep, second_keep, norm_total = kept
        unit, _ = standardize(first_ref[own, :])
        second = affine(unit, norm_ref, 0)
        for k in range(parts):
            second += dot_nt(mix_ref[k, all_rows, :], wc[k][1])
        yield
        unit_two, inv_two = standardize(second)
        third = affine(unit_two, norm_ref, 2)
        low = third.astype(BF16)
        low_keep[all_rows, :] = low
        inner = dot_nn(low, wu[0][...])
        yield
        slopes = []
        for k in range(parts):
            act, slope = gelu_both(inner)
            act = act.astype(BF16)
            slopes.append(slope)
            if k + 1 < parts:
                inner = dot_nn(low, wu[k + 1][...])
            act_keep[all_rows, k * units : (k + 1) * units] = act
            third += dot_nn(act, wd[k][...])
            yield
        unit_three, inv_three = standardize(third)
        result_ref[own, :] = affine(unit_three, norm_ref, 1).astype(BF16)
        grad = norm_back(
            unit_three, inv_three, norm_ref, 1, cot_ref[own, :].astype(F32), norm_total
        )
        grad_low = grad.astype(BF16)
        third_keep[all_rows, :] = grad_low
        grad_act = dot_nt(grad_low, wd[0][...])
        yield
        for k in range(parts):
            grad_inner = (grad_act * slopes[k]).astype(BF16)
            if k + 1 < parts:
                grad_act = dot_nt(grad_low, wd[k + 1][...])
            inner_keep[all_rows, k * units : (k + 1) * units] = grad_inner
            grad += dot_nt(grad_inner, wu[k][...])
            yield
        grad = norm_back(unit_two, inv_two, norm_ref, 2, grad, norm_total)
        second_grad_ref[own, :] = grad
        grad_low = grad.astype(BF16)
        second_keep[all_rows, :] = grad_low
        yield
        for k in range(parts):
            mix_grad_ref[k, own, :] = dot_nn(grad_low, wc[k][1]).astype(BF16)

    def finish(ins, kept, outs):
        mix_ref = ins[0]
        low_keep, act_keep, inner_keep, third_keep, second_keep, norm_total = kept
        for k in range(parts):
            outs[0][k] = dot_tn(second_keep[...], mix_ref[k]).astype(BF16)
        ffn_finals(
            low_keep, act_keep, inner_keep, third_keep, parts, units, paired, outs[1], outs[2]
        )
        outs[-1][...] = norm_total[...]

    ffn = (
        [((2, parts, units, width), BF16)]
        if paired
        else [((parts, width, units), BF16), ((parts, units, width), BF16)]
    )
    whole = (rows, width)
    return row_call(
        body,
        "decoder_turn",
        rows,
        [(first, 0), (cotangent, 0)],
        [mix, norm, *cross, *up, *down],
        [(whole, BF16, 0), (whole, F32, 0), ((parts, rows, part), BF16, 1)],
        [
            (whole, BF16),
            ((rows, parts * units), BF16),
            ((rows, parts * units), BF16),
            (whole, BF16),
            (whole, BF16),
            ((3, 2, width), F32),
        ],
        [((parts, width, part), BF16), *ffn, ((3, 2, width), F32)],
        finish,
        6 * rows * width * width + 12 * rows * width * units * parts,
    )


def decoder_middle_back(first, mix, query_grad, second_grad, norm, out, cross, into=None):
    rows, width = first.shape
    parts, part = len(out), out[0].shape[0]

    def body(ins, outs, kept, own, all_rows):
        first_ref, second_grad_ref, mix_ref, query_grad_ref, norm_ref = ins[:5]
        wo, wc = split(ins[5:], parts, 2)
        first_grad_ref, mix_grad_ref = outs
        low_keep, grad_keep, norm_total = kept
        unit, inv = standardize(first_ref[own, :])
        low_keep[all_rows, :] = affine(unit, norm_ref, 0).astype(BF16)
        grad = second_grad_ref[own, :]
        for k in range(parts):
            grad += dot_nt(query_grad_ref[k, all_rows, :], wc[k][0])
        yield
        grad = norm_back(unit, inv, norm_ref, 0, grad, norm_total)
        first_grad_ref[own, :] = grad
        grad_low = grad.astype(BF16)
        grad_keep[all_rows, :] = grad_low
        yield
        for k in range(parts):
            mix_grad_ref[k, own, :] = dot_nt(grad_low, wo[k][...]).astype(BF16)

    def finish(ins, kept, outs):
        mix_ref, query_grad_ref = ins[:2]
        low_keep, grad_keep, norm_total = kept
        for k in range(parts):
            outs[0][k] = dot_tn(low_keep[...], query_grad_ref[k]).astype(BF16)
            outs[1][k] = dot_tn(mix_ref[k], grad_keep[...]).astype(BF16)
        outs[2][...] = norm_total[...]

    whole = (rows, width)
    return row_call(
        body,
        "decoder_middle_back",
        rows,
        [(first, 0), (second_grad, 0)],
        [mix, query_grad, norm, *out, *cross],
        [(whole, F32, 0), ((parts, rows, part), BF16, 1)],
        [(whole, BF16), (whole, BF16), ((3, 2, width), F32)],
        [
            ((parts, width, part), BF16),
            ((parts, part, width), BF16),
            ((3, 2, width), F32),
        ],
        finish,
        8 * rows * width * width,
        into,
    )


def added(refs, *index):
    total = refs[0][index]
    for ref in refs[1:]:
        total = total.astype(F32) + ref[index].astype(F32)
    return total.astype(BF16)


def encoder_back(
    first, third, mix, memory_grads, cotangent, norm, out, up, down, cross, paired=None, into=None
):
    rows, width = first.shape
    parts, part, units = len(out), out[0].shape[0], up[0].shape[1]
    pieces = len(memory_grads)

    def body(ins, outs, kept, own, all_rows):
        first_ref, third_ref, cot_ref = ins[:3]
        memory_refs, mix_ref, norm_ref = ins[3 : 3 + pieces], ins[3 + pieces], ins[4 + pieces]
        wo, wu, wd, wc = split(ins[5 + pieces :], parts, 4)
        first_grad_ref, mix_grad_ref = outs
        low_keep, memory_keep, mid_keep, act_keep, inner_keep, third_keep, first_keep, norm_total = (
            kept
        )
        grad = cot_ref[own, :].astype(F32)
        for k in range(parts):
            for i in range(2):
                memory = added(memory_refs, k, i, own)
                memory_keep[k, i, all_rows, :] = memory
                grad += dot_nt(memory, wc[k][i])
        yield
        unit, inv = standardize(third_ref[own, :])
        low_keep[all_rows, :] = affine(unit, norm_ref, 1).astype(BF16)
        unit_one, inv_one = standardize(first_ref[own, :])
        low = affine(unit_one, norm_ref, 0).astype(BF16)
        mid_keep[all_rows, :] = low
        inner = dot_nn(low, wu[0][...])
        grad = norm_back(unit, inv, norm_ref, 1, grad, norm_total)
        grad_low = grad.astype(BF16)
        third_keep[all_rows, :] = grad_low
        grad_act = dot_nt(grad_low, wd[0][...])
        yield
        for k in range(parts):
            act, slope = gelu_both(inner)
            if k + 1 < parts:
                inner = dot_nn(low, wu[k + 1][...])
            act_keep[all_rows, k * units : (k + 1) * units] = act.astype(BF16)
            grad_inner = (grad_act * slope).astype(BF16)
            if k + 1 < parts:
                grad_act = dot_nt(grad_low, wd[k + 1][...])
            inner_keep[all_rows, k * units : (k + 1) * units] = grad_inner
            grad += dot_nt(grad_inner, wu[k][...])
            yield
        grad = norm_back(unit_one, inv_one, norm_ref, 0, grad, norm_total)
        first_grad_ref[own, :] = grad
        grad_low = grad.astype(BF16)
        first_keep[all_rows, :] = grad_low
        yield
        for k in range(parts):
            mix_grad_ref[k, own, :] = dot_nt(grad_low, wo[k][...]).astype(BF16)

    def finish(ins, kept, outs):
        mix_ref = ins[0]
        low_keep, memory_keep, mid_keep, act_keep, inner_keep, third_keep, first_keep, norm_total = (
            kept
        )
        if paired:
            ffn_finals(
                mid_keep, act_keep, inner_keep, third_keep, parts, units, True, outs[0], None
            )
            dec_out, dec_query, dec_cross = ins[-3:]
            sides = outs[1]
            for k in range(parts):
                column_blocks(dot_tn(mix_ref[k], first_keep[...]), sides, 0, k, 0)
                column_blocks(dec_out[k], sides, 1, k, 0)
                for i in range(2):
                    here = slice((1 + i) * width, (2 + i) * width)
                    sides[0, k, here, :] = dot_tn(low_keep[...], memory_keep[k, i]).astype(BF16)
                    sides[1, k, here, :] = (dec_query, dec_cross)[i][k]
        else:
            for k in range(parts):
                for i in range(2):
                    outs[0][k, i] = dot_tn(low_keep[...], memory_keep[k, i]).astype(BF16)
                outs[1][k] = dot_tn(mix_ref[k], first_keep[...]).astype(BF16)
            ffn_finals(
                mid_keep, act_keep, inner_keep, third_keep, parts, units, False, outs[2], outs[3]
            )
        outs[-1][...] = norm_total[...]

    if paired:
        finals = [((2, parts, units, width), BF16), ((2, parts, 3 * width, part), BF16)]
    else:
        finals = [
            ((parts, 2, width, part), BF16),
            ((parts, part, width), BF16),
            ((parts, width, units), BF16),
            ((parts, units, width), BF16),
        ]
    whole = (rows, width)
    return row_call(
        body,
        "encoder_back",
        rows,
        [(first, 0), (third, 0), (cotangent, 0)] + [(m, 2) for m in memory_grads],
        [mix, norm, *out, *up, *down, *cross, *(paired or [])],
        [(whole, F32, 0), ((parts, rows, part), BF16, 1)],
        [
            (whole, BF16),
            ((parts, 2, rows, part), BF16),
            (whole, BF16),
            ((rows, parts * units), BF16),
            ((rows, parts * units), BF16),
            (whole, BF16),
            (whole, BF16),
            ((3, 2, width), F32),
        ],
        [*finals, ((3, 2, width), F32)],
        finish,
        12 * rows * width * width + 10 * rows * width * units * parts,
        into,
    )


def column_blocks(wide, into, core, k, row):
    rows, columns = wide.shape[0], wide.shape[1] // 2
    for half in range(2):
        into[core, k, row + half * rows : row + (half + 1) * rows, :] = wide[
            :, half * columns : (half + 1) * columns
        ].astype(BF16)


def input_part(refs, kept, own, all_rows, norm_ref, w, with_norm):
    x_ref, first_grad_ref, key_refs, query_grad_ref, grad_ref = refs
    low_keep, key_keep, norm_total = kept
    grad = first_grad_ref[own, :]
    for k in range(len(w)):
        grad += dot_nt(query_grad_ref[k, all_rows, :], w[k][0])
        for i in range(2):
            member = added(key_refs, k, i, own)
            key_keep[k, i, all_rows, :] = member
            grad += dot_nt(member, w[k][1 + i])
    yield
    low = x_ref[own, :]
    if with_norm:
        unit, inv = standardize(low.astype(F32))
        low = affine(unit, norm_ref, 2).astype(BF16)
        grad = norm_back(unit, inv, norm_ref, 2, grad, norm_total)
    low_keep[all_rows, :] = low
    grad_ref[own, :] = grad.astype(BF16)


def input_sums(kept, query_grad_ref, into, parts):
    low_keep, key_keep, _ = kept
    for k in range(parts):
        both = jnp.concatenate(
            [dot_tn(low_keep[...], query_grad_ref[k])]
            + [dot_tn(low_keep[...], key_keep[k, i]) for i in range(2)],
            axis=0,
        )
        half = both.shape[0] // 2
        for core in range(2):
            column_blocks(both[core * half : (core + 1) * half], into, core, k, 0)


def norm_lines(sides, into, parts, row):
    for core, table in enumerate(sides):
        lines = [
            table[slot, i : i + 1, h * PAIR : (h + 1) * PAIR]
            for slot in range(3)
            for i in range(2)
            for h in range(table.shape[-1] // PAIR)
        ]
        lines.append(jnp.zeros((2 * PAIR - len(lines), PAIR), F32))
        lines = jnp.concatenate(lines, axis=0).astype(BF16)
        for k in range(parts):
            into[core, k, row:, :] = lines


def input_back(x, first_grad, query_grad, key_grads, norm, weights, with_norm):
    x = at(x)
    rows, width = x.shape
    parts, part = len(weights), weights[0].shape[-1]
    pieces = len(key_grads)
    key_grads = [at(g) for g in key_grads]

    def body(ins, outs, kept, own, all_rows):
        x_ref, first_grad_ref = ins[:2]
        key_refs, query_grad_ref, norm_ref = ins[2 : 2 + pieces], ins[2 + pieces], ins[3 + pieces]
        refs = x_ref, first_grad_ref, key_refs, query_grad_ref, outs[0]
        yield from input_part(refs, kept, own, all_rows, norm_ref, ins[4 + pieces :], with_norm)

    def finish(ins, kept, outs):
        query_grad_ref = ins[0]
        low_keep, key_keep, norm_total = kept
        for k in range(parts):
            outs[0][k, 0] = dot_tn(low_keep[...], query_grad_ref[k]).astype(BF16)
            for i in range(2):
                outs[0][k, 1 + i] = dot_tn(low_keep[...], key_keep[k, i]).astype(BF16)
        outs[1][...] = norm_total[...]

    whole = (rows, width)
    return row_call(
        body,
        "input_back",
        rows,
        [(x, 0), (first_grad, 0)] + [(g, 2) for g in key_grads],
        [query_grad, norm, *weights],
        [(whole, BF16, 0)],
        [(whole, BF16), ((parts, 2, rows, part), BF16), ((3, 2, width), F32)],
        [((parts, 3, width, part), BF16), ((3, 2, width), F32)],
        finish,
        12 * rows * width * width,
    )


def widen_keys(span, kv_refs, key_e, key_o, value_e, value_o, rows):
    lane = lax.broadcasted_iota(jnp.int32, (rows, PAIR), 1)
    place = lax.broadcasted_iota(jnp.int32, (rows, PAIR), 0)
    low = lane < HALF
    for g, kv_ref in enumerate(kv_refs):
        spot = place + span[2 + g]
        live = (spot >= span[0]) & (spot < span[1])
        bias = jnp.where(live, 0.0, MASKED)
        keys, values = kv_ref[0].astype(F32), kv_ref[1].astype(F32)
        own = pl.ds(g * rows, rows)
        key_e[own, :] = jnp.where(low, keys, jnp.where(lane == HALF, bias, 1.0)).astype(BF16)
        key_o[own, :] = jnp.where(low, jnp.where(lane == 0, bias, 1.0), keys).astype(BF16)
        value_e[own, :] = jnp.where(low, values, 1.0).astype(BF16)
        value_o[own, :] = jnp.where(low, 1.0, values).astype(BF16)


class Lengths:
    def __init__(self, lengths, asking=None, answering=None):
        self.lengths, self.asking, self.answering = lengths, asking, answering

    def span(self, ref, side, rows):
        section, _, tensor = spots()
        asks, answers = [
            [ref[side if own is None else own, tensor, j] for j in range(2)]
            for own in (self.asking, self.answering)
        ]
        paired = asks[1] > 0
        second = paired & (section * rows >= asks[0])
        begin = jnp.where(second, answers[0], 0)
        end = jnp.where(second | jnp.logical_not(paired), answers[0] + answers[1], answers[0])
        return [begin, end, section * rows, (1 - section) * rows]


class Pairs:
    def __init__(self, query):
        self.sides = query.shape[:-3]
        self.parts, self.rows, self.part = query.shape[-3:]
        self.per_part = self.part // PAIR
        self.per_side = self.parts * self.per_part
        self.count = self.per_side * math.prod(self.sides)

    def side(self, i):
        return (i // self.per_side,) if self.sides else ()

    def place(self, i):
        i = i % self.per_side
        return i // self.per_part, i % self.per_part

    def query_spec(self, array):
        def index(i):
            part, column = self.place(i)
            return *self.side(i), part, 0, column

        none = (None,) * len(self.sides)
        return at(array).spec((*none, None, self.rows, PAIR), index)

    def kv_spec(self, array):
        def index(i):
            part, column = self.place(i)
            return *self.side(i), part, 0, 0, column

        none = (None,) * len(self.sides)
        return at(array).spec((*none, None, 2, self.rows, PAIR), index)

    def lse_spec(self):
        none = (None,) * len(self.sides)
        return pl.BlockSpec(
            (*none, self.rows, PAIR), lambda i: (*self.side(i), 0, i % self.per_side)
        )

    def span(self, span, span_ref, i):
        side = i // self.per_side if self.sides else 0
        if isinstance(span, Lengths):
            return span.span(span_ref, side, self.rows)
        return [span_ref[side, j] for j in range(span_ref.shape[1])]


def attend(query, kv_pieces, span, block, carrier=None, slots=1):
    query, kv_pieces = at(query), [at(piece) for piece in kv_pieces]
    carrier = carrier or Carry()
    heads_of = Pairs(query)
    rows, pairs = heads_of.rows, heads_of.count
    pieces = len(kv_pieces)
    keys = rows * pieces
    n_carry = len(carrier.ins)
    blocks = rows // block
    stride = blocks // slots

    def kernel(span_ref, q_ref, *refs):
        kv_refs, refs = refs[:pieces], refs[pieces:]
        carry_ins, refs = refs[:n_carry], refs[n_carry:]
        out_ref, lse_ref, refs = refs[0], refs[1], refs[2:]
        carry_outs, refs = refs[: len(carrier.outs)], refs[len(carrier.outs) :]
        key_e, key_o, value_e, value_o = refs[:4]

        def carry(slot):
            place = pl.program_id(0)
            carrier.run(place, slot, slots, pairs * slots, carry_ins, carry_outs, refs[4:])

        carry(0)
        seen = heads_of.span(span, span_ref, pl.program_id(0))
        widen_keys(seen, kv_refs, key_e, key_o, value_e, value_o, rows)
        lane = lax.broadcasted_iota(jnp.int32, (block, PAIR), 1)
        low = lane < HALF
        units = []
        for i in range(blocks):
            query = q_ref[i * block : (i + 1) * block, :].astype(F32)
            first = jnp.where(low, query, jnp.where(lane == HALF, 1.0, 0.0)).astype(BF16)
            second = jnp.where(low, jnp.where(lane == 0, 1.0, 0.0), query).astype(BF16)
            units += [(first, key_e, value_e), (second, key_o, value_o)]

        def scores_of(unit):
            return dot_nt(unit[0], unit[1][...])

        ahead = scores_of(units[0])
        tops, sums = [], []
        for u, unit in enumerate(units):
            if u and u % (2 * stride) == 0:
                carry(u // (2 * stride))
            scores = ahead
            if u + 1 < len(units):
                ahead = scores_of(units[u + 1])
            top = jnp.max(scores, axis=1, keepdims=True)
            tops.append(top)
            sums.append(dot_nn(jnp.exp2(scores - top).astype(BF16), unit[2][...]))
            if u % 2:
                own = slice(u // 2 * block, (u // 2 + 1) * block)
                top = jnp.where(low, tops[u], tops[u - 1])
                weight = jnp.where(low, sums[u], sums[u - 1])
                lse_ref[own, :] = top + LOG2E * jnp.log(weight)
                mixed = jnp.where(low, sums[u - 1], sums[u])
                out_ref[own, :] = (mixed / pltpu.roll(weight, HALF, 1)).astype(BF16)

    query_spec, kv_spec = heads_of.query_spec, heads_of.kv_spec
    lse_spec = heads_of.lse_spec()
    plain = jax.ShapeDtypeStruct(query.shape, BF16)
    hold = pl.BlockSpec(memory_space=pl.ANY)
    return pl.pallas_call(
        kernel,
        grid=(pairs,),
        in_specs=[pl.BlockSpec(memory_space=pltpu.SMEM), query_spec(query)]
        + [kv_spec(piece) for piece in kv_pieces]
        + [hold] * n_carry,
        out_specs=[query_spec(plain), lse_spec] + [hold] * len(carrier.outs),
        scratch_shapes=[pltpu.VMEM((keys, PAIR), BF16)] * 4 + carrier.scratch,
        out_shape=[plain, jax.ShapeDtypeStruct((*heads_of.sides, rows, heads_of.per_side * PAIR), F32)] + carrier.outs,
        compiler_params=pltpu.CompilerParams(vmem_limit_bytes=VMEM, **carrier.params),
        cost_estimate=pl.CostEstimate(
            flops=16 * rows * keys * pairs * PAIR,
            bytes_accessed=8 * rows * pairs * PAIR * pieces,
            transcendentals=0,
        ),
        name="attend",
    )(
        span.lengths if isinstance(span, Lengths) else span, query.array, *[piece.array for piece in kv_pieces], *carrier.ins)


def attend_back(
    query, kv_pieces, mix, mix_grad, lse, span, chunk, carrier=None, slots=1
):
    query, kv_pieces = at(query), [at(piece) for piece in kv_pieces]
    mix, mix_grad = at(mix), at(mix_grad)
    heads_of = Pairs(query)
    rows, pairs = heads_of.rows, heads_of.count
    pieces = len(kv_pieces)
    keys = rows * pieces
    scale = 1.0 / math.sqrt(HALF)
    swaps = carrier is not None
    carrier = carrier or Carry()
    n_carry = len(carrier.ins)
    kept = 1 if swaps else pieces
    chunks = keys // chunk
    stride = chunks // slots

    def kernel(span_ref, q_ref, mix_ref, grad_ref, lse_ref, *refs):
        kv_refs, refs = refs[:pieces], refs[pieces:]
        carry_ins, refs = refs[:n_carry], refs[n_carry:]
        dq_ref, dkv_refs, refs = refs[0], refs[1 : pieces + 1], refs[pieces + 1 :]
        carry_outs, refs = refs[: len(carrier.outs)], refs[len(carrier.outs) :]
        key_e, key_o, value_e, value_o, key_t = refs[:5]
        refs = refs[5:]
        if swaps:
            given, swap_sems, refs = refs[0], refs[1], refs[2:]
        pair = pl.program_id(0)

        def carry(slot):
            carrier.run(pair, slot, slots, pairs * slots, carry_ins, carry_outs, refs)

        carry(0)
        seen = heads_of.span(span, span_ref, pl.program_id(0))
        widen_keys(seen, kv_refs, key_e, key_o, value_e, value_o, rows)
        for g, kv_ref in enumerate(kv_refs):
            key_t[:, g * rows : (g + 1) * rows] = kv_ref[0].T
        lane = lax.broadcasted_iota(jnp.int32, (rows, PAIR), 1)
        low = lane < HALF
        query, grad = q_ref[...].astype(F32), grad_ref[...].astype(F32)
        product = mix_ref[...].astype(F32) * grad
        inner = jnp.where(
            low,
            jnp.sum(jnp.where(low, 0.0, product), axis=1, keepdims=True),
            jnp.sum(jnp.where(low, product, 0.0), axis=1, keepdims=True),
        )
        spot = jnp.where(low, lane, lane - HALF)

        def three(value, shift):
            high = value.astype(BF16).astype(F32)
            rest = value - high
            mid = rest.astype(BF16).astype(F32)
            return jnp.where(
                spot == shift,
                high,
                jnp.where(
                    spot == shift + 1, mid, jnp.where(spot == shift + 2, rest - mid, 0.0)
                ),
            )

        lse = three(-lse_ref[...], 1) + jnp.where(spot == 0, 1.0, 0.0)
        inner = three(-inner, 0)
        heads = [
            (
                key,
                value,
                jnp.where(own, query, lse).astype(BF16).T,
                jnp.where(own, grad, inner).astype(BF16).T,
                jnp.where(own, query, 0.0).astype(BF16),
                jnp.where(own, grad, 0.0).astype(BF16),
            )
            for own, key, value in ((low, key_e, value_e), (~low, key_o, value_o))
        ]
        units = [(c * chunk, h) for c in range(chunks) for h in range(2)]

        def front(unit):
            begin, h = unit
            own = slice(begin, begin + chunk)
            key, value, q_wide, g_wide, _, _ = heads[h]
            return dot_nn(key[own, :], q_wide), dot_nn(value[own, :], g_wide)

        ahead = front(units[0])
        dq = [None, None]
        for u, (begin, h) in enumerate(units):
            if u and u % (2 * stride) == 0:
                carry(u // (2 * stride))
            scores, dprobs = ahead
            if u + 1 < len(units):
                ahead = front(units[u + 1])
            probs = jnp.exp2(scores)
            dscores = (probs * dprobs).astype(BF16)
            _, _, _, _, q_own, g_own = heads[h]
            step_v = dot_nn(probs.astype(BF16), g_own)
            step_k = dot_nn(dscores, q_own)
            step_q = dot_nn(key_t[h * HALF : (h + 1) * HALF, begin : begin + chunk], dscores)
            dq[h] = step_q if dq[h] is None else dq[h] + step_q
            if h == 0:
                dv, dk = step_v, step_k
            else:
                g, first = begin // rows, begin % rows
                own = slice(first, first + chunk)
                dk = ((dk + step_k) * (1.0 / LOG2E)).astype(BF16)
                dv = (dv + step_v).astype(BF16)
                if g < kept:
                    dkv_refs[g][0, own, :] = dk
                    dkv_refs[g][1, own, :] = dv
                else:
                    given[pair, 0, own, :] = dk
                    given[pair, 1, own, :] = dv
        dq_ref[...] = (jnp.concatenate(dq, axis=0).T * scale).astype(BF16)
        if swaps:
            part, column = heads_of.place(pair)
            columns = pl.ds(pl.multiple_of(column * PAIR, PAIR), PAIR)
            spot = (*heads_of.side(pair), part, slice(None), slice(None), columns)

            def swap(i):
                return remote(
                    given.at[i],
                    dkv_refs[1].at[spot],
                    swap_sems.at[0, i],
                    swap_sems.at[1, i],
                    where_is("near"),
                )

            swap(pair).start()

            @pl.when(pair == pairs - 1)
            def _():
                for i in range(pairs):
                    swap(i).wait()

    query_spec, kv_spec = heads_of.query_spec, heads_of.kv_spec
    lse_spec = heads_of.lse_spec()
    plain = jax.ShapeDtypeStruct(query.shape, BF16)
    plain_kv = jax.ShapeDtypeStruct(
        (*heads_of.sides, heads_of.parts, 2, rows, heads_of.part), BF16
    )
    hold = pl.BlockSpec(memory_space=pl.ANY)
    swap_scratch = [
        pltpu.VMEM((pairs, 2, rows, PAIR), BF16),
        pltpu.SemaphoreType.DMA((2, pairs)),
    ]
    out = pl.pallas_call(
        kernel,
        grid=(pairs,),
        in_specs=[pl.BlockSpec(memory_space=pltpu.SMEM)]
        + [query_spec(a) for a in (query, mix, mix_grad)]
        + [lse_spec]
        + [kv_spec(piece) for piece in kv_pieces]
        + [hold] * n_carry,
        out_specs=[query_spec(plain)]
        + [kv_spec(plain_kv)] * kept
        + [hold] * (pieces - kept + len(carrier.outs)),
        scratch_shapes=[pltpu.VMEM((keys, PAIR), BF16)] * 4
        + [pltpu.VMEM((PAIR, keys), BF16)]
        + (swap_scratch if swaps else [])
        + carrier.scratch,
        out_shape=[plain] + [plain_kv] * pieces + carrier.outs,
        compiler_params=pltpu.CompilerParams(vmem_limit_bytes=VMEM, **carrier.params),
        cost_estimate=pl.CostEstimate(
            flops=40 * rows * keys * pairs * PAIR,
            bytes_accessed=16 * rows * pairs * PAIR * pieces,
            transcendentals=0,
        ),
        name="attend_back",
    )(
        span.lengths if isinstance(span, Lengths) else span,
        query.array,
        mix.array,
        mix_grad.array,
        lse,
        *[piece.array for piece in kv_pieces],
        *carrier.ins,
    )
    return out[0], out[1 : pieces + 1], out[pieces + 1 :]


def spots():
    return lax.axis_index("section"), lax.axis_index("dp"), lax.axis_index("tensor")


def dp_peer(group, level):
    return group + (1 << level) * (1 - 2 * ((group // (1 << level)) % 2))


def where_is(peer):
    section, group, tensor = spots()
    if peer == "near":
        return {"section": 1 - section}
    if peer == "over":
        return {"tensor": 1 - tensor}
    if peer == "cross":
        return {"section": 1 - section, "tensor": 1 - tensor}
    return {"dp": dp_peer(group, peer)}


def remote(source, target, sent, landed, where):
    return pltpu.make_async_remote_copy(
        src_ref=source,
        dst_ref=target,
        send_sem=sent,
        recv_sem=landed,
        device_id=where,
        device_id_type=pl.DeviceIdType.MESH,
    )


def greet(peers):
    barrier = pltpu.get_barrier_semaphore()
    for peer in peers:
        pl.semaphore_signal(
            barrier, inc=1, device_id=where_is(peer), device_id_type=pl.DeviceIdType.MESH
        )
    pl.semaphore_wait(barrier, len(peers))


class Carry:
    def __init__(self, tasks=(), collective=None):
        self.tasks = list(tasks)
        self.ins = [a for task in self.tasks for a in task.ins]
        self.outs = [a for task in self.tasks for a in task.outs]
        self.scratch = [a for task in self.tasks for a in task.scratch]
        self.peers = []
        for task in self.tasks:
            self.peers += [peer for peer in task.peers if peer not in self.peers]
        self.params = (
            dict(collective_id=collective, has_side_effects=True) if self.tasks else {}
        )

    def plan(self, steps, ins, outs, scratch):
        plan = {}
        if self.tasks:
            plan[0] = [lambda: greet(self.peers)]
        events = []
        for task in self.tasks:
            i, o, s = len(task.ins), len(task.outs), len(task.scratch)
            events += task.events(steps, ins[:i], outs[:o], scratch[:s])
            ins, outs, scratch = ins[i:], outs[o:], scratch[s:]
        for step, rank, action in sorted(events, key=lambda event: event[:2]):
            assert 0 <= step < steps
            plan.setdefault(step, []).append(action)
        return plan

    def run(self, place, slot, slots, steps, ins, outs, scratch):
        for step, actions in self.plan(steps, ins, outs, scratch).items():
            if step % slots == slot:

                @pl.when(place == step // slots)
                def _():
                    for action in actions:
                        action()


GROUP = ["near", "over", "cross"]


class RowCopies:
    def __init__(self, copies, arrivals, sems, room=None):
        self.copies, self.arrivals, self.room = copies, arrivals, room
        self.sent, self.landed, self.kept = sems

    def copy(self, i):
        source, target, slot, section, tensor, _ = self.copies[i]
        return remote(
            source,
            target,
            self.sent.at[i],
            self.landed.at[slot],
            {"section": section, "tensor": tensor},
        )

    def keep(self, i):
        source, target, slot = self.copies[i][:3]
        return pltpu.make_async_copy(
            source, target if self.room is None else self.room, self.kept.at[slot]
        )

    def keep_on(self):
        for i in range(len(self.copies)):

            @pl.when(self.here(i, True))
            def _():
                self.keep(i).wait()
                target, slot = self.copies[i][1:3]
                pltpu.make_async_copy(self.room, target, self.kept.at[slot]).start()

    def here(self, i, stays):
        section, _, tensor = spots()
        _, _, _, to_section, to_tensor, condition = self.copies[i]
        own = (to_section == section) & (to_tensor == tensor)
        return condition & (own if stays else jnp.logical_not(own))

    def start(self):
        for i in range(len(self.copies)):

            @pl.when(self.here(i, True))
            def _():
                self.keep(i).start()

            @pl.when(self.here(i, False))
            def _():
                self.copy(i).start()

    def wait_sent(self):
        for i in range(len(self.copies)):

            @pl.when(self.here(i, False))
            def _():
                self.copy(i).wait_send()

    def wait_arrival(self, i):
        section, _, tensor = spots()
        target, slot, from_section, from_tensor, condition = self.arrivals[i]
        own = (from_section == section) & (from_tensor == tensor)
        source = self.copies[0][0]

        @pl.when(condition & own)
        def _():
            stays = source if self.room is None else self.room
            pltpu.make_async_copy(stays, target, self.kept.at[slot]).wait()

        @pl.when(condition & jnp.logical_not(own))
        def _():
            remote(
                source, target, self.sent.at[0], self.landed.at[slot], where_is("near")
            ).wait_recv()


def row_sems(pieces=1):
    return [pltpu.SemaphoreType.DMA((2 * pieces,))] * 3


def spread_rows(source, target, sems, sides=(0, 1), room=None, pieces=1):
    section, _, tensor = spots()
    yes = section >= 0
    sends = yes if len(sides) == 2 else section == sides[0]
    count = source.shape[1] // pieces
    copies, arrivals = [], []
    for i in range(pieces):
        own = pl.ds(i * count, count)
        for row in range(2):
            slot = 2 * i + section
            copies.append(
                (source.at[row, own, :], target.at[section, own, :], slot, tensor, row, sends)
            )
        for side in sides:
            arrivals.append((target.at[side, own, :], 2 * i + side, side, section, yes))
    return RowCopies(copies, arrivals, sems, room)


def return_rows(source, target, sems, side, room):
    section, _, tensor = spots()
    copies = [(source, target.at[tensor], tensor, side, section, section >= 0)]
    arrivals = [(target.at[row], row, tensor, row, section == side) for row in range(2)]
    return RowCopies(copies, arrivals, sems, room)


class SpreadRows:
    peers = GROUP
    staged = True

    def __init__(self, array, sides, begin=0):
        self.ins, self.sides, self.begin = [array], sides, begin
        self.outs = [jax.ShapeDtypeStruct(array.shape, array.dtype)]
        self.scratch = row_sems() + [pltpu.VMEM(array.shape[-2:], array.dtype)]

    def make(self, ins, outs, scratch):
        return spread_rows(ins[0], outs[0], scratch[:3], self.sides, scratch[3])

    def events(self, steps, ins, outs, scratch):
        def make():
            return self.make(ins, outs, scratch)

        def finish():
            rows = make()
            for i in range(len(rows.arrivals)):
                rows.wait_arrival(i)
            rows.wait_sent()

        events = [(self.begin, 1, lambda: make().start()), (steps - 1, LAST, finish)]
        if self.staged:
            events.append((self.begin + 1, 1, lambda: make().keep_on()))
        return events


class ReturnRows(SpreadRows):
    def __init__(self, array, side, begin=0, staged=True):
        self.ins, self.side, self.begin, self.staged = [array], side, begin, staged
        self.outs = [jax.ShapeDtypeStruct((2, *array.shape), array.dtype)]
        self.scratch = row_sems() + [pltpu.VMEM(array.shape, array.dtype)] * staged

    def make(self, ins, outs, scratch):
        room = scratch[3] if len(scratch) > 3 else None
        return return_rows(ins[0], outs[0], scratch[:3], self.side, room)


class WeightCopies:
    @staticmethod
    def sems(count):
        return pltpu.SemaphoreType.DMA((3 + 8 * count,))

    def __init__(self, source, target, sem, room=None, count=1):
        section, group, _ = spots()
        rows = source.shape[0] // (2 * count)
        bit = group % 2
        here, stays = target.at[section, 1], target.at[section, 0]
        self.room = room
        if room is None:
            self.kept = pltpu.make_async_copy(source, stays, sem.at[0])
        else:
            self.first = pltpu.make_async_copy(source, room, sem.at[0])
            self.kept = pltpu.make_async_copy(room, stays, sem.at[0])
        self.near = remote(source, stays, sem.at[1], sem.at[2], where_is("near"))
        self.over, self.side, self.onward, self.last = [], [], [], []
        for i in range(count):
            own = pl.ds(pl.multiple_of((bit * count + i) * rows, 16), rows)
            other = pl.ds(pl.multiple_of(((1 - bit) * count + i) * rows, 16), rows)
            source_own, own, other = source.at[own], here.at[own], here.at[other]
            pairs = [(sem.at[3 + 8 * i + 2 * j], sem.at[4 + 8 * i + 2 * j]) for j in range(4)]
            self.over.append(remote(source_own, own, *pairs[0], where_is("over")))
            self.side.append(remote(own, own, *pairs[1], where_is(0)))
            self.onward.append(remote(own, own, *pairs[2], where_is("near")))
            self.last.append(remote(other, other, *pairs[3], where_is("near")))

    def start(self):
        for copy in self.over:
            copy.start()
        self.near.start()
        if self.room is None:
            self.kept.start()
        else:
            self.first.start()

    def keep_on(self):
        self.first.wait()
        self.kept.start()

    def forward(self, i):
        self.over[i].wait_recv()
        self.side[i].start()
        self.onward[i].start()

    def forward_last(self, i):
        self.side[i].wait_recv()
        self.last[i].start()

    def finish(self):
        self.kept.wait()
        self.near.wait()
        for over, side, onward, last in zip(self.over, self.side, self.onward, self.last):
            over.wait_send()
            side.wait_send()
            onward.wait()
            last.wait()


class SpreadWeight:
    peers = ["near", "over", 0]

    def __init__(self, weight, forwards, lasts):
        self.ins = [weight]
        self.outs = [jax.ShapeDtypeStruct((2, 2, *weight.shape), weight.dtype)]
        self.forwards, self.lasts = forwards, lasts
        self.scratch = [
            WeightCopies.sems(len(forwards)),
            pltpu.VMEM(weight.shape, weight.dtype),
        ]

    def events(self, steps, ins, outs, scratch):
        def copies():
            return WeightCopies(ins[0], outs[0], *scratch, len(self.forwards))

        def forward(i):
            return lambda: copies().forward(i)

        def forward_last(i):
            return lambda: copies().forward_last(i)

        return (
            [(0, 0, lambda: copies().start()), (1, 0, lambda: copies().keep_on())]
            + [(when, 1, forward(i)) for i, when in enumerate(self.forwards)]
            + [(when, 2, forward_last(i)) for i, when in enumerate(self.lasts)]
            + [(steps - 1, LAST, lambda: copies().finish())]
        )


class Reduce:
    def __init__(self, source, chunk, begins, pace, only=None, levels=None):
        self.ins = [source]
        self.chunk, self.begins, self.only = chunk, begins, only
        self.count = source.shape[-2] // chunk
        assert self.count == len(begins)
        self.levels = list(range(lax.axis_size("dp").bit_length() - 1))
        if levels is not None:
            self.levels = levels
        depth = len(self.levels)
        self.peers = []
        self.stages = []
        if only != "slice":
            self.peers += ["near", "over"]
            self.stages += ["enter", "cross", "over"]
        if only != "chip":
            self.peers += ["near", *self.levels]
            self.stages += ["load", "loaded"] if only == "slice" else []
            self.stages += [("halve", i) for i in range(depth)]
            self.stages += [("double", i) for i in reversed(range(depth))]
        assert len(pace) == len(self.stages) - 1
        self.dues = [sum(pace[:i]) for i in range(len(self.stages))]
        width = source.shape[-1]
        whole = jax.ShapeDtypeStruct((self.count * chunk, width), BF16)
        self.outs = [whole] if only == "chip" else [whole] * 2

        def room(*shape):
            return pltpu.VMEM((self.count, *shape, width), BF16)

        self.scratch = [room(2, chunk)]
        if only != "slice":
            self.scratch += [room(2, chunk), room(chunk)]
        if only != "chip":
            halves = [room(chunk >> (i + 1)) for i in range(depth)]
            self.scratch += [room(chunk)] + halves + halves
        self.scratch += [pltpu.SemaphoreType.DMA((2 + 2 * (3 + 2 * depth), self.count))]

    def events(self, steps, ins, outs, scratch):
        chunk, depth = self.chunk, len(self.levels)
        source, refs = ins[0], list(scratch)
        own, sems = refs[0], refs[-1]
        refs = refs[1:-1]
        if self.only != "slice":
            chip, other = refs[:2]
            refs = refs[2:]
        if self.only != "chip":
            full, halves, doubles = refs[0], refs[1 : 1 + depth], refs[1 + depth :]

        def bounds(i):
            _, group, _ = spots()
            begin = 0
            for j in range(i):
                bit = (group // (1 << self.levels[j])) % 2
                begin = begin + bit * (chunk >> (j + 1))
            return begin

        def keeps(i):
            return pl.ds(pl.multiple_of(bounds(i + 1), 16), chunk >> (i + 1))

        def gives(i):
            begin = 2 * bounds(i) + (chunk >> (i + 1)) - bounds(i + 1)
            return pl.ds(pl.multiple_of(begin, 16), chunk >> (i + 1))

        def pair(kind, c):
            return sems.at[2 + 2 * kind, c], sems.at[3 + 2 * kind, c]

        def rows_of(c):
            return pl.ds(c * chunk, chunk)

        def load(c):
            if self.only == "slice":
                return pltpu.make_async_copy(
                    source.at[rows_of(c), :], own.at[c, 0], sems.at[0, c]
                )
            section, _, _ = spots()
            return pltpu.make_async_copy(
                source.at[section, :, rows_of(c), :], own.at[c], sems.at[0, c]
            )

        def cross(c):
            section, _, _ = spots()
            return remote(
                source.at[1 - section, :, rows_of(c), :],
                chip.at[c],
                *pair(0, c),
                where_is("near"),
            )

        def over(c):
            return remote(own.at[c, 1], other.at[c], *pair(1, c), where_is("over"))

        def halve(i, c):
            return remote(
                own.at[c, 0, gives(i), :],
                halves[i].at[c],
                *pair(3 + i, c),
                where_is(self.levels[i]),
            )

        def double(i, c):
            return remote(
                full.at[c, keeps(i), :],
                doubles[i].at[c],
                *pair(3 + depth + i, c),
                where_is(self.levels[i]),
            )

        def store(c):
            kept = own.at[c, 0] if self.only == "chip" else full.at[c]
            return pltpu.make_async_copy(kept, outs[0].at[rows_of(c), :], sems.at[1, c])

        def tell(c):
            return remote(
                full.at[c], outs[1].at[rows_of(c), :], *pair(2, c), where_is("near")
            )

        def act(stage, c):
            if stage == "enter":
                load(c).start()
                cross(c).start()
            elif stage == "load":
                load(c).start()
            elif stage == "loaded":
                load(c).wait()
                halve(0, c).start()
            elif stage == "cross":
                load(c).wait()
                cross(c).wait()
                own[c] = own[c] + chip[c]
                over(c).start()
            elif stage == "over":
                over(c).wait()
                own[c, 0] = own[c, 0] + other[c]
                if self.only == "chip":
                    store(c).start()
                else:
                    halve(0, c).start()
            elif stage[0] == "halve":
                i = stage[1]
                halve(i, c).wait()
                mine = keeps(i)
                total = own[c, 0, mine, :] + halves[i][c]
                if i < depth - 1:
                    own[c, 0, mine, :] = total
                    halve(i + 1, c).start()
                else:
                    full[c, mine, :] = total
                    double(i, c).start()
            else:
                i = stage[1]
                double(i, c).wait()
                full[c, gives(i), :] = doubles[i][c]
                if i:
                    double(i - 1, c).start()
                else:
                    store(c).start()
                    tell(c).start()

        def leave(c):
            store(c).wait()
            if self.only != "chip":
                tell(c).wait()

        events = []
        for c, begin in enumerate(self.begins):
            for i, (stage, due) in enumerate(zip(self.stages, self.dues)):
                events.append((begin + due, -i, functools.partial(act, stage, c)))
            events.append((steps - 1, LAST, functools.partial(leave, c)))
        return events


def close_down(x, firsts, q_grad, kv_grads, norm, qkv, norm_grads, schedule, collective):
    _, rows, width = x.shape
    parts, _, _, part = qkv.shape[1:]
    half = 3 * width // 2
    shapes = [(2, parts, 2 * half + extra, PAIR) for extra in (2 * PAIR, 0)]
    dec_steps, enc_steps, returns, steps = schedule
    whole = (rows, width)
    grad_shape = jax.ShapeDtypeStruct(whole, BF16)
    carrier = Carry(
        [
            Reduce(jax.ShapeDtypeStruct(shapes[0], BF16), 2 * PAIR, *enc_steps),
            Reduce(jax.ShapeDtypeStruct(shapes[1], BF16), 2 * PAIR, *dec_steps),
            ReturnRows(grad_shape, 0, returns[0], False),
            ReturnRows(grad_shape, 1, returns[1], False),
        ],
        collective,
    )
    halves = 2
    count, sub = rows // halves, min(256, rows // halves)

    def kernel(*refs):
        x_in, first_ins, q_in, kv_ins, norm_in, qkv_in, refs = (
            refs[0],
            refs[1:3],
            refs[3],
            refs[4:6],
            refs[6],
            refs[7],
            refs[8:],
        )
        norm_grad_refs, refs = refs[: len(norm_grads)], refs[len(norm_grads) :]
        outs, refs = refs[: len(carrier.outs)], refs[len(carrier.outs) :]
        x_room, first_room, q_room, kv_room, norm_room, qkv_room, sems = refs[:7]
        low, keys, total, grads, enc_sum, dec_sum, *rest = refs[7:]
        ins = [enc_sum, dec_sum, grads.at[0], grads.at[1]]
        plan = carrier.plan(steps, ins, outs, rest)
        loads = []

        def load(source, target):
            copy = pltpu.make_async_copy(source, target, sems.at[len(loads)])
            copy.start()
            loads.append(copy)
            return copy

        arrivals = {}
        for side in (1, 0):
            for i in range(halves):
                own = pl.ds(i * count, count)
                arrivals[side, i] = [
                    load(first_ins[side].at[own, :], first_room.at[side, own, :]),
                    load(q_in.at[side, :, own, :], q_room.at[side, :, own, :]),
                    load(kv_ins[0].at[side, :, :, own, :], kv_room.at[0, side, :, :, own, :]),
                    load(kv_ins[1].at[side, :, :, own, :], kv_room.at[1, side, :, :, own, :]),
                    load(x_in.at[side, own, :], x_room.at[side, own, :]),
                ]
                if i == 0:
                    arrivals[side, i] += [
                        load(qkv_in.at[side], qkv_room.at[side]),
                        load(norm_in.at[side], norm_room.at[side]),
                    ]
        total[...] = jnp.zeros_like(total)

        def piece(side, i):
            for copy in arrivals[side, i]:
                copy.wait()
            kept = low, keys, total
            refs = (
                x_room.at[side],
                first_room.at[side],
                [kv_room.at[0, side], kv_room.at[1, side]],
                q_room.at[side],
                grads.at[side],
            )
            w = [qkv_room.at[side, k] for k in range(parts)]
            turns = []
            for begin in range(i * count, (i + 1) * count, sub):
                own = slice(begin, begin + sub)
                turns.append(
                    input_part(refs, kept, own, own, norm_room.at[side], w, side == 0)
                )
            while turns:
                turns = [turn for turn in turns if next(turn, LAST) is not LAST]
            if i == halves - 1:
                into = (enc_sum, dec_sum)[side]
                input_sums(kept, q_room.at[side], into, parts)
                if side == 0:
                    sides = [
                        norm_grad_refs[0][...] + total[...],
                        sum(ref[...] for ref in norm_grad_refs[1:]),
                    ]
                    norm_lines(sides, into, parts, 2 * half)

        for step in range(steps):
            for action in plan.get(step, []):
                action()
            if step < 2 * halves:
                piece(1 - step // halves, step % halves)

    hold = pl.BlockSpec(memory_space=pl.ANY)
    vmem = pl.BlockSpec(memory_space=pltpu.VMEM)
    arrays = [x, *firsts, q_grad, *kv_grads, norm, qkv]
    rooms = [
        pltpu.VMEM(x.shape, BF16),
        pltpu.VMEM((2, *whole), F32),
        pltpu.VMEM(q_grad.shape, BF16),
        pltpu.VMEM((2, *kv_grads[0].shape), BF16),
        pltpu.VMEM(norm.shape, F32),
        pltpu.VMEM(qkv.shape, BF16),
        pltpu.SemaphoreType.DMA((2 * (5 * halves + 2),)),
        pltpu.VMEM(whole, BF16),
        pltpu.VMEM((parts, 2, rows, part), BF16),
        pltpu.VMEM((3, 2, width), F32),
        pltpu.VMEM((2, *whole), BF16),
        pltpu.VMEM(shapes[0], BF16),
        pltpu.VMEM(shapes[1], BF16),
    ]
    return pl.pallas_call(
        kernel,
        in_specs=[hold] * len(arrays) + [vmem] * len(norm_grads),
        out_specs=[hold] * len(carrier.outs),
        out_shape=carrier.outs,
        scratch_shapes=rooms + carrier.scratch,
        compiler_params=pltpu.CompilerParams(vmem_limit_bytes=VMEM, **carrier.params),
        name="close_down",
    )(*arrays, *norm_grads)


def lay_out(pairs, singles, shapes, finish):
    arrays = [array for pair in pairs for array in pair] + [single[0] for single in singles]
    spans = [(0, min(a.shape[0], b.shape[0])) for a, b in pairs] + [s[1:] for s in singles]
    loaded = [
        jax.ShapeDtypeStruct((span[1], *array.shape[1:]), array.dtype)
        for array, span in zip([a for a, _ in pairs] + [s[0] for s in singles], spans)
    ]

    def kernel(*refs):
        ins, outs = refs[: len(arrays)], refs[len(arrays) : len(arrays) + len(shapes)]
        refs = refs[len(arrays) + len(shapes) :]
        rooms, refs = refs[: len(loaded)], refs[len(loaded) :]
        out_rooms, load_sems, store_sems = refs[: len(shapes)], refs[-2], refs[-1]
        section = lax.axis_index("section")

        def load(i, choice):
            source = ins[2 * i + choice] if i < len(pairs) else ins[len(pairs) + i]
            return pltpu.make_async_copy(
                source.at[pl.ds(*spans[i])], rooms[i], load_sems.at[i]
            )

        for i in range(len(loaded)):
            if i < len(pairs):

                @pl.when(section == 0)
                def _():
                    load(i, 0).start()

                @pl.when(section != 0)
                def _():
                    load(i, 1).start()

            else:
                load(i, 0).start()
        stores = []

        def fetch(i):
            load(i, 0).wait()
            return rooms[i]

        for i, room in enumerate(finish(fetch, out_rooms)):
            copy = pltpu.make_async_copy(room, outs[i], store_sems.at[i])
            copy.start()
            stores.append(copy)
        for copy in stores:
            copy.wait()

    hold = pl.BlockSpec(memory_space=pl.ANY)
    return pl.pallas_call(
        kernel,
        in_specs=[hold] * len(arrays),
        out_specs=[hold] * len(shapes),
        out_shape=[jax.ShapeDtypeStruct(*s) for s in shapes],
        scratch_shapes=[pltpu.VMEM(a.shape, a.dtype) for a in loaded]
        + [pltpu.VMEM(*s) for s in shapes]
        + [pltpu.SemaphoreType.DMA((len(loaded),)), pltpu.SemaphoreType.DMA((len(shapes),))],
        compiler_params=pltpu.CompilerParams(vmem_limit_bytes=VMEM),
        name="lay_out",
    )(*arrays)


def open_up(tokens, qkv, norm, block, collective):
    _, rows, width = tokens.shape
    part = qkv.shape[-1]
    score = LOG2E / math.sqrt(width // HEADS)
    count = min(block, rows)
    pieces = rows // count

    def kernel(tokens_ref, qkv_ref, norm_ref, *refs):
        x_out, w_out, n_out, q_out, own_out, other_out = refs[:6]
        x, w, n, q, kv = refs[6:11]
        row_sems_, weight_sems, norm_sems, store_sems, kv_sems = (
            refs[11:14],
            refs[14:15],
            refs[15],
            refs[16],
            refs[17],
        )
        section, _, _ = spots()
        greet([*GROUP, 0])
        rows_in = spread_rows(tokens_ref, x, row_sems_, pieces=pieces)
        weight = WeightCopies(qkv_ref, w, weight_sems[0])
        weight.start()
        rows_in.start()
        norm_kept = pltpu.make_async_copy(norm_ref, n.at[section], norm_sems.at[0])
        norm_near = remote(
            norm_ref, n.at[section], norm_sems.at[1], norm_sems.at[2], where_is("near")
        )
        norm_kept.start()
        norm_near.start()
        stores, kv_copies = [], []

        def save(source, target):
            copy = pltpu.make_async_copy(source, target, store_sems.at[len(stores)])
            copy.start()
            stores.append(copy)

        def project(side, own, rows_low):
            for k in range(2):

                def product(m):
                    return dot_nn(rows_low, w[side, k, m * width : (m + 1) * width, :])

                q[side, k, own, :] = (product(0) * score).astype(BF16)
                kv[side, k, 0, own, :] = product(1).astype(BF16)
                kv[side, k, 1, own, :] = product(2).astype(BF16)

        norm_kept.wait()
        norm_near.wait()
        save(n, n_out)
        weight.forward(0)
        weight.forward_last(0)
        weight.finish()
        save(w, w_out)
        for i in range(pieces):
            own = slice(i * count, (i + 1) * count)
            for side in range(2):
                rows_in.wait_arrival(2 * i + side)
                rows_low = x[side, own, :]
                if side == 0:
                    unit, _ = standardize(rows_low.astype(F32))
                    rows_low = affine(unit, n.at[0], 2).astype(BF16)
                project(side, own, rows_low)
                copy = remote(
                    kv.at[side, :, :, own, :],
                    other_out.at[side, :, :, own, :],
                    kv_sems.at[0, 2 * i + side],
                    kv_sems.at[1, 2 * i + side],
                    where_is("near"),
                )
                copy.start()
                kv_copies.append(copy)
                save(x.at[side, own, :], x_out.at[side, own, :])
                save(kv.at[side, :, :, own, :], own_out.at[side, :, :, own, :])
                save(q.at[side, :, own, :], q_out.at[side, :, own, :])
        rows_in.wait_sent()
        for copy in kv_copies + stores:
            copy.wait()

    hold = pl.BlockSpec(memory_space=pl.ANY)
    shapes = [
        ((2, rows, width), BF16),
        ((2, 2, *qkv.shape), BF16),
        ((2, *norm.shape), F32),
        ((2, 2, rows, part), BF16),
        ((2, 2, 2, rows, part), BF16),
    ]
    return pl.pallas_call(
        kernel,
        in_specs=[hold] * 3,
        out_specs=[hold] * 6,
        out_shape=[jax.ShapeDtypeStruct(*s) for s in shapes + shapes[-1:]],
        scratch_shapes=[pltpu.VMEM(*s) for s in shapes]
        + row_sems(pieces)
        + [WeightCopies.sems(1)]
        + [
            pltpu.SemaphoreType.DMA((3,)),
            pltpu.SemaphoreType.DMA((6 * pieces + 2,)),
            pltpu.SemaphoreType.DMA((2, 2 * pieces)),
        ],
        compiler_params=pltpu.CompilerParams(
            vmem_limit_bytes=VMEM, collective_id=collective, has_side_effects=True
        ),
        name="open_up",
    )(tokens, qkv, norm)


def local_general(tokens, lengths, self_qkv, self_out, cross_proj, ffn_up, ffn_down, norms, cotangent):
    section = lax.axis_index("section")
    tensor = lax.axis_index("tensor")
    tensors = lax.axis_size("tensor")
    _, row_count, rows, width = tokens.shape
    assert row_count == 2 and tensors % row_count == 0
    spread = tensors // row_count
    pieces = 2 * spread
    axes = ("section", "tensor")
    is_first = section == 0
    own_row = tensor // spread
    place = section * spread + tensor % spread

    def device(row, spot):
        return (spot // spread) * tensors + row * spread + spot % spread

    def each():
        return [(s, t) for s in range(2) for t in range(tensors)]

    straight = [(s * tensors + t, device(s, t)) for s, t in each()]
    turned = [(s * tensors + t, device(1 - s, t)) for s, t in each()]

    def bring(shares):
        stays = lax.dynamic_index_in_dim(shares, section, 0, keepdims=False)
        moves = lax.dynamic_index_in_dim(shares, 1 - section, 0, keepdims=False)
        one = lax.ppermute(stays, axes, straight)
        two = lax.ppermute(moves, axes, turned)
        return jnp.where(own_row == 0, one, two), jnp.where(own_row == 0, two, one)

    def take_back(source, target):
        one = jnp.where(own_row == 0, source, target)
        two = jnp.where(own_row == 0, target, source)
        one = lax.ppermute(one, axes, [(b, a) for a, b in straight])
        two = lax.ppermute(two, axes, [(b, a) for a, b in turned])
        return jnp.stack([jnp.where(is_first, one, two), jnp.where(is_first, two, one)])

    def rotate(value, by):
        pairs = [
            (device(r, p), device(r, (p + by) % pieces))
            for r in range(row_count)
            for p in range(pieces)
        ]
        return lax.ppermute(value, axes, pairs)

    def pieces_of(value):
        return [value] + [rotate(value, by) for by in range(1, pieces)]

    def pieces_home(values):
        return [values[0]] + [rotate(values[by], -by) for by in range(1, pieces)]

    def swap_sections(value):
        return lax.ppermute(value, "section", [(0, 1), (1, 0)])

    def both_sides(weight, dim):
        if spread == 1:
            other = lax.ppermute(weight, "tensor", [(t, 1 - t) for t in range(tensors)])
            parts = [weight, other]
        else:
            parts = [lax.all_gather(weight, "tensor", axis=dim, tiled=True)]
        swapped = [swap_sections(part) for part in parts]
        pairs = list(zip(parts, swapped))
        return (
            [jnp.where(is_first, mine, theirs) for mine, theirs in pairs],
            [jnp.where(is_first, theirs, mine) for mine, theirs in pairs],
        )

    def home(source_grad, target_grad, dim):
        keep = jnp.where(is_first, source_grad, target_grad).astype(F32)
        sent = swap_sections(jnp.where(is_first, target_grad, source_grad))
        total = (keep + sent.astype(F32)).astype(BF16)
        if spread == 1:
            other = lax.ppermute(total[1], "tensor", [(t, 1 - t) for t in range(tensors)])
            total = (total[0].astype(F32) + other.astype(F32)).astype(BF16)
        else:
            total = lax.psum_scatter(total[0], "tensor", scatter_dimension=dim, tiled=True)
        return total

    def span_of(query_side, key_side):
        own = lax.dynamic_index_in_dim(lengths, own_row, 1, keepdims=False)
        asks, answers = own[query_side], own[key_side]
        paired = asks[1] > 0
        second = paired & (place * rows >= asks[0])
        begin = jnp.where(second, answers[0], 0)
        end = jnp.where(second | ~paired, answers[0] + answers[1], answers[0])
        offsets = [(place - by) % pieces * rows for by in range(pieces)]
        return jnp.stack([begin, end, *offsets]).astype(jnp.int32)[None]

    query_block = min(256, rows)
    chunk = 256

    source, target = bring(tokens[0])
    source_norm, target_norm = (
        jnp.where(is_first, a, b)
        for a, b in (lambda own, other: ((own, other), (other, own)))(
            norms[0], swap_sections(norms[0])
        )
    )
    source_qkv, target_qkv = both_sides(self_qkv[0], 2)
    source_out, target_out = both_sides(self_out[0], 0)
    source_up, target_up = both_sides(ffn_up[0], 1)
    source_down, target_down = both_sides(ffn_down[0], 0)
    source_cross, target_cross = both_sides(cross_proj[0], 2)
    source_cot, target_cot = bring(cotangent[0])
    source_span, target_span, cross_span = span_of(0, 0), span_of(1, 1), span_of(1, 0)

    enc_q, enc_kv = project_qkv(source, source_norm, source_qkv, True)
    enc_kv = pieces_of(enc_kv)
    dec_q, dec_kv = project_qkv(target, target_norm, target_qkv, False)
    dec_kv = pieces_of(dec_kv)
    enc_mix, enc_lse = attend(enc_q, enc_kv, source_span, query_block)
    encoded, memory, enc_first, enc_third = encoder_forward(
        source, enc_mix, source_norm, source_out, source_up, source_down, source_cross
    )
    memory = pieces_of(memory)
    dec_mix, dec_lse = attend(dec_q, dec_kv, target_span, query_block)
    cross_q, dec_first = decoder_middle(
        target, dec_mix, target_norm, target_out, target_cross
    )
    cross_mix, cross_lse = attend(cross_q, memory, cross_span, query_block)
    decoded, second_grad, cross_mix_grad, cross_out_grad, dec_up, dec_down, dec_norm = decoder_turn(
        dec_first, cross_mix, target_cot, target_norm, target_cross, target_up, target_down
    )
    result = take_back(encoded, decoded)
    cross_q_grad, memory_grads, _ = attend_back(
        cross_q, memory, cross_mix, cross_mix_grad, cross_lse, cross_span, chunk
    )
    memory_grads = pieces_home(memory_grads)
    dec_first_grad, dec_mix_grad, cross_query_grad, dec_out, step = decoder_middle_back(
        dec_first,
        dec_mix,
        cross_q_grad,
        second_grad,
        target_norm,
        target_out,
        target_cross
    )
    dec_norm += step
    enc_first_grad, enc_mix_grad, enc_cross, enc_out, enc_up, enc_down, enc_norm = encoder_back(
        enc_first,
        enc_third,
        enc_mix,
        memory_grads,
        source_cot,
        source_norm,
        source_out,
        source_up,
        source_down,
        source_cross
    )
    dec_cross = jnp.stack([cross_query_grad, cross_out_grad], axis=1)
    up_grad, down_grad = home(enc_up, dec_up, 1), home(enc_down, dec_down, 0)
    out_grad, cross_grad = home(enc_out, dec_out, 0), home(enc_cross, dec_cross, 2)
    dec_q_grad, dec_kv_grads, _ = attend_back(
        dec_q, dec_kv, dec_mix, dec_mix_grad, dec_lse, target_span, chunk
    )
    dec_kv_grads = pieces_home(dec_kv_grads)
    enc_q_grad, enc_kv_grads, _ = attend_back(
        enc_q, enc_kv, enc_mix, enc_mix_grad, enc_lse, source_span, chunk
    )
    enc_kv_grads = pieces_home(enc_kv_grads)
    target_grad, dec_qkv, _ = input_back(
        target, dec_first_grad, dec_q_grad, dec_kv_grads, target_norm, target_qkv, False
    )
    source_grad, enc_qkv, step = input_back(
        source, enc_first_grad, enc_q_grad, enc_kv_grads, source_norm, source_qkv, True
    )
    enc_norm += step
    token_grad = take_back(source_grad, target_grad).astype(F32)
    qkv_grad = home(enc_qkv, dec_qkv, 2)
    norm_total = lax.psum(jnp.stack([enc_norm, dec_norm]), ("section", "dp", "tensor"))
    norm_grad = lax.dynamic_index_in_dim(norm_total, section, 0, keepdims=False)
    summed = [
        lax.psum(grad, "dp").astype(F32)
        for grad in (qkv_grad, out_grad, cross_grad, up_grad, down_grad)
    ]
    return (
        result[None],
        token_grad[None],
        summed[0][None],
        summed[1][None],
        summed[2][None],
        summed[3][None],
        summed[4][None],
        norm_grad[None],
    )


def local_fast(tokens, lengths, self_qkv, self_out, cross_proj, ffn_up, ffn_down, norms, cotangent):
    _, row_count, rows, width = tokens.shape
    assert row_count == 2
    block = min(256, rows)
    query_block = min(256, rows)
    chunk = 256
    levels = lax.axis_size("dp").bit_length() - 1

    def hops(*steps):
        return list(steps[:levels]) + list(steps[3 : 3 + levels])

    def flat(weight):
        return weight.reshape(-1, weight.shape[-1])

    self_spans, cross_span = Lengths(lengths), Lengths(lengths, 1, 0)
    x, qkv, norm, q, *kv = open_up(tokens[0], flat(self_qkv), norms[0], block, 1)
    qkv = qkv.reshape(2, 2, *self_qkv.shape[1:])

    def parts(weight, side):
        return [At(weight, side, k) for k in range(2)]

    enc_x, dec_x, enc_norm_in, dec_norm_in = At(x, 0), At(x, 1), At(norm, 0), At(norm, 1)
    mix, lse, out, up, cross, down = attend(
        q,
        kv,
        self_spans,
        query_block,
        Carry(
            [
                SpreadWeight(self_out[0], [1], [3]),
                SpreadWeight(ffn_up[0], [2, 3], [4, 5]),
                SpreadWeight(flat(cross_proj), [4], [6]),
                SpreadWeight(ffn_down[0], [5, 6], [7, 7]),
            ],
            2,
        ),
    )
    cross = cross.reshape(2, 2, *cross_proj.shape[1:])
    enc_mix, dec_mix = At(mix, 0), At(mix, 1)
    encoded, memory, enc_first, enc_third, pushed = encoder_forward(
        enc_x,
        enc_mix,
        enc_norm_in,
        parts(out, 0),
        parts(up, 0),
        parts(down, 0),
        parts(cross, 0),
        8,
    )
    memory = [memory, pushed]
    cross_q, dec_first = decoder_middle(
        dec_x, dec_mix, dec_norm_in, parts(out, 1), parts(cross, 1)
    )
    cross_mix, cross_lse, dec_cot = attend(
        cross_q,
        memory,
        cross_span,
        query_block,
        Carry([SpreadRows(cotangent[0], (1,))], 4),
    )
    decoded, second_grad, cross_mix_grad, cross_out_grad, ffn_dec, dec_norm = decoder_turn(
        dec_first,
        cross_mix,
        At(dec_cot, 1),
        dec_norm_in,
        parts(cross, 1),
        parts(up, 1),
        parts(down, 1),
        True,
    )
    cross_q_grad, memory_grads, (ffn_dec, enc_cot) = attend_back(
        cross_q,
        memory,
        cross_mix,
        cross_mix_grad,
        cross_lse,
        cross_span,
        2 * chunk,
        Carry(
            [
                Reduce(ffn_dec, 256, [0, 1, 2, 3], [1, 2], "chip"),
                SpreadRows(cotangent[0], (0,), 4),
            ],
            5,
        ),
        2,
    )
    dec_first_grad, mix_grad, cross_query_grad, dec_out, mid_norm = decoder_middle_back(
        dec_first,
        dec_mix,
        cross_q_grad,
        second_grad,
        dec_norm_in,
        parts(out, 1),
        parts(cross, 1),
        (1, None),
    )
    enc_first_grad, mix_grad, ffn_enc, sides, enc_norm = encoder_back(
        enc_first,
        enc_third,
        enc_mix,
        memory_grads,
        At(enc_cot, 0),
        enc_norm_in,
        parts(out, 0),
        parts(up, 0),
        parts(down, 0),
        parts(cross, 0),
        [dec_out, cross_query_grad, cross_out_grad],
        (0, mix_grad),
    )
    q_grad, kv_grads, moved = attend_back(
        q,
        kv,
        mix,
        mix_grad,
        lse,
        self_spans,
        chunk,
        Carry(
            [
                Reduce(ffn_dec, 512, [0, 1], [1, *hops(2, 1, 1, 1, 2, 3)], "slice"),
                Reduce(ffn_enc, 512, [2, 0], [1, 3, *hops(2, 1, 2, 1, 1, 2)]),
                Reduce(sides, 768, [3, 1], [1, 3, *hops(1, 2, 1, 2, 1, 1)]),
                ReturnRows(encoded, 0, 11),
                ReturnRows(decoded, 1, 12),
            ],
            6,
        ),
        2,
    )
    ffn_dec, ffn_dec_other, ffn_enc, ffn_enc_other, sides, _, encoded, decoded = moved
    tail = (
        ([2, 2, 2, 2, 2, 3], [1, 2, *hops(1, 1, 1, 1, 1, 2)]),
        ([4, 4, 4, 4, 4, 4, 4], [1, 2, *hops(1, 1, 1, 1, 1, 1)]),
        (8, 6),
        8 + 2 * levels,
    )
    enc_last, enc_other, dec_last, dec_other, source_grad, target_grad = close_down(
        x,
        [enc_first_grad, dec_first_grad],
        q_grad,
        kv_grads,
        norm,
        qkv,
        [enc_norm, dec_norm, mid_norm],
        tail,
        7,
    )

    half = 3 * width // 2
    units = ffn_up.shape[-1]

    def columns(source, row, count, target, to):
        wide = source.shape[-1]
        for h in range(2):
            target[to : to + count, h * wide : (h + 1) * wide] = source[
                row + h * count : row + (h + 1) * count, :
            ].astype(F32)

    def finish(fetch, rooms):
        grads, result, up, down, first, second, side, norm_part = range(8)
        room = fetch(grads)
        for row in range(2):
            rooms[0][row] = room[row].astype(F32)
        yield rooms[0]
        yield fetch(result)
        columns(fetch(up), 0, width, rooms[2], 0)
        yield rooms[2]
        rooms[3][...] = fetch(down)[...].astype(F32)
        yield rooms[3]
        room = fetch(side)
        columns(room, 0, width // 2, rooms[4], 0)
        yield rooms[4]
        rooms[5][...] = room[width:, :].astype(F32)
        yield rooms[5]
        columns(fetch(first), 0, half, rooms[6], 0)
        columns(fetch(second), 0, half, rooms[6], half)
        yield rooms[6]
        lines = fetch(norm_part)[...].astype(F32)
        wide = width // PAIR
        for slot in range(3):
            for i in range(2):
                for h in range(wide):
                    line = (2 * slot + i) * wide + h
                    rooms[7][slot, i : i + 1, h * PAIR : (h + 1) * PAIR] = lines[
                        line : line + 1, :
                    ]
        yield rooms[7]

    part = qkv.shape[-1]
    token_grad, result, up_grad, down_grad, out_grad, cross_grad, qkv_grad, norm_grad = lay_out(
        [
            (source_grad, target_grad),
            (encoded, decoded),
            (ffn_enc, ffn_dec_other),
            (ffn_enc_other, ffn_dec),
            (enc_last, dec_other),
            (enc_other, dec_last),
        ],
        [(sides, 0, sides.shape[0]), (enc_last, 2 * half, 32)],
        [
            ((2, rows, width), F32),
            ((2, rows, width), BF16),
            ((width, units), F32),
            ((units, width), F32),
            ((part, width), F32),
            ((2 * width, part), F32),
            ((2 * half, part), F32),
            (norms.shape[1:], F32),
        ],
        finish,
    )
    return (
        result[None],
        token_grad[None],
        qkv_grad.reshape(self_qkv.shape),
        out_grad[None],
        cross_grad.reshape(cross_proj.shape),
        up_grad[None],
        down_grad[None],
        norm_grad[None],
    )


def solution(mesh):
    placed = (
        P("section", "dp", "tensor", None),
        P(None, "dp", None),
        P("section", None, None, "tensor"),
        P("section", "tensor", None),
        P("section", None, None, "tensor"),
        P("section", None, "tensor"),
        P("section", "tensor", None),
        P("section", None, None, None),
        P("section", "dp", "tensor", None),
    )
    sizes = dict(mesh.shape)
    steps = sizes["dp"].bit_length() - 1
    fast = sizes["tensor"] == 2 and sizes["dp"] == 1 << steps and 0 < steps <= 3
    return jax.shard_map(
        local_fast if fast else local_general,
        mesh=mesh,
        in_specs=placed,
        out_specs=(
            P("section", "dp", "tensor", None),
            P("section", "dp", "tensor", None),
            P("section", None, None, "tensor"),
            P("section", "tensor", None),
            P("section", None, None, "tensor"),
            P("section", None, "tensor"),
            P("section", "tensor", None),
            P("section", None, None, None),
        ),
        check_vma=False,
    )
```

```python
import functools
import math

import jax
import jax.numpy as jnp
from jax import lax
from jax.experimental import pallas as pl
from jax.experimental.pallas import tpu as pltpu
from jax.sharding import PartitionSpec as P

HEADS = 8
EPSILON = 1e-05
MASKED = -1000000000.0
LOG2E = 1.0 / math.log(2.0)
PAIR = 128
HALF = 64
VMEM = 60 * 1024 * 1024
BF16 = jnp.bfloat16
F32 = jnp.float32


def standardize(rows):
    mean = jnp.mean(rows, axis=-1, keepdims=True)
    centered = rows - mean
    inv = lax.rsqrt(jnp.mean(centered * centered, axis=-1, keepdims=True) + EPSILON)
    return centered * inv, inv


def affine(unit, norm_ref, slot):
    return unit * norm_ref[slot, 0:1, :] + norm_ref[slot, 1:2, :]


def norm_back(unit, inv, norm_ref, slot, grad, grad_ref):
    grad_ref[slot, 0:1, :] += jnp.sum(grad * unit, axis=0, keepdims=True)
    grad_ref[slot, 1:2, :] += jnp.sum(grad, axis=0, keepdims=True)
    scaled = grad * norm_ref[slot, 0:1, :]
    first = jnp.mean(scaled, axis=-1, keepdims=True)
    second = jnp.mean(scaled * unit, axis=-1, keepdims=True)
    return inv * (scaled - first - unit * second)


def gelu_tanh(inner):
    return jnp.tanh(0.7978845608028654 * (inner + 0.044715 * inner * inner * inner))


def gelu(inner):
    return 0.5 * inner * (1.0 + gelu_tanh(inner))


def gelu_both(inner):
    bent = gelu_tanh(inner)
    slope = 0.7978845608028654 * (1.0 + 0.134145 * inner * inner)
    half = 0.5 * (1.0 + bent)
    return inner * half, half + 0.5 * inner * (1.0 - bent * bent) * slope


def dot_nn(a, b):
    return jnp.dot(a, b, preferred_element_type=F32)


def dot_nt(a, b):
    return lax.dot_general(a, b, (((1,), (1,)), ((), ())), preferred_element_type=F32)


def dot_tn(a, b):
    return lax.dot_general(a, b, (((0,), (0,)), ((), ())), preferred_element_type=F32)


class At:
    def __init__(self, array, *lead):
        self.array, self.lead = array, lead
        self.shape = array.shape[len(lead) :]
        self.dtype = array.dtype

    def spec(self, sizes, index, **options):
        nones = (None,) * len(self.lead)
        return pl.BlockSpec(nones + tuple(sizes), lambda *g: self.lead + tuple(index(*g)), **options)


def at(array):
    return array if isinstance(array, At) else At(array)


def row_call(
    body, name, rows, row_ins, whole_ins, row_outs, keeps, finals, finish, flops, into=None, push=None
):
    block, part = min(512, rows), min(256, rows)
    row_ins = [(at(a), dim) for a, dim in row_ins]
    whole_ins = [at(a) for a in whole_ins]

    def blocked(array, dim):
        sizes = tuple(block if i == dim else size for i, size in enumerate(array.shape))
        return array.spec(sizes, lambda g: tuple(g if i == dim else 0 for i in range(len(sizes))))

    def blocked_out(shape, dim):
        sizes = tuple(block if i == dim else size for i, size in enumerate(shape))
        return pl.BlockSpec(
            sizes, lambda g: tuple(g if i == dim else 0 for i in range(len(shape)))
        )

    def sided_out(shape, dim):
        plain = blocked_out(shape, dim)
        return pl.BlockSpec(
            (None, *plain.block_shape), lambda g: (into[0], *plain.index_map(g))
        )

    def whole(array):
        return array.spec(
            array.shape,
            lambda g: (0,) * len(array.shape),
            pipeline_mode=pl.Buffered(buffer_count=1),
        )

    def whole_out(shape):
        return pl.BlockSpec(
            shape, lambda g: (0,) * len(shape), pipeline_mode=pl.Buffered(buffer_count=1)
        )

    n_rows_in = len(row_ins)
    n_in = n_rows_in + len(whole_ins)
    n_row, n_final = len(row_outs), len(finals)
    out_specs = [blocked_out(shape, dim) for shape, _, dim in row_outs]
    out_shapes = [jax.ShapeDtypeStruct(shape, dtype) for shape, dtype, _ in row_outs]
    push_outs, push_scratch, push_params = [], [], {}
    if push is not None:
        push_outs = [out_shapes[push[0]]]
        push_scratch = [
            pltpu.VMEM(push_outs[0].shape, push_outs[0].dtype),
            pltpu.SemaphoreType.DMA((2, rows // block)),
        ]
        push_params = dict(collective_id=push[1], has_side_effects=True)
    held, aliases = [], {}
    if into is not None:
        shape, dtype, dim = row_outs[-1]
        out_specs[-1] = sided_out(shape, dim)
        out_shapes[-1] = jax.ShapeDtypeStruct((2, *shape), dtype)
        if into[1] is not None:
            held, aliases = [into[1]], {n_in: n_row - 1}

    def kernel(*refs):
        ins, refs = refs[:n_in], refs[len(held) :]
        outs = refs[n_in : n_in + n_row]
        last_outs, kept = refs[n_in + n_row : n_in + n_row + n_final], refs[n_in + n_row + n_final :]
        step = pl.program_id(0)
        if push is not None:
            pushed, kept = kept[0], kept[1:]
            kept, (push_room, push_sems) = kept[:-2], kept[-2:]

            def send(i):
                own = pl.ds(i * block, block)
                return remote(
                    push_room.at[:, :, own, :],
                    pushed.at[:, :, own, :],
                    push_sems.at[0, i],
                    push_sems.at[1, i],
                    where_is("near"),
                )

            @pl.when(step == 0)
            def _():
                greet(["near"])
        if finals:

            @pl.when(step == 0)
            def _():
                kept[-1][...] = jnp.zeros_like(kept[-1])

        turns = []
        for begin in range(0, block, part):
            all_rows = pl.ds(pl.multiple_of(step * block + begin, part), part)
            turns.append(body(ins, outs, kept, slice(begin, begin + part), all_rows))
        waiting, running = turns[1:], turns[:1]
        while running:
            running = [turn for turn in running if next(turn, LAST) is not LAST]
            if waiting:
                running.append(waiting.pop(0))

        if push is not None:
            for i in range(rows // block):

                @pl.when(step == i)
                def _():
                    push_room[:, :, i * block : (i + 1) * block, :] = outs[push[0]][...]
                    send(i).start()

            @pl.when(step == pl.num_programs(0) - 1)
            def _():
                for i in range(rows // block):
                    send(i).wait()

        if finals:

            @pl.when(step == pl.num_programs(0) - 1)
            def _():
                finish(ins[n_rows_in:], kept, last_outs)

    arrays = [array for array, _ in row_ins] + whole_ins
    size = sum(math.prod(a.shape) * a.dtype.itemsize for a in arrays)
    return pl.pallas_call(
        kernel,
        grid=(rows // block,),
        in_specs=[blocked(a, dim) for a, dim in row_ins]
        + [whole(a) for a in whole_ins]
        + [pl.BlockSpec(memory_space=pl.ANY)] * len(held),
        out_specs=out_specs
        + [whole_out(shape) for shape, _ in finals]
        + [pl.BlockSpec(memory_space=pl.ANY)] * len(push_outs),
        out_shape=out_shapes
        + [jax.ShapeDtypeStruct(shape, dtype) for shape, dtype in finals]
        + push_outs,
        input_output_aliases=aliases,
        scratch_shapes=[pltpu.VMEM(shape, dtype) for shape, dtype in keeps] + push_scratch,
        compiler_params=pltpu.CompilerParams(vmem_limit_bytes=VMEM, **push_params),
        cost_estimate=pl.CostEstimate(flops=flops, bytes_accessed=size, transcendentals=0),
        name=name,
    )(*[a.array for a in arrays], *held)


LAST = 1000


def split(refs, parts, count):
    return [refs[i * parts : (i + 1) * parts] for i in range(count)]


def project_qkv(x, norm, weights, with_norm):
    x = at(x)
    rows, width = x.shape
    parts, part = len(weights), weights[0].shape[-1]
    score = LOG2E / math.sqrt(width // HEADS)

    def body(ins, outs, kept, own, all_rows):
        x_ref, norm_ref, *w = ins
        q_ref, kv_ref = outs
        low = x_ref[own, :]
        if with_norm:
            unit, _ = standardize(low.astype(F32))
            low = affine(unit, norm_ref, 2).astype(BF16)
        yield
        for k in range(parts):
            q_ref[k, own, :] = (dot_nn(low, w[k][0]) * score).astype(BF16)
            kv_ref[k, 0, own, :] = dot_nn(low, w[k][1]).astype(BF16)
            kv_ref[k, 1, own, :] = dot_nn(low, w[k][2]).astype(BF16)
            yield

    return row_call(
        body,
        "project_qkv",
        rows,
        [(x, 0)],
        [norm, *weights],
        [((parts, rows, part), BF16, 1), ((parts, 2, rows, part), BF16, 2)],
        [],
        [],
        None,
        6 * rows * width * width,
    )


def encoder_forward(x, mix, norm, out, up, down, cross, push=None):
    x = at(x)
    rows, width = x.shape
    parts, part = len(out), out[0].shape[0]

    def body(ins, outs, kept, own, all_rows):
        x_ref, mix_ref, norm_ref = ins[:3]
        wo, wu, wd, wc = split(ins[3:], parts, 4)
        result_ref, kv_ref, first_ref, third_ref = outs
        unit, _ = standardize(x_ref[own, :].astype(F32))
        first = affine(unit, norm_ref, 2)
        for k in range(parts):
            first += dot_nn(mix_ref[k, own, :], wo[k][...])
        yield
        first_ref[own, :] = first
        unit, _ = standardize(first)
        third = affine(unit, norm_ref, 0)
        low = third.astype(BF16)
        inner = dot_nn(low, wu[0][...])
        yield
        for k in range(parts):
            act = gelu(inner).astype(BF16)
            if k + 1 < parts:
                inner = dot_nn(low, wu[k + 1][...])
            third += dot_nn(act, wd[k][...])
            yield
        third_ref[own, :] = third
        unit, _ = standardize(third)
        low = affine(unit, norm_ref, 1).astype(BF16)
        result_ref[own, :] = low
        yield
        for k in range(parts):
            kv_ref[k, 0, own, :] = dot_nn(low, wc[k][0]).astype(BF16)
            kv_ref[k, 1, own, :] = dot_nn(low, wc[k][1]).astype(BF16)

    units = sum(w.shape[1] for w in up)
    return row_call(
        body,
        "encoder_forward",
        rows,
        [(x, 0), (mix, 1)],
        [norm, *out, *up, *down, *cross],
        [
            ((rows, width), BF16, 0),
            ((parts, 2, rows, part), BF16, 2),
            ((rows, width), F32, 0),
            ((rows, width), F32, 0),
        ],
        [],
        [],
        None,
        6 * rows * width * width + 4 * rows * width * units,
        push=None if push is None else (1, push),
    )


def decoder_middle(x, mix, norm, out, cross):
    x = at(x)
    rows, width = x.shape
    parts, part = len(out), out[0].shape[0]
    score = LOG2E / math.sqrt(width // HEADS)

    def body(ins, outs, kept, own, all_rows):
        x_ref, mix_ref, norm_ref = ins[:3]
        wo, wc = split(ins[3:], parts, 2)
        q_ref, first_ref = outs
        first = x_ref[own, :].astype(F32)
        for k in range(parts):
            first += dot_nn(mix_ref[k, own, :], wo[k][...])
        yield
        first_ref[own, :] = first
        unit, _ = standardize(first)
        low = affine(unit, norm_ref, 0).astype(BF16)
        yield
        for k in range(parts):
            q_ref[k, own, :] = (dot_nn(low, wc[k][0]) * score).astype(BF16)

    return row_call(
        body,
        "decoder_middle",
        rows,
        [(x, 0), (mix, 1)],
        [norm, *out, *cross],
        [((parts, rows, part), BF16, 1), ((rows, width), F32, 0)],
        [],
        [],
        None,
        4 * rows * width * width,
    )


def ffn_finals(low, act, inner, grad, parts, units, paired, up_out, down_out):
    for k in range(parts):
        if paired:
            half = units // 2
            for h in range(2):
                begin = k * units + h * half
                up_out[0, k, h * half : (h + 1) * half, :] = dot_tn(
                    low[...], inner[:, begin : begin + half]
                ).astype(BF16)
            into = up_out.at[1, k]
        else:
            up_out[k] = dot_tn(low[...], inner[:, k * units : (k + 1) * units]).astype(BF16)
            into = down_out.at[k]
        into[...] = dot_tn(act[:, k * units : (k + 1) * units], grad[...]).astype(BF16)


def decoder_turn(first, mix, cotangent, norm, cross, up, down, paired=False):
    rows, width = first.shape
    parts, part, units = len(cross), cross[0].shape[-1], up[0].shape[1]

    def body(ins, outs, kept, own, all_rows):
        first_ref, cot_ref, mix_ref, norm_ref = ins[:4]
        wc, wu, wd = split(ins[4:], parts, 3)
        result_ref, second_grad_ref, mix_grad_ref = outs
        low_keep, act_keep, inner_keep, third_keep, second_keep, norm_total = kept
        unit, _ = standardize(first_ref[own, :])
        second = affine(unit, norm_ref, 0)
        for k in range(parts):
            second += dot_nt(mix_ref[k, all_rows, :], wc[k][1])
        yield
        unit_two, inv_two = standardize(second)
        third = affine(unit_two, norm_ref, 2)
        low = third.astype(BF16)
        low_keep[all_rows, :] = low
        inner = dot_nn(low, wu[0][...])
        yield
        slopes = []
        for k in range(parts):
            act, slope = gelu_both(inner)
            act = act.astype(BF16)
            slopes.append(slope)
            if k + 1 < parts:
                inner = dot_nn(low, wu[k + 1][...])
            act_keep[all_rows, k * units : (k + 1) * units] = act
            third += dot_nn(act, wd[k][...])
            yield
        unit_three, inv_three = standardize(third)
        result_ref[own, :] = affine(unit_three, norm_ref, 1).astype(BF16)
        grad = norm_back(
            unit_three, inv_three, norm_ref, 1, cot_ref[own, :].astype(F32), norm_total
        )
        grad_low = grad.astype(BF16)
        third_keep[all_rows, :] = grad_low
        grad_act = dot_nt(grad_low, wd[0][...])
        yield
        for k in range(parts):
            grad_inner = (grad_act * slopes[k]).astype(BF16)
            if k + 1 < parts:
                grad_act = dot_nt(grad_low, wd[k + 1][...])
            inner_keep[all_rows, k * units : (k + 1) * units] = grad_inner
            grad += dot_nt(grad_inner, wu[k][...])
            yield
        grad = norm_back(unit_two, inv_two, norm_ref, 2, grad, norm_total)
        second_grad_ref[own, :] = grad
        grad_low = grad.astype(BF16)
        second_keep[all_rows, :] = grad_low
        yield
        for k in range(parts):
            mix_grad_ref[k, own, :] = dot_nn(grad_low, wc[k][1]).astype(BF16)

    def finish(ins, kept, outs):
        mix_ref = ins[0]
        low_keep, act_keep, inner_keep, third_keep, second_keep, norm_total = kept
        for k in range(parts):
            outs[0][k] = dot_tn(second_keep[...], mix_ref[k]).astype(BF16)
        ffn_finals(
            low_keep, act_keep, inner_keep, third_keep, parts, units, paired, outs[1], outs[2]
        )
        outs[-1][...] = norm_total[...]

    ffn = (
        [((2, parts, units, width), BF16)]
        if paired
        else [((parts, width, units), BF16), ((parts, units, width), BF16)]
    )
    whole = (rows, width)
    return row_call(
        body,
        "decoder_turn",
        rows,
        [(first, 0), (cotangent, 0)],
        [mix, norm, *cross, *up, *down],
        [(whole, BF16, 0), (whole, F32, 0), ((parts, rows, part), BF16, 1)],
        [
            (whole, BF16),
            ((rows, parts * units), BF16),
            ((rows, parts * units), BF16),
            (whole, BF16),
            (whole, BF16),
            ((3, 2, width), F32),
        ],
        [((parts, width, part), BF16), *ffn, ((3, 2, width), F32)],
        finish,
        6 * rows * width * width + 12 * rows * width * units * parts,
    )


def decoder_middle_back(first, mix, query_grad, second_grad, norm, out, cross, into=None):
    rows, width = first.shape
    parts, part = len(out), out[0].shape[0]

    def body(ins, outs, kept, own, all_rows):
        first_ref, second_grad_ref, mix_ref, query_grad_ref, norm_ref = ins[:5]
        wo, wc = split(ins[5:], parts, 2)
        first_grad_ref, mix_grad_ref = outs
        low_keep, grad_keep, norm_total = kept
        unit, inv = standardize(first_ref[own, :])
        low_keep[all_rows, :] = affine(unit, norm_ref, 0).astype(BF16)
        grad = second_grad_ref[own, :]
        for k in range(parts):
            grad += dot_nt(query_grad_ref[k, all_rows, :], wc[k][0])
        yield
        grad = norm_back(unit, inv, norm_ref, 0, grad, norm_total)
        first_grad_ref[own, :] = grad
        grad_low = grad.astype(BF16)
        grad_keep[all_rows, :] = grad_low
        yield
        for k in range(parts):
            mix_grad_ref[k, own, :] = dot_nt(grad_low, wo[k][...]).astype(BF16)

    def finish(ins, kept, outs):
        mix_ref, query_grad_ref = ins[:2]
        low_keep, grad_keep, norm_total = kept
        for k in range(parts):
            outs[0][k] = dot_tn(low_keep[...], query_grad_ref[k]).astype(BF16)
            outs[1][k] = dot_tn(mix_ref[k], grad_keep[...]).astype(BF16)
        outs[2][...] = norm_total[...]

    whole = (rows, width)
    return row_call(
        body,
        "decoder_middle_back",
        rows,
        [(first, 0), (second_grad, 0)],
        [mix, query_grad, norm, *out, *cross],
        [(whole, F32, 0), ((parts, rows, part), BF16, 1)],
        [(whole, BF16), (whole, BF16), ((3, 2, width), F32)],
        [
            ((parts, width, part), BF16),
            ((parts, part, width), BF16),
            ((3, 2, width), F32),
        ],
        finish,
        8 * rows * width * width,
        into,
    )


def added(refs, *index):
    total = refs[0][index]
    for ref in refs[1:]:
        total = total.astype(F32) + ref[index].astype(F32)
    return total.astype(BF16)


def encoder_back(
    first, third, mix, memory_grads, cotangent, norm, out, up, down, cross, paired=None, into=None
):
    rows, width = first.shape
    parts, part, units = len(out), out[0].shape[0], up[0].shape[1]
    pieces = len(memory_grads)

    def body(ins, outs, kept, own, all_rows):
        first_ref, third_ref, cot_ref = ins[:3]
        memory_refs, mix_ref, norm_ref = ins[3 : 3 + pieces], ins[3 + pieces], ins[4 + pieces]
        wo, wu, wd, wc = split(ins[5 + pieces :], parts, 4)
        first_grad_ref, mix_grad_ref = outs
        low_keep, memory_keep, mid_keep, act_keep, inner_keep, third_keep, first_keep, norm_total = (
            kept
        )
        grad = cot_ref[own, :].astype(F32)
        for k in range(parts):
            for i in range(2):
                memory = added(memory_refs, k, i, own)
                memory_keep[k, i, all_rows, :] = memory
                grad += dot_nt(memory, wc[k][i])
        yield
        unit, inv = standardize(third_ref[own, :])
        low_keep[all_rows, :] = affine(unit, norm_ref, 1).astype(BF16)
        unit_one, inv_one = standardize(first_ref[own, :])
        low = affine(unit_one, norm_ref, 0).astype(BF16)
        mid_keep[all_rows, :] = low
        inner = dot_nn(low, wu[0][...])
        grad = norm_back(unit, inv, norm_ref, 1, grad, norm_total)
        grad_low = grad.astype(BF16)
        third_keep[all_rows, :] = grad_low
        grad_act = dot_nt(grad_low, wd[0][...])
        yield
        for k in range(parts):
            act, slope = gelu_both(inner)
            if k + 1 < parts:
                inner = dot_nn(low, wu[k + 1][...])
            act_keep[all_rows, k * units : (k + 1) * units] = act.astype(BF16)
            grad_inner = (grad_act * slope).astype(BF16)
            if k + 1 < parts:
                grad_act = dot_nt(grad_low, wd[k + 1][...])
            inner_keep[all_rows, k * units : (k + 1) * units] = grad_inner
            grad += dot_nt(grad_inner, wu[k][...])
            yield
        grad = norm_back(unit_one, inv_one, norm_ref, 0, grad, norm_total)
        first_grad_ref[own, :] = grad
        grad_low = grad.astype(BF16)
        first_keep[all_rows, :] = grad_low
        yield
        for k in range(parts):
            mix_grad_ref[k, own, :] = dot_nt(grad_low, wo[k][...]).astype(BF16)

    def finish(ins, kept, outs):
        mix_ref = ins[0]
        low_keep, memory_keep, mid_keep, act_keep, inner_keep, third_keep, first_keep, norm_total = (
            kept
        )
        if paired:
            ffn_finals(
                mid_keep, act_keep, inner_keep, third_keep, parts, units, True, outs[0], None
            )
            dec_out, dec_query, dec_cross = ins[-3:]
            sides = outs[1]
            for k in range(parts):
                column_blocks(dot_tn(mix_ref[k], first_keep[...]), sides, 0, k, 0)
                column_blocks(dec_out[k], sides, 1, k, 0)
                for i in range(2):
                    here = slice((1 + i) * width, (2 + i) * width)
                    sides[0, k, here, :] = dot_tn(low_keep[...], memory_keep[k, i]).astype(BF16)
                    sides[1, k, here, :] = (dec_query, dec_cross)[i][k]
        else:
            for k in range(parts):
                for i in range(2):
                    outs[0][k, i] = dot_tn(low_keep[...], memory_keep[k, i]).astype(BF16)
                outs[1][k] = dot_tn(mix_ref[k], first_keep[...]).astype(BF16)
            ffn_finals(
                mid_keep, act_keep, inner_keep, third_keep, parts, units, False, outs[2], outs[3]
            )
        outs[-1][...] = norm_total[...]

    if paired:
        finals = [((2, parts, units, width), BF16), ((2, parts, 3 * width, part), BF16)]
    else:
        finals = [
            ((parts, 2, width, part), BF16),
            ((parts, part, width), BF16),
            ((parts, width, units), BF16),
            ((parts, units, width), BF16),
        ]
    whole = (rows, width)
    return row_call(
        body,
        "encoder_back",
        rows,
        [(first, 0), (third, 0), (cotangent, 0)] + [(m, 2) for m in memory_grads],
        [mix, norm, *out, *up, *down, *cross, *(paired or [])],
        [(whole, F32, 0), ((parts, rows, part), BF16, 1)],
        [
            (whole, BF16),
            ((parts, 2, rows, part), BF16),
            (whole, BF16),
            ((rows, parts * units), BF16),
            ((rows, parts * units), BF16),
            (whole, BF16),
            (whole, BF16),
            ((3, 2, width), F32),
        ],
        [*finals, ((3, 2, width), F32)],
        finish,
        12 * rows * width * width + 10 * rows * width * units * parts,
        into,
    )


def column_blocks(wide, into, core, k, row):
    rows, columns = wide.shape[0], wide.shape[1] // 2
    for half in range(2):
        into[core, k, row + half * rows : row + (half + 1) * rows, :] = wide[
            :, half * columns : (half + 1) * columns
        ].astype(BF16)


def input_part(refs, kept, own, all_rows, norm_ref, w, with_norm):
    x_ref, first_grad_ref, key_refs, query_grad_ref, grad_ref = refs
    low_keep, key_keep, norm_total = kept
    grad = first_grad_ref[own, :]
    for k in range(len(w)):
        grad += dot_nt(query_grad_ref[k, all_rows, :], w[k][0])
        for i in range(2):
            member = added(key_refs, k, i, own)
            key_keep[k, i, all_rows, :] = member
            grad += dot_nt(member, w[k][1 + i])
    yield
    low = x_ref[own, :]
    if with_norm:
        unit, inv = standardize(low.astype(F32))
        low = affine(unit, norm_ref, 2).astype(BF16)
        grad = norm_back(unit, inv, norm_ref, 2, grad, norm_total)
    low_keep[all_rows, :] = low
    grad_ref[own, :] = grad.astype(BF16)


def input_sums(kept, query_grad_ref, into, parts):
    low_keep, key_keep, _ = kept
    for k in range(parts):
        both = jnp.concatenate(
            [dot_tn(low_keep[...], query_grad_ref[k])]
            + [dot_tn(low_keep[...], key_keep[k, i]) for i in range(2)],
            axis=0,
        )
        half = both.shape[0] // 2
        for core in range(2):
            column_blocks(both[core * half : (core + 1) * half], into, core, k, 0)


def norm_lines(sides, into, parts, row):
    for core, table in enumerate(sides):
        lines = [
            table[slot, i : i + 1, h * PAIR : (h + 1) * PAIR]
            for slot in range(3)
            for i in range(2)
            for h in range(table.shape[-1] // PAIR)
        ]
        lines.append(jnp.zeros((2 * PAIR - len(lines), PAIR), F32))
        lines = jnp.concatenate(lines, axis=0).astype(BF16)
        for k in range(parts):
            into[core, k, row:, :] = lines


def input_back(x, first_grad, query_grad, key_grads, norm, weights, with_norm):
    x = at(x)
    rows, width = x.shape
    parts, part = len(weights), weights[0].shape[-1]
    pieces = len(key_grads)
    key_grads = [at(g) for g in key_grads]

    def body(ins, outs, kept, own, all_rows):
        x_ref, first_grad_ref = ins[:2]
        key_refs, query_grad_ref, norm_ref = ins[2 : 2 + pieces], ins[2 + pieces], ins[3 + pieces]
        refs = x_ref, first_grad_ref, key_refs, query_grad_ref, outs[0]
        yield from input_part(refs, kept, own, all_rows, norm_ref, ins[4 + pieces :], with_norm)

    def finish(ins, kept, outs):
        query_grad_ref = ins[0]
        low_keep, key_keep, norm_total = kept
        for k in range(parts):
            outs[0][k, 0] = dot_tn(low_keep[...], query_grad_ref[k]).astype(BF16)
            for i in range(2):
                outs[0][k, 1 + i] = dot_tn(low_keep[...], key_keep[k, i]).astype(BF16)
        outs[1][...] = norm_total[...]

    whole = (rows, width)
    return row_call(
        body,
        "input_back",
        rows,
        [(x, 0), (first_grad, 0)] + [(g, 2) for g in key_grads],
        [query_grad, norm, *weights],
        [(whole, BF16, 0)],
        [(whole, BF16), ((parts, 2, rows, part), BF16), ((3, 2, width), F32)],
        [((parts, 3, width, part), BF16), ((3, 2, width), F32)],
        finish,
        12 * rows * width * width,
    )


def widen_keys(span, kv_refs, key_e, key_o, value_e, value_o, rows):
    lane = lax.broadcasted_iota(jnp.int32, (rows, PAIR), 1)
    place = lax.broadcasted_iota(jnp.int32, (rows, PAIR), 0)
    low = lane < HALF
    for g, kv_ref in enumerate(kv_refs):
        spot = place + span[2 + g]
        live = (spot >= span[0]) & (spot < span[1])
        bias = jnp.where(live, 0.0, MASKED)
        keys, values = kv_ref[0].astype(F32), kv_ref[1].astype(F32)
        own = pl.ds(g * rows, rows)
        key_e[own, :] = jnp.where(low, keys, jnp.where(lane == HALF, bias, 1.0)).astype(BF16)
        key_o[own, :] = jnp.where(low, jnp.where(lane == 0, bias, 1.0), keys).astype(BF16)
        value_e[own, :] = jnp.where(low, values, 1.0).astype(BF16)
        value_o[own, :] = jnp.where(low, 1.0, values).astype(BF16)


class Lengths:
    def __init__(self, lengths, asking=None, answering=None):
        self.lengths, self.asking, self.answering = lengths, asking, answering

    def span(self, ref, side, rows):
        section, _, tensor = spots()
        asks, answers = [
            [ref[side if own is None else own, tensor, j] for j in range(2)]
            for own in (self.asking, self.answering)
        ]
        paired = asks[1] > 0
        second = paired & (section * rows >= asks[0])
        begin = jnp.where(second, answers[0], 0)
        end = jnp.where(second | jnp.logical_not(paired), answers[0] + answers[1], answers[0])
        return [begin, end, section * rows, (1 - section) * rows]


class Pairs:
    def __init__(self, query):
        self.sides = query.shape[:-3]
        self.parts, self.rows, self.part = query.shape[-3:]
        self.per_part = self.part // PAIR
        self.per_side = self.parts * self.per_part
        self.count = self.per_side * math.prod(self.sides)

    def side(self, i):
        return (i // self.per_side,) if self.sides else ()

    def place(self, i):
        i = i % self.per_side
        return i // self.per_part, i % self.per_part

    def query_spec(self, array):
        def index(i):
            part, column = self.place(i)
            return *self.side(i), part, 0, column

        none = (None,) * len(self.sides)
        return at(array).spec((*none, None, self.rows, PAIR), index)

    def kv_spec(self, array):
        def index(i):
            part, column = self.place(i)
            return *self.side(i), part, 0, 0, column

        none = (None,) * len(self.sides)
        return at(array).spec((*none, None, 2, self.rows, PAIR), index)

    def lse_spec(self):
        none = (None,) * len(self.sides)
        return pl.BlockSpec(
            (*none, self.rows, PAIR), lambda i: (*self.side(i), 0, i % self.per_side)
        )

    def span(self, span, span_ref, i):
        side = i // self.per_side if self.sides else 0
        if isinstance(span, Lengths):
            return span.span(span_ref, side, self.rows)
        return [span_ref[side, j] for j in range(span_ref.shape[1])]


def attend(query, kv_pieces, span, block, carrier=None, slots=1):
    query, kv_pieces = at(query), [at(piece) for piece in kv_pieces]
    carrier = carrier or Carry()
    heads_of = Pairs(query)
    rows, pairs = heads_of.rows, heads_of.count
    pieces = len(kv_pieces)
    keys = rows * pieces
    n_carry = len(carrier.ins)
    blocks = rows // block
    stride = blocks // slots

    def kernel(span_ref, q_ref, *refs):
        kv_refs, refs = refs[:pieces], refs[pieces:]
        carry_ins, refs = refs[:n_carry], refs[n_carry:]
        out_ref, lse_ref, refs = refs[0], refs[1], refs[2:]
        carry_outs, refs = refs[: len(carrier.outs)], refs[len(carrier.outs) :]
        key_e, key_o, value_e, value_o = refs[:4]

        def carry(slot):
            place = pl.program_id(0)
            carrier.run(place, slot, slots, pairs * slots, carry_ins, carry_outs, refs[4:])

        carry(0)
        seen = heads_of.span(span, span_ref, pl.program_id(0))
        widen_keys(seen, kv_refs, key_e, key_o, value_e, value_o, rows)
        lane = lax.broadcasted_iota(jnp.int32, (block, PAIR), 1)
        low = lane < HALF
        units = []
        for i in range(blocks):
            query = q_ref[i * block : (i + 1) * block, :].astype(F32)
            first = jnp.where(low, query, jnp.where(lane == HALF, 1.0, 0.0)).astype(BF16)
            second = jnp.where(low, jnp.where(lane == 0, 1.0, 0.0), query).astype(BF16)
            units += [(first, key_e, value_e), (second, key_o, value_o)]

        def scores_of(unit):
            return dot_nt(unit[0], unit[1][...])

        ahead = scores_of(units[0])
        tops, sums = [], []
        for u, unit in enumerate(units):
            if u and u % (2 * stride) == 0:
                carry(u // (2 * stride))
            scores = ahead
            if u + 1 < len(units):
                ahead = scores_of(units[u + 1])
            top = jnp.max(scores, axis=1, keepdims=True)
            tops.append(top)
            sums.append(dot_nn(jnp.exp2(scores - top).astype(BF16), unit[2][...]))
            if u % 2:
                own = slice(u // 2 * block, (u // 2 + 1) * block)
                top = jnp.where(low, tops[u], tops[u - 1])
                weight = jnp.where(low, sums[u], sums[u - 1])
                lse_ref[own, :] = top + LOG2E * jnp.log(weight)
                mixed = jnp.where(low, sums[u - 1], sums[u])
                out_ref[own, :] = (mixed / pltpu.roll(weight, HALF, 1)).astype(BF16)
        carry(slots)

    query_spec, kv_spec = heads_of.query_spec, heads_of.kv_spec
    lse_spec = heads_of.lse_spec()
    plain = jax.ShapeDtypeStruct(query.shape, BF16)
    hold = pl.BlockSpec(memory_space=pl.ANY)
    return pl.pallas_call(
        kernel,
        grid=(pairs,),
        in_specs=[pl.BlockSpec(memory_space=pltpu.SMEM), query_spec(query)]
        + [kv_spec(piece) for piece in kv_pieces]
        + [hold] * n_carry,
        out_specs=[query_spec(plain), lse_spec] + [hold] * len(carrier.outs),
        scratch_shapes=[pltpu.VMEM((keys, PAIR), BF16)] * 4 + carrier.scratch,
        out_shape=[plain, jax.ShapeDtypeStruct((*heads_of.sides, rows, heads_of.per_side * PAIR), F32)] + carrier.outs,
        compiler_params=pltpu.CompilerParams(vmem_limit_bytes=VMEM, **carrier.params),
        cost_estimate=pl.CostEstimate(
            flops=16 * rows * keys * pairs * PAIR,
            bytes_accessed=8 * rows * pairs * PAIR * pieces,
            transcendentals=0,
        ),
        name="attend",
    )(
        span.lengths if isinstance(span, Lengths) else span, query.array, *[piece.array for piece in kv_pieces], *carrier.ins)


def attend_back(
    query, kv_pieces, mix, mix_grad, lse, span, chunk, carrier=None, slots=1
):
    query, kv_pieces = at(query), [at(piece) for piece in kv_pieces]
    mix, mix_grad = at(mix), at(mix_grad)
    heads_of = Pairs(query)
    rows, pairs = heads_of.rows, heads_of.count
    pieces = len(kv_pieces)
    keys = rows * pieces
    scale = 1.0 / math.sqrt(HALF)
    swaps = carrier is not None
    carrier = carrier or Carry()
    n_carry = len(carrier.ins)
    kept = 1 if swaps else pieces
    chunks = keys // chunk
    stride = chunks // slots

    def kernel(span_ref, q_ref, mix_ref, grad_ref, lse_ref, *refs):
        kv_refs, refs = refs[:pieces], refs[pieces:]
        carry_ins, refs = refs[:n_carry], refs[n_carry:]
        dq_ref, dkv_refs, refs = refs[0], refs[1 : pieces + 1], refs[pieces + 1 :]
        carry_outs, refs = refs[: len(carrier.outs)], refs[len(carrier.outs) :]
        key_e, key_o, value_e, value_o, key_t = refs[:5]
        refs = refs[5:]
        if swaps:
            given, swap_sems, refs = refs[0], refs[1], refs[2:]
        pair = pl.program_id(0)

        def carry(slot):
            carrier.run(pair, slot, slots, pairs * slots, carry_ins, carry_outs, refs)

        carry(0)
        seen = heads_of.span(span, span_ref, pl.program_id(0))
        widen_keys(seen, kv_refs, key_e, key_o, value_e, value_o, rows)
        for g, kv_ref in enumerate(kv_refs):
            key_t[:, g * rows : (g + 1) * rows] = kv_ref[0].T
        lane = lax.broadcasted_iota(jnp.int32, (rows, PAIR), 1)
        low = lane < HALF
        query, grad = q_ref[...].astype(F32), grad_ref[...].astype(F32)
        product = mix_ref[...].astype(F32) * grad
        inner = jnp.where(
            low,
            jnp.sum(jnp.where(low, 0.0, product), axis=1, keepdims=True),
            jnp.sum(jnp.where(low, product, 0.0), axis=1, keepdims=True),
        )
        spot = jnp.where(low, lane, lane - HALF)

        def three(value, shift):
            high = value.astype(BF16).astype(F32)
            rest = value - high
            mid = rest.astype(BF16).astype(F32)
            return jnp.where(
                spot == shift,
                high,
                jnp.where(
                    spot == shift + 1, mid, jnp.where(spot == shift + 2, rest - mid, 0.0)
                ),
            )

        lse = three(-lse_ref[...], 1) + jnp.where(spot == 0, 1.0, 0.0)
        inner = three(-inner, 0)
        heads = [
            (
                key,
                value,
                jnp.where(own, query, lse).astype(BF16).T,
                jnp.where(own, grad, inner).astype(BF16).T,
                jnp.where(own, query, 0.0).astype(BF16),
                jnp.where(own, grad, 0.0).astype(BF16),
            )
            for own, key, value in ((low, key_e, value_e), (~low, key_o, value_o))
        ]
        units = [(c * chunk, h) for c in range(chunks) for h in range(2)]

        def front(unit):
            begin, h = unit
            own = slice(begin, begin + chunk)
            key, value, q_wide, g_wide, _, _ = heads[h]
            return dot_nn(key[own, :], q_wide), dot_nn(value[own, :], g_wide)

        ahead = front(units[0])
        dq = [None, None]
        for u, (begin, h) in enumerate(units):
            if u and u % (2 * stride) == 0:
                carry(u // (2 * stride))
            scores, dprobs = ahead
            if u + 1 < len(units):
                ahead = front(units[u + 1])
            probs = jnp.exp2(scores)
            dscores = (probs * dprobs).astype(BF16)
            _, _, _, _, q_own, g_own = heads[h]
            step_v = dot_nn(probs.astype(BF16), g_own)
            step_k = dot_nn(dscores, q_own)
            step_q = dot_nn(key_t[h * HALF : (h + 1) * HALF, begin : begin + chunk], dscores)
            dq[h] = step_q if dq[h] is None else dq[h] + step_q
            if h == 0:
                dv, dk = step_v, step_k
            else:
                g, first = begin // rows, begin % rows
                own = slice(first, first + chunk)
                dk = ((dk + step_k) * (1.0 / LOG2E)).astype(BF16)
                dv = (dv + step_v).astype(BF16)
                if g < kept:
                    dkv_refs[g][0, own, :] = dk
                    dkv_refs[g][1, own, :] = dv
                else:
                    given[pair, 0, own, :] = dk
                    given[pair, 1, own, :] = dv
        dq_ref[...] = (jnp.concatenate(dq, axis=0).T * scale).astype(BF16)
        if swaps:
            part, column = heads_of.place(pair)
            columns = pl.ds(pl.multiple_of(column * PAIR, PAIR), PAIR)
            spot = (*heads_of.side(pair), part, slice(None), slice(None), columns)

            def swap(i):
                return remote(
                    given.at[i],
                    dkv_refs[1].at[spot],
                    swap_sems.at[0, i],
                    swap_sems.at[1, i],
                    where_is("near"),
                )

            swap(pair).start()

            @pl.when(pair == pairs - 1)
            def _():
                for i in range(pairs):
                    swap(i).wait()

        carry(slots)

    query_spec, kv_spec = heads_of.query_spec, heads_of.kv_spec
    lse_spec = heads_of.lse_spec()
    plain = jax.ShapeDtypeStruct(query.shape, BF16)
    plain_kv = jax.ShapeDtypeStruct(
        (*heads_of.sides, heads_of.parts, 2, rows, heads_of.part), BF16
    )
    hold = pl.BlockSpec(memory_space=pl.ANY)
    swap_scratch = [
        pltpu.VMEM((pairs, 2, rows, PAIR), BF16),
        pltpu.SemaphoreType.DMA((2, pairs)),
    ]
    out = pl.pallas_call(
        kernel,
        grid=(pairs,),
        in_specs=[pl.BlockSpec(memory_space=pltpu.SMEM)]
        + [query_spec(a) for a in (query, mix, mix_grad)]
        + [lse_spec]
        + [kv_spec(piece) for piece in kv_pieces]
        + [hold] * n_carry,
        out_specs=[query_spec(plain)]
        + [kv_spec(plain_kv)] * kept
        + [hold] * (pieces - kept + len(carrier.outs)),
        scratch_shapes=[pltpu.VMEM((keys, PAIR), BF16)] * 4
        + [pltpu.VMEM((PAIR, keys), BF16)]
        + (swap_scratch if swaps else [])
        + carrier.scratch,
        out_shape=[plain] + [plain_kv] * pieces + carrier.outs,
        compiler_params=pltpu.CompilerParams(vmem_limit_bytes=VMEM, **carrier.params),
        cost_estimate=pl.CostEstimate(
            flops=40 * rows * keys * pairs * PAIR,
            bytes_accessed=16 * rows * pairs * PAIR * pieces,
            transcendentals=0,
        ),
        name="attend_back",
    )(
        span.lengths if isinstance(span, Lengths) else span,
        query.array,
        mix.array,
        mix_grad.array,
        lse,
        *[piece.array for piece in kv_pieces],
        *carrier.ins,
    )
    return out[0], out[1 : pieces + 1], out[pieces + 1 :]


def spots():
    return lax.axis_index("section"), lax.axis_index("dp"), lax.axis_index("tensor")


def dp_peer(group, level):
    return group + (1 << level) * (1 - 2 * ((group // (1 << level)) % 2))


def where_is(peer):
    section, group, tensor = spots()
    if peer == "near":
        return {"section": 1 - section}
    if peer == "over":
        return {"tensor": 1 - tensor}
    if peer == "cross":
        return {"section": 1 - section, "tensor": 1 - tensor}
    return {"dp": dp_peer(group, peer)}


def remote(source, target, sent, landed, where):
    return pltpu.make_async_remote_copy(
        src_ref=source,
        dst_ref=target,
        send_sem=sent,
        recv_sem=landed,
        device_id=where,
        device_id_type=pl.DeviceIdType.MESH,
    )


def greet(peers):
    barrier = pltpu.get_barrier_semaphore()
    for peer in peers:
        pl.semaphore_signal(
            barrier, inc=1, device_id=where_is(peer), device_id_type=pl.DeviceIdType.MESH
        )
    pl.semaphore_wait(barrier, len(peers))


class Carry:
    def __init__(self, tasks=(), collective=None):
        self.tasks = list(tasks)
        self.ins = [a for task in self.tasks for a in task.ins]
        self.outs = [a for task in self.tasks for a in task.outs]
        self.scratch = [a for task in self.tasks for a in task.scratch]
        self.peers = []
        for task in self.tasks:
            self.peers += [peer for peer in task.peers if peer not in self.peers]
        self.params = (
            dict(collective_id=collective, has_side_effects=True) if self.tasks else {}
        )

    def plan(self, steps, ins, outs, scratch):
        plan = {}
        if self.tasks:
            plan[0] = [lambda: greet(self.peers)]
        events = []
        for task in self.tasks:
            i, o, s = len(task.ins), len(task.outs), len(task.scratch)
            events += task.events(steps, ins[:i], outs[:o], scratch[:s])
            ins, outs, scratch = ins[i:], outs[o:], scratch[s:]
        for step, rank, action in sorted(events, key=lambda event: event[:2]):
            assert 0 <= step < steps
            plan.setdefault(steps if rank == LAST else step, []).append(action)
        return plan

    def run(self, place, slot, slots, steps, ins, outs, scratch):
        for step, actions in self.plan(steps, ins, outs, scratch).items():
            if step == steps:
                if slot == slots:

                    @pl.when(place == steps // slots - 1)
                    def _():
                        for action in actions:
                            action()

            elif step % slots == slot:

                @pl.when(place == step // slots)
                def _():
                    for action in actions:
                        action()


GROUP = ["near", "over", "cross"]


class RowCopies:
    def __init__(self, copies, arrivals, sems, room=None):
        self.copies, self.arrivals, self.room = copies, arrivals, room
        self.sent, self.landed, self.kept = sems

    def copy(self, i):
        source, target, slot, section, tensor, _ = self.copies[i]
        return remote(
            source,
            target,
            self.sent.at[i],
            self.landed.at[slot],
            {"section": section, "tensor": tensor},
        )

    def keep(self, i):
        source, target, slot = self.copies[i][:3]
        return pltpu.make_async_copy(
            source, target if self.room is None else self.room, self.kept.at[slot]
        )

    def keep_on(self):
        for i in range(len(self.copies)):

            @pl.when(self.here(i, True))
            def _():
                self.keep(i).wait()
                target, slot = self.copies[i][1:3]
                pltpu.make_async_copy(self.room, target, self.kept.at[slot]).start()

    def here(self, i, stays):
        section, _, tensor = spots()
        _, _, _, to_section, to_tensor, condition = self.copies[i]
        own = (to_section == section) & (to_tensor == tensor)
        return condition & (own if stays else jnp.logical_not(own))

    def start(self):
        for i in range(len(self.copies)):

            @pl.when(self.here(i, True))
            def _():
                self.keep(i).start()

            @pl.when(self.here(i, False))
            def _():
                self.copy(i).start()

    def wait_sent(self):
        for i in range(len(self.copies)):

            @pl.when(self.here(i, False))
            def _():
                self.copy(i).wait_send()

    def wait_arrival(self, i):
        section, _, tensor = spots()
        target, slot, from_section, from_tensor, condition = self.arrivals[i]
        own = (from_section == section) & (from_tensor == tensor)
        source = self.copies[0][0]

        @pl.when(condition & own)
        def _():
            stays = source if self.room is None else self.room
            pltpu.make_async_copy(stays, target, self.kept.at[slot]).wait()

        @pl.when(condition & jnp.logical_not(own))
        def _():
            remote(
                source, target, self.sent.at[0], self.landed.at[slot], where_is("near")
            ).wait_recv()


def row_sems(pieces=1):
    return [pltpu.SemaphoreType.DMA((2 * pieces,))] * 3


def spread_rows(source, target, sems, sides=(0, 1), room=None, pieces=1):
    section, _, tensor = spots()
    yes = section >= 0
    sends = yes if len(sides) == 2 else section == sides[0]
    count = source.shape[1] // pieces
    copies, arrivals = [], []
    for i in range(pieces):
        own = pl.ds(i * count, count)
        for row in range(2):
            slot = 2 * i + section
            copies.append(
                (source.at[row, own, :], target.at[section, own, :], slot, tensor, row, sends)
            )
        for side in sides:
            arrivals.append((target.at[side, own, :], 2 * i + side, side, section, yes))
    return RowCopies(copies, arrivals, sems, room)


def return_rows(source, target, sems, side, room):
    section, _, tensor = spots()
    copies = [(source, target.at[tensor], tensor, side, section, section >= 0)]
    arrivals = [(target.at[row], row, tensor, row, section == side) for row in range(2)]
    return RowCopies(copies, arrivals, sems, room)


class SpreadRows:
    peers = GROUP

    def __init__(self, array, sides, begin=0):
        self.ins, self.sides, self.begin = [array], sides, begin
        self.outs = [jax.ShapeDtypeStruct(array.shape, array.dtype)]
        self.scratch = [
            *row_sems(),
            pltpu.VMEM(array.shape, array.dtype),
            pltpu.SemaphoreType.DMA((2,)),
        ]

    def events(self, steps, ins, outs, scratch):
        room, sems = scratch[3], scratch[4]

        def make():
            return spread_rows(ins[0], room, scratch[:3], self.sides)

        def store(side):
            return pltpu.make_async_copy(room.at[side], outs[0].at[side], sems.at[side])

        def arrive():
            rows = make()
            for i, side in enumerate(self.sides):
                rows.wait_arrival(i)
                store(side).start()

        def finish():
            for side in self.sides:
                store(side).wait()
            make().wait_sent()

        return [
            (self.begin, 1, lambda: make().start()),
            (steps - 1, 1, arrive),
            (steps - 1, LAST, finish),
        ]


class ReturnRows:
    peers = GROUP

    def __init__(self, array, side, begin=0, staged=True):
        self.ins, self.side, self.begin, self.staged = [array], side, begin, staged
        self.outs = [jax.ShapeDtypeStruct((2, *array.shape), array.dtype)]
        self.scratch = row_sems() + [pltpu.VMEM(array.shape, array.dtype)] * staged

    def events(self, steps, ins, outs, scratch):
        def make():
            room = scratch[3] if self.staged else None
            return return_rows(ins[0], outs[0], scratch[:3], self.side, room)

        def finish():
            rows = make()
            for i in range(len(rows.arrivals)):
                rows.wait_arrival(i)
            rows.wait_sent()

        events = [(self.begin, 1, lambda: make().start()), (steps - 1, LAST, finish)]
        if self.staged:
            events.append((self.begin + 1, 1, lambda: make().keep_on()))
        return events


class WeightCopies:
    @staticmethod
    def sems(count):
        return pltpu.SemaphoreType.DMA((3 + 8 * count,))

    def __init__(self, source, target, sem, room=None, count=1):
        section, group, _ = spots()
        rows = source.shape[0] // (2 * count)
        bit = group % 2
        here, stays = target.at[section, 1], target.at[section, 0]
        self.room = room
        if room is None:
            self.kept = pltpu.make_async_copy(source, stays, sem.at[0])
        else:
            self.first = pltpu.make_async_copy(source, room, sem.at[0])
            self.kept = pltpu.make_async_copy(room, stays, sem.at[0])
        self.near = remote(source, stays, sem.at[1], sem.at[2], where_is("near"))
        self.over, self.side, self.onward, self.last = [], [], [], []
        for i in range(count):
            own = pl.ds(pl.multiple_of((bit * count + i) * rows, 16), rows)
            other = pl.ds(pl.multiple_of(((1 - bit) * count + i) * rows, 16), rows)
            source_own, own, other = source.at[own], here.at[own], here.at[other]
            pairs = [(sem.at[3 + 8 * i + 2 * j], sem.at[4 + 8 * i + 2 * j]) for j in range(4)]
            self.over.append(remote(source_own, own, *pairs[0], where_is("over")))
            self.side.append(remote(own, own, *pairs[1], where_is(0)))
            self.onward.append(remote(own, own, *pairs[2], where_is("near")))
            self.last.append(remote(other, other, *pairs[3], where_is("near")))

    def start(self):
        for copy in self.over:
            copy.start()
        self.near.start()
        if self.room is None:
            self.kept.start()
        else:
            self.first.start()

    def keep_on(self):
        self.first.wait()
        self.kept.start()

    def forward(self, i):
        self.over[i].wait_recv()
        self.side[i].start()
        self.onward[i].start()

    def forward_last(self, i):
        self.side[i].wait_recv()
        self.last[i].start()

    def finish(self):
        self.kept.wait()
        self.near.wait()
        for over, side, onward, last in zip(self.over, self.side, self.onward, self.last):
            over.wait_send()
            side.wait_send()
            onward.wait()
            last.wait()


class SpreadWeight:
    peers = ["near", "over", 0]

    def __init__(self, weight, forwards, lasts):
        self.ins = [weight]
        self.outs = [jax.ShapeDtypeStruct((2, 2, *weight.shape), weight.dtype)]
        self.forwards, self.lasts = forwards, lasts
        self.scratch = [
            WeightCopies.sems(len(forwards)),
            pltpu.VMEM(weight.shape, weight.dtype),
        ]

    def events(self, steps, ins, outs, scratch):
        def copies():
            return WeightCopies(ins[0], outs[0], *scratch, len(self.forwards))

        def forward(i):
            return lambda: copies().forward(i)

        def forward_last(i):
            return lambda: copies().forward_last(i)

        return (
            [(0, 0, lambda: copies().start()), (1, 0, lambda: copies().keep_on())]
            + [(when, 1, forward(i)) for i, when in enumerate(self.forwards)]
            + [(when, 2, forward_last(i)) for i, when in enumerate(self.lasts)]
            + [(steps - 1, LAST, lambda: copies().finish())]
        )


class Reduce:
    def __init__(self, source, chunk, begins, pace, only=None, levels=None):
        self.ins = [source]
        self.chunk, self.begins, self.only = chunk, begins, only
        self.count = source.shape[-2] // chunk
        assert self.count == len(begins)
        self.levels = list(range(lax.axis_size("dp").bit_length() - 1))
        if levels is not None:
            self.levels = levels
        depth = len(self.levels)
        self.peers = []
        self.stages = []
        if only != "slice":
            self.peers += ["near", "over"]
            self.stages += ["enter", "cross", "over"]
        if only != "chip":
            self.peers += ["near", *self.levels]
            self.stages += ["load", "loaded"] if only == "slice" else []
            self.stages += [("halve", i) for i in range(depth)]
            self.stages += [("double", i) for i in reversed(range(depth))]
        assert len(pace) == len(self.stages) - 1
        self.dues = [sum(pace[:i]) for i in range(len(self.stages))]
        width = source.shape[-1]
        whole = jax.ShapeDtypeStruct((self.count * chunk, width), BF16)
        self.outs = [whole] if only == "chip" else [whole] * 2

        def room(*shape):
            return pltpu.VMEM((self.count, *shape, width), BF16)

        self.scratch = [room(2, chunk)]
        if only != "slice":
            self.scratch += [room(2, chunk), room(chunk)]
        if only != "chip":
            halves = [room(chunk >> (i + 1)) for i in range(depth)]
            self.scratch += [room(chunk)] + halves + halves
        self.scratch += [pltpu.SemaphoreType.DMA((2 + 2 * (3 + 2 * depth), self.count))]

    def events(self, steps, ins, outs, scratch):
        chunk, depth = self.chunk, len(self.levels)
        source, refs = ins[0], list(scratch)
        own, sems = refs[0], refs[-1]
        refs = refs[1:-1]
        if self.only != "slice":
            chip, other = refs[:2]
            refs = refs[2:]
        if self.only != "chip":
            full, halves, doubles = refs[0], refs[1 : 1 + depth], refs[1 + depth :]

        def bounds(i):
            _, group, _ = spots()
            begin = 0
            for j in range(i):
                bit = (group // (1 << self.levels[j])) % 2
                begin = begin + bit * (chunk >> (j + 1))
            return begin

        def keeps(i):
            return pl.ds(pl.multiple_of(bounds(i + 1), 16), chunk >> (i + 1))

        def gives(i):
            begin = 2 * bounds(i) + (chunk >> (i + 1)) - bounds(i + 1)
            return pl.ds(pl.multiple_of(begin, 16), chunk >> (i + 1))

        def pair(kind, c):
            return sems.at[2 + 2 * kind, c], sems.at[3 + 2 * kind, c]

        def rows_of(c):
            return pl.ds(c * chunk, chunk)

        def load(c):
            if self.only == "slice":
                return pltpu.make_async_copy(
                    source.at[rows_of(c), :], own.at[c, 0], sems.at[0, c]
                )
            section, _, _ = spots()
            return pltpu.make_async_copy(
                source.at[section, :, rows_of(c), :], own.at[c], sems.at[0, c]
            )

        def cross(c):
            section, _, _ = spots()
            return remote(
                source.at[1 - section, :, rows_of(c), :],
                chip.at[c],
                *pair(0, c),
                where_is("near"),
            )

        def over(c):
            return remote(own.at[c, 1], other.at[c], *pair(1, c), where_is("over"))

        def halve(i, c):
            return remote(
                own.at[c, 0, gives(i), :],
                halves[i].at[c],
                *pair(3 + i, c),
                where_is(self.levels[i]),
            )

        def double(i, c):
            return remote(
                full.at[c, keeps(i), :],
                doubles[i].at[c],
                *pair(3 + depth + i, c),
                where_is(self.levels[i]),
            )

        def store(c):
            kept = own.at[c, 0] if self.only == "chip" else full.at[c]
            return pltpu.make_async_copy(kept, outs[0].at[rows_of(c), :], sems.at[1, c])

        def tell(c):
            return remote(
                full.at[c], outs[1].at[rows_of(c), :], *pair(2, c), where_is("near")
            )

        def act(stage, c):
            if stage == "enter":
                load(c).start()
                cross(c).start()
            elif stage == "load":
                load(c).start()
            elif stage == "loaded":
                load(c).wait()
                halve(0, c).start()
            elif stage == "cross":
                load(c).wait()
                cross(c).wait()
                own[c] = own[c] + chip[c]
                over(c).start()
            elif stage == "over":
                over(c).wait()
                own[c, 0] = own[c, 0] + other[c]
                if self.only == "chip":
                    store(c).start()
                else:
                    halve(0, c).start()
            elif stage[0] == "halve":
                i = stage[1]
                halve(i, c).wait()
                mine = keeps(i)
                total = own[c, 0, mine, :] + halves[i][c]
                if i < depth - 1:
                    own[c, 0, mine, :] = total
                    halve(i + 1, c).start()
                else:
                    full[c, mine, :] = total
                    double(i, c).start()
            else:
                i = stage[1]
                double(i, c).wait()
                full[c, gives(i), :] = doubles[i][c]
                if i:
                    double(i - 1, c).start()
                else:
                    store(c).start()
                    tell(c).start()

        def leave(c):
            store(c).wait()
            if self.only != "chip":
                tell(c).wait()

        events = []
        for c, begin in enumerate(self.begins):
            for i, (stage, due) in enumerate(zip(self.stages, self.dues)):
                events.append((begin + due, -i, functools.partial(act, stage, c)))
            events.append((steps - 1, LAST, functools.partial(leave, c)))
        return events


def close_down(x, firsts, q_grad, kv_grads, norm, qkv, norm_grads, schedule, collective):
    _, rows, width = x.shape
    parts, _, _, part = qkv.shape[1:]
    half = 3 * width // 2
    shapes = [(2, parts, 2 * half + extra, PAIR) for extra in (2 * PAIR, 0)]
    dec_steps, enc_steps, returns, steps = schedule
    whole = (rows, width)
    grad_shape = jax.ShapeDtypeStruct(whole, BF16)
    carrier = Carry(
        [
            Reduce(jax.ShapeDtypeStruct(shapes[0], BF16), 2 * PAIR, *enc_steps),
            Reduce(jax.ShapeDtypeStruct(shapes[1], BF16), 2 * PAIR, *dec_steps),
            ReturnRows(grad_shape, 0, returns[0], False),
            ReturnRows(grad_shape, 1, returns[1], False),
        ],
        collective,
    )
    halves = 2
    count, sub = rows // halves, min(256, rows // halves)

    def kernel(*refs):
        x_in, first_ins, q_in, kv_ins, norm_in, qkv_in, refs = (
            refs[0],
            refs[1:3],
            refs[3],
            refs[4:6],
            refs[6],
            refs[7],
            refs[8:],
        )
        norm_grad_refs, refs = refs[: len(norm_grads)], refs[len(norm_grads) :]
        outs, refs = refs[: len(carrier.outs)], refs[len(carrier.outs) :]
        x_room, first_room, q_room, kv_room, norm_room, qkv_room, sems = refs[:7]
        low, keys, total, grads, enc_sum, dec_sum, *rest = refs[7:]
        ins = [enc_sum, dec_sum, grads.at[0], grads.at[1]]
        plan = carrier.plan(steps, ins, outs, rest)
        loads = []

        def load(source, target):
            copy = pltpu.make_async_copy(source, target, sems.at[len(loads)])
            copy.start()
            loads.append(copy)
            return copy

        arrivals = {}
        for side in (1, 0):
            for i in range(halves):
                own = pl.ds(i * count, count)
                arrivals[side, i] = [
                    load(first_ins[side].at[own, :], first_room.at[side, own, :]),
                    load(q_in.at[side, :, own, :], q_room.at[side, :, own, :]),
                    load(kv_ins[0].at[side, :, :, own, :], kv_room.at[0, side, :, :, own, :]),
                    load(kv_ins[1].at[side, :, :, own, :], kv_room.at[1, side, :, :, own, :]),
                    load(x_in.at[side, own, :], x_room.at[side, own, :]),
                ]
                if i == 0:
                    arrivals[side, i] += [
                        load(qkv_in.at[side], qkv_room.at[side]),
                        load(norm_in.at[side], norm_room.at[side]),
                    ]
        total[...] = jnp.zeros_like(total)

        def piece(side, i):
            for copy in arrivals[side, i]:
                copy.wait()
            kept = low, keys, total
            refs = (
                x_room.at[side],
                first_room.at[side],
                [kv_room.at[0, side], kv_room.at[1, side]],
                q_room.at[side],
                grads.at[side],
            )
            w = [qkv_room.at[side, k] for k in range(parts)]
            turns = []
            for begin in range(i * count, (i + 1) * count, sub):
                own = slice(begin, begin + sub)
                turns.append(
                    input_part(refs, kept, own, own, norm_room.at[side], w, side == 0)
                )
            while turns:
                turns = [turn for turn in turns if next(turn, LAST) is not LAST]
            if i == halves - 1:
                into = (enc_sum, dec_sum)[side]
                input_sums(kept, q_room.at[side], into, parts)
                if side == 0:
                    sides = [
                        norm_grad_refs[0][...] + total[...],
                        sum(ref[...] for ref in norm_grad_refs[1:]),
                    ]
                    norm_lines(sides, into, parts, 2 * half)

        for step in range(steps + 1):
            for action in plan.get(step, []):
                action()
            if step < 2 * halves:
                piece(1 - step // halves, step % halves)

    hold = pl.BlockSpec(memory_space=pl.ANY)
    vmem = pl.BlockSpec(memory_space=pltpu.VMEM)
    arrays = [x, *firsts, q_grad, *kv_grads, norm, qkv]
    rooms = [
        pltpu.VMEM(x.shape, BF16),
        pltpu.VMEM((2, *whole), F32),
        pltpu.VMEM(q_grad.shape, BF16),
        pltpu.VMEM((2, *kv_grads[0].shape), BF16),
        pltpu.VMEM(norm.shape, F32),
        pltpu.VMEM(qkv.shape, BF16),
        pltpu.SemaphoreType.DMA((2 * (5 * halves + 2),)),
        pltpu.VMEM(whole, BF16),
        pltpu.VMEM((parts, 2, rows, part), BF16),
        pltpu.VMEM((3, 2, width), F32),
        pltpu.VMEM((2, *whole), BF16),
        pltpu.VMEM(shapes[0], BF16),
        pltpu.VMEM(shapes[1], BF16),
    ]
    return pl.pallas_call(
        kernel,
        in_specs=[hold] * len(arrays) + [vmem] * len(norm_grads),
        out_specs=[hold] * len(carrier.outs),
        out_shape=carrier.outs,
        scratch_shapes=rooms + carrier.scratch,
        compiler_params=pltpu.CompilerParams(vmem_limit_bytes=VMEM, **carrier.params),
        name="close_down",
    )(*arrays, *norm_grads)


def lay_out(pairs, singles, shapes, finish):
    arrays = [array for pair in pairs for array in pair] + [single[0] for single in singles]
    spans = [(0, min(a.shape[0], b.shape[0])) for a, b in pairs] + [s[1:] for s in singles]
    loaded = [
        jax.ShapeDtypeStruct((span[1], *array.shape[1:]), array.dtype)
        for array, span in zip([a for a, _ in pairs] + [s[0] for s in singles], spans)
    ]

    def kernel(*refs):
        ins, outs = refs[: len(arrays)], refs[len(arrays) : len(arrays) + len(shapes)]
        refs = refs[len(arrays) + len(shapes) :]
        rooms, refs = refs[: len(loaded)], refs[len(loaded) :]
        out_rooms, load_sems, store_sems = refs[: len(shapes)], refs[-2], refs[-1]
        section = lax.axis_index("section")

        def load(i, choice):
            source = ins[2 * i + choice] if i < len(pairs) else ins[len(pairs) + i]
            return pltpu.make_async_copy(
                source.at[pl.ds(*spans[i])], rooms[i], load_sems.at[i]
            )

        for i in range(len(loaded)):
            if i < len(pairs):

                @pl.when(section == 0)
                def _():
                    load(i, 0).start()

                @pl.when(section != 0)
                def _():
                    load(i, 1).start()

            else:
                load(i, 0).start()
        stores = []

        def fetch(i):
            load(i, 0).wait()
            return rooms[i]

        for i, room in enumerate(finish(fetch, out_rooms)):
            copy = pltpu.make_async_copy(room, outs[i], store_sems.at[i])
            copy.start()
            stores.append(copy)
        for copy in stores:
            copy.wait()

    hold = pl.BlockSpec(memory_space=pl.ANY)
    return pl.pallas_call(
        kernel,
        in_specs=[hold] * len(arrays),
        out_specs=[hold] * len(shapes),
        out_shape=[jax.ShapeDtypeStruct(*s) for s in shapes],
        scratch_shapes=[pltpu.VMEM(a.shape, a.dtype) for a in loaded]
        + [pltpu.VMEM(*s) for s in shapes]
        + [pltpu.SemaphoreType.DMA((len(loaded),)), pltpu.SemaphoreType.DMA((len(shapes),))],
        compiler_params=pltpu.CompilerParams(vmem_limit_bytes=VMEM),
        name="lay_out",
    )(*arrays)


def open_up(tokens, qkv, norm, block, collective):
    _, rows, width = tokens.shape
    part = qkv.shape[-1]
    score = LOG2E / math.sqrt(width // HEADS)
    count = min(block, rows)
    pieces = rows // count

    def kernel(tokens_ref, qkv_ref, norm_ref, *refs):
        x_out, w_out, n_out, q_out, own_out, other_out = refs[:6]
        x, w, n, q, kv = refs[6:11]
        row_sems_, weight_sems, norm_sems, store_sems, kv_sems = (
            refs[11:14],
            refs[14:15],
            refs[15],
            refs[16],
            refs[17],
        )
        section, _, _ = spots()
        greet([*GROUP, 0])
        rows_in = spread_rows(tokens_ref, x, row_sems_, pieces=pieces)
        weight = WeightCopies(qkv_ref, w, weight_sems[0])
        weight.start()
        rows_in.start()
        norm_kept = pltpu.make_async_copy(norm_ref, n.at[section], norm_sems.at[0])
        norm_near = remote(
            norm_ref, n.at[section], norm_sems.at[1], norm_sems.at[2], where_is("near")
        )
        norm_kept.start()
        norm_near.start()
        stores, kv_copies = [], []

        def save(source, target):
            copy = pltpu.make_async_copy(source, target, store_sems.at[len(stores)])
            copy.start()
            stores.append(copy)

        def project(side, own, rows_low):
            for k in range(2):

                def product(m):
                    return dot_nn(rows_low, w[side, k, m * width : (m + 1) * width, :])

                q[side, k, own, :] = (product(0) * score).astype(BF16)
                kv[side, k, 0, own, :] = product(1).astype(BF16)
                kv[side, k, 1, own, :] = product(2).astype(BF16)

        norm_kept.wait()
        norm_near.wait()
        save(n, n_out)
        weight.forward(0)
        weight.forward_last(0)
        weight.finish()
        save(w, w_out)
        for i in range(pieces):
            own = slice(i * count, (i + 1) * count)
            for side in range(2):
                rows_in.wait_arrival(2 * i + side)
                rows_low = x[side, own, :]
                if side == 0:
                    unit, _ = standardize(rows_low.astype(F32))
                    rows_low = affine(unit, n.at[0], 2).astype(BF16)
                project(side, own, rows_low)
                copy = remote(
                    kv.at[side, :, :, own, :],
                    other_out.at[side, :, :, own, :],
                    kv_sems.at[0, 2 * i + side],
                    kv_sems.at[1, 2 * i + side],
                    where_is("near"),
                )
                copy.start()
                kv_copies.append(copy)
                save(x.at[side, own, :], x_out.at[side, own, :])
                save(kv.at[side, :, :, own, :], own_out.at[side, :, :, own, :])
                save(q.at[side, :, own, :], q_out.at[side, :, own, :])
        rows_in.wait_sent()
        for copy in kv_copies + stores:
            copy.wait()

    hold = pl.BlockSpec(memory_space=pl.ANY)
    shapes = [
        ((2, rows, width), BF16),
        ((2, 2, *qkv.shape), BF16),
        ((2, *norm.shape), F32),
        ((2, 2, rows, part), BF16),
        ((2, 2, 2, rows, part), BF16),
    ]
    return pl.pallas_call(
        kernel,
        in_specs=[hold] * 3,
        out_specs=[hold] * 6,
        out_shape=[jax.ShapeDtypeStruct(*s) for s in shapes + shapes[-1:]],
        scratch_shapes=[pltpu.VMEM(*s) for s in shapes]
        + row_sems(pieces)
        + [WeightCopies.sems(1)]
        + [
            pltpu.SemaphoreType.DMA((3,)),
            pltpu.SemaphoreType.DMA((6 * pieces + 2,)),
            pltpu.SemaphoreType.DMA((2, 2 * pieces)),
        ],
        compiler_params=pltpu.CompilerParams(
            vmem_limit_bytes=VMEM, collective_id=collective, has_side_effects=True
        ),
        name="open_up",
    )(tokens, qkv, norm)


def local_general(tokens, lengths, self_qkv, self_out, cross_proj, ffn_up, ffn_down, norms, cotangent):
    section = lax.axis_index("section")
    tensor = lax.axis_index("tensor")
    tensors = lax.axis_size("tensor")
    _, row_count, rows, width = tokens.shape
    assert row_count == 2 and tensors % row_count == 0
    spread = tensors // row_count
    pieces = 2 * spread
    axes = ("section", "tensor")
    is_first = section == 0
    own_row = tensor // spread
    place = section * spread + tensor % spread

    def device(row, spot):
        return (spot // spread) * tensors + row * spread + spot % spread

    def each():
        return [(s, t) for s in range(2) for t in range(tensors)]

    straight = [(s * tensors + t, device(s, t)) for s, t in each()]
    turned = [(s * tensors + t, device(1 - s, t)) for s, t in each()]

    def bring(shares):
        stays = lax.dynamic_index_in_dim(shares, section, 0, keepdims=False)
        moves = lax.dynamic_index_in_dim(shares, 1 - section, 0, keepdims=False)
        one = lax.ppermute(stays, axes, straight)
        two = lax.ppermute(moves, axes, turned)
        return jnp.where(own_row == 0, one, two), jnp.where(own_row == 0, two, one)

    def take_back(source, target):
        one = jnp.where(own_row == 0, source, target)
        two = jnp.where(own_row == 0, target, source)
        one = lax.ppermute(one, axes, [(b, a) for a, b in straight])
        two = lax.ppermute(two, axes, [(b, a) for a, b in turned])
        return jnp.stack([jnp.where(is_first, one, two), jnp.where(is_first, two, one)])

    def rotate(value, by):
        pairs = [
            (device(r, p), device(r, (p + by) % pieces))
            for r in range(row_count)
            for p in range(pieces)
        ]
        return lax.ppermute(value, axes, pairs)

    def pieces_of(value):
        return [value] + [rotate(value, by) for by in range(1, pieces)]

    def pieces_home(values):
        return [values[0]] + [rotate(values[by], -by) for by in range(1, pieces)]

    def swap_sections(value):
        return lax.ppermute(value, "section", [(0, 1), (1, 0)])

    def both_sides(weight, dim):
        if spread == 1:
            other = lax.ppermute(weight, "tensor", [(t, 1 - t) for t in range(tensors)])
            parts = [weight, other]
        else:
            parts = [lax.all_gather(weight, "tensor", axis=dim, tiled=True)]
        swapped = [swap_sections(part) for part in parts]
        pairs = list(zip(parts, swapped))
        return (
            [jnp.where(is_first, mine, theirs) for mine, theirs in pairs],
            [jnp.where(is_first, theirs, mine) for mine, theirs in pairs],
        )

    def home(source_grad, target_grad, dim):
        keep = jnp.where(is_first, source_grad, target_grad).astype(F32)
        sent = swap_sections(jnp.where(is_first, target_grad, source_grad))
        total = (keep + sent.astype(F32)).astype(BF16)
        if spread == 1:
            other = lax.ppermute(total[1], "tensor", [(t, 1 - t) for t in range(tensors)])
            total = (total[0].astype(F32) + other.astype(F32)).astype(BF16)
        else:
            total = lax.psum_scatter(total[0], "tensor", scatter_dimension=dim, tiled=True)
        return total

    def span_of(query_side, key_side):
        own = lax.dynamic_index_in_dim(lengths, own_row, 1, keepdims=False)
        asks, answers = own[query_side], own[key_side]
        paired = asks[1] > 0
        second = paired & (place * rows >= asks[0])
        begin = jnp.where(second, answers[0], 0)
        end = jnp.where(second | ~paired, answers[0] + answers[1], answers[0])
        offsets = [(place - by) % pieces * rows for by in range(pieces)]
        return jnp.stack([begin, end, *offsets]).astype(jnp.int32)[None]

    query_block = min(256, rows)
    chunk = 256

    source, target = bring(tokens[0])
    source_norm, target_norm = (
        jnp.where(is_first, a, b)
        for a, b in (lambda own, other: ((own, other), (other, own)))(
            norms[0], swap_sections(norms[0])
        )
    )
    source_qkv, target_qkv = both_sides(self_qkv[0], 2)
    source_out, target_out = both_sides(self_out[0], 0)
    source_up, target_up = both_sides(ffn_up[0], 1)
    source_down, target_down = both_sides(ffn_down[0], 0)
    source_cross, target_cross = both_sides(cross_proj[0], 2)
    source_cot, target_cot = bring(cotangent[0])
    source_span, target_span, cross_span = span_of(0, 0), span_of(1, 1), span_of(1, 0)

    enc_q, enc_kv = project_qkv(source, source_norm, source_qkv, True)
    enc_kv = pieces_of(enc_kv)
    dec_q, dec_kv = project_qkv(target, target_norm, target_qkv, False)
    dec_kv = pieces_of(dec_kv)
    enc_mix, enc_lse = attend(enc_q, enc_kv, source_span, query_block)
    encoded, memory, enc_first, enc_third = encoder_forward(
        source, enc_mix, source_norm, source_out, source_up, source_down, source_cross
    )
    memory = pieces_of(memory)
    dec_mix, dec_lse = attend(dec_q, dec_kv, target_span, query_block)
    cross_q, dec_first = decoder_middle(
        target, dec_mix, target_norm, target_out, target_cross
    )
    cross_mix, cross_lse = attend(cross_q, memory, cross_span, query_block)
    decoded, second_grad, cross_mix_grad, cross_out_grad, dec_up, dec_down, dec_norm = decoder_turn(
        dec_first, cross_mix, target_cot, target_norm, target_cross, target_up, target_down
    )
    result = take_back(encoded, decoded)
    cross_q_grad, memory_grads, _ = attend_back(
        cross_q, memory, cross_mix, cross_mix_grad, cross_lse, cross_span, chunk
    )
    memory_grads = pieces_home(memory_grads)
    dec_first_grad, dec_mix_grad, cross_query_grad, dec_out, step = decoder_middle_back(
        dec_first,
        dec_mix,
        cross_q_grad,
        second_grad,
        target_norm,
        target_out,
        target_cross
    )
    dec_norm += step
    enc_first_grad, enc_mix_grad, enc_cross, enc_out, enc_up, enc_down, enc_norm = encoder_back(
        enc_first,
        enc_third,
        enc_mix,
        memory_grads,
        source_cot,
        source_norm,
        source_out,
        source_up,
        source_down,
        source_cross
    )
    dec_cross = jnp.stack([cross_query_grad, cross_out_grad], axis=1)
    up_grad, down_grad = home(enc_up, dec_up, 1), home(enc_down, dec_down, 0)
    out_grad, cross_grad = home(enc_out, dec_out, 0), home(enc_cross, dec_cross, 2)
    dec_q_grad, dec_kv_grads, _ = attend_back(
        dec_q, dec_kv, dec_mix, dec_mix_grad, dec_lse, target_span, chunk
    )
    dec_kv_grads = pieces_home(dec_kv_grads)
    enc_q_grad, enc_kv_grads, _ = attend_back(
        enc_q, enc_kv, enc_mix, enc_mix_grad, enc_lse, source_span, chunk
    )
    enc_kv_grads = pieces_home(enc_kv_grads)
    target_grad, dec_qkv, _ = input_back(
        target, dec_first_grad, dec_q_grad, dec_kv_grads, target_norm, target_qkv, False
    )
    source_grad, enc_qkv, step = input_back(
        source, enc_first_grad, enc_q_grad, enc_kv_grads, source_norm, source_qkv, True
    )
    enc_norm += step
    token_grad = take_back(source_grad, target_grad).astype(F32)
    qkv_grad = home(enc_qkv, dec_qkv, 2)
    norm_total = lax.psum(jnp.stack([enc_norm, dec_norm]), ("section", "dp", "tensor"))
    norm_grad = lax.dynamic_index_in_dim(norm_total, section, 0, keepdims=False)
    summed = [
        lax.psum(grad, "dp").astype(F32)
        for grad in (qkv_grad, out_grad, cross_grad, up_grad, down_grad)
    ]
    return (
        result[None],
        token_grad[None],
        summed[0][None],
        summed[1][None],
        summed[2][None],
        summed[3][None],
        summed[4][None],
        norm_grad[None],
    )


def local_fast(tokens, lengths, self_qkv, self_out, cross_proj, ffn_up, ffn_down, norms, cotangent):
    _, row_count, rows, width = tokens.shape
    assert row_count == 2
    block = min(256, rows)
    query_block = min(256, rows)
    chunk = 256
    levels = lax.axis_size("dp").bit_length() - 1

    def hops(*steps):
        return list(steps[:levels]) + list(steps[3 : 3 + levels])

    def flat(weight):
        return weight.reshape(-1, weight.shape[-1])

    self_spans, cross_span = Lengths(lengths), Lengths(lengths, 1, 0)
    x, qkv, norm, q, *kv = open_up(tokens[0], flat(self_qkv), norms[0], block, 1)
    qkv = qkv.reshape(2, 2, *self_qkv.shape[1:])

    def parts(weight, side):
        return [At(weight, side, k) for k in range(2)]

    enc_x, dec_x, enc_norm_in, dec_norm_in = At(x, 0), At(x, 1), At(norm, 0), At(norm, 1)
    mix, lse, out, up, cross, down = attend(
        q,
        kv,
        self_spans,
        query_block,
        Carry(
            [
                SpreadWeight(self_out[0], [1], [3]),
                SpreadWeight(ffn_up[0], [2, 3], [4, 5]),
                SpreadWeight(flat(cross_proj), [4], [6]),
                SpreadWeight(ffn_down[0], [5, 6], [7, 7]),
            ],
            2,
        ),
    )
    cross = cross.reshape(2, 2, *cross_proj.shape[1:])
    enc_mix, dec_mix = At(mix, 0), At(mix, 1)
    encoded, memory, enc_first, enc_third, pushed = encoder_forward(
        enc_x,
        enc_mix,
        enc_norm_in,
        parts(out, 0),
        parts(up, 0),
        parts(down, 0),
        parts(cross, 0),
        8,
    )
    memory = [memory, pushed]
    cross_q, dec_first = decoder_middle(
        dec_x, dec_mix, dec_norm_in, parts(out, 1), parts(cross, 1)
    )
    cross_mix, cross_lse, dec_cot = attend(
        cross_q,
        memory,
        cross_span,
        query_block,
        Carry([SpreadRows(cotangent[0], (1,))], 4),
    )
    decoded, second_grad, cross_mix_grad, cross_out_grad, ffn_dec, dec_norm = decoder_turn(
        dec_first,
        cross_mix,
        At(dec_cot, 1),
        dec_norm_in,
        parts(cross, 1),
        parts(up, 1),
        parts(down, 1),
        True,
    )
    cross_q_grad, memory_grads, (ffn_dec, enc_cot) = attend_back(
        cross_q,
        memory,
        cross_mix,
        cross_mix_grad,
        cross_lse,
        cross_span,
        2 * chunk,
        Carry(
            [
                Reduce(ffn_dec, 256, [0, 1, 2, 3], [1, 2], "chip"),
                SpreadRows(cotangent[0], (0,), 4),
            ],
            5,
        ),
        2,
    )
    dec_first_grad, mix_grad, cross_query_grad, dec_out, mid_norm = decoder_middle_back(
        dec_first,
        dec_mix,
        cross_q_grad,
        second_grad,
        dec_norm_in,
        parts(out, 1),
        parts(cross, 1),
        (1, None),
    )
    enc_first_grad, mix_grad, ffn_enc, sides, enc_norm = encoder_back(
        enc_first,
        enc_third,
        enc_mix,
        memory_grads,
        At(enc_cot, 0),
        enc_norm_in,
        parts(out, 0),
        parts(up, 0),
        parts(down, 0),
        parts(cross, 0),
        [dec_out, cross_query_grad, cross_out_grad],
        (0, mix_grad),
    )
    q_grad, kv_grads, moved = attend_back(
        q,
        kv,
        mix,
        mix_grad,
        lse,
        self_spans,
        chunk,
        Carry(
            [
                Reduce(ffn_dec, 512, [0, 1], [1, *hops(2, 1, 1, 1, 2, 3)], "slice"),
                Reduce(ffn_enc, 512, [2, 0], [1, 3, *hops(2, 1, 2, 1, 1, 2)]),
                Reduce(sides, 768, [3, 1], [1, 3, *hops(1, 2, 1, 2, 1, 1)]),
                ReturnRows(encoded, 0, 11),
                ReturnRows(decoded, 1, 12),
            ],
            6,
        ),
        2,
    )
    ffn_dec, ffn_dec_other, ffn_enc, ffn_enc_other, sides, _, encoded, decoded = moved
    tail = (
        ([2, 2, 2, 2, 2, 3], [1, 2, *hops(1, 1, 1, 1, 1, 2)]),
        ([4, 4, 4, 4, 4, 4, 4], [1, 2, *hops(1, 1, 1, 1, 1, 1)]),
        (8, 6),
        8 + 2 * levels,
    )
    enc_last, enc_other, dec_last, dec_other, source_grad, target_grad = close_down(
        x,
        [enc_first_grad, dec_first_grad],
        q_grad,
        kv_grads,
        norm,
        qkv,
        [enc_norm, dec_norm, mid_norm],
        tail,
        7,
    )

    half = 3 * width // 2
    units = ffn_up.shape[-1]

    def columns(source, row, count, target, to):
        wide = source.shape[-1]
        for h in range(2):
            target[to : to + count, h * wide : (h + 1) * wide] = source[
                row + h * count : row + (h + 1) * count, :
            ].astype(F32)

    def finish(fetch, rooms):
        grads, result, up, down, first, second, side, norm_part = range(8)
        room = fetch(grads)
        for row in range(2):
            rooms[0][row] = room[row].astype(F32)
        yield rooms[0]
        yield fetch(result)
        columns(fetch(up), 0, width, rooms[2], 0)
        yield rooms[2]
        rooms[3][...] = fetch(down)[...].astype(F32)
        yield rooms[3]
        room = fetch(side)
        columns(room, 0, width // 2, rooms[4], 0)
        yield rooms[4]
        rooms[5][...] = room[width:, :].astype(F32)
        yield rooms[5]
        columns(fetch(first), 0, half, rooms[6], 0)
        columns(fetch(second), 0, half, rooms[6], half)
        yield rooms[6]
        lines = fetch(norm_part)[...].astype(F32)
        wide = width // PAIR
        for slot in range(3):
            for i in range(2):
                for h in range(wide):
                    line = (2 * slot + i) * wide + h
                    rooms[7][slot, i : i + 1, h * PAIR : (h + 1) * PAIR] = lines[
                        line : line + 1, :
                    ]
        yield rooms[7]

    part = qkv.shape[-1]
    token_grad, result, up_grad, down_grad, out_grad, cross_grad, qkv_grad, norm_grad = lay_out(
        [
            (source_grad, target_grad),
            (encoded, decoded),
            (ffn_enc, ffn_dec_other),
            (ffn_enc_other, ffn_dec),
            (enc_last, dec_other),
            (enc_other, dec_last),
        ],
        [(sides, 0, sides.shape[0]), (enc_last, 2 * half, 32)],
        [
            ((2, rows, width), F32),
            ((2, rows, width), BF16),
            ((width, units), F32),
            ((units, width), F32),
            ((part, width), F32),
            ((2 * width, part), F32),
            ((2 * half, part), F32),
            (norms.shape[1:], F32),
        ],
        finish,
    )
    return (
        result[None],
        token_grad[None],
        qkv_grad.reshape(self_qkv.shape),
        out_grad[None],
        cross_grad.reshape(cross_proj.shape),
        up_grad[None],
        down_grad[None],
        norm_grad[None],
    )


def solution(mesh):
    placed = (
        P("section", "dp", "tensor", None),
        P(None, "dp", None),
        P("section", None, None, "tensor"),
        P("section", "tensor", None),
        P("section", None, None, "tensor"),
        P("section", None, "tensor"),
        P("section", "tensor", None),
        P("section", None, None, None),
        P("section", "dp", "tensor", None),
    )
    sizes = dict(mesh.shape)
    steps = sizes["dp"].bit_length() - 1
    fast = sizes["tensor"] == 2 and sizes["dp"] == 1 << steps and 0 < steps <= 3
    return jax.shard_map(
        local_fast if fast else local_general,
        mesh=mesh,
        in_specs=placed,
        out_specs=(
            P("section", "dp", "tensor", None),
            P("section", "dp", "tensor", None),
            P("section", None, None, "tensor"),
            P("section", "tensor", None),
            P("section", None, None, "tensor"),
            P("section", None, "tensor"),
            P("section", "tensor", None),
            P("section", None, None, None),
        ),
        check_vma=False,
    )
```

```python
import functools
import math

import jax
import jax.numpy as jnp
from jax import lax
from jax.experimental import pallas as pl
from jax.experimental.pallas import tpu as pltpu
from jax.sharding import PartitionSpec as P

HEADS = 8
EPSILON = 1e-05
MASKED = -1000000000.0
LOG2E = 1.0 / math.log(2.0)
PAIR = 128
HALF = 64
VMEM = 60 * 1024 * 1024
BF16 = jnp.bfloat16
F32 = jnp.float32


def standardize(rows):
    mean = jnp.mean(rows, axis=-1, keepdims=True)
    centered = rows - mean
    inv = lax.rsqrt(jnp.mean(centered * centered, axis=-1, keepdims=True) + EPSILON)
    return centered * inv, inv


def affine(unit, norm_ref, slot):
    return unit * norm_ref[slot, 0:1, :] + norm_ref[slot, 1:2, :]


def norm_back(unit, inv, norm_ref, slot, grad, grad_ref):
    grad_ref[slot, 0:1, :] += jnp.sum(grad * unit, axis=0, keepdims=True)
    grad_ref[slot, 1:2, :] += jnp.sum(grad, axis=0, keepdims=True)
    scaled = grad * norm_ref[slot, 0:1, :]
    first = jnp.mean(scaled, axis=-1, keepdims=True)
    second = jnp.mean(scaled * unit, axis=-1, keepdims=True)
    return inv * (scaled - first - unit * second)


def gelu_tanh(inner):
    return jnp.tanh(0.7978845608028654 * (inner + 0.044715 * inner * inner * inner))


def gelu(inner):
    return 0.5 * inner * (1.0 + gelu_tanh(inner))


def gelu_both(inner):
    bent = gelu_tanh(inner)
    slope = 0.7978845608028654 * (1.0 + 0.134145 * inner * inner)
    half = 0.5 * (1.0 + bent)
    return inner * half, half + 0.5 * inner * (1.0 - bent * bent) * slope


def dot_nn(a, b):
    return jnp.dot(a, b, preferred_element_type=F32)


def dot_nt(a, b):
    return lax.dot_general(a, b, (((1,), (1,)), ((), ())), preferred_element_type=F32)


def dot_tn(a, b):
    return lax.dot_general(a, b, (((0,), (0,)), ((), ())), preferred_element_type=F32)


class At:
    def __init__(self, array, *lead):
        self.array, self.lead = array, lead
        self.shape = array.shape[len(lead) :]
        self.dtype = array.dtype

    def spec(self, sizes, index, **options):
        nones = (None,) * len(self.lead)
        return pl.BlockSpec(nones + tuple(sizes), lambda *g: self.lead + tuple(index(*g)), **options)


def at(array):
    return array if isinstance(array, At) else At(array)


def row_call(
    body, name, rows, row_ins, whole_ins, row_outs, keeps, finals, finish, flops, into=None, push=None
):
    block, part = min(512, rows), min(256, rows)
    row_ins = [(at(a), dim) for a, dim in row_ins]
    whole_ins = [at(a) for a in whole_ins]

    def blocked(array, dim):
        sizes = tuple(block if i == dim else size for i, size in enumerate(array.shape))
        return array.spec(sizes, lambda g: tuple(g if i == dim else 0 for i in range(len(sizes))))

    def blocked_out(shape, dim):
        sizes = tuple(block if i == dim else size for i, size in enumerate(shape))
        return pl.BlockSpec(
            sizes, lambda g: tuple(g if i == dim else 0 for i in range(len(shape)))
        )

    def sided_out(shape, dim):
        plain = blocked_out(shape, dim)
        return pl.BlockSpec(
            (None, *plain.block_shape), lambda g: (into[0], *plain.index_map(g))
        )

    def whole(array):
        return array.spec(
            array.shape,
            lambda g: (0,) * len(array.shape),
            pipeline_mode=pl.Buffered(buffer_count=1),
        )

    def whole_out(shape):
        return pl.BlockSpec(
            shape, lambda g: (0,) * len(shape), pipeline_mode=pl.Buffered(buffer_count=1)
        )

    n_rows_in = len(row_ins)
    n_in = n_rows_in + len(whole_ins)
    n_row, n_final = len(row_outs), len(finals)
    out_specs = [blocked_out(shape, dim) for shape, _, dim in row_outs]
    out_shapes = [jax.ShapeDtypeStruct(shape, dtype) for shape, dtype, _ in row_outs]
    push_outs, push_scratch, push_params = [], [], {}
    if push is not None:
        push_outs = [out_shapes[push[0]]]
        push_scratch = [
            pltpu.VMEM(push_outs[0].shape, push_outs[0].dtype),
            pltpu.SemaphoreType.DMA((2, rows // block)),
        ]
        push_params = dict(collective_id=push[1], has_side_effects=True)
    held, aliases = [], {}
    if into is not None:
        shape, dtype, dim = row_outs[-1]
        out_specs[-1] = sided_out(shape, dim)
        out_shapes[-1] = jax.ShapeDtypeStruct((2, *shape), dtype)
        if into[1] is not None:
            held, aliases = [into[1]], {n_in: n_row - 1}

    def kernel(*refs):
        ins, refs = refs[:n_in], refs[len(held) :]
        outs = refs[n_in : n_in + n_row]
        last_outs, kept = refs[n_in + n_row : n_in + n_row + n_final], refs[n_in + n_row + n_final :]
        step = pl.program_id(0)
        if push is not None:
            pushed, kept = kept[0], kept[1:]
            kept, (push_room, push_sems) = kept[:-2], kept[-2:]

            def send(i):
                own = pl.ds(i * block, block)
                return remote(
                    push_room.at[:, :, own, :],
                    pushed.at[:, :, own, :],
                    push_sems.at[0, i],
                    push_sems.at[1, i],
                    where_is("near"),
                )

            @pl.when(step == 0)
            def _():
                greet(["near"])
        if finals:

            @pl.when(step == 0)
            def _():
                kept[-1][...] = jnp.zeros_like(kept[-1])

        turns = []
        for begin in range(0, block, part):
            all_rows = pl.ds(pl.multiple_of(step * block + begin, part), part)
            turns.append(body(ins, outs, kept, slice(begin, begin + part), all_rows))
        waiting, running = turns[1:], turns[:1]
        while running:
            running = [turn for turn in running if next(turn, LAST) is not LAST]
            if waiting:
                running.append(waiting.pop(0))

        if push is not None:
            for i in range(rows // block):

                @pl.when(step == i)
                def _():
                    push_room[:, :, i * block : (i + 1) * block, :] = outs[push[0]][...]
                    send(i).start()

            @pl.when(step == pl.num_programs(0) - 1)
            def _():
                for i in range(rows // block):
                    send(i).wait()

        if finals:

            @pl.when(step == pl.num_programs(0) - 1)
            def _():
                finish(ins[n_rows_in:], kept, last_outs)

    arrays = [array for array, _ in row_ins] + whole_ins
    size = sum(math.prod(a.shape) * a.dtype.itemsize for a in arrays)
    return pl.pallas_call(
        kernel,
        grid=(rows // block,),
        in_specs=[blocked(a, dim) for a, dim in row_ins]
        + [whole(a) for a in whole_ins]
        + [pl.BlockSpec(memory_space=pl.ANY)] * len(held),
        out_specs=out_specs
        + [whole_out(shape) for shape, _ in finals]
        + [pl.BlockSpec(memory_space=pl.ANY)] * len(push_outs),
        out_shape=out_shapes
        + [jax.ShapeDtypeStruct(shape, dtype) for shape, dtype in finals]
        + push_outs,
        input_output_aliases=aliases,
        scratch_shapes=[pltpu.VMEM(shape, dtype) for shape, dtype in keeps] + push_scratch,
        compiler_params=pltpu.CompilerParams(vmem_limit_bytes=VMEM, **push_params),
        cost_estimate=pl.CostEstimate(flops=flops, bytes_accessed=size, transcendentals=0),
        name=name,
    )(*[a.array for a in arrays], *held)


LAST = 1000


def split(refs, parts, count):
    return [refs[i * parts : (i + 1) * parts] for i in range(count)]


def project_qkv(x, norm, weights, with_norm):
    x = at(x)
    rows, width = x.shape
    parts, part = len(weights), weights[0].shape[-1]
    score = LOG2E / math.sqrt(width // HEADS)

    def body(ins, outs, kept, own, all_rows):
        x_ref, norm_ref, *w = ins
        q_ref, kv_ref = outs
        low = x_ref[own, :]
        if with_norm:
            unit, _ = standardize(low.astype(F32))
            low = affine(unit, norm_ref, 2).astype(BF16)
        yield
        for k in range(parts):
            q_ref[k, own, :] = (dot_nn(low, w[k][0]) * score).astype(BF16)
            kv_ref[k, 0, own, :] = dot_nn(low, w[k][1]).astype(BF16)
            kv_ref[k, 1, own, :] = dot_nn(low, w[k][2]).astype(BF16)
            yield

    return row_call(
        body,
        "project_qkv",
        rows,
        [(x, 0)],
        [norm, *weights],
        [((parts, rows, part), BF16, 1), ((parts, 2, rows, part), BF16, 2)],
        [],
        [],
        None,
        6 * rows * width * width,
    )


def encoder_forward(x, mix, norm, out, up, down, cross, push=None):
    x = at(x)
    rows, width = x.shape
    parts, part = len(out), out[0].shape[0]

    def body(ins, outs, kept, own, all_rows):
        x_ref, mix_ref, norm_ref = ins[:3]
        wo, wu, wd, wc = split(ins[3:], parts, 4)
        result_ref, kv_ref, first_ref, third_ref = outs
        unit, _ = standardize(x_ref[own, :].astype(F32))
        first = affine(unit, norm_ref, 2)
        for k in range(parts):
            first += dot_nn(mix_ref[k, own, :], wo[k][...])
        yield
        first_ref[own, :] = first
        unit, _ = standardize(first)
        third = affine(unit, norm_ref, 0)
        low = third.astype(BF16)
        inner = dot_nn(low, wu[0][...])
        yield
        for k in range(parts):
            act = gelu(inner).astype(BF16)
            if k + 1 < parts:
                inner = dot_nn(low, wu[k + 1][...])
            third += dot_nn(act, wd[k][...])
            yield
        third_ref[own, :] = third
        unit, _ = standardize(third)
        low = affine(unit, norm_ref, 1).astype(BF16)
        result_ref[own, :] = low
        yield
        for k in range(parts):
            kv_ref[k, 0, own, :] = dot_nn(low, wc[k][0]).astype(BF16)
            kv_ref[k, 1, own, :] = dot_nn(low, wc[k][1]).astype(BF16)

    units = sum(w.shape[1] for w in up)
    return row_call(
        body,
        "encoder_forward",
        rows,
        [(x, 0), (mix, 1)],
        [norm, *out, *up, *down, *cross],
        [
            ((rows, width), BF16, 0),
            ((parts, 2, rows, part), BF16, 2),
            ((rows, width), F32, 0),
            ((rows, width), F32, 0),
        ],
        [],
        [],
        None,
        6 * rows * width * width + 4 * rows * width * units,
        push=None if push is None else (1, push),
    )


def decoder_middle(x, mix, norm, out, cross):
    x = at(x)
    rows, width = x.shape
    parts, part = len(out), out[0].shape[0]
    score = LOG2E / math.sqrt(width // HEADS)

    def body(ins, outs, kept, own, all_rows):
        x_ref, mix_ref, norm_ref = ins[:3]
        wo, wc = split(ins[3:], parts, 2)
        q_ref, first_ref = outs
        first = x_ref[own, :].astype(F32)
        for k in range(parts):
            first += dot_nn(mix_ref[k, own, :], wo[k][...])
        yield
        first_ref[own, :] = first
        unit, _ = standardize(first)
        low = affine(unit, norm_ref, 0).astype(BF16)
        yield
        for k in range(parts):
            q_ref[k, own, :] = (dot_nn(low, wc[k][0]) * score).astype(BF16)

    return row_call(
        body,
        "decoder_middle",
        rows,
        [(x, 0), (mix, 1)],
        [norm, *out, *cross],
        [((parts, rows, part), BF16, 1), ((rows, width), F32, 0)],
        [],
        [],
        None,
        4 * rows * width * width,
    )


def ffn_finals(low, act, inner, grad, parts, units, paired, up_out, down_out):
    for k in range(parts):
        if paired:
            half = units // 2
            for h in range(2):
                begin = k * units + h * half
                up_out[0, k, h * half : (h + 1) * half, :] = dot_tn(
                    low[...], inner[:, begin : begin + half]
                ).astype(BF16)
            into = up_out.at[1, k]
        else:
            up_out[k] = dot_tn(low[...], inner[:, k * units : (k + 1) * units]).astype(BF16)
            into = down_out.at[k]
        into[...] = dot_tn(act[:, k * units : (k + 1) * units], grad[...]).astype(BF16)


def decoder_turn(first, mix, cotangent, norm, cross, up, down, paired=False):
    rows, width = first.shape
    parts, part, units = len(cross), cross[0].shape[-1], up[0].shape[1]

    def body(ins, outs, kept, own, all_rows):
        first_ref, cot_ref, mix_ref, norm_ref = ins[:4]
        wc, wu, wd = split(ins[4:], parts, 3)
        result_ref, second_grad_ref, mix_grad_ref = outs
        low_keep, act_keep, inner_keep, third_keep, second_keep, norm_total = kept
        unit, _ = standardize(first_ref[own, :])
        second = affine(unit, norm_ref, 0)
        for k in range(parts):
            second += dot_nt(mix_ref[k, all_rows, :], wc[k][1])
        yield
        unit_two, inv_two = standardize(second)
        third = affine(unit_two, norm_ref, 2)
        low = third.astype(BF16)
        low_keep[all_rows, :] = low
        inner = dot_nn(low, wu[0][...])
        yield
        slopes = []
        for k in range(parts):
            act, slope = gelu_both(inner)
            act = act.astype(BF16)
            slopes.append(slope)
            if k + 1 < parts:
                inner = dot_nn(low, wu[k + 1][...])
            act_keep[all_rows, k * units : (k + 1) * units] = act
            third += dot_nn(act, wd[k][...])
            yield
        unit_three, inv_three = standardize(third)
        result_ref[own, :] = affine(unit_three, norm_ref, 1).astype(BF16)
        grad = norm_back(
            unit_three, inv_three, norm_ref, 1, cot_ref[own, :].astype(F32), norm_total
        )
        grad_low = grad.astype(BF16)
        third_keep[all_rows, :] = grad_low
        grad_act = dot_nt(grad_low, wd[0][...])
        yield
        for k in range(parts):
            grad_inner = (grad_act * slopes[k]).astype(BF16)
            if k + 1 < parts:
                grad_act = dot_nt(grad_low, wd[k + 1][...])
            inner_keep[all_rows, k * units : (k + 1) * units] = grad_inner
            grad += dot_nt(grad_inner, wu[k][...])
            yield
        grad = norm_back(unit_two, inv_two, norm_ref, 2, grad, norm_total)
        second_grad_ref[own, :] = grad
        grad_low = grad.astype(BF16)
        second_keep[all_rows, :] = grad_low
        yield
        for k in range(parts):
            mix_grad_ref[k, own, :] = dot_nn(grad_low, wc[k][1]).astype(BF16)

    def finish(ins, kept, outs):
        mix_ref = ins[0]
        low_keep, act_keep, inner_keep, third_keep, second_keep, norm_total = kept
        for k in range(parts):
            outs[0][k] = dot_tn(second_keep[...], mix_ref[k]).astype(BF16)
        ffn_finals(
            low_keep, act_keep, inner_keep, third_keep, parts, units, paired, outs[1], outs[2]
        )
        outs[-1][...] = norm_total[...]

    ffn = (
        [((2, parts, units, width), BF16)]
        if paired
        else [((parts, width, units), BF16), ((parts, units, width), BF16)]
    )
    whole = (rows, width)
    return row_call(
        body,
        "decoder_turn",
        rows,
        [(first, 0), (cotangent, 0)],
        [mix, norm, *cross, *up, *down],
        [(whole, BF16, 0), (whole, F32, 0), ((parts, rows, part), BF16, 1)],
        [
            (whole, BF16),
            ((rows, parts * units), BF16),
            ((rows, parts * units), BF16),
            (whole, BF16),
            (whole, BF16),
            ((3, 2, width), F32),
        ],
        [((parts, width, part), BF16), *ffn, ((3, 2, width), F32)],
        finish,
        6 * rows * width * width + 12 * rows * width * units * parts,
    )


def decoder_middle_back(first, mix, query_grad, second_grad, norm, out, cross, into=None):
    rows, width = first.shape
    parts, part = len(out), out[0].shape[0]

    def body(ins, outs, kept, own, all_rows):
        first_ref, second_grad_ref, mix_ref, query_grad_ref, norm_ref = ins[:5]
        wo, wc = split(ins[5:], parts, 2)
        first_grad_ref, mix_grad_ref = outs
        low_keep, grad_keep, norm_total = kept
        unit, inv = standardize(first_ref[own, :])
        low_keep[all_rows, :] = affine(unit, norm_ref, 0).astype(BF16)
        grad = second_grad_ref[own, :]
        for k in range(parts):
            grad += dot_nt(query_grad_ref[k, all_rows, :], wc[k][0])
        yield
        grad = norm_back(unit, inv, norm_ref, 0, grad, norm_total)
        first_grad_ref[own, :] = grad
        grad_low = grad.astype(BF16)
        grad_keep[all_rows, :] = grad_low
        yield
        for k in range(parts):
            mix_grad_ref[k, own, :] = dot_nt(grad_low, wo[k][...]).astype(BF16)

    def finish(ins, kept, outs):
        mix_ref, query_grad_ref = ins[:2]
        low_keep, grad_keep, norm_total = kept
        for k in range(parts):
            outs[0][k] = dot_tn(low_keep[...], query_grad_ref[k]).astype(BF16)
            outs[1][k] = dot_tn(mix_ref[k], grad_keep[...]).astype(BF16)
        outs[2][...] = norm_total[...]

    whole = (rows, width)
    return row_call(
        body,
        "decoder_middle_back",
        rows,
        [(first, 0), (second_grad, 0)],
        [mix, query_grad, norm, *out, *cross],
        [(whole, F32, 0), ((parts, rows, part), BF16, 1)],
        [(whole, BF16), (whole, BF16), ((3, 2, width), F32)],
        [
            ((parts, width, part), BF16),
            ((parts, part, width), BF16),
            ((3, 2, width), F32),
        ],
        finish,
        8 * rows * width * width,
        into,
    )


def added(refs, *index):
    total = refs[0][index]
    for ref in refs[1:]:
        total = total.astype(F32) + ref[index].astype(F32)
    return total.astype(BF16)


def encoder_back(
    first, third, mix, memory_grads, cotangent, norm, out, up, down, cross, paired=None, into=None
):
    rows, width = first.shape
    parts, part, units = len(out), out[0].shape[0], up[0].shape[1]
    pieces = len(memory_grads)

    def body(ins, outs, kept, own, all_rows):
        first_ref, third_ref, cot_ref = ins[:3]
        memory_refs, mix_ref, norm_ref = ins[3 : 3 + pieces], ins[3 + pieces], ins[4 + pieces]
        wo, wu, wd, wc = split(ins[5 + pieces :], parts, 4)
        first_grad_ref, mix_grad_ref = outs
        low_keep, memory_keep, mid_keep, act_keep, inner_keep, third_keep, first_keep, norm_total = (
            kept
        )
        grad = cot_ref[own, :].astype(F32)
        for k in range(parts):
            for i in range(2):
                memory = added(memory_refs, k, i, own)
                memory_keep[k, i, all_rows, :] = memory
                grad += dot_nt(memory, wc[k][i])
        yield
        unit, inv = standardize(third_ref[own, :])
        low_keep[all_rows, :] = affine(unit, norm_ref, 1).astype(BF16)
        unit_one, inv_one = standardize(first_ref[own, :])
        low = affine(unit_one, norm_ref, 0).astype(BF16)
        mid_keep[all_rows, :] = low
        inner = dot_nn(low, wu[0][...])
        grad = norm_back(unit, inv, norm_ref, 1, grad, norm_total)
        grad_low = grad.astype(BF16)
        third_keep[all_rows, :] = grad_low
        grad_act = dot_nt(grad_low, wd[0][...])
        yield
        for k in range(parts):
            act, slope = gelu_both(inner)
            if k + 1 < parts:
                inner = dot_nn(low, wu[k + 1][...])
            act_keep[all_rows, k * units : (k + 1) * units] = act.astype(BF16)
            grad_inner = (grad_act * slope).astype(BF16)
            if k + 1 < parts:
                grad_act = dot_nt(grad_low, wd[k + 1][...])
            inner_keep[all_rows, k * units : (k + 1) * units] = grad_inner
            grad += dot_nt(grad_inner, wu[k][...])
            yield
        grad = norm_back(unit_one, inv_one, norm_ref, 0, grad, norm_total)
        first_grad_ref[own, :] = grad
        grad_low = grad.astype(BF16)
        first_keep[all_rows, :] = grad_low
        yield
        for k in range(parts):
            mix_grad_ref[k, own, :] = dot_nt(grad_low, wo[k][...]).astype(BF16)

    def finish(ins, kept, outs):
        mix_ref = ins[0]
        low_keep, memory_keep, mid_keep, act_keep, inner_keep, third_keep, first_keep, norm_total = (
            kept
        )
        if paired:
            ffn_finals(
                mid_keep, act_keep, inner_keep, third_keep, parts, units, True, outs[0], None
            )
            dec_out, dec_query, dec_cross = ins[-3:]
            sides = outs[1]
            for k in range(parts):
                column_blocks(dot_tn(mix_ref[k], first_keep[...]), sides, 0, k, 0)
                column_blocks(dec_out[k], sides, 1, k, 0)
                for i in range(2):
                    here = slice((1 + i) * width, (2 + i) * width)
                    sides[0, k, here, :] = dot_tn(low_keep[...], memory_keep[k, i]).astype(BF16)
                    sides[1, k, here, :] = (dec_query, dec_cross)[i][k]
        else:
            for k in range(parts):
                for i in range(2):
                    outs[0][k, i] = dot_tn(low_keep[...], memory_keep[k, i]).astype(BF16)
                outs[1][k] = dot_tn(mix_ref[k], first_keep[...]).astype(BF16)
            ffn_finals(
                mid_keep, act_keep, inner_keep, third_keep, parts, units, False, outs[2], outs[3]
            )
        outs[-1][...] = norm_total[...]

    if paired:
        finals = [((2, parts, units, width), BF16), ((2, parts, 3 * width, part), BF16)]
    else:
        finals = [
            ((parts, 2, width, part), BF16),
            ((parts, part, width), BF16),
            ((parts, width, units), BF16),
            ((parts, units, width), BF16),
        ]
    whole = (rows, width)
    return row_call(
        body,
        "encoder_back",
        rows,
        [(first, 0), (third, 0), (cotangent, 0)] + [(m, 2) for m in memory_grads],
        [mix, norm, *out, *up, *down, *cross, *(paired or [])],
        [(whole, F32, 0), ((parts, rows, part), BF16, 1)],
        [
            (whole, BF16),
            ((parts, 2, rows, part), BF16),
            (whole, BF16),
            ((rows, parts * units), BF16),
            ((rows, parts * units), BF16),
            (whole, BF16),
            (whole, BF16),
            ((3, 2, width), F32),
        ],
        [*finals, ((3, 2, width), F32)],
        finish,
        12 * rows * width * width + 10 * rows * width * units * parts,
        into,
    )


def column_blocks(wide, into, core, k, row):
    rows, columns = wide.shape[0], wide.shape[1] // 2
    for half in range(2):
        into[core, k, row + half * rows : row + (half + 1) * rows, :] = wide[
            :, half * columns : (half + 1) * columns
        ].astype(BF16)


def input_part(refs, kept, own, all_rows, norm_ref, w, with_norm):
    x_ref, first_grad_ref, key_refs, query_grad_ref, grad_ref = refs
    low_keep, key_keep, norm_total = kept
    grad = first_grad_ref[own, :]
    for k in range(len(w)):
        grad += dot_nt(query_grad_ref[k, all_rows, :], w[k][0])
        for i in range(2):
            member = added(key_refs, k, i, own)
            key_keep[k, i, all_rows, :] = member
            grad += dot_nt(member, w[k][1 + i])
    yield
    low = x_ref[own, :]
    if with_norm:
        unit, inv = standardize(low.astype(F32))
        low = affine(unit, norm_ref, 2).astype(BF16)
        grad = norm_back(unit, inv, norm_ref, 2, grad, norm_total)
    low_keep[all_rows, :] = low
    grad_ref[own, :] = grad.astype(BF16)


def input_sums(kept, query_grad_ref, into, parts):
    low_keep, key_keep, _ = kept
    for k in range(parts):
        both = jnp.concatenate(
            [dot_tn(low_keep[...], query_grad_ref[k])]
            + [dot_tn(low_keep[...], key_keep[k, i]) for i in range(2)],
            axis=0,
        )
        half = both.shape[0] // 2
        for core in range(2):
            column_blocks(both[core * half : (core + 1) * half], into, core, k, 0)


def norm_lines(sides, into, parts, row):
    for core, table in enumerate(sides):
        lines = [
            table[slot, i : i + 1, h * PAIR : (h + 1) * PAIR]
            for slot in range(3)
            for i in range(2)
            for h in range(table.shape[-1] // PAIR)
        ]
        lines.append(jnp.zeros((2 * PAIR - len(lines), PAIR), F32))
        lines = jnp.concatenate(lines, axis=0).astype(BF16)
        for k in range(parts):
            into[core, k, row:, :] = lines


def input_back(x, first_grad, query_grad, key_grads, norm, weights, with_norm):
    x = at(x)
    rows, width = x.shape
    parts, part = len(weights), weights[0].shape[-1]
    pieces = len(key_grads)
    key_grads = [at(g) for g in key_grads]

    def body(ins, outs, kept, own, all_rows):
        x_ref, first_grad_ref = ins[:2]
        key_refs, query_grad_ref, norm_ref = ins[2 : 2 + pieces], ins[2 + pieces], ins[3 + pieces]
        refs = x_ref, first_grad_ref, key_refs, query_grad_ref, outs[0]
        yield from input_part(refs, kept, own, all_rows, norm_ref, ins[4 + pieces :], with_norm)

    def finish(ins, kept, outs):
        query_grad_ref = ins[0]
        low_keep, key_keep, norm_total = kept
        for k in range(parts):
            outs[0][k, 0] = dot_tn(low_keep[...], query_grad_ref[k]).astype(BF16)
            for i in range(2):
                outs[0][k, 1 + i] = dot_tn(low_keep[...], key_keep[k, i]).astype(BF16)
        outs[1][...] = norm_total[...]

    whole = (rows, width)
    return row_call(
        body,
        "input_back",
        rows,
        [(x, 0), (first_grad, 0)] + [(g, 2) for g in key_grads],
        [query_grad, norm, *weights],
        [(whole, BF16, 0)],
        [(whole, BF16), ((parts, 2, rows, part), BF16), ((3, 2, width), F32)],
        [((parts, 3, width, part), BF16), ((3, 2, width), F32)],
        finish,
        12 * rows * width * width,
    )


def widen_keys(span, kv_refs, key_e, key_o, value_e, value_o, rows):
    lane = lax.broadcasted_iota(jnp.int32, (rows, PAIR), 1)
    place = lax.broadcasted_iota(jnp.int32, (rows, PAIR), 0)
    low = lane < HALF
    for g, kv_ref in enumerate(kv_refs):
        spot = place + span[2 + g]
        live = (spot >= span[0]) & (spot < span[1])
        bias = jnp.where(live, 0.0, MASKED)
        keys, values = kv_ref[0].astype(F32), kv_ref[1].astype(F32)
        own = pl.ds(g * rows, rows)
        key_e[own, :] = jnp.where(low, keys, jnp.where(lane == HALF, bias, 1.0)).astype(BF16)
        key_o[own, :] = jnp.where(low, jnp.where(lane == 0, bias, 1.0), keys).astype(BF16)
        value_e[own, :] = jnp.where(low, values, 1.0).astype(BF16)
        value_o[own, :] = jnp.where(low, 1.0, values).astype(BF16)


class Lengths:
    def __init__(self, lengths, asking=None, answering=None):
        self.lengths, self.asking, self.answering = lengths, asking, answering

    def span(self, ref, side, rows):
        section, _, tensor = spots()
        asks, answers = [
            [ref[side if own is None else own, tensor, j] for j in range(2)]
            for own in (self.asking, self.answering)
        ]
        paired = asks[1] > 0
        second = paired & (section * rows >= asks[0])
        begin = jnp.where(second, answers[0], 0)
        end = jnp.where(second | jnp.logical_not(paired), answers[0] + answers[1], answers[0])
        return [begin, end, section * rows, (1 - section) * rows]


class Pairs:
    def __init__(self, query):
        self.sides = query.shape[:-3]
        self.parts, self.rows, self.part = query.shape[-3:]
        self.per_part = self.part // PAIR
        self.per_side = self.parts * self.per_part
        self.count = self.per_side * math.prod(self.sides)

    def side(self, i):
        return (i // self.per_side,) if self.sides else ()

    def place(self, i):
        i = i % self.per_side
        return i // self.per_part, i % self.per_part

    def query_spec(self, array):
        def index(i):
            part, column = self.place(i)
            return *self.side(i), part, 0, column

        none = (None,) * len(self.sides)
        return at(array).spec((*none, None, self.rows, PAIR), index)

    def kv_spec(self, array):
        def index(i):
            part, column = self.place(i)
            return *self.side(i), part, 0, 0, column

        none = (None,) * len(self.sides)
        return at(array).spec((*none, None, 2, self.rows, PAIR), index)

    def lse_spec(self):
        none = (None,) * len(self.sides)
        return pl.BlockSpec(
            (*none, self.rows, PAIR), lambda i: (*self.side(i), 0, i % self.per_side)
        )

    def span(self, span, span_ref, i):
        side = i // self.per_side if self.sides else 0
        if isinstance(span, Lengths):
            return span.span(span_ref, side, self.rows)
        return [span_ref[side, j] for j in range(span_ref.shape[1])]


def attend(query, kv_pieces, span, block, carrier=None, slots=1):
    query, kv_pieces = at(query), [at(piece) for piece in kv_pieces]
    carrier = carrier or Carry()
    heads_of = Pairs(query)
    rows, pairs = heads_of.rows, heads_of.count
    pieces = len(kv_pieces)
    keys = rows * pieces
    n_carry = len(carrier.ins)
    blocks = rows // block
    stride = blocks // slots

    def kernel(span_ref, q_ref, *refs):
        kv_refs, refs = refs[:pieces], refs[pieces:]
        carry_ins, refs = refs[:n_carry], refs[n_carry:]
        out_ref, lse_ref, refs = refs[0], refs[1], refs[2:]
        carry_outs, refs = refs[: len(carrier.outs)], refs[len(carrier.outs) :]
        key_e, key_o, value_e, value_o = refs[:4]

        def carry(slot):
            place = pl.program_id(0)
            carrier.run(place, slot, slots, pairs * slots, carry_ins, carry_outs, refs[4:])

        carry(0)
        seen = heads_of.span(span, span_ref, pl.program_id(0))
        widen_keys(seen, kv_refs, key_e, key_o, value_e, value_o, rows)
        lane = lax.broadcasted_iota(jnp.int32, (block, PAIR), 1)
        low = lane < HALF
        units = []
        for i in range(blocks):
            query = q_ref[i * block : (i + 1) * block, :].astype(F32)
            first = jnp.where(low, query, jnp.where(lane == HALF, 1.0, 0.0)).astype(BF16)
            second = jnp.where(low, jnp.where(lane == 0, 1.0, 0.0), query).astype(BF16)
            units += [(first, key_e, value_e), (second, key_o, value_o)]

        def scores_of(unit):
            return dot_nt(unit[0], unit[1][...])

        ahead = scores_of(units[0])
        tops, sums = [], []
        for u, unit in enumerate(units):
            if u and u % (2 * stride) == 0:
                carry(u // (2 * stride))
            scores = ahead
            if u + 1 < len(units):
                ahead = scores_of(units[u + 1])
            top = jnp.max(scores, axis=1, keepdims=True)
            tops.append(top)
            sums.append(dot_nn(jnp.exp2(scores - top).astype(BF16), unit[2][...]))
            if u % 2:
                own = slice(u // 2 * block, (u // 2 + 1) * block)
                top = jnp.where(low, tops[u], tops[u - 1])
                weight = jnp.where(low, sums[u], sums[u - 1])
                lse_ref[own, :] = top + LOG2E * jnp.log(weight)
                mixed = jnp.where(low, sums[u - 1], sums[u])
                out_ref[own, :] = (mixed / pltpu.roll(weight, HALF, 1)).astype(BF16)
        carry(slots)

    query_spec, kv_spec = heads_of.query_spec, heads_of.kv_spec
    lse_spec = heads_of.lse_spec()
    plain = jax.ShapeDtypeStruct(query.shape, BF16)
    hold = pl.BlockSpec(memory_space=pl.ANY)
    return pl.pallas_call(
        kernel,
        grid=(pairs,),
        in_specs=[pl.BlockSpec(memory_space=pltpu.SMEM), query_spec(query)]
        + [kv_spec(piece) for piece in kv_pieces]
        + [hold] * n_carry,
        out_specs=[query_spec(plain), lse_spec] + [hold] * len(carrier.outs),
        scratch_shapes=[pltpu.VMEM((keys, PAIR), BF16)] * 4 + carrier.scratch,
        out_shape=[plain, jax.ShapeDtypeStruct((*heads_of.sides, rows, heads_of.per_side * PAIR), F32)] + carrier.outs,
        compiler_params=pltpu.CompilerParams(vmem_limit_bytes=VMEM, **carrier.params),
        cost_estimate=pl.CostEstimate(
            flops=16 * rows * keys * pairs * PAIR,
            bytes_accessed=8 * rows * pairs * PAIR * pieces,
            transcendentals=0,
        ),
        name="attend",
    )(
        span.lengths if isinstance(span, Lengths) else span, query.array, *[piece.array for piece in kv_pieces], *carrier.ins)


def attend_back(
    query, kv_pieces, mix, mix_grad, lse, span, chunk, carrier=None, slots=1
):
    query, kv_pieces = at(query), [at(piece) for piece in kv_pieces]
    mix, mix_grad = at(mix), at(mix_grad)
    heads_of = Pairs(query)
    rows, pairs = heads_of.rows, heads_of.count
    pieces = len(kv_pieces)
    keys = rows * pieces
    scale = 1.0 / math.sqrt(HALF)
    swaps = carrier is not None
    carrier = carrier or Carry()
    n_carry = len(carrier.ins)
    kept = 1 if swaps else pieces
    chunks = keys // chunk
    stride = chunks // slots

    def kernel(span_ref, q_ref, mix_ref, grad_ref, lse_ref, *refs):
        kv_refs, refs = refs[:pieces], refs[pieces:]
        carry_ins, refs = refs[:n_carry], refs[n_carry:]
        dq_ref, dkv_refs, refs = refs[0], refs[1 : pieces + 1], refs[pieces + 1 :]
        carry_outs, refs = refs[: len(carrier.outs)], refs[len(carrier.outs) :]
        key_e, key_o, value_e, value_o, key_t = refs[:5]
        refs = refs[5:]
        if swaps:
            given, swap_sems, refs = refs[0], refs[1], refs[2:]
        pair = pl.program_id(0)

        def carry(slot):
            carrier.run(pair, slot, slots, pairs * slots, carry_ins, carry_outs, refs)

        carry(0)
        seen = heads_of.span(span, span_ref, pl.program_id(0))
        widen_keys(seen, kv_refs, key_e, key_o, value_e, value_o, rows)
        for g, kv_ref in enumerate(kv_refs):
            key_t[:, g * rows : (g + 1) * rows] = kv_ref[0].T
        lane = lax.broadcasted_iota(jnp.int32, (rows, PAIR), 1)
        low = lane < HALF
        query, grad = q_ref[...].astype(F32), grad_ref[...].astype(F32)
        product = mix_ref[...].astype(F32) * grad
        inner = jnp.where(
            low,
            jnp.sum(jnp.where(low, 0.0, product), axis=1, keepdims=True),
            jnp.sum(jnp.where(low, product, 0.0), axis=1, keepdims=True),
        )
        spot = jnp.where(low, lane, lane - HALF)

        def three(value, shift):
            high = value.astype(BF16).astype(F32)
            rest = value - high
            mid = rest.astype(BF16).astype(F32)
            return jnp.where(
                spot == shift,
                high,
                jnp.where(
                    spot == shift + 1, mid, jnp.where(spot == shift + 2, rest - mid, 0.0)
                ),
            )

        lse = three(-lse_ref[...], 1) + jnp.where(spot == 0, 1.0, 0.0)
        inner = three(-inner, 0)
        heads = [
            (
                key,
                value,
                jnp.where(own, query, lse).astype(BF16).T,
                jnp.where(own, grad, inner).astype(BF16).T,
                jnp.where(own, query, 0.0).astype(BF16),
                jnp.where(own, grad, 0.0).astype(BF16),
            )
            for own, key, value in ((low, key_e, value_e), (~low, key_o, value_o))
        ]
        units = [(c * chunk, h) for c in range(chunks) for h in range(2)]

        def front(unit):
            begin, h = unit
            own = slice(begin, begin + chunk)
            key, value, q_wide, g_wide, _, _ = heads[h]
            return dot_nn(key[own, :], q_wide), dot_nn(value[own, :], g_wide)

        ahead = front(units[0])
        dq = [None, None]
        for u, (begin, h) in enumerate(units):
            if u and u % (2 * stride) == 0:
                carry(u // (2 * stride))
            scores, dprobs = ahead
            if u + 1 < len(units):
                ahead = front(units[u + 1])
            probs = jnp.exp2(scores)
            dscores = (probs * dprobs).astype(BF16)
            _, _, _, _, q_own, g_own = heads[h]
            step_v = dot_nn(probs.astype(BF16), g_own)
            step_k = dot_nn(dscores, q_own)
            step_q = dot_nn(key_t[h * HALF : (h + 1) * HALF, begin : begin + chunk], dscores)
            dq[h] = step_q if dq[h] is None else dq[h] + step_q
            if h == 0:
                dv, dk = step_v, step_k
            else:
                g, first = begin // rows, begin % rows
                own = slice(first, first + chunk)
                dk = ((dk + step_k) * (1.0 / LOG2E)).astype(BF16)
                dv = (dv + step_v).astype(BF16)
                if g < kept:
                    dkv_refs[g][0, own, :] = dk
                    dkv_refs[g][1, own, :] = dv
                else:
                    given[pair, 0, own, :] = dk
                    given[pair, 1, own, :] = dv
        dq_ref[...] = (jnp.concatenate(dq, axis=0).T * scale).astype(BF16)
        if swaps:
            part, column = heads_of.place(pair)
            columns = pl.ds(pl.multiple_of(column * PAIR, PAIR), PAIR)
            spot = (*heads_of.side(pair), part, slice(None), slice(None), columns)

            def swap(i):
                return remote(
                    given.at[i],
                    dkv_refs[1].at[spot],
                    swap_sems.at[0, i],
                    swap_sems.at[1, i],
                    where_is("near"),
                )

            swap(pair).start()

            @pl.when(pair == pairs - 1)
            def _():
                for i in range(pairs):
                    swap(i).wait()

        carry(slots)

    query_spec, kv_spec = heads_of.query_spec, heads_of.kv_spec
    lse_spec = heads_of.lse_spec()
    plain = jax.ShapeDtypeStruct(query.shape, BF16)
    plain_kv = jax.ShapeDtypeStruct(
        (*heads_of.sides, heads_of.parts, 2, rows, heads_of.part), BF16
    )
    hold = pl.BlockSpec(memory_space=pl.ANY)
    swap_scratch = [
        pltpu.VMEM((pairs, 2, rows, PAIR), BF16),
        pltpu.SemaphoreType.DMA((2, pairs)),
    ]
    out = pl.pallas_call(
        kernel,
        grid=(pairs,),
        in_specs=[pl.BlockSpec(memory_space=pltpu.SMEM)]
        + [query_spec(a) for a in (query, mix, mix_grad)]
        + [lse_spec]
        + [kv_spec(piece) for piece in kv_pieces]
        + [hold] * n_carry,
        out_specs=[query_spec(plain)]
        + [kv_spec(plain_kv)] * kept
        + [hold] * (pieces - kept + len(carrier.outs)),
        scratch_shapes=[pltpu.VMEM((keys, PAIR), BF16)] * 4
        + [pltpu.VMEM((PAIR, keys), BF16)]
        + (swap_scratch if swaps else [])
        + carrier.scratch,
        out_shape=[plain] + [plain_kv] * pieces + carrier.outs,
        compiler_params=pltpu.CompilerParams(vmem_limit_bytes=VMEM, **carrier.params),
        cost_estimate=pl.CostEstimate(
            flops=40 * rows * keys * pairs * PAIR,
            bytes_accessed=16 * rows * pairs * PAIR * pieces,
            transcendentals=0,
        ),
        name="attend_back",
    )(
        span.lengths if isinstance(span, Lengths) else span,
        query.array,
        mix.array,
        mix_grad.array,
        lse,
        *[piece.array for piece in kv_pieces],
        *carrier.ins,
    )
    return out[0], out[1 : pieces + 1], out[pieces + 1 :]


def spots():
    return lax.axis_index("section"), lax.axis_index("dp"), lax.axis_index("tensor")


def dp_peer(group, level):
    return group + (1 << level) * (1 - 2 * ((group // (1 << level)) % 2))


def where_is(peer):
    section, group, tensor = spots()
    if peer == "near":
        return {"section": 1 - section}
    if peer == "over":
        return {"tensor": 1 - tensor}
    if peer == "cross":
        return {"section": 1 - section, "tensor": 1 - tensor}
    return {"dp": dp_peer(group, peer)}


def remote(source, target, sent, landed, where):
    return pltpu.make_async_remote_copy(
        src_ref=source,
        dst_ref=target,
        send_sem=sent,
        recv_sem=landed,
        device_id=where,
        device_id_type=pl.DeviceIdType.MESH,
    )


def greet(peers):
    barrier = pltpu.get_barrier_semaphore()
    for peer in peers:
        pl.semaphore_signal(
            barrier, inc=1, device_id=where_is(peer), device_id_type=pl.DeviceIdType.MESH
        )
    pl.semaphore_wait(barrier, len(peers))


class Carry:
    def __init__(self, tasks=(), collective=None):
        self.tasks = list(tasks)
        self.ins = [a for task in self.tasks for a in task.ins]
        self.outs = [a for task in self.tasks for a in task.outs]
        self.scratch = [a for task in self.tasks for a in task.scratch]
        self.peers = []
        for task in self.tasks:
            self.peers += [peer for peer in task.peers if peer not in self.peers]
        self.params = (
            dict(collective_id=collective, has_side_effects=True) if self.tasks else {}
        )

    def plan(self, steps, ins, outs, scratch):
        plan = {}
        if self.tasks:
            plan[0] = [lambda: greet(self.peers)]
        events = []
        for task in self.tasks:
            i, o, s = len(task.ins), len(task.outs), len(task.scratch)
            events += task.events(steps, ins[:i], outs[:o], scratch[:s])
            ins, outs, scratch = ins[i:], outs[o:], scratch[s:]
        for step, rank, action in sorted(events, key=lambda event: event[:2]):
            assert 0 <= step < steps
            plan.setdefault(steps if rank == LAST else step, []).append(action)
        return plan

    def run(self, place, slot, slots, steps, ins, outs, scratch):
        for step, actions in self.plan(steps, ins, outs, scratch).items():
            if step == steps:
                if slot == slots:

                    @pl.when(place == steps // slots - 1)
                    def _():
                        for action in actions:
                            action()

            elif step % slots == slot:

                @pl.when(place == step // slots)
                def _():
                    for action in actions:
                        action()


GROUP = ["near", "over", "cross"]


class RowCopies:
    def __init__(self, copies, arrivals, sems, room=None):
        self.copies, self.arrivals, self.room = copies, arrivals, room
        self.sent, self.landed, self.kept = sems

    def copy(self, i):
        source, target, slot, section, tensor, _ = self.copies[i]
        return remote(
            source,
            target,
            self.sent.at[i],
            self.landed.at[slot],
            {"section": section, "tensor": tensor},
        )

    def keep(self, i):
        source, target, slot = self.copies[i][:3]
        return pltpu.make_async_copy(
            source, target if self.room is None else self.room, self.kept.at[slot]
        )

    def keep_on(self):
        for i in range(len(self.copies)):

            @pl.when(self.here(i, True))
            def _():
                self.keep(i).wait()
                target, slot = self.copies[i][1:3]
                pltpu.make_async_copy(self.room, target, self.kept.at[slot]).start()

    def here(self, i, stays):
        section, _, tensor = spots()
        _, _, _, to_section, to_tensor, condition = self.copies[i]
        own = (to_section == section) & (to_tensor == tensor)
        return condition & (own if stays else jnp.logical_not(own))

    def start(self):
        for i in range(len(self.copies)):

            @pl.when(self.here(i, True))
            def _():
                self.keep(i).start()

            @pl.when(self.here(i, False))
            def _():
                self.copy(i).start()

    def wait_sent(self):
        for i in range(len(self.copies)):

            @pl.when(self.here(i, False))
            def _():
                self.copy(i).wait_send()

    def wait_arrival(self, i):
        section, _, tensor = spots()
        target, slot, from_section, from_tensor, condition = self.arrivals[i]
        own = (from_section == section) & (from_tensor == tensor)
        source = self.copies[0][0]

        @pl.when(condition & own)
        def _():
            stays = source if self.room is None else self.room
            pltpu.make_async_copy(stays, target, self.kept.at[slot]).wait()

        @pl.when(condition & jnp.logical_not(own))
        def _():
            remote(
                source, target, self.sent.at[0], self.landed.at[slot], where_is("near")
            ).wait_recv()


def row_sems(pieces=1):
    return [pltpu.SemaphoreType.DMA((2 * pieces,))] * 3


def spread_rows(source, target, sems, sides=(0, 1), room=None, pieces=1):
    section, _, tensor = spots()
    yes = section >= 0
    sends = yes if len(sides) == 2 else section == sides[0]
    count = source.shape[1] // pieces
    copies, arrivals = [], []
    for i in range(pieces):
        own = pl.ds(i * count, count)
        for row in range(2):
            slot = 2 * i + section
            copies.append(
                (source.at[row, own, :], target.at[section, own, :], slot, tensor, row, sends)
            )
        for side in sides:
            arrivals.append((target.at[side, own, :], 2 * i + side, side, section, yes))
    return RowCopies(copies, arrivals, sems, room)


def return_rows(source, target, sems, side, room):
    section, _, tensor = spots()
    copies = [(source, target.at[tensor], tensor, side, section, section >= 0)]
    arrivals = [(target.at[row], row, tensor, row, section == side) for row in range(2)]
    return RowCopies(copies, arrivals, sems, room)


class SpreadRows:
    peers = GROUP

    def __init__(self, array, sides, begin=0):
        self.ins, self.sides, self.begin = [array], sides, begin
        self.outs = [jax.ShapeDtypeStruct(array.shape, array.dtype)]
        self.scratch = [
            *row_sems(),
            pltpu.VMEM(array.shape, array.dtype),
            pltpu.SemaphoreType.DMA((2,)),
        ]

    def events(self, steps, ins, outs, scratch):
        room, sems = scratch[3], scratch[4]

        def make():
            return spread_rows(ins[0], room, scratch[:3], self.sides)

        def store(side):
            return pltpu.make_async_copy(room.at[side], outs[0].at[side], sems.at[side])

        def arrive():
            rows = make()
            for i, side in enumerate(self.sides):
                rows.wait_arrival(i)
                store(side).start()

        def finish():
            for side in self.sides:
                store(side).wait()
            make().wait_sent()

        return [
            (self.begin, 1, lambda: make().start()),
            (steps - 1, 1, arrive),
            (steps - 1, LAST, finish),
        ]


class ReturnRows:
    peers = GROUP

    def __init__(self, array, side, begin=0, staged=True):
        self.ins, self.side, self.begin, self.staged = [array], side, begin, staged
        self.outs = [jax.ShapeDtypeStruct((2, *array.shape), array.dtype)]
        self.scratch = row_sems() + [pltpu.VMEM(array.shape, array.dtype)] * staged

    def events(self, steps, ins, outs, scratch):
        def make():
            room = scratch[3] if self.staged else None
            return return_rows(ins[0], outs[0], scratch[:3], self.side, room)

        def finish():
            rows = make()
            for i in range(len(rows.arrivals)):
                rows.wait_arrival(i)
            rows.wait_sent()

        events = [(self.begin, 1, lambda: make().start()), (steps - 1, LAST, finish)]
        if self.staged:
            events.append((self.begin + 1, 1, lambda: make().keep_on()))
        return events


class WeightCopies:
    @staticmethod
    def sems(count):
        return pltpu.SemaphoreType.DMA((3 + 8 * count,))

    def __init__(self, source, target, sem, room=None, count=1):
        section, group, _ = spots()
        rows = source.shape[0] // (2 * count)
        bit = group % 2
        here, stays = target.at[section, 1], target.at[section, 0]
        self.room = room
        if room is None:
            self.kept = pltpu.make_async_copy(source, stays, sem.at[0])
        else:
            self.first = pltpu.make_async_copy(source, room, sem.at[0])
            self.kept = pltpu.make_async_copy(room, stays, sem.at[0])
        self.near = remote(source, stays, sem.at[1], sem.at[2], where_is("near"))
        self.over, self.side, self.onward, self.last = [], [], [], []
        for i in range(count):
            own = pl.ds(pl.multiple_of((bit * count + i) * rows, 16), rows)
            other = pl.ds(pl.multiple_of(((1 - bit) * count + i) * rows, 16), rows)
            source_own, own, other = source.at[own], here.at[own], here.at[other]
            pairs = [(sem.at[3 + 8 * i + 2 * j], sem.at[4 + 8 * i + 2 * j]) for j in range(4)]
            self.over.append(remote(source_own, own, *pairs[0], where_is("over")))
            self.side.append(remote(own, own, *pairs[1], where_is(0)))
            self.onward.append(remote(own, own, *pairs[2], where_is("near")))
            self.last.append(remote(other, other, *pairs[3], where_is("near")))

    def start(self):
        for copy in self.over:
            copy.start()
        self.near.start()
        if self.room is None:
            self.kept.start()
        else:
            self.first.start()

    def keep_on(self):
        self.first.wait()
        self.kept.start()

    def forward(self, i):
        self.over[i].wait_recv()
        self.side[i].start()
        self.onward[i].start()

    def forward_last(self, i):
        self.side[i].wait_recv()
        self.last[i].start()

    def finish(self):
        self.kept.wait()
        self.near.wait()
        for over, side, onward, last in zip(self.over, self.side, self.onward, self.last):
            over.wait_send()
            side.wait_send()
            onward.wait()
            last.wait()


class SpreadWeight:
    peers = ["near", "over", 0]

    def __init__(self, weight, forwards, lasts):
        self.ins = [weight]
        self.outs = [jax.ShapeDtypeStruct((2, 2, *weight.shape), weight.dtype)]
        self.forwards, self.lasts = forwards, lasts
        self.scratch = [
            WeightCopies.sems(len(forwards)),
            pltpu.VMEM(weight.shape, weight.dtype),
        ]

    def events(self, steps, ins, outs, scratch):
        def copies():
            return WeightCopies(ins[0], outs[0], *scratch, len(self.forwards))

        def forward(i):
            return lambda: copies().forward(i)

        def forward_last(i):
            return lambda: copies().forward_last(i)

        return (
            [(0, 0, lambda: copies().start()), (1, 0, lambda: copies().keep_on())]
            + [(when, 1, forward(i)) for i, when in enumerate(self.forwards)]
            + [(when, 2, forward_last(i)) for i, when in enumerate(self.lasts)]
            + [(steps - 1, LAST, lambda: copies().finish())]
        )


class Reduce:
    def __init__(self, source, chunk, begins, pace, only=None, levels=None):
        self.ins = [source]
        self.chunk, self.begins, self.only = chunk, begins, only
        self.count = source.shape[-2] // chunk
        assert self.count == len(begins)
        self.levels = list(range(lax.axis_size("dp").bit_length() - 1))
        if levels is not None:
            self.levels = levels
        depth = len(self.levels)
        self.peers = []
        self.stages = []
        if only != "slice":
            self.peers += ["near", "over"]
            self.stages += ["enter", "cross", "over"]
        if only != "chip":
            self.peers += ["near", *self.levels]
            self.stages += ["load", "loaded"] if only == "slice" else []
            self.stages += [("halve", i) for i in range(depth)]
            self.stages += [("double", i) for i in reversed(range(depth))]
        assert len(pace) == len(self.stages) - 1
        self.dues = [sum(pace[:i]) for i in range(len(self.stages))]
        width = source.shape[-1]
        whole = jax.ShapeDtypeStruct((self.count * chunk, width), BF16)
        self.outs = [whole] if only == "chip" else [whole] * 2

        def room(*shape):
            return pltpu.VMEM((self.count, *shape, width), BF16)

        self.scratch = [room(2, chunk)]
        if only != "slice":
            self.scratch += [room(2, chunk), room(chunk)]
        if only != "chip":
            halves = [room(chunk >> (i + 1)) for i in range(depth)]
            self.scratch += [room(chunk)] + halves + halves
        self.scratch += [pltpu.SemaphoreType.DMA((2 + 2 * (3 + 2 * depth), self.count))]

    def events(self, steps, ins, outs, scratch):
        chunk, depth = self.chunk, len(self.levels)
        source, refs = ins[0], list(scratch)
        own, sems = refs[0], refs[-1]
        refs = refs[1:-1]
        if self.only != "slice":
            chip, other = refs[:2]
            refs = refs[2:]
        if self.only != "chip":
            full, halves, doubles = refs[0], refs[1 : 1 + depth], refs[1 + depth :]

        def bounds(i):
            _, group, _ = spots()
            begin = 0
            for j in range(i):
                bit = (group // (1 << self.levels[j])) % 2
                begin = begin + bit * (chunk >> (j + 1))
            return begin

        def keeps(i):
            return pl.ds(pl.multiple_of(bounds(i + 1), 16), chunk >> (i + 1))

        def gives(i):
            begin = 2 * bounds(i) + (chunk >> (i + 1)) - bounds(i + 1)
            return pl.ds(pl.multiple_of(begin, 16), chunk >> (i + 1))

        def pair(kind, c):
            return sems.at[2 + 2 * kind, c], sems.at[3 + 2 * kind, c]

        def rows_of(c):
            return pl.ds(c * chunk, chunk)

        def load(c):
            if self.only == "slice":
                return pltpu.make_async_copy(
                    source.at[rows_of(c), :], own.at[c, 0], sems.at[0, c]
                )
            section, _, _ = spots()
            return pltpu.make_async_copy(
                source.at[section, :, rows_of(c), :], own.at[c], sems.at[0, c]
            )

        def cross(c):
            section, _, _ = spots()
            return remote(
                source.at[1 - section, :, rows_of(c), :],
                chip.at[c],
                *pair(0, c),
                where_is("near"),
            )

        def over(c):
            return remote(own.at[c, 1], other.at[c], *pair(1, c), where_is("over"))

        def halve(i, c):
            return remote(
                own.at[c, 0, gives(i), :],
                halves[i].at[c],
                *pair(3 + i, c),
                where_is(self.levels[i]),
            )

        def double(i, c):
            return remote(
                full.at[c, keeps(i), :],
                doubles[i].at[c],
                *pair(3 + depth + i, c),
                where_is(self.levels[i]),
            )

        def store(c):
            kept = own.at[c, 0] if self.only == "chip" else full.at[c]
            return pltpu.make_async_copy(kept, outs[0].at[rows_of(c), :], sems.at[1, c])

        def tell(c):
            return remote(
                full.at[c], outs[1].at[rows_of(c), :], *pair(2, c), where_is("near")
            )

        def act(stage, c):
            if stage == "enter":
                load(c).start()
                cross(c).start()
            elif stage == "load":
                load(c).start()
            elif stage == "loaded":
                load(c).wait()
                halve(0, c).start()
            elif stage == "cross":
                load(c).wait()
                cross(c).wait()
                own[c] = own[c] + chip[c]
                over(c).start()
            elif stage == "over":
                over(c).wait()
                own[c, 0] = own[c, 0] + other[c]
                if self.only == "chip":
                    store(c).start()
                else:
                    halve(0, c).start()
            elif stage[0] == "halve":
                i = stage[1]
                halve(i, c).wait()
                mine = keeps(i)
                total = own[c, 0, mine, :] + halves[i][c]
                if i < depth - 1:
                    own[c, 0, mine, :] = total
                    halve(i + 1, c).start()
                else:
                    full[c, mine, :] = total
                    double(i, c).start()
            else:
                i = stage[1]
                double(i, c).wait()
                full[c, gives(i), :] = doubles[i][c]
                if i:
                    double(i - 1, c).start()
                else:
                    store(c).start()
                    tell(c).start()

        def leave(c):
            store(c).wait()
            if self.only != "chip":
                tell(c).wait()

        events = []
        for c, begin in enumerate(self.begins):
            for i, (stage, due) in enumerate(zip(self.stages, self.dues)):
                events.append((begin + due, -i, functools.partial(act, stage, c)))
            events.append((steps - 1, LAST, functools.partial(leave, c)))
        return events


def close_down(x, firsts, q_grad, kv_grads, norm, qkv, norm_grads, schedule, collective):
    _, rows, width = x.shape
    parts, _, _, part = qkv.shape[1:]
    half = 3 * width // 2
    shapes = [(2, parts, 2 * half + extra, PAIR) for extra in (2 * PAIR, 0)]
    dec_steps, enc_steps, returns, steps = schedule
    whole = (rows, width)
    grad_shape = jax.ShapeDtypeStruct(whole, BF16)
    carrier = Carry(
        [
            Reduce(jax.ShapeDtypeStruct(shapes[0], BF16), 2 * PAIR, *enc_steps),
            Reduce(jax.ShapeDtypeStruct(shapes[1], BF16), 2 * PAIR, *dec_steps),
            ReturnRows(grad_shape, 0, returns[0], False),
            ReturnRows(grad_shape, 1, returns[1], False),
        ],
        collective,
    )
    halves = 2
    count, sub = rows // halves, min(256, rows // halves)

    def kernel(*refs):
        x_in, first_ins, q_in, kv_ins, norm_in, qkv_in, refs = (
            refs[0],
            refs[1:3],
            refs[3],
            refs[4:6],
            refs[6],
            refs[7],
            refs[8:],
        )
        norm_grad_refs, refs = refs[: len(norm_grads)], refs[len(norm_grads) :]
        outs, refs = refs[: len(carrier.outs)], refs[len(carrier.outs) :]
        x_room, first_room, q_room, kv_room, norm_room, qkv_room, sems = refs[:7]
        low, keys, total, grads, enc_sum, dec_sum, *rest = refs[7:]
        ins = [enc_sum, dec_sum, grads.at[0], grads.at[1]]
        plan = carrier.plan(steps, ins, outs, rest)
        loads = []

        def load(source, target):
            copy = pltpu.make_async_copy(source, target, sems.at[len(loads)])
            copy.start()
            loads.append(copy)
            return copy

        arrivals = {}
        for side in (1, 0):
            for i in range(halves):
                own = pl.ds(i * count, count)
                arrivals[side, i] = [
                    load(first_ins[side].at[own, :], first_room.at[side, own, :]),
                    load(q_in.at[side, :, own, :], q_room.at[side, :, own, :]),
                    load(kv_ins[0].at[side, :, :, own, :], kv_room.at[0, side, :, :, own, :]),
                    load(kv_ins[1].at[side, :, :, own, :], kv_room.at[1, side, :, :, own, :]),
                    load(x_in.at[side, own, :], x_room.at[side, own, :]),
                ]
                if i == 0:
                    arrivals[side, i] += [
                        load(qkv_in.at[side], qkv_room.at[side]),
                        load(norm_in.at[side], norm_room.at[side]),
                    ]
        total[...] = jnp.zeros_like(total)

        def piece(side, i):
            for copy in arrivals[side, i]:
                copy.wait()
            kept = low, keys, total
            refs = (
                x_room.at[side],
                first_room.at[side],
                [kv_room.at[0, side], kv_room.at[1, side]],
                q_room.at[side],
                grads.at[side],
            )
            w = [qkv_room.at[side, k] for k in range(parts)]
            turns = []
            for begin in range(i * count, (i + 1) * count, sub):
                own = slice(begin, begin + sub)
                turns.append(
                    input_part(refs, kept, own, own, norm_room.at[side], w, side == 0)
                )
            while turns:
                turns = [turn for turn in turns if next(turn, LAST) is not LAST]
            if i == halves - 1:
                into = (enc_sum, dec_sum)[side]
                input_sums(kept, q_room.at[side], into, parts)
                if side == 0:
                    sides = [
                        norm_grad_refs[0][...] + total[...],
                        sum(ref[...] for ref in norm_grad_refs[1:]),
                    ]
                    norm_lines(sides, into, parts, 2 * half)

        for step in range(steps + 1):
            for action in plan.get(step, []):
                action()
            if step < 2 * halves:
                piece(1 - step // halves, step % halves)

    hold = pl.BlockSpec(memory_space=pl.ANY)
    vmem = pl.BlockSpec(memory_space=pltpu.VMEM)
    arrays = [x, *firsts, q_grad, *kv_grads, norm, qkv]
    rooms = [
        pltpu.VMEM(x.shape, BF16),
        pltpu.VMEM((2, *whole), F32),
        pltpu.VMEM(q_grad.shape, BF16),
        pltpu.VMEM((2, *kv_grads[0].shape), BF16),
        pltpu.VMEM(norm.shape, F32),
        pltpu.VMEM(qkv.shape, BF16),
        pltpu.SemaphoreType.DMA((2 * (5 * halves + 2),)),
        pltpu.VMEM(whole, BF16),
        pltpu.VMEM((parts, 2, rows, part), BF16),
        pltpu.VMEM((3, 2, width), F32),
        pltpu.VMEM((2, *whole), BF16),
        pltpu.VMEM(shapes[0], BF16),
        pltpu.VMEM(shapes[1], BF16),
    ]
    return pl.pallas_call(
        kernel,
        in_specs=[hold] * len(arrays) + [vmem] * len(norm_grads),
        out_specs=[hold] * len(carrier.outs),
        out_shape=carrier.outs,
        scratch_shapes=rooms + carrier.scratch,
        compiler_params=pltpu.CompilerParams(vmem_limit_bytes=VMEM, **carrier.params),
        name="close_down",
    )(*arrays, *norm_grads)


def lay_out(pairs, singles, shapes, finish):
    arrays = [array for pair in pairs for array in pair] + [single[0] for single in singles]
    spans = [(0, min(a.shape[0], b.shape[0])) for a, b in pairs] + [s[1:] for s in singles]
    loaded = [
        jax.ShapeDtypeStruct((span[1], *array.shape[1:]), array.dtype)
        for array, span in zip([a for a, _ in pairs] + [s[0] for s in singles], spans)
    ]

    def kernel(*refs):
        ins, outs = refs[: len(arrays)], refs[len(arrays) : len(arrays) + len(shapes)]
        refs = refs[len(arrays) + len(shapes) :]
        rooms, refs = refs[: len(loaded)], refs[len(loaded) :]
        out_rooms, load_sems, store_sems = refs[: len(shapes)], refs[-2], refs[-1]
        section = lax.axis_index("section")

        def load(i, choice):
            source = ins[2 * i + choice] if i < len(pairs) else ins[len(pairs) + i]
            return pltpu.make_async_copy(
                source.at[pl.ds(*spans[i])], rooms[i], load_sems.at[i]
            )

        for i in range(len(loaded)):
            if i < len(pairs):

                @pl.when(section == 0)
                def _():
                    load(i, 0).start()

                @pl.when(section != 0)
                def _():
                    load(i, 1).start()

            else:
                load(i, 0).start()
        stores = []

        def fetch(i):
            load(i, 0).wait()
            return rooms[i]

        for i, room in enumerate(finish(fetch, out_rooms)):
            copy = pltpu.make_async_copy(room, outs[i], store_sems.at[i])
            copy.start()
            stores.append(copy)
        for copy in stores:
            copy.wait()

    hold = pl.BlockSpec(memory_space=pl.ANY)
    return pl.pallas_call(
        kernel,
        in_specs=[hold] * len(arrays),
        out_specs=[hold] * len(shapes),
        out_shape=[jax.ShapeDtypeStruct(*s) for s in shapes],
        scratch_shapes=[pltpu.VMEM(a.shape, a.dtype) for a in loaded]
        + [pltpu.VMEM(*s) for s in shapes]
        + [pltpu.SemaphoreType.DMA((len(loaded),)), pltpu.SemaphoreType.DMA((len(shapes),))],
        compiler_params=pltpu.CompilerParams(vmem_limit_bytes=VMEM),
        name="lay_out",
    )(*arrays)


def open_up(tokens, qkv, norm, block, collective):
    _, rows, width = tokens.shape
    part = qkv.shape[-1]
    score = LOG2E / math.sqrt(width // HEADS)
    count = min(block, rows)
    pieces = rows // count

    def kernel(tokens_ref, qkv_ref, norm_ref, *refs):
        x_out, w_out, n_out, q_out, own_out, other_out = refs[:6]
        x, w, n, q, kv = refs[6:11]
        row_sems_, weight_sems, norm_sems, store_sems, kv_sems = (
            refs[11:14],
            refs[14:15],
            refs[15],
            refs[16],
            refs[17],
        )
        section, _, _ = spots()
        greet([*GROUP, 0])
        rows_in = spread_rows(tokens_ref, x, row_sems_, pieces=pieces)
        weight = WeightCopies(qkv_ref, w, weight_sems[0])
        weight.start()
        rows_in.start()
        norm_kept = pltpu.make_async_copy(norm_ref, n.at[section], norm_sems.at[0])
        norm_near = remote(
            norm_ref, n.at[section], norm_sems.at[1], norm_sems.at[2], where_is("near")
        )
        norm_kept.start()
        norm_near.start()
        stores, kv_copies = [], []

        def save(source, target):
            copy = pltpu.make_async_copy(source, target, store_sems.at[len(stores)])
            copy.start()
            stores.append(copy)

        def project(side, own, rows_low):
            for k in range(2):

                def product(m):
                    return dot_nn(rows_low, w[side, k, m * width : (m + 1) * width, :])

                q[side, k, own, :] = (product(0) * score).astype(BF16)
                kv[side, k, 0, own, :] = product(1).astype(BF16)
                kv[side, k, 1, own, :] = product(2).astype(BF16)

        norm_kept.wait()
        norm_near.wait()
        save(n, n_out)
        weight.forward(0)
        weight.forward_last(0)
        weight.finish()
        save(w, w_out)
        for i in range(pieces):
            own = slice(i * count, (i + 1) * count)
            for side in range(2):
                rows_in.wait_arrival(2 * i + side)
                rows_low = x[side, own, :]
                if side == 0:
                    unit, _ = standardize(rows_low.astype(F32))
                    rows_low = affine(unit, n.at[0], 2).astype(BF16)
                project(side, own, rows_low)
                copy = remote(
                    kv.at[side, :, :, own, :],
                    other_out.at[side, :, :, own, :],
                    kv_sems.at[0, 2 * i + side],
                    kv_sems.at[1, 2 * i + side],
                    where_is("near"),
                )
                copy.start()
                kv_copies.append(copy)
                save(x.at[side, own, :], x_out.at[side, own, :])
                save(kv.at[side, :, :, own, :], own_out.at[side, :, :, own, :])
                save(q.at[side, :, own, :], q_out.at[side, :, own, :])
        rows_in.wait_sent()
        for copy in kv_copies + stores:
            copy.wait()

    hold = pl.BlockSpec(memory_space=pl.ANY)
    shapes = [
        ((2, rows, width), BF16),
        ((2, 2, *qkv.shape), BF16),
        ((2, *norm.shape), F32),
        ((2, 2, rows, part), BF16),
        ((2, 2, 2, rows, part), BF16),
    ]
    return pl.pallas_call(
        kernel,
        in_specs=[hold] * 3,
        out_specs=[hold] * 6,
        out_shape=[jax.ShapeDtypeStruct(*s) for s in shapes + shapes[-1:]],
        scratch_shapes=[pltpu.VMEM(*s) for s in shapes]
        + row_sems(pieces)
        + [WeightCopies.sems(1)]
        + [
            pltpu.SemaphoreType.DMA((3,)),
            pltpu.SemaphoreType.DMA((6 * pieces + 2,)),
            pltpu.SemaphoreType.DMA((2, 2 * pieces)),
        ],
        compiler_params=pltpu.CompilerParams(
            vmem_limit_bytes=VMEM, collective_id=collective, has_side_effects=True
        ),
        name="open_up",
    )(tokens, qkv, norm)


def local_general(tokens, lengths, self_qkv, self_out, cross_proj, ffn_up, ffn_down, norms, cotangent):
    section = lax.axis_index("section")
    tensor = lax.axis_index("tensor")
    tensors = lax.axis_size("tensor")
    _, row_count, rows, width = tokens.shape
    assert row_count == 2 and tensors % row_count == 0
    spread = tensors // row_count
    pieces = 2 * spread
    axes = ("section", "tensor")
    is_first = section == 0
    own_row = tensor // spread
    place = section * spread + tensor % spread

    def device(row, spot):
        return (spot // spread) * tensors + row * spread + spot % spread

    def each():
        return [(s, t) for s in range(2) for t in range(tensors)]

    straight = [(s * tensors + t, device(s, t)) for s, t in each()]
    turned = [(s * tensors + t, device(1 - s, t)) for s, t in each()]

    def bring(shares):
        stays = lax.dynamic_index_in_dim(shares, section, 0, keepdims=False)
        moves = lax.dynamic_index_in_dim(shares, 1 - section, 0, keepdims=False)
        one = lax.ppermute(stays, axes, straight)
        two = lax.ppermute(moves, axes, turned)
        return jnp.where(own_row == 0, one, two), jnp.where(own_row == 0, two, one)

    def take_back(source, target):
        one = jnp.where(own_row == 0, source, target)
        two = jnp.where(own_row == 0, target, source)
        one = lax.ppermute(one, axes, [(b, a) for a, b in straight])
        two = lax.ppermute(two, axes, [(b, a) for a, b in turned])
        return jnp.stack([jnp.where(is_first, one, two), jnp.where(is_first, two, one)])

    def rotate(value, by):
        pairs = [
            (device(r, p), device(r, (p + by) % pieces))
            for r in range(row_count)
            for p in range(pieces)
        ]
        return lax.ppermute(value, axes, pairs)

    def pieces_of(value):
        return [value] + [rotate(value, by) for by in range(1, pieces)]

    def pieces_home(values):
        return [values[0]] + [rotate(values[by], -by) for by in range(1, pieces)]

    def swap_sections(value):
        return lax.ppermute(value, "section", [(0, 1), (1, 0)])

    def both_sides(weight, dim):
        if spread == 1:
            other = lax.ppermute(weight, "tensor", [(t, 1 - t) for t in range(tensors)])
            parts = [weight, other]
        else:
            parts = [lax.all_gather(weight, "tensor", axis=dim, tiled=True)]
        swapped = [swap_sections(part) for part in parts]
        pairs = list(zip(parts, swapped))
        return (
            [jnp.where(is_first, mine, theirs) for mine, theirs in pairs],
            [jnp.where(is_first, theirs, mine) for mine, theirs in pairs],
        )

    def home(source_grad, target_grad, dim):
        keep = jnp.where(is_first, source_grad, target_grad).astype(F32)
        sent = swap_sections(jnp.where(is_first, target_grad, source_grad))
        total = (keep + sent.astype(F32)).astype(BF16)
        if spread == 1:
            other = lax.ppermute(total[1], "tensor", [(t, 1 - t) for t in range(tensors)])
            total = (total[0].astype(F32) + other.astype(F32)).astype(BF16)
        else:
            total = lax.psum_scatter(total[0], "tensor", scatter_dimension=dim, tiled=True)
        return total

    def span_of(query_side, key_side):
        own = lax.dynamic_index_in_dim(lengths, own_row, 1, keepdims=False)
        asks, answers = own[query_side], own[key_side]
        paired = asks[1] > 0
        second = paired & (place * rows >= asks[0])
        begin = jnp.where(second, answers[0], 0)
        end = jnp.where(second | ~paired, answers[0] + answers[1], answers[0])
        offsets = [(place - by) % pieces * rows for by in range(pieces)]
        return jnp.stack([begin, end, *offsets]).astype(jnp.int32)[None]

    query_block = min(256, rows)
    chunk = 256

    source, target = bring(tokens[0])
    source_norm, target_norm = (
        jnp.where(is_first, a, b)
        for a, b in (lambda own, other: ((own, other), (other, own)))(
            norms[0], swap_sections(norms[0])
        )
    )
    source_qkv, target_qkv = both_sides(self_qkv[0], 2)
    source_out, target_out = both_sides(self_out[0], 0)
    source_up, target_up = both_sides(ffn_up[0], 1)
    source_down, target_down = both_sides(ffn_down[0], 0)
    source_cross, target_cross = both_sides(cross_proj[0], 2)
    source_cot, target_cot = bring(cotangent[0])
    source_span, target_span, cross_span = span_of(0, 0), span_of(1, 1), span_of(1, 0)

    enc_q, enc_kv = project_qkv(source, source_norm, source_qkv, True)
    enc_kv = pieces_of(enc_kv)
    dec_q, dec_kv = project_qkv(target, target_norm, target_qkv, False)
    dec_kv = pieces_of(dec_kv)
    enc_mix, enc_lse = attend(enc_q, enc_kv, source_span, query_block)
    encoded, memory, enc_first, enc_third = encoder_forward(
        source, enc_mix, source_norm, source_out, source_up, source_down, source_cross
    )
    memory = pieces_of(memory)
    dec_mix, dec_lse = attend(dec_q, dec_kv, target_span, query_block)
    cross_q, dec_first = decoder_middle(
        target, dec_mix, target_norm, target_out, target_cross
    )
    cross_mix, cross_lse = attend(cross_q, memory, cross_span, query_block)
    decoded, second_grad, cross_mix_grad, cross_out_grad, dec_up, dec_down, dec_norm = decoder_turn(
        dec_first, cross_mix, target_cot, target_norm, target_cross, target_up, target_down
    )
    result = take_back(encoded, decoded)
    cross_q_grad, memory_grads, _ = attend_back(
        cross_q, memory, cross_mix, cross_mix_grad, cross_lse, cross_span, chunk
    )
    memory_grads = pieces_home(memory_grads)
    dec_first_grad, dec_mix_grad, cross_query_grad, dec_out, step = decoder_middle_back(
        dec_first,
        dec_mix,
        cross_q_grad,
        second_grad,
        target_norm,
        target_out,
        target_cross
    )
    dec_norm += step
    enc_first_grad, enc_mix_grad, enc_cross, enc_out, enc_up, enc_down, enc_norm = encoder_back(
        enc_first,
        enc_third,
        enc_mix,
        memory_grads,
        source_cot,
        source_norm,
        source_out,
        source_up,
        source_down,
        source_cross
    )
    dec_cross = jnp.stack([cross_query_grad, cross_out_grad], axis=1)
    up_grad, down_grad = home(enc_up, dec_up, 1), home(enc_down, dec_down, 0)
    out_grad, cross_grad = home(enc_out, dec_out, 0), home(enc_cross, dec_cross, 2)
    dec_q_grad, dec_kv_grads, _ = attend_back(
        dec_q, dec_kv, dec_mix, dec_mix_grad, dec_lse, target_span, chunk
    )
    dec_kv_grads = pieces_home(dec_kv_grads)
    enc_q_grad, enc_kv_grads, _ = attend_back(
        enc_q, enc_kv, enc_mix, enc_mix_grad, enc_lse, source_span, chunk
    )
    enc_kv_grads = pieces_home(enc_kv_grads)
    target_grad, dec_qkv, _ = input_back(
        target, dec_first_grad, dec_q_grad, dec_kv_grads, target_norm, target_qkv, False
    )
    source_grad, enc_qkv, step = input_back(
        source, enc_first_grad, enc_q_grad, enc_kv_grads, source_norm, source_qkv, True
    )
    enc_norm += step
    token_grad = take_back(source_grad, target_grad).astype(F32)
    qkv_grad = home(enc_qkv, dec_qkv, 2)
    norm_total = lax.psum(jnp.stack([enc_norm, dec_norm]), ("section", "dp", "tensor"))
    norm_grad = lax.dynamic_index_in_dim(norm_total, section, 0, keepdims=False)
    summed = [
        lax.psum(grad, "dp").astype(F32)
        for grad in (qkv_grad, out_grad, cross_grad, up_grad, down_grad)
    ]
    return (
        result[None],
        token_grad[None],
        summed[0][None],
        summed[1][None],
        summed[2][None],
        summed[3][None],
        summed[4][None],
        norm_grad[None],
    )


def local_fast(tokens, lengths, self_qkv, self_out, cross_proj, ffn_up, ffn_down, norms, cotangent):
    _, row_count, rows, width = tokens.shape
    assert row_count == 2
    block = min(256, rows)
    query_block = min(256, rows)
    chunk = 256
    levels = lax.axis_size("dp").bit_length() - 1

    def hops(*steps):
        return list(steps[:levels]) + list(steps[3 : 3 + levels])

    def flat(weight):
        return weight.reshape(-1, weight.shape[-1])

    self_spans, cross_span = Lengths(lengths), Lengths(lengths, 1, 0)
    x, qkv, norm, q, *kv = open_up(tokens[0], flat(self_qkv), norms[0], block, 1)
    qkv = qkv.reshape(2, 2, *self_qkv.shape[1:])

    def parts(weight, side):
        return [At(weight, side, k) for k in range(2)]

    enc_x, dec_x, enc_norm_in, dec_norm_in = At(x, 0), At(x, 1), At(norm, 0), At(norm, 1)
    mix, lse, out, up, cross, down = attend(
        q,
        kv,
        self_spans,
        query_block,
        Carry(
            [
                SpreadWeight(self_out[0], [1], [3]),
                SpreadWeight(ffn_up[0], [2, 3], [4, 5]),
                SpreadWeight(flat(cross_proj), [4], [6]),
                SpreadWeight(ffn_down[0], [5, 6], [7, 7]),
            ],
            2,
        ),
    )
    cross = cross.reshape(2, 2, *cross_proj.shape[1:])
    enc_mix, dec_mix = At(mix, 0), At(mix, 1)
    encoded, memory, enc_first, enc_third, pushed = encoder_forward(
        enc_x,
        enc_mix,
        enc_norm_in,
        parts(out, 0),
        parts(up, 0),
        parts(down, 0),
        parts(cross, 0),
        8,
    )
    memory = [memory, pushed]
    cross_q, dec_first = decoder_middle(
        dec_x, dec_mix, dec_norm_in, parts(out, 1), parts(cross, 1)
    )
    cross_mix, cross_lse, dec_cot = attend(
        cross_q,
        memory,
        cross_span,
        query_block,
        Carry([SpreadRows(cotangent[0], (1,))], 4),
    )
    decoded, second_grad, cross_mix_grad, cross_out_grad, ffn_dec, dec_norm = decoder_turn(
        dec_first,
        cross_mix,
        At(dec_cot, 1),
        dec_norm_in,
        parts(cross, 1),
        parts(up, 1),
        parts(down, 1),
        True,
    )
    cross_q_grad, memory_grads, (ffn_dec, enc_cot) = attend_back(
        cross_q,
        memory,
        cross_mix,
        cross_mix_grad,
        cross_lse,
        cross_span,
        2 * chunk,
        Carry(
            [
                Reduce(ffn_dec, 256, [0, 1, 2, 3], [1, 2], "chip"),
                SpreadRows(cotangent[0], (0,), 4),
            ],
            5,
        ),
        2,
    )
    dec_first_grad, mix_grad, cross_query_grad, dec_out, mid_norm = decoder_middle_back(
        dec_first,
        dec_mix,
        cross_q_grad,
        second_grad,
        dec_norm_in,
        parts(out, 1),
        parts(cross, 1),
        (1, None),
    )
    enc_first_grad, mix_grad, ffn_enc, sides, enc_norm = encoder_back(
        enc_first,
        enc_third,
        enc_mix,
        memory_grads,
        At(enc_cot, 0),
        enc_norm_in,
        parts(out, 0),
        parts(up, 0),
        parts(down, 0),
        parts(cross, 0),
        [dec_out, cross_query_grad, cross_out_grad],
        (0, mix_grad),
    )
    q_grad, kv_grads, moved = attend_back(
        q,
        kv,
        mix,
        mix_grad,
        lse,
        self_spans,
        chunk,
        Carry(
            [
                Reduce(ffn_dec, 512, [0, 1], [1, *hops(2, 1, 1, 1, 2, 3)], "slice"),
                Reduce(ffn_enc, 512, [2, 0], [1, 3, *hops(2, 1, 2, 1, 1, 2)]),
                Reduce(sides, 768, [3, 1], [1, 3, *hops(1, 2, 1, 2, 1, 1)]),
                ReturnRows(encoded, 0, 11),
                ReturnRows(decoded, 1, 12),
            ],
            6,
        ),
        2,
    )
    ffn_dec, ffn_dec_other, ffn_enc, ffn_enc_other, sides, _, encoded, decoded = moved
    tail = (
        ([2, 2, 2, 2, 3, 2], [1, 3, *hops(1, 1, 1, 1, 1, 3)]),
        ([4, 4, 4, 4, 5, 5, 5], [1, 2, *hops(1, 1, 1, 1, 1, 2)]),
        (7, 6),
        10 + 2 * levels,
    )
    enc_last, enc_other, dec_last, dec_other, source_grad, target_grad = close_down(
        x,
        [enc_first_grad, dec_first_grad],
        q_grad,
        kv_grads,
        norm,
        qkv,
        [enc_norm, dec_norm, mid_norm],
        tail,
        7,
    )

    half = 3 * width // 2
    units = ffn_up.shape[-1]

    def columns(source, row, count, target, to):
        wide = source.shape[-1]
        for h in range(2):
            target[to : to + count, h * wide : (h + 1) * wide] = source[
                row + h * count : row + (h + 1) * count, :
            ].astype(F32)

    def finish(fetch, rooms):
        grads, result, up, down, first, second, side, norm_part = range(8)
        room = fetch(grads)
        for row in range(2):
            rooms[0][row] = room[row].astype(F32)
        yield rooms[0]
        yield fetch(result)
        columns(fetch(up), 0, width, rooms[2], 0)
        yield rooms[2]
        rooms[3][...] = fetch(down)[...].astype(F32)
        yield rooms[3]
        room = fetch(side)
        columns(room, 0, width // 2, rooms[4], 0)
        yield rooms[4]
        rooms[5][...] = room[width:, :].astype(F32)
        yield rooms[5]
        columns(fetch(first), 0, half, rooms[6], 0)
        columns(fetch(second), 0, half, rooms[6], half)
        yield rooms[6]
        lines = fetch(norm_part)[...].astype(F32)
        wide = width // PAIR
        for slot in range(3):
            for i in range(2):
                for h in range(wide):
                    line = (2 * slot + i) * wide + h
                    rooms[7][slot, i : i + 1, h * PAIR : (h + 1) * PAIR] = lines[
                        line : line + 1, :
                    ]
        yield rooms[7]

    part = qkv.shape[-1]
    token_grad, result, up_grad, down_grad, out_grad, cross_grad, qkv_grad, norm_grad = lay_out(
        [
            (source_grad, target_grad),
            (encoded, decoded),
            (ffn_enc, ffn_dec_other),
            (ffn_enc_other, ffn_dec),
            (enc_last, dec_other),
            (enc_other, dec_last),
        ],
        [(sides, 0, sides.shape[0]), (enc_last, 2 * half, 32)],
        [
            ((2, rows, width), F32),
            ((2, rows, width), BF16),
            ((width, units), F32),
            ((units, width), F32),
            ((part, width), F32),
            ((2 * width, part), F32),
            ((2 * half, part), F32),
            (norms.shape[1:], F32),
        ],
        finish,
    )
    return (
        result[None],
        token_grad[None],
        qkv_grad.reshape(self_qkv.shape),
        out_grad[None],
        cross_grad.reshape(cross_proj.shape),
        up_grad[None],
        down_grad[None],
        norm_grad[None],
    )


def solution(mesh):
    placed = (
        P("section", "dp", "tensor", None),
        P(None, "dp", None),
        P("section", None, None, "tensor"),
        P("section", "tensor", None),
        P("section", None, None, "tensor"),
        P("section", None, "tensor"),
        P("section", "tensor", None),
        P("section", None, None, None),
        P("section", "dp", "tensor", None),
    )
    sizes = dict(mesh.shape)
    steps = sizes["dp"].bit_length() - 1
    fast = sizes["tensor"] == 2 and sizes["dp"] == 1 << steps and 0 < steps <= 3
    return jax.shard_map(
        local_fast if fast else local_general,
        mesh=mesh,
        in_specs=placed,
        out_specs=(
            P("section", "dp", "tensor", None),
            P("section", "dp", "tensor", None),
            P("section", None, None, "tensor"),
            P("section", "tensor", None),
            P("section", None, None, "tensor"),
            P("section", None, "tensor"),
            P("section", "tensor", None),
            P("section", None, None, None),
        ),
        check_vma=False,
    )
```
